32 devices in a mesh: seq: 8 (over z, core), chan: 4 (over y, x).
Axes of the slice: x: 2, y: 2, z: 4, core: 2. Of those that a mesh axis runs over, the one named last changes fastest.
Arguments:
- mixer_input: bfloat16 [1024, 2048], P('seq', 'chan'), may hold values from -6 to 6
- gate_branch: bfloat16 [1024, 2048], P('seq', 'chan'), may hold values from -6 to 6
- skip_gain: float32 [2048], P('chan'), may hold values from -3 to 3
- decay_rate: float32 [2048], P('chan'), may hold values from 0.1 to 64
- first_weight: float32 [33, 64], replicated, may hold values from -1 to 1
- first_bias: float32 [64], replicated, may hold values from -4 to 4
- second_weight: float32 [64, 64], replicated, may hold values from -0.75 to 0.75
- second_bias: float32 [64], replicated, may hold values from -4 to 4
- last_weight: float32 [64, 2048], P(None, 'chan'), may hold values from -0.75 to 0.75
- output_weight: bfloat16 [2048, 4096], P('chan'), may hold values from -0.1875 to 0.1875
Outputs:
- projected: bfloat16 [1024, 4096], P('seq', 'chan')
The draws below stay inside these ranges and needn't reach their ends.
All inputs are finite; a program needn't handle non-finite values.
Results may differ from the reference program's by a relative error of at most 0.0049.
Values may be sent and summed in bfloat16 or wider, within the bound.
No kernel may reach another device: no remote copies, remote signals or barrier semaphores. Data moves between devices by JAX's collectives and lax.ppermute only.
A program may use at most 64 MiB of HBM per device.

```python
import math
import jax
import jax.numpy as jnp
from jax import lax

CHANNELS = 2048
D_MODEL = 4096
ORDER = 64
EMB = 33
SEQ = 1024


def draw_decay_rate(key, part):
    key_pick, key_slow, key_fast = jax.random.split(key, 3)
    keep_share = 0.5
    slow_rate = jax.random.uniform(key_slow, (CHANNELS,), jnp.float32, 0.1, 2.0)
    fast_rate = jnp.exp(jax.random.uniform(key_fast, (CHANNELS,), jnp.float32, math.log(2.0), math.log(SEQ / 16.0)))
    picked = jax.random.uniform(key_pick, (CHANNELS,), jnp.float32) < keep_share
    return jnp.where(picked, slow_rate, fast_rate)


def spiked(result, key, source, target, blocks, factor):
    owner, partner = [(jnp.arange(result.shape[dim]) // (result.shape[dim] // blocks)).reshape([-1 if axis == dim else 1 for axis in range(result.ndim)]) for dim in (source, target)]
    chosen = jax.random.permutation(key, blocks)[partner]
    strong = (owner == chosen) | (owner == (partner + blocks // 2) % blocks)
    return jnp.where(strong, factor * result, result)


def block_scale(rng, dims, shards, smallest, largest):
    gain = 1.0
    for position, shards_of in shards:
        heights = jax.random.uniform(jax.random.fold_in(jax.random.fold_in(rng, 6), position), (shards_of,), jnp.float32, smallest / len(shards), largest / len(shards))
        gain = gain * jnp.repeat(jnp.exp(heights), dims[position] // shards_of).reshape((-1,) + (1,) * (len(dims) - 1 - position))
    return gain


def centred(own_key, extent, scale, most, cuts=(), held_as=jnp.bfloat16):
    result = scale * jax.random.normal(own_key, extent, jnp.float32)
    if cuts:
        result = result * block_scale(own_key, extent, cuts, -0.22, 0.18)
    return jnp.clip(result, -most, most).astype(held_as)


def gaussian_with(rng, dims, width, limit, cuts, heavy, kind=jnp.bfloat16):
    drawn = width * jax.random.normal(rng, dims, jnp.float32)
    if cuts:
        drawn = drawn * block_scale(rng, dims, cuts, -0.22, 0.18)
    return jnp.clip(spiked(drawn, jax.random.fold_in(rng, 3), *heavy), -limit, limit).astype(kind)


def setup_inputs(seed: int = 0) -> dict:
    key_of = jax.random.split(jax.random.key(seed), 11)
    return {
        "mixer_input": centred(key_of[0], (SEQ, CHANNELS), 1.0, 6.0, ((0, 8), (1, 4))),
        "gate_branch": centred(key_of[1], (SEQ, CHANNELS), 1.0, 6.0, ((0, 8), (1, 4))),
        "skip_gain": centred(key_of[2], (CHANNELS,), 1.0, 3.0, ((0, 4),), jnp.float32),
        "decay_rate": draw_decay_rate(jax.random.fold_in(key_of[10], 71), 0),
        "first_weight": centred(key_of[4], (EMB, ORDER), EMB ** -0.5, 1.0, (), jnp.float32),
        "first_bias": centred(key_of[5], (ORDER,), 1.0, 4.0, (), jnp.float32),
        "second_weight": centred(key_of[6], (ORDER, ORDER), ORDER ** -0.5, 0.75, (), jnp.float32),
        "second_bias": centred(key_of[7], (ORDER,), 1.0, 4.0, (), jnp.float32),
        "last_weight": centred(key_of[8], (ORDER, CHANNELS), ORDER ** -0.5, 0.75, ((1, 4),), jnp.float32),
        "output_weight": gaussian_with(key_of[9], (CHANNELS, D_MODEL), CHANNELS ** -0.5, 0.1875, ((0, 4),), (0, 1, 4, 2.0)),
    }


def position_features(length, emb_width):
    band_count = (emb_width - 1) // 2
    positions = jnp.arange(length, dtype=jnp.int32)
    feature_rows = [positions.astype(jnp.float32) / length]
    for band_index in range(1, band_count + 1):
        frequency = min(length // 2, max(band_index, int((length / 2) ** ((band_index - 1) / (band_count - 1)))))
        phase_angle = (positions * frequency % length).astype(jnp.float32) * (2.0 * math.pi / length)
        feature_rows.append(jnp.cos(phase_angle))
        feature_rows.append(jnp.sin(phase_angle))
    return jnp.stack(feature_rows, axis=0)

def contract_first(left_matrix, right_matrix):
    return lax.dot_general(left_matrix, right_matrix, (((0,), (0,)), ((), ())), precision=lax.Precision.HIGHEST, preferred_element_type=jnp.float32)

def filter_taps(first_weight, first_bias, second_weight, second_bias, last_weight, decay_rate, length, emb_width):
    features = position_features(length, emb_width)
    hidden_one = jnp.sin(contract_first(first_weight, features) + first_bias[:, None])
    hidden_two = jnp.sin(contract_first(second_weight, hidden_one) + second_bias[:, None])
    shaped = contract_first(hidden_two, last_weight)
    positions = jnp.arange(length, dtype=jnp.int32).astype(jnp.float32)
    envelope = jnp.exp(-decay_rate[None, :] * (positions[:, None] / length))
    energy = jnp.expm1(-2.0 * decay_rate) / jnp.expm1(-2.0 * decay_rate / length)
    return shaped * envelope / jnp.sqrt(energy)[None, :]

def reference(mixer_input, gate_branch, skip_gain, decay_rate, first_weight, first_bias, second_weight, second_bias, last_weight, output_weight):
    kernel_taps = filter_taps(first_weight, first_bias, second_weight, second_bias, last_weight, decay_rate, SEQ, EMB)
    values = mixer_input.astype(jnp.float32)
    padded_length = 2 * SEQ
    spectrum = jnp.fft.rfft(values, n=padded_length, axis=0) * jnp.fft.rfft(kernel_taps, n=padded_length, axis=0)
    convolved = jnp.fft.irfft(spectrum, n=padded_length, axis=0)[:SEQ]
    gated_mix = (gate_branch.astype(jnp.float32) * (convolved + skip_gain[None, :] * values)).astype(jnp.bfloat16)
    return jnp.dot(gated_mix, output_weight, preferred_element_type=jnp.float32).astype(jnp.bfloat16)
```

```python
import functools
import math

import jax
import jax.numpy as jnp
import numpy as np
from jax import lax
from jax.experimental import pallas as pl
from jax.experimental.pallas import tpu as pltpu
from jax.sharding import PartitionSpec as P

HIGHEST = lax.Precision.HIGHEST
F32 = jnp.float32
BF16 = jnp.bfloat16
LANES = 128
VMEM = pltpu.VMEM


def feature_table(length, emb_width):
    band_count = (emb_width - 1) // 2
    positions = np.arange(length, dtype=np.int64)
    columns = [positions / length]
    for band in range(1, band_count + 1):
        frequency = min(
            length // 2, max(band, int((length / 2) ** ((band - 1) / (band_count - 1))))
        )
        angle = (positions * frequency % length) * (2.0 * math.pi / length)
        columns.append(np.cos(angle))
        columns.append(np.sin(angle))
    return np.stack(columns, axis=1).astype(np.float32)


def split_bf16(table):
    high = table.astype(np.float32).astype(jnp.bfloat16)
    low = (table - high.astype(np.float64)).astype(np.float32).astype(jnp.bfloat16)
    return high, low


def dft_tables(block):
    size = 2 * block
    bins = np.arange(block)[:, None]
    times = np.arange(block)[None, :]
    angle = (bins * times % size) * (2.0 * math.pi / size)
    imag = -np.sin(angle)
    imag[0] = 1.0 - 2.0 * (np.arange(block) % 2)
    forward = np.concatenate([np.cos(angle), imag], axis=0)
    weight = np.where(bins == 0, 1.0, 2.0) / size
    back_imag = -weight * np.sin(angle)
    back_imag[0] = (1.0 - 2.0 * (np.arange(block) % 2)) / size
    inverse = np.concatenate([weight * np.cos(angle), back_imag], axis=0).T
    return forward, inverse


def fast_sin(x):
    turns = jnp.floor(x * (1.0 / math.pi) + 0.5)
    rest = x - turns * 3.140625
    rest = rest - turns * 9.67502593994140625e-4
    rest = rest - turns * 1.509957990978376432e-7
    parity = turns - 2.0 * jnp.floor(turns * 0.5)
    rest = rest * (1.0 - 2.0 * parity)
    square = rest * rest
    poly = -2.5052108e-8
    for coeff in (2.7557319e-6, -1.9841270e-4, 8.3333333e-3, -1.6666667e-1):
        poly = poly * square + coeff
    return rest + rest * square * poly


def expm1_of_negative(x):
    near = jnp.maximum(x, -0.5)
    series = jnp.full_like(x, 1.0 / 3628800.0)
    for denom in (362880.0, 40320.0, 5040.0, 720.0, 120.0, 24.0, 6.0, 2.0, 1.0):
        series = series * near + 1.0 / denom
    return jnp.where(x > -0.5, near * series, jnp.exp(x) - 1.0)


def split_value(value):
    high = value.astype(BF16)
    return high, (value - high.astype(F32)).astype(BF16)


def filter_kernel(
    blocks,
    block,
    group_ref,
    feat_ref,
    w1_ref,
    b1_ref,
    w2_ref,
    b2_ref,
    w3_ref,
    decay_ref,
    table_ref,
    hre_ref,
    him_ref,
    hfirst_ref,
):
    length = blocks * block
    hidden = fast_sin(
        jnp.dot(feat_ref[...], w1_ref[...], precision=HIGHEST, preferred_element_type=F32)
        + b1_ref[...]
    )
    hidden = fast_sin(
        jnp.dot(hidden, w2_ref[...], precision=HIGHEST, preferred_element_type=F32) + b2_ref[...]
    )
    shaped = jnp.dot(hidden, w3_ref[...], precision=HIGHEST, preferred_element_type=F32)
    decay = decay_ref[...]
    energy = expm1_of_negative(-2.0 * decay) / expm1_of_negative(decay * (-2.0 / length))
    times = lax.broadcasted_iota(jnp.int32, (length, LANES), 0).astype(F32) * (1.0 / length)
    taps = shaped * jnp.exp(-(decay * times)) * (1.0 / jnp.sqrt(energy))
    high, low = split_value(taps)
    rows = lax.broadcasted_iota(jnp.int32, (2 * block, LANES), 0)
    sign = (1 - 2 * lax.rem(rows, 2)).astype(F32)
    first_row = lax.broadcasted_iota(jnp.int32, (block, LANES), 0) == 0
    before = None
    for k in range(blocks):
        part = slice(k * block, (k + 1) * block)
        stacked = jnp.concatenate([high[part], high[part], low[part]], axis=0)
        now = jnp.dot(table_ref[...], stacked, preferred_element_type=F32)
        spec = now if before is None else now + sign * before
        before = now
        real, imag = spec[:block], spec[block:]
        lanes = slice(k * LANES, (k + 1) * LANES)
        hre_ref[:, lanes] = real
        him_ref[:, lanes] = jnp.where(first_row, 0.0, imag)
        hfirst_ref[:, lanes] = jnp.where(first_row, imag, real)[:8]


def conv_kernel(
    blocks,
    outs,
    block,
    info_ref,
    xs_ref,
    gate_ref,
    skip_ref,
    hre_ref,
    him_ref,
    hfirst_ref,
    table_ref,
    inverse_ref,
    gated_ref,
    wre_ref,
    wim_ref,
    yre_ref,
    yim_ref,
):
    half = info_ref[0]
    earlier = blocks - outs
    keep = jnp.where(half > 0, 1.0, 0.0).astype(F32)
    for j in range(blocks):
        if j < earlier:
            values = xs_ref[j]
        else:
            values = xs_ref[half * outs + (j - earlier)]
        spec = jnp.dot(
            table_ref[...],
            jnp.concatenate([values, values], axis=0),
            preferred_element_type=F32,
        )
        if j < earlier:
            spec = spec * keep
        lanes = slice(j * LANES, (j + 1) * LANES)
        wre_ref[:, lanes] = spec[:block]
        wim_ref[:, lanes] = spec[block:]

    def rows_at(start, first):
        rows = pl.ds(start, 8)
        wre = [wre_ref[rows, j * LANES : (j + 1) * LANES] for j in range(blocks)]
        wim = [wim_ref[rows, j * LANES : (j + 1) * LANES] for j in range(blocks)]
        for o in range(outs):
            total_re = total_im = None
            for j in range(earlier + o + 1):
                k = earlier + o - j
                lanes = slice(k * LANES, (k + 1) * LANES)
                hre = hre_ref[rows, lanes]
                him = him_ref[rows, lanes]
                hother = hfirst_ref[:, lanes] if first else hre
                add_re = wre[j] * hre - wim[j] * him
                add_im = wre[j] * him + wim[j] * hother
                total_re = add_re if total_re is None else total_re + add_re
                total_im = add_im if total_im is None else total_im + add_im
            lanes = slice(o * LANES, (o + 1) * LANES)
            yre_ref[rows, lanes] = total_re
            yim_ref[rows, lanes] = total_im

    rows_at(0, True)

    @pl.loop(1, block // 8)
    def _(tile):
        rows_at(pl.multiple_of(tile * 8, 8), False)

    for o in range(outs):
        lanes = slice(o * LANES, (o + 1) * LANES)
        re_high, re_low = split_value(yre_ref[:, lanes])
        im_high, im_low = split_value(yim_ref[:, lanes])
        stacked = jnp.concatenate([re_high, im_high, re_high, im_high, re_low, im_low], axis=0)
        conv = jnp.dot(inverse_ref[...], stacked, preferred_element_type=F32)
        values = xs_ref[half * outs + o].astype(F32)
        gate = gate_ref[o].astype(F32)
        gated_ref[o] = (gate * (conv + skip_ref[...] * values)).astype(BF16)


def project_kernel(groups, gated_ref, weight_ref, out_ref):
    left = jnp.concatenate([gated_ref[g] for g in range(groups)], axis=1)
    out_ref[0] = jnp.dot(left, weight_ref[...], preferred_element_type=F32).astype(BF16)


def call_filter(group, weights, blocks, block):
    w1, b1, w2, b2, w3, decay = weights
    length = blocks * block
    emb, order = w1.shape
    forward, _ = dft_tables(block)
    high, low = split_bf16(forward)
    table = np.concatenate([high, low, high], axis=1)
    feats = feature_table(length, emb)
    whole = lambda *shape: pl.BlockSpec(shape, lambda i, s: (0,) * len(shape))
    chosen = lambda rows: pl.BlockSpec((rows, LANES), lambda i, s: (0, s[0]))
    grid_spec = pltpu.PrefetchScalarGridSpec(
        num_scalar_prefetch=1,
        grid=(1,),
        in_specs=[
            whole(length, emb),
            whole(emb, order),
            whole(1, order),
            whole(order, order),
            whole(1, order),
            chosen(order),
            chosen(1),
            whole(2 * block, 3 * block),
        ],
        out_specs=[
            whole(block, blocks * LANES),
            whole(block, blocks * LANES),
            whole(8, blocks * LANES),
        ],
    )
    return pl.pallas_call(
        functools.partial(filter_kernel, blocks, block),
        grid_spec=grid_spec,
        out_shape=[
            jax.ShapeDtypeStruct((block, blocks * LANES), F32),
            jax.ShapeDtypeStruct((block, blocks * LANES), F32),
            jax.ShapeDtypeStruct((8, blocks * LANES), F32),
        ],
        compiler_params=pltpu.CompilerParams(vmem_limit_bytes=32 * 2**20),
        cost_estimate=pl.CostEstimate(
            flops=2 * 6 * length * 3 * 128 * 128, bytes_accessed=3 * 2**20, transcendentals=length * 128
        ),
        name="filter_spectra",
    )(group, feats, w1, b1[None], w2, b2[None], w3, decay[None], table)


def call_conv(info, xs, gate, skip, spectra, blocks, outs, block):
    forward, inverse = dft_tables(block)
    table = np.concatenate(split_bf16(forward), axis=1)
    high, low = split_bf16(inverse)
    back = np.concatenate([high, low, high], axis=1)
    whole = lambda *shape: pl.BlockSpec(shape, lambda i, s: (0,) * len(shape))
    grid_spec = pltpu.PrefetchScalarGridSpec(
        num_scalar_prefetch=1,
        grid=(1,),
        in_specs=[
            whole(blocks, block, LANES),
            whole(outs, block, LANES),
            pl.BlockSpec((1, LANES), lambda i, s: (0, s[1])),
            whole(block, blocks * LANES),
            whole(block, blocks * LANES),
            whole(8, blocks * LANES),
            whole(2 * block, 2 * block),
            whole(block, 6 * block),
        ],
        out_specs=whole(outs, block, LANES),
        scratch_shapes=[
            VMEM((block, blocks * LANES), F32),
            VMEM((block, blocks * LANES), F32),
            VMEM((block, outs * LANES), F32),
            VMEM((block, outs * LANES), F32),
        ],
    )
    return pl.pallas_call(
        functools.partial(conv_kernel, blocks, outs, block),
        grid_spec=grid_spec,
        out_shape=jax.ShapeDtypeStruct((outs, block, LANES), BF16),
        compiler_params=pltpu.CompilerParams(vmem_limit_bytes=32 * 2**20),
        cost_estimate=pl.CostEstimate(
            flops=2 * 10**8, bytes_accessed=3 * 2**20, transcendentals=0
        ),
        name="conv_gate",
    )(info, xs, gate, skip[None], *spectra, table, back)


def call_project(gated, weight, parts):
    groups, block, _ = gated.shape
    width = weight.shape[1] // parts
    return pl.pallas_call(
        functools.partial(project_kernel, groups),
        grid=(parts,),
        in_specs=[
            pl.BlockSpec((groups, block, LANES), lambda i: (0, 0, 0)),
            pl.BlockSpec((groups * LANES, width), lambda i: (0, i)),
        ],
        out_specs=pl.BlockSpec((1, block, width), lambda i: (i, 0, 0)),
        out_shape=jax.ShapeDtypeStruct((parts, block, width), BF16),
        compiler_params=pltpu.CompilerParams(vmem_limit_bytes=32 * 2**20),
        cost_estimate=pl.CostEstimate(
            flops=2 * block * weight.size, bytes_accessed=2 * weight.size, transcendentals=0
        ),
        name="projection",
    )(gated, weight)


def split_shards(
    mixer_input,
    gate_branch,
    skip_gain,
    decay_rate,
    first_weight,
    first_bias,
    second_weight,
    second_bias,
    last_weight,
    output_weight,
):
    block, width = mixer_input.shape
    blocks = lax.axis_size("seq")
    parts = lax.axis_size("chan")
    outs = width // LANES
    me = lax.axis_index("seq")
    half, group = me // outs, me % outs
    halves = [list(range(h * outs, (h + 1) * outs)) for h in range(blocks // outs)]

    pieces = mixer_input.reshape(block, outs, LANES).transpose(1, 0, 2)
    xs = lax.all_to_all(
        jnp.concatenate([pieces] * (blocks // outs), axis=0), "seq", 0, 0, tiled=True
    )
    gate = lax.all_to_all(
        gate_branch.reshape(block, outs, LANES).transpose(1, 0, 2),
        "seq",
        0,
        0,
        axis_index_groups=halves,
        tiled=True,
    )
    spectra = call_filter(
        group[None].astype(jnp.int32),
        (first_weight, first_bias, second_weight, second_bias, last_weight, decay_rate),
        blocks,
        block,
    )
    info = jnp.stack([half, group]).astype(jnp.int32)
    gated = call_conv(info, xs, gate, skip_gain, spectra, blocks, outs, block)
    gated = lax.all_to_all(gated, "seq", 0, 0, axis_index_groups=halves, tiled=True)
    partial_out = call_project(gated, output_weight, parts)
    partial_out = lax.all_to_all(partial_out, "chan", 0, 0, tiled=True)
    return jnp.sum(partial_out.astype(F32), axis=0).astype(BF16)


def contract_first(left_matrix, right_matrix):
    return lax.dot_general(
        left_matrix,
        right_matrix,
        (((0,), (0,)), ((), ())),
        precision=HIGHEST,
        preferred_element_type=F32,
    )


def filter_taps(
    first_weight, first_bias, second_weight, second_bias, last_weight, decay_rate, length
):
    features = jnp.asarray(feature_table(length, first_weight.shape[0]).T)
    hidden_one = jnp.sin(contract_first(first_weight, features) + first_bias[:, None])
    hidden_two = jnp.sin(contract_first(second_weight, hidden_one) + second_bias[:, None])
    shaped = contract_first(hidden_two, last_weight)
    positions = jnp.arange(length, dtype=jnp.int32).astype(F32)
    envelope = jnp.exp(-decay_rate[None, :] * (positions[:, None] / length))
    energy = jnp.expm1(-2.0 * decay_rate) / jnp.expm1(-2.0 * decay_rate / length)
    return shaped * envelope / jnp.sqrt(energy)[None, :]


def transform_tables(block_len):
    padded_len = 2 * block_len
    freq_index = jnp.arange(block_len + 1, dtype=jnp.int32)[:, None]
    time_index = jnp.arange(padded_len, dtype=jnp.int32)[None, :]
    angle = (freq_index * time_index % padded_len).astype(F32) * (2.0 * math.pi / padded_len)
    forward = jnp.concatenate([jnp.cos(angle), -jnp.sin(angle)], axis=0)
    later_angle = angle[:, block_len:]
    weights = jnp.where((freq_index == 0) | (freq_index == block_len), 1.0, 2.0) / padded_len
    inverse = jnp.concatenate(
        [(weights * jnp.cos(later_angle)).T, (-weights * jnp.sin(later_angle)).T], axis=1
    )
    return (forward, inverse)


def spectral_product(left_spec, right_spec, half_rows):
    left_real, left_imag = (left_spec[:half_rows], left_spec[half_rows:])
    right_real, right_imag = (right_spec[:half_rows], right_spec[half_rows:])
    return jnp.concatenate(
        [
            left_real * right_real - left_imag * right_imag,
            left_real * right_imag + left_imag * right_real,
        ],
        axis=0,
    )


def gathered_shards(
    mixer_input,
    gate_branch,
    skip_gain,
    decay_rate,
    first_weight,
    first_bias,
    second_weight,
    second_bias,
    last_weight,
    output_weight,
):
    block_len, chan_width = mixer_input.shape
    seq_count = lax.axis_size("seq")
    device = lax.axis_index("seq")
    half_rows = block_len + 1
    kernel_taps = filter_taps(
        first_weight,
        first_bias,
        second_weight,
        second_bias,
        last_weight,
        decay_rate,
        block_len * seq_count,
    )
    padded_taps = jnp.concatenate([jnp.zeros((block_len, chan_width), F32), kernel_taps], axis=0)
    forward, inverse = transform_tables(block_len)
    forward_head = forward[:, :block_len]
    gathered = lax.all_gather(mixer_input, "seq", axis=0, tiled=True)

    def one_block(block_index, total):
        rows = lax.dynamic_slice_in_dim(gathered, block_index * block_len, block_len, 0)
        source_spec = jnp.dot(
            forward_head, rows.astype(F32), precision=HIGHEST, preferred_element_type=F32
        )
        segment = lax.dynamic_slice_in_dim(
            padded_taps, (device - block_index) * block_len, 2 * block_len, 0
        )
        lag_spec = jnp.dot(forward, segment, precision=HIGHEST, preferred_element_type=F32)
        return total + spectral_product(lag_spec, source_spec, half_rows)

    total = lax.fori_loop(0, device + 1, one_block, jnp.zeros((2 * half_rows, chan_width), F32))
    convolved = jnp.dot(inverse, total, precision=HIGHEST, preferred_element_type=F32)
    values = mixer_input.astype(F32)
    gated_mix = (
        gate_branch.astype(F32) * (convolved + skip_gain[None, :] * values)
    ).astype(BF16)
    partial_out = jnp.dot(gated_mix, output_weight, preferred_element_type=F32)
    return lax.psum_scatter(partial_out, "chan", scatter_dimension=1, tiled=True).astype(BF16)


def solution(mesh):
    seq_count, chan_count = mesh.shape["seq"], mesh.shape["chan"]

    def shards(mixer_input, *rest):
        block, width = mixer_input.shape
        outs = width // LANES
        splits = (
            width % LANES == 0 and block % LANES == 0 and outs > 1 and seq_count == 2 * outs
        )
        plan = split_shards if splits else gathered_shards
        return plan(mixer_input, *rest)

    in_specs = (
        P("seq", "chan"),
        P("seq", "chan"),
        P("chan"),
        P("chan"),
        P(),
        P(),
        P(),
        P(),
        P(None, "chan"),
        P("chan", None),
    )
    out_specs = P("seq", "chan")
    return jax.shard_map(shards, mesh=mesh, in_specs=in_specs, out_specs=out_specs, check_vma=False)
```

```python
import functools
import math

import jax
import jax.numpy as jnp
import numpy as np
from jax import lax
from jax.experimental import pallas as pl
from jax.experimental.pallas import tpu as pltpu
from jax.sharding import PartitionSpec as P

HIGHEST = lax.Precision.HIGHEST
F32 = jnp.float32
BF16 = jnp.bfloat16
LANES = 128
VMEM = pltpu.VMEM


def feature_table(length, emb_width):
    band_count = (emb_width - 1) // 2
    positions = np.arange(length, dtype=np.int64)
    columns = [positions / length]
    for band in range(1, band_count + 1):
        frequency = min(
            length // 2, max(band, int((length / 2) ** ((band - 1) / (band_count - 1))))
        )
        angle = (positions * frequency % length) * (2.0 * math.pi / length)
        columns.append(np.cos(angle))
        columns.append(np.sin(angle))
    return np.stack(columns, axis=1).astype(np.float32)


def split_bf16(table):
    high = table.astype(np.float32).astype(jnp.bfloat16)
    low = (table - high.astype(np.float64)).astype(np.float32).astype(jnp.bfloat16)
    return high, low


def dft_tables(block):
    size = 2 * block
    bins = np.arange(block)[:, None]
    times = np.arange(block)[None, :]
    angle = (bins * times % size) * (2.0 * math.pi / size)
    imag = -np.sin(angle)
    imag[0] = 1.0 - 2.0 * (np.arange(block) % 2)
    forward = np.concatenate([np.cos(angle), imag], axis=0)
    weight = np.where(bins == 0, 1.0, 2.0) / size
    back_imag = -weight * np.sin(angle)
    back_imag[0] = (1.0 - 2.0 * (np.arange(block) % 2)) / size
    inverse = np.concatenate([weight * np.cos(angle), back_imag], axis=0).T
    return forward, inverse


def fast_sin(x):
    turns = jnp.floor(x * (1.0 / math.pi) + 0.5)
    rest = x - turns * 3.140625
    rest = rest - turns * 9.67502593994140625e-4
    rest = rest - turns * 1.509957990978376432e-7
    parity = turns - 2.0 * jnp.floor(turns * 0.5)
    rest = rest * (1.0 - 2.0 * parity)
    square = rest * rest
    poly = -2.5052108e-8
    for coeff in (2.7557319e-6, -1.9841270e-4, 8.3333333e-3, -1.6666667e-1):
        poly = poly * square + coeff
    return rest + rest * square * poly


def expm1_of_negative(x):
    near = jnp.maximum(x, -0.5)
    series = jnp.full_like(x, 1.0 / 3628800.0)
    for denom in (362880.0, 40320.0, 5040.0, 720.0, 120.0, 24.0, 6.0, 2.0, 1.0):
        series = series * near + 1.0 / denom
    return jnp.where(x > -0.5, near * series, jnp.exp(x) - 1.0)


def split_value(value):
    high = value.astype(BF16)
    return high, (value - high.astype(F32)).astype(BF16)


def filter_kernel(
    blocks,
    block,
    info_ref,
    feat_ref,
    w1_ref,
    b1_ref,
    w2_ref,
    b2_ref,
    w3_ref,
    decay_ref,
    table_ref,
    hre_ref,
    him_ref,
    hfirst_ref,
):
    length = blocks * block
    hidden = fast_sin(
        jnp.dot(feat_ref[...], w1_ref[...], precision=HIGHEST, preferred_element_type=F32)
        + b1_ref[...]
    )
    hidden = fast_sin(
        jnp.dot(hidden, w2_ref[...], precision=HIGHEST, preferred_element_type=F32) + b2_ref[...]
    )
    shaped = jnp.dot(hidden, w3_ref[...], precision=HIGHEST, preferred_element_type=F32)
    decay = decay_ref[...]
    energy = expm1_of_negative(-2.0 * decay) / expm1_of_negative(decay * (-2.0 / length))
    times = lax.broadcasted_iota(jnp.int32, (length, LANES), 0).astype(F32) * (1.0 / length)
    taps = shaped * jnp.exp(-(decay * times)) * (1.0 / jnp.sqrt(energy))
    high, low = split_value(taps)
    rows = lax.broadcasted_iota(jnp.int32, (2 * block, LANES), 0)
    sign = (1 - 2 * lax.rem(rows, 2)).astype(F32)
    first_row = lax.broadcasted_iota(jnp.int32, (block, LANES), 0) == 0
    before = None
    for k in range(blocks):
        part = slice(k * block, (k + 1) * block)
        stacked = jnp.concatenate([high[part], high[part], low[part]], axis=0)
        now = jnp.dot(table_ref[...], stacked, preferred_element_type=F32)
        spec = now if before is None else now + sign * before
        before = now
        real, imag = spec[:block], spec[block:]
        lanes = slice(k * LANES, (k + 1) * LANES)
        hre_ref[:, lanes] = real
        him_ref[:, lanes] = jnp.where(first_row, 0.0, imag)
        hfirst_ref[:, lanes] = jnp.where(first_row, imag, real)[:8]


def pack_kernel(outs, info_ref, x_ref, gate_ref, *out_refs):
    group = info_ref[1]
    block = x_ref.shape[0]
    for k in range(outs):
        lanes = pl.ds(pl.multiple_of((group ^ k) * LANES, LANES), LANES)
        values = x_ref[:, lanes]
        out_refs[k][:block] = values
        out_refs[k][block:] = gate_ref[:, lanes]
        out_refs[outs + k][...] = values


def conv_kernel(blocks, outs, block, info_ref, *refs):
    own_refs, refs = refs[:outs], refs[outs:]
    cross_refs, refs = refs[:outs], refs[outs:]
    skip_ref, hre_ref, him_ref, hfirst_ref, table_ref, inverse_ref = refs[:6]
    gated_refs, refs = refs[6 : 6 + outs], refs[6 + outs :]
    wre_ref, wim_ref, yre_ref, yim_ref = refs
    half, group = info_ref[0], info_ref[1]
    earlier = blocks - outs
    keep = jnp.where(half > 0, 1.0, 0.0).astype(F32)
    for k in range(outs):
        slot = group ^ k
        for place, values in ((slot, cross_refs[k][...]), (earlier + slot, own_refs[k][:block])):
            spec = jnp.dot(
                table_ref[...],
                jnp.concatenate([values, values], axis=0),
                preferred_element_type=F32,
            )
            if place is slot:
                spec = jnp.where(half > 0, spec, 0.0)
            wre_ref[place] = spec[:block]
            wim_ref[place] = spec[block:]

    def rows_at(start, first):
        rows = pl.ds(start, 8)
        wre = [wre_ref[j, rows, :] for j in range(blocks)]
        wim = [wim_ref[j, rows, :] for j in range(blocks)]
        for o in range(outs):
            total_re = total_im = None
            for j in range(earlier + o + 1):
                k = earlier + o - j
                lanes = slice(k * LANES, (k + 1) * LANES)
                hre = hre_ref[rows, lanes]
                him = him_ref[rows, lanes]
                hother = hfirst_ref[:, lanes] if first else hre
                add_re = wre[j] * hre - wim[j] * him
                add_im = wre[j] * him + wim[j] * hother
                total_re = add_re if total_re is None else total_re + add_re
                total_im = add_im if total_im is None else total_im + add_im
            yre_ref[o, rows, :] = total_re
            yim_ref[o, rows, :] = total_im

    rows_at(0, True)

    @pl.loop(1, block // 8)
    def _(tile):
        rows_at(pl.multiple_of(tile * 8, 8), False)

    for k in range(outs):
        slot = group ^ k
        re_high, re_low = split_value(yre_ref[slot])
        im_high, im_low = split_value(yim_ref[slot])
        stacked = jnp.concatenate([re_high, im_high, re_high, im_high, re_low, im_low], axis=0)
        conv = jnp.dot(inverse_ref[...], stacked, preferred_element_type=F32)
        values = own_refs[k][:block].astype(F32)
        gate = own_refs[k][block:].astype(F32)
        gated_refs[k][...] = (gate * (conv + skip_ref[...] * values)).astype(BF16)


def project_kernel(outs, info_ref, *refs):
    gated_refs, (weight_ref, out_ref, left_ref) = refs[:outs], refs[outs:]

    @pl.when(pl.program_id(0) == 0)
    def _():
        for k in range(outs):
            lanes = pl.ds(pl.multiple_of((info_ref[1] ^ k) * LANES, LANES), LANES)
            left_ref[:, lanes] = gated_refs[k][...]

    out_ref[...] = jnp.dot(
        left_ref[...], weight_ref[...], preferred_element_type=F32
    ).astype(out_ref.dtype)


def call_pack(info, x, gate, outs):
    block, width = x.shape
    whole = lambda *shape: pl.BlockSpec(shape, lambda i, s: (0,) * len(shape))
    return pl.pallas_call(
        functools.partial(pack_kernel, outs),
        grid_spec=pltpu.PrefetchScalarGridSpec(
            num_scalar_prefetch=1,
            grid=(1,),
            in_specs=[whole(block, width), whole(block, width)],
            out_specs=[whole(2 * block, LANES)] * outs + [whole(block, LANES)] * outs,
        ),
        out_shape=[jax.ShapeDtypeStruct((2 * block, LANES), BF16)] * outs
        + [jax.ShapeDtypeStruct((block, LANES), BF16)] * outs,
        cost_estimate=pl.CostEstimate(flops=0, bytes_accessed=6 * x.size, transcendentals=0),
        name="pack_pieces",
    )(info, x, gate)


def call_filter(info, weights, blocks, block):
    w1, b1, w2, b2, w3, decay = weights
    length = blocks * block
    emb, order = w1.shape
    forward, _ = dft_tables(block)
    high, low = split_bf16(forward)
    table = np.concatenate([high, low, high], axis=1)
    feats = feature_table(length, emb)
    whole = lambda *shape: pl.BlockSpec(shape, lambda i, s: (0,) * len(shape))
    chosen = lambda rows: pl.BlockSpec((rows, LANES), lambda i, s: (0, s[1]))
    grid_spec = pltpu.PrefetchScalarGridSpec(
        num_scalar_prefetch=1,
        grid=(1,),
        in_specs=[
            whole(length, emb),
            whole(emb, order),
            whole(1, order),
            whole(order, order),
            whole(1, order),
            chosen(order),
            chosen(1),
            whole(2 * block, 3 * block),
        ],
        out_specs=[
            whole(block, blocks * LANES),
            whole(block, blocks * LANES),
            whole(8, blocks * LANES),
        ],
    )
    return pl.pallas_call(
        functools.partial(filter_kernel, blocks, block),
        grid_spec=grid_spec,
        out_shape=[
            jax.ShapeDtypeStruct((block, blocks * LANES), F32),
            jax.ShapeDtypeStruct((block, blocks * LANES), F32),
            jax.ShapeDtypeStruct((8, blocks * LANES), F32),
        ],
        compiler_params=pltpu.CompilerParams(vmem_limit_bytes=32 * 2**20),
        cost_estimate=pl.CostEstimate(
            flops=2 * 6 * length * 3 * 128 * 128, bytes_accessed=3 * 2**20, transcendentals=length * 128
        ),
        name="filter_spectra",
    )(info, feats, w1, b1[None], w2, b2[None], w3, decay[None], table)


def call_conv(info, own, cross, skip, spectra, blocks, outs, block):
    forward, inverse = dft_tables(block)
    table = np.concatenate(split_bf16(forward), axis=1)
    high, low = split_bf16(inverse)
    back = np.concatenate([high, low, high], axis=1)
    whole = lambda *shape: pl.BlockSpec(shape, lambda i, s: (0,) * len(shape))
    grid_spec = pltpu.PrefetchScalarGridSpec(
        num_scalar_prefetch=1,
        grid=(1,),
        in_specs=[whole(2 * block, LANES)] * outs
        + [whole(block, LANES)] * outs
        + [
            pl.BlockSpec((1, LANES), lambda i, s: (0, s[1])),
            whole(block, blocks * LANES),
            whole(block, blocks * LANES),
            whole(8, blocks * LANES),
            whole(2 * block, 2 * block),
            whole(block, 6 * block),
        ],
        out_specs=[whole(block, LANES)] * outs,
        scratch_shapes=[
            VMEM((blocks, block, LANES), F32),
            VMEM((blocks, block, LANES), F32),
            VMEM((outs, block, LANES), F32),
            VMEM((outs, block, LANES), F32),
        ],
    )
    return pl.pallas_call(
        functools.partial(conv_kernel, blocks, outs, block),
        grid_spec=grid_spec,
        out_shape=[jax.ShapeDtypeStruct((block, LANES), BF16)] * outs,
        compiler_params=pltpu.CompilerParams(vmem_limit_bytes=32 * 2**20),
        cost_estimate=pl.CostEstimate(
            flops=2 * 10**8, bytes_accessed=3 * 2**20, transcendentals=0
        ),
        name="conv_gate",
    )(info, *own, *cross, skip[None], *spectra, table, back)


def call_project(info, gated, weight, place, parts, kind):
    outs = len(gated)
    block = gated[0].shape[0]
    rows, columns = weight.shape
    width = columns // parts
    steps = 2
    return pl.pallas_call(
        functools.partial(project_kernel, outs),
        grid_spec=pltpu.PrefetchScalarGridSpec(
            num_scalar_prefetch=1,
            grid=(steps,),
            in_specs=[pl.BlockSpec((block, LANES), lambda i, s: (0, 0))] * outs
            + [pl.BlockSpec((rows, width // steps), lambda i, s: (0, s[place] * steps + i))],
            out_specs=pl.BlockSpec((block, width // steps), lambda i, s: (0, i)),
            scratch_shapes=[VMEM((block, rows), BF16)],
        ),
        out_shape=jax.ShapeDtypeStruct((block, width), kind),
        compiler_params=pltpu.CompilerParams(vmem_limit_bytes=16 * 2**20),
        cost_estimate=pl.CostEstimate(
            flops=2 * block * rows * width, bytes_accessed=2 * rows * width, transcendentals=0
        ),
        name="projection",
    )(info, *gated, weight)


def split_shards(
    mixer_input,
    gate_branch,
    skip_gain,
    decay_rate,
    first_weight,
    first_bias,
    second_weight,
    second_bias,
    last_weight,
    output_weight,
):
    block, width = mixer_input.shape
    blocks = lax.axis_size("seq")
    parts = lax.axis_size("chan")
    outs = width // LANES
    me, column = lax.axis_index("seq"), lax.axis_index("chan")
    half, group = me // outs, me % outs
    info = jnp.stack([half, group] + [column ^ k for k in range(parts)]).astype(jnp.int32)

    packed = call_pack(info, mixer_input, gate_branch, outs)
    own = [packed[0]] + [
        lax.ppermute(packed[k], "seq", [(s, s ^ k) for s in range(blocks)]) for k in range(1, outs)
    ]
    cross = [
        lax.ppermute(packed[outs + k], "seq", [(s, outs + (s ^ k)) for s in range(outs)])
        for k in range(outs)
    ]
    spectra = call_filter(
        info,
        (first_weight, first_bias, second_weight, second_bias, last_weight, decay_rate),
        blocks,
        block,
    )
    gated = call_conv(info, own, cross, skip_gain, spectra, blocks, outs, block)
    gated = [gated[0]] + [
        lax.ppermute(gated[k], "seq", [(s, s ^ k) for s in range(blocks)]) for k in range(1, outs)
    ]
    arrived = []
    for k in reversed(range(1, parts)):
        part = call_project(info, gated, output_weight, 2 + k, parts, BF16)
        arrived.append(lax.ppermute(part, "chan", [(c, c ^ k) for c in range(parts)]))
    total = call_project(info, gated, output_weight, 2, parts, F32)
    for part in arrived:
        total = total + part.astype(F32)
    return total.astype(BF16)


def contract_first(left_matrix, right_matrix):
    return lax.dot_general(
        left_matrix,
        right_matrix,
        (((0,), (0,)), ((), ())),
        precision=HIGHEST,
        preferred_element_type=F32,
    )


def filter_taps(
    first_weight, first_bias, second_weight, second_bias, last_weight, decay_rate, length
):
    features = jnp.asarray(feature_table(length, first_weight.shape[0]).T)
    hidden_one = jnp.sin(contract_first(first_weight, features) + first_bias[:, None])
    hidden_two = jnp.sin(contract_first(second_weight, hidden_one) + second_bias[:, None])
    shaped = contract_first(hidden_two, last_weight)
    positions = jnp.arange(length, dtype=jnp.int32).astype(F32)
    envelope = jnp.exp(-decay_rate[None, :] * (positions[:, None] / length))
    energy = jnp.expm1(-2.0 * decay_rate) / jnp.expm1(-2.0 * decay_rate / length)
    return shaped * envelope / jnp.sqrt(energy)[None, :]


def transform_tables(block_len):
    padded_len = 2 * block_len
    freq_index = jnp.arange(block_len + 1, dtype=jnp.int32)[:, None]
    time_index = jnp.arange(padded_len, dtype=jnp.int32)[None, :]
    angle = (freq_index * time_index % padded_len).astype(F32) * (2.0 * math.pi / padded_len)
    forward = jnp.concatenate([jnp.cos(angle), -jnp.sin(angle)], axis=0)
    later_angle = angle[:, block_len:]
    weights = jnp.where((freq_index == 0) | (freq_index == block_len), 1.0, 2.0) / padded_len
    inverse = jnp.concatenate(
        [(weights * jnp.cos(later_angle)).T, (-weights * jnp.sin(later_angle)).T], axis=1
    )
    return (forward, inverse)


def spectral_product(left_spec, right_spec, half_rows):
    left_real, left_imag = (left_spec[:half_rows], left_spec[half_rows:])
    right_real, right_imag = (right_spec[:half_rows], right_spec[half_rows:])
    return jnp.concatenate(
        [
            left_real * right_real - left_imag * right_imag,
            left_real * right_imag + left_imag * right_real,
        ],
        axis=0,
    )


def gathered_shards(
    mixer_input,
    gate_branch,
    skip_gain,
    decay_rate,
    first_weight,
    first_bias,
    second_weight,
    second_bias,
    last_weight,
    output_weight,
):
    block_len, chan_width = mixer_input.shape
    seq_count = lax.axis_size("seq")
    device = lax.axis_index("seq")
    half_rows = block_len + 1
    kernel_taps = filter_taps(
        first_weight,
        first_bias,
        second_weight,
        second_bias,
        last_weight,
        decay_rate,
        block_len * seq_count,
    )
    padded_taps = jnp.concatenate([jnp.zeros((block_len, chan_width), F32), kernel_taps], axis=0)
    forward, inverse = transform_tables(block_len)
    forward_head = forward[:, :block_len]
    gathered = lax.all_gather(mixer_input, "seq", axis=0, tiled=True)

    def one_block(block_index, total):
        rows = lax.dynamic_slice_in_dim(gathered, block_index * block_len, block_len, 0)
        source_spec = jnp.dot(
            forward_head, rows.astype(F32), precision=HIGHEST, preferred_element_type=F32
        )
        segment = lax.dynamic_slice_in_dim(
            padded_taps, (device - block_index) * block_len, 2 * block_len, 0
        )
        lag_spec = jnp.dot(forward, segment, precision=HIGHEST, preferred_element_type=F32)
        return total + spectral_product(lag_spec, source_spec, half_rows)

    total = lax.fori_loop(0, device + 1, one_block, jnp.zeros((2 * half_rows, chan_width), F32))
    convolved = jnp.dot(inverse, total, precision=HIGHEST, preferred_element_type=F32)
    values = mixer_input.astype(F32)
    gated_mix = (
        gate_branch.astype(F32) * (convolved + skip_gain[None, :] * values)
    ).astype(BF16)
    partial_out = jnp.dot(gated_mix, output_weight, preferred_element_type=F32)
    return lax.psum_scatter(partial_out, "chan", scatter_dimension=1, tiled=True).astype(BF16)


def solution(mesh):
    seq_count, chan_count = mesh.shape["seq"], mesh.shape["chan"]

    def shards(mixer_input, *rest):
        block, width = mixer_input.shape
        outs = width // LANES
        splits = (
            width % LANES == 0
            and block % LANES == 0
            and seq_count == 2 * outs
            and outs in (2, 4, 8)
            and chan_count in (1, 2, 4, 8)
        )
        plan = split_shards if splits else gathered_shards
        return plan(mixer_input, *rest)

    in_specs = (
        P("seq", "chan"),
        P("seq", "chan"),
        P("chan"),
        P("chan"),
        P(),
        P(),
        P(),
        P(),
        P(None, "chan"),
        P("chan", None),
    )
    out_specs = P("seq", "chan")
    return jax.shard_map(shards, mesh=mesh, in_specs=in_specs, out_specs=out_specs, check_vma=False)
```

```python
import functools
import math

import jax
import jax.numpy as jnp
import numpy as np
from jax import lax
from jax.experimental import pallas as pl
from jax.experimental.pallas import tpu as pltpu
from jax.sharding import PartitionSpec as P

HIGHEST = lax.Precision.HIGHEST
F32 = jnp.float32
BF16 = jnp.bfloat16
LANES = 128
VMEM = pltpu.VMEM


def feature_table(length, emb_width):
    band_count = (emb_width - 1) // 2
    positions = np.arange(length, dtype=np.int64)
    columns = [positions / length]
    for band in range(1, band_count + 1):
        frequency = min(
            length // 2, max(band, int((length / 2) ** ((band - 1) / (band_count - 1))))
        )
        angle = (positions * frequency % length) * (2.0 * math.pi / length)
        columns.append(np.cos(angle))
        columns.append(np.sin(angle))
    return np.stack(columns, axis=1).astype(np.float32)


def split_bf16(table):
    high = table.astype(np.float32).astype(jnp.bfloat16)
    low = (table - high.astype(np.float64)).astype(np.float32).astype(jnp.bfloat16)
    return high, low


def dft_tables(block):
    size = 2 * block
    bins = np.arange(block)[:, None]
    times = np.arange(block)[None, :]
    angle = (bins * times % size) * (2.0 * math.pi / size)
    imag = -np.sin(angle)
    imag[0] = 1.0 - 2.0 * (np.arange(block) % 2)
    forward = np.concatenate([np.cos(angle), imag], axis=0)
    weight = np.where(bins == 0, 1.0, 2.0) / size
    back_imag = -weight * np.sin(angle)
    back_imag[0] = (1.0 - 2.0 * (np.arange(block) % 2)) / size
    inverse = np.concatenate([weight * np.cos(angle), back_imag], axis=0).T
    return forward, inverse


def fast_sin(x):
    turns = jnp.floor(x * (1.0 / math.pi) + 0.5)
    rest = x - turns * 3.140625
    rest = rest - turns * 9.67502593994140625e-4
    rest = rest - turns * 1.509957990978376432e-7
    parity = turns - 2.0 * jnp.floor(turns * 0.5)
    rest = rest * (1.0 - 2.0 * parity)
    square = rest * rest
    poly = -2.5052108e-8
    for coeff in (2.7557319e-6, -1.9841270e-4, 8.3333333e-3, -1.6666667e-1):
        poly = poly * square + coeff
    return rest + rest * square * poly


def expm1_of_negative(x):
    near = jnp.maximum(x, -0.5)
    series = jnp.full_like(x, 1.0 / 3628800.0)
    for denom in (362880.0, 40320.0, 5040.0, 720.0, 120.0, 24.0, 6.0, 2.0, 1.0):
        series = series * near + 1.0 / denom
    return jnp.where(x > -0.5, near * series, jnp.exp(x) - 1.0)


def split_value(value):
    high = value.astype(BF16)
    return high, (value - high.astype(F32)).astype(BF16)


def filter_feature_table(length, emb_width, pad):
    table = feature_table(length, emb_width)
    columns = []
    for half in (table[: length // 2], table[length // 2 :]):
        high, low = (part.astype(np.float32) for part in split_bf16(half))
        for part in (high, high, low):
            columns.append(np.pad(part, ((0, 0), (0, pad - emb_width))))
    return np.concatenate(columns, axis=1)


def twice_diagonal(value):
    zero = jnp.zeros_like(value)
    return jnp.concatenate(
        [jnp.concatenate([value, zero], axis=1), jnp.concatenate([zero, value], axis=1)], axis=0
    )


def stacked_diagonal(value):
    high, low = split_value(value)
    high = twice_diagonal(high.astype(F32))
    low = twice_diagonal(low.astype(F32))
    return jnp.concatenate([high, low, high], axis=0).astype(BF16)


def layer(value, weight):
    high, low = split_value(value)
    return jnp.dot(
        jnp.concatenate([high, high, low], axis=1), weight, preferred_element_type=F32
    )


def filter_kernel(blocks, block, outs, pad, *refs):
    hbm, refs = refs[:13], refs[13:]
    hre_ref, him_ref, hfirst_ref, fwd_ref, inv_ref, weight_ref, gate_ref, base_ref = refs[:8]
    refs = refs[8:]
    w1_ref, b1_ref, w2_ref, b2_ref, w3_ref, decay_ref, feat_ref, table_ref, back_ref = refs[:9]
    skip_ref, x_ref, first_ref, sems = refs[9:]
    targets = [
        w1_ref, feat_ref, b1_ref, w2_ref, b2_ref, w3_ref, decay_ref, table_ref, back_ref,
        skip_ref, x_ref, gate_ref, weight_ref,
    ]
    copies = [
        pltpu.make_async_copy(hbm[i], targets[i], sems.at[i]) for i in range(len(targets))
    ]
    for copy in copies:
        copy.start()
    group = lax.axis_index("seq") % outs
    length = blocks * block
    emb, order = w1_ref.shape
    first_ref[...] = jnp.zeros_like(first_ref)
    for copy in copies[:7]:
        copy.wait()

    high, low = split_value(w1_ref[...])
    high, low = high.astype(F32), low.astype(F32)
    zero = jnp.zeros_like(high)
    for i, part in enumerate((high, low, high)):
        first_ref[i * pad : i * pad + emb] = jnp.concatenate([part, zero], axis=1)
        first_ref[(3 + i) * pad : (3 + i) * pad + emb] = jnp.concatenate([zero, part], axis=1)
    b1 = jnp.concatenate([b1_ref[...]] * 2, axis=1)
    b2 = jnp.concatenate([b2_ref[...]] * 2, axis=1)
    hidden = fast_sin(
        jnp.dot(
            feat_ref[...].astype(BF16), first_ref[...].astype(BF16), preferred_element_type=F32
        )
        + b1
    )
    hidden = fast_sin(layer(hidden, stacked_diagonal(w2_ref[...])) + b2)
    lanes = pl.ds(pl.multiple_of(group * LANES, LANES), LANES)
    shaped = layer(hidden, stacked_diagonal(w3_ref[:, lanes]))

    decay = decay_ref[:, lanes]
    energy = expm1_of_negative(-2.0 * decay) / expm1_of_negative(decay * (-2.0 / length))
    times = lax.broadcasted_iota(jnp.int32, (length // 2, LANES), 0).astype(F32) * (1.0 / length)
    window = jnp.exp(-(decay * times)) * (1.0 / jnp.sqrt(energy))
    window = jnp.concatenate([window, window * jnp.exp(-0.5 * decay)], axis=1)
    taps_high, taps_low = split_value(shaped * window)

    copies[7].wait()
    high, low = split_value(table_ref[...])
    fwd_ref[:, :block] = high
    fwd_ref[:, block:] = low
    table = jnp.concatenate([high, low, high], axis=1)
    rows = lax.broadcasted_iota(jnp.int32, (2 * block, LANES), 0)
    sign = (1 - 2 * lax.rem(rows, 2)).astype(F32)
    first_row = lax.broadcasted_iota(jnp.int32, (block, LANES), 0) == 0
    spectra = [None] * blocks
    for k in range(blocks // 2):
        part = slice(k * block, (k + 1) * block)
        stacked = jnp.concatenate([taps_high[part], taps_high[part], taps_low[part]], axis=0)
        now = jnp.dot(table, stacked, preferred_element_type=F32)
        spectra[k], spectra[k + blocks // 2] = now[:, :LANES], now[:, LANES:]
    for k in range(blocks):
        spec = spectra[k] if k == 0 else spectra[k] + sign * spectra[k - 1]
        real, imag = spec[:block], spec[block:]
        hre_ref[k] = real
        him_ref[k] = jnp.where(first_row, 0.0, imag)
        hfirst_ref[k] = jnp.where(first_row, imag, real)[:8]

    for copy in copies[8:]:
        copy.wait()
    high, low = split_value(back_ref[...])
    inv_ref[:, : 2 * block] = high
    inv_ref[:, 2 * block : 4 * block] = low
    inv_ref[:, 4 * block :] = high
    base_ref[...] = skip_ref[...] * x_ref[...].astype(F32)


def call_filter(weights, skip, x, gate, weight, blocks, outs):
    w1, b1, w2, b2, w3, decay = weights
    block, width = x.shape
    length = blocks * block
    emb, order = w1.shape
    pad = -(-emb // 8) * 8
    forward, inverse = dft_tables(block)
    feats = filter_feature_table(length, emb, pad)
    hbm = [
        w1, feats, b1[None], w2, b2[None], w3, decay[None], forward.astype(np.float32),
        inverse.astype(np.float32), skip[None], x, gate, weight,
    ]
    shape = jax.ShapeDtypeStruct
    out_shape = [
        shape((blocks, block, LANES), F32),
        shape((blocks, block, LANES), F32),
        shape((blocks, 8, LANES), F32),
        shape((2 * block, 2 * block), BF16),
        shape((block, 6 * block), BF16),
        shape(weight.shape, BF16),
        shape(gate.shape, BF16),
        shape(x.shape, F32),
    ]
    return pl.pallas_call(
        functools.partial(filter_kernel, blocks, block, outs, pad),
        in_specs=[pl.BlockSpec(memory_space=pltpu.HBM)] * len(hbm),
        out_specs=[pl.BlockSpec(memory_space=VMEM)] * len(out_shape),
        out_shape=out_shape,
        scratch_shapes=[
            VMEM(w1.shape, F32),
            VMEM((1, order), F32),
            VMEM(w2.shape, F32),
            VMEM((1, order), F32),
            VMEM(w3.shape, F32),
            VMEM((1, width), F32),
            VMEM(feats.shape, F32),
            VMEM(forward.shape, F32),
            VMEM(inverse.shape, F32),
            VMEM((1, width), F32),
            VMEM(x.shape, BF16),
            VMEM((6 * pad, 2 * order), F32),
            pltpu.SemaphoreType.DMA((len(hbm),)),
        ],
        compiler_params=pltpu.CompilerParams(vmem_limit_bytes=32 * 2**20),
        cost_estimate=pl.CostEstimate(
            flops=4 * 10**8, bytes_accessed=8 * 2**20, transcendentals=length * LANES
        ),
        name="filter_spectra",
    )(*(pltpu.with_memory_space_constraint(jnp.asarray(each), pltpu.HBM) for each in hbm))


def pack_kernel(blocks, outs, x_ref, out_ref, sems):
    copies = [
        pltpu.make_async_copy(
            x_ref.at[:, (d % outs) * LANES : (d % outs + 1) * LANES], out_ref.at[d], sems.at[d]
        )
        for d in range(blocks)
    ]
    for copy in copies:
        copy.start()
    for copy in copies:
        copy.wait()


def call_pack(x, blocks, outs):
    block, width = x.shape
    return pl.pallas_call(
        functools.partial(pack_kernel, blocks, outs),
        in_specs=[pl.BlockSpec(memory_space=pltpu.HBM)],
        out_specs=pl.BlockSpec(memory_space=VMEM),
        out_shape=jax.ShapeDtypeStruct((blocks, block, LANES), BF16),
        scratch_shapes=[pltpu.SemaphoreType.DMA((blocks,))],
        cost_estimate=pl.CostEstimate(flops=0, bytes_accessed=6 * x.size, transcendentals=0),
        name="pack_pieces",
    )(pltpu.with_memory_space_constraint(x, pltpu.HBM))


def conv_kernel(blocks, outs, block, xs_ref, hre_ref, him_ref, hfirst_ref, fwd_ref, inv_ref, *refs):
    conv_refs, (wre_ref, wim_ref, yre_ref, yim_ref) = refs[:outs], refs[outs:]
    me = lax.axis_index("seq")
    half, group = me // outs, me % outs
    earlier = blocks - outs
    for j in range(outs):
        values = jnp.concatenate([xs_ref[j], xs_ref[half * outs + j]], axis=1)
        spec = jnp.dot(
            fwd_ref[...], jnp.concatenate([values, values], axis=0), preferred_element_type=F32
        )
        before = jnp.where(half > 0, spec[:, :LANES], 0.0)
        wre_ref[j] = before[:block]
        wim_ref[j] = before[block:]
        wre_ref[earlier + j] = spec[:block, LANES:]
        wim_ref[earlier + j] = spec[block:, LANES:]

    def rows_at(start, first):
        rows = pl.ds(start, 8)
        wre = [wre_ref[j, rows, :] for j in range(blocks)]
        wim = [wim_ref[j, rows, :] for j in range(blocks)]
        for o in range(outs):
            total_re = total_im = None
            for j in range(earlier + o + 1):
                k = earlier + o - j
                hre = hre_ref[k, rows, :]
                him = him_ref[k, rows, :]
                hother = hfirst_ref[k] if first else hre
                add_re = wre[j] * hre - wim[j] * him
                add_im = wre[j] * him + wim[j] * hother
                total_re = add_re if total_re is None else total_re + add_re
                total_im = add_im if total_im is None else total_im + add_im
            yre_ref[o, rows, :] = total_re
            yim_ref[o, rows, :] = total_im

    rows_at(0, True)

    @pl.loop(1, block // 8)
    def _(tile):
        rows_at(pl.multiple_of(tile * 8, 8), False)

    def stacked(slot):
        re_high, re_low = split_value(yre_ref[slot])
        im_high, im_low = split_value(yim_ref[slot])
        return jnp.concatenate([re_high, im_high, re_high, im_high, re_low, im_low], axis=0)

    for k in range(0, outs, 2):
        pair = jnp.concatenate([stacked(group ^ k), stacked(group ^ (k + 1))], axis=1)
        conv = jnp.dot(inv_ref[...], pair, preferred_element_type=F32)
        conv_refs[k][...] = conv[:, :LANES]
        conv_refs[k + 1][...] = conv[:, LANES:]


def call_conv(xs, spectra, fwd, inv, outs):
    blocks, block, _ = xs.shape
    operands = [xs, *spectra, fwd, inv]
    return pl.pallas_call(
        functools.partial(conv_kernel, blocks, outs, block),
        in_specs=[pl.BlockSpec(memory_space=VMEM)] * len(operands),
        out_specs=[pl.BlockSpec(memory_space=VMEM)] * outs,
        out_shape=[jax.ShapeDtypeStruct((block, LANES), F32)] * outs,
        scratch_shapes=[
            VMEM((blocks, block, LANES), F32),
            VMEM((blocks, block, LANES), F32),
            VMEM((outs, block, LANES), F32),
            VMEM((outs, block, LANES), F32),
        ],
        compiler_params=pltpu.CompilerParams(vmem_limit_bytes=16 * 2**20),
        cost_estimate=pl.CostEstimate(
            flops=2 * 10**8, bytes_accessed=3 * 2**20, transcendentals=0
        ),
        name="convolve",
    )(*operands)


def project_block(left, weight_ref, part, width, out_ref):
    step = min(width, 2 * LANES)
    for start in range(0, width, step):
        lanes = pl.ds(pl.multiple_of(part * width + start, LANES), step)
        out_ref[:, start : start + step] = jnp.dot(
            left, weight_ref[:, lanes], preferred_element_type=F32
        ).astype(out_ref.dtype)


def gate_kernel(outs, parts, width, *refs):
    conv_refs, (gate_ref, base_ref, weight_ref, gated_ref, far_ref) = refs[:outs], refs[outs:]
    group = lax.axis_index("seq") % outs
    for k in range(outs):
        lanes = pl.ds(pl.multiple_of((group ^ k) * LANES, LANES), LANES)
        gate = gate_ref[:, lanes].astype(F32)
        gated_ref[:, lanes] = (gate * (conv_refs[k][...] + base_ref[:, lanes])).astype(BF16)
    part = lax.axis_index("chan") ^ (parts - 1)
    project_block(gated_ref[...], weight_ref, part, width, far_ref)


def project_kernel(parts, width, gated_ref, weight_ref, *out_refs):
    left = gated_ref[...]
    for k in reversed(range(parts - 1)):
        project_block(left, weight_ref, lax.axis_index("chan") ^ k, width, out_refs[k])


def call_gate(conv, gate, base, weight, parts):
    outs = len(conv)
    block, width = gate.shape
    columns = weight.shape[1] // parts
    operands = [*conv, gate, base, weight]
    return pl.pallas_call(
        functools.partial(gate_kernel, outs, parts, columns),
        in_specs=[pl.BlockSpec(memory_space=VMEM)] * len(operands),
        out_specs=[pl.BlockSpec(memory_space=VMEM)] * 2,
        out_shape=[
            jax.ShapeDtypeStruct((block, width), BF16),
            jax.ShapeDtypeStruct((block, columns), BF16 if parts > 1 else F32),
        ],
        compiler_params=pltpu.CompilerParams(vmem_limit_bytes=16 * 2**20),
        cost_estimate=pl.CostEstimate(
            flops=2 * block * width * columns, bytes_accessed=2 * width * columns, transcendentals=0
        ),
        name="gate_and_far_projection",
    )(*operands)


def call_project(gated, weight, parts):
    block, width = gated.shape
    columns = weight.shape[1] // parts
    return pl.pallas_call(
        functools.partial(project_kernel, parts, columns),
        in_specs=[pl.BlockSpec(memory_space=VMEM)] * 2,
        out_specs=[pl.BlockSpec(memory_space=VMEM)] * (parts - 1),
        out_shape=[
            jax.ShapeDtypeStruct((block, columns), BF16 if k else F32) for k in range(parts - 1)
        ],
        compiler_params=pltpu.CompilerParams(vmem_limit_bytes=16 * 2**20),
        cost_estimate=pl.CostEstimate(
            flops=2 * block * width * columns * (parts - 1),
            bytes_accessed=2 * width * columns * (parts - 1),
            transcendentals=0,
        ),
        name="projection",
    )(gated, weight)


def split_shards(
    mixer_input,
    gate_branch,
    skip_gain,
    decay_rate,
    first_weight,
    first_bias,
    second_weight,
    second_bias,
    last_weight,
    output_weight,
):
    block, width = mixer_input.shape
    blocks = lax.axis_size("seq")
    parts = lax.axis_size("chan")
    outs = width // LANES

    pieces = call_pack(mixer_input, blocks, outs)
    xs = lax.all_to_all(pieces, "seq", 0, 0, tiled=True)
    *spectra, fwd, inv, weight, gate, base = call_filter(
        (first_weight, first_bias, second_weight, second_bias, last_weight, decay_rate),
        skip_gain,
        mixer_input,
        gate_branch,
        output_weight,
        blocks,
        outs,
    )
    conv = call_conv(xs, spectra, fwd, inv, outs)
    conv = [conv[0]] + [
        lax.ppermute(conv[k], "seq", [(s, s ^ k) for s in range(blocks)]) for k in range(1, outs)
    ]
    send = lambda part, k: lax.ppermute(part, "chan", [(c, c ^ k) for c in range(parts)])
    gated, far = call_gate(conv, gate, base, weight, parts)
    if parts == 1:
        return far.astype(BF16)
    far = send(far, parts - 1)
    total, *near = call_project(gated, weight, parts)
    near = [send(near[k - 1], k) for k in range(1, parts - 1)]
    for part in (far, *near):
        total = total + part.astype(F32)
    return total.astype(BF16)


def contract_first(left_matrix, right_matrix):
    return lax.dot_general(
        left_matrix,
        right_matrix,
        (((0,), (0,)), ((), ())),
        precision=HIGHEST,
        preferred_element_type=F32,
    )


def filter_taps(
    first_weight, first_bias, second_weight, second_bias, last_weight, decay_rate, length
):
    features = jnp.asarray(feature_table(length, first_weight.shape[0]).T)
    hidden_one = jnp.sin(contract_first(first_weight, features) + first_bias[:, None])
    hidden_two = jnp.sin(contract_first(second_weight, hidden_one) + second_bias[:, None])
    shaped = contract_first(hidden_two, last_weight)
    positions = jnp.arange(length, dtype=jnp.int32).astype(F32)
    envelope = jnp.exp(-decay_rate[None, :] * (positions[:, None] / length))
    energy = jnp.expm1(-2.0 * decay_rate) / jnp.expm1(-2.0 * decay_rate / length)
    return shaped * envelope / jnp.sqrt(energy)[None, :]


def transform_tables(block_len):
    padded_len = 2 * block_len
    freq_index = jnp.arange(block_len + 1, dtype=jnp.int32)[:, None]
    time_index = jnp.arange(padded_len, dtype=jnp.int32)[None, :]
    angle = (freq_index * time_index % padded_len).astype(F32) * (2.0 * math.pi / padded_len)
    forward = jnp.concatenate([jnp.cos(angle), -jnp.sin(angle)], axis=0)
    later_angle = angle[:, block_len:]
    weights = jnp.where((freq_index == 0) | (freq_index == block_len), 1.0, 2.0) / padded_len
    inverse = jnp.concatenate(
        [(weights * jnp.cos(later_angle)).T, (-weights * jnp.sin(later_angle)).T], axis=1
    )
    return (forward, inverse)


def spectral_product(left_spec, right_spec, half_rows):
    left_real, left_imag = (left_spec[:half_rows], left_spec[half_rows:])
    right_real, right_imag = (right_spec[:half_rows], right_spec[half_rows:])
    return jnp.concatenate(
        [
            left_real * right_real - left_imag * right_imag,
            left_real * right_imag + left_imag * right_real,
        ],
        axis=0,
    )


def gathered_shards(
    mixer_input,
    gate_branch,
    skip_gain,
    decay_rate,
    first_weight,
    first_bias,
    second_weight,
    second_bias,
    last_weight,
    output_weight,
):
    block_len, chan_width = mixer_input.shape
    seq_count = lax.axis_size("seq")
    device = lax.axis_index("seq")
    half_rows = block_len + 1
    kernel_taps = filter_taps(
        first_weight,
        first_bias,
        second_weight,
        second_bias,
        last_weight,
        decay_rate,
        block_len * seq_count,
    )
    padded_taps = jnp.concatenate([jnp.zeros((block_len, chan_width), F32), kernel_taps], axis=0)
    forward, inverse = transform_tables(block_len)
    forward_head = forward[:, :block_len]
    gathered = lax.all_gather(mixer_input, "seq", axis=0, tiled=True)

    def one_block(block_index, total):
        rows = lax.dynamic_slice_in_dim(gathered, block_index * block_len, block_len, 0)
        source_spec = jnp.dot(
            forward_head, rows.astype(F32), precision=HIGHEST, preferred_element_type=F32
        )
        segment = lax.dynamic_slice_in_dim(
            padded_taps, (device - block_index) * block_len, 2 * block_len, 0
        )
        lag_spec = jnp.dot(forward, segment, precision=HIGHEST, preferred_element_type=F32)
        return total + spectral_product(lag_spec, source_spec, half_rows)

    total = lax.fori_loop(0, device + 1, one_block, jnp.zeros((2 * half_rows, chan_width), F32))
    convolved = jnp.dot(inverse, total, precision=HIGHEST, preferred_element_type=F32)
    values = mixer_input.astype(F32)
    gated_mix = (
        gate_branch.astype(F32) * (convolved + skip_gain[None, :] * values)
    ).astype(BF16)
    partial_out = jnp.dot(gated_mix, output_weight, preferred_element_type=F32)
    return lax.psum_scatter(partial_out, "chan", scatter_dimension=1, tiled=True).astype(BF16)


def solution(mesh):
    seq_count, chan_count = mesh.shape["seq"], mesh.shape["chan"]

    def shards(mixer_input, *rest):
        block, width = mixer_input.shape
        outs = width // LANES
        splits = (
            width % LANES == 0
            and block % LANES == 0
            and seq_count == 2 * outs
            and outs in (2, 4, 8)
            and chan_count in (1, 2, 4, 8)
        )
        plan = split_shards if splits else gathered_shards
        return plan(mixer_input, *rest)

    in_specs = (
        P("seq", "chan"),
        P("seq", "chan"),
        P("chan"),
        P("chan"),
        P(),
        P(),
        P(),
        P(),
        P(None, "chan"),
        P("chan", None),
    )
    out_specs = P("seq", "chan")
    return jax.shard_map(shards, mesh=mesh, in_specs=in_specs, out_specs=out_specs, check_vma=False)
```

```python
import functools
import math

import jax
import jax.numpy as jnp
import numpy as np
from jax import lax
from jax.experimental import pallas as pl
from jax.experimental.pallas import tpu as pltpu
from jax.sharding import PartitionSpec as P

HIGHEST = lax.Precision.HIGHEST
F32 = jnp.float32
BF16 = jnp.bfloat16
LANES = 128
FACE = 4
VMEM = pltpu.VMEM


def feature_table(length, emb_width):
    band_count = (emb_width - 1) // 2
    positions = np.arange(length, dtype=np.int64)
    columns = [positions / length]
    for band in range(1, band_count + 1):
        frequency = min(
            length // 2, max(band, int((length / 2) ** ((band - 1) / (band_count - 1))))
        )
        angle = (positions * frequency % length) * (2.0 * math.pi / length)
        columns.append(np.cos(angle))
        columns.append(np.sin(angle))
    return np.stack(columns, axis=1).astype(np.float32)


def split_bf16(table):
    high = table.astype(np.float32).astype(jnp.bfloat16)
    low = (table - high.astype(np.float64)).astype(np.float32).astype(jnp.bfloat16)
    return high, low


def dft_tables(block):
    size = 2 * block
    bins = np.arange(block)[:, None]
    times = np.arange(block)[None, :]
    angle = (bins * times % size) * (2.0 * math.pi / size)
    imag = -np.sin(angle)
    imag[0] = 1.0 - 2.0 * (np.arange(block) % 2)
    forward = np.concatenate([np.cos(angle), imag], axis=0)
    weight = np.where(bins == 0, 1.0, 2.0) / size
    back_imag = -weight * np.sin(angle)
    back_imag[0] = (1.0 - 2.0 * (np.arange(block) % 2)) / size
    inverse = np.concatenate([weight * np.cos(angle), back_imag], axis=0).T
    return forward, inverse


def fast_sin(x):
    turns = jnp.floor(x * (1.0 / math.pi) + 0.5)
    rest = x - turns * 3.140625
    rest = rest - turns * 9.67502593994140625e-4
    rest = rest - turns * 1.509957990978376432e-7
    parity = turns - 2.0 * jnp.floor(turns * 0.5)
    rest = rest * (1.0 - 2.0 * parity)
    square = rest * rest
    poly = -2.5052108e-8
    for coeff in (2.7557319e-6, -1.9841270e-4, 8.3333333e-3, -1.6666667e-1):
        poly = poly * square + coeff
    return rest + rest * square * poly


def expm1_of_negative(x):
    near = jnp.maximum(x, -0.5)
    series = jnp.full_like(x, 1.0 / 3628800.0)
    for denom in (362880.0, 40320.0, 5040.0, 720.0, 120.0, 24.0, 6.0, 2.0, 1.0):
        series = series * near + 1.0 / denom
    return jnp.where(x > -0.5, near * series, jnp.exp(x) - 1.0)


def split_value(value):
    high = value.astype(BF16)
    return high, (value - high.astype(F32)).astype(BF16)


def filter_feature_table(length, emb_width, pad):
    table = feature_table(length, emb_width)
    columns = []
    for half in (table[: length // 2], table[length // 2 :]):
        high, low = (part.astype(np.float32) for part in split_bf16(half))
        for part in (high, high, low):
            columns.append(np.pad(part, ((0, 0), (0, pad - emb_width))))
    return np.concatenate(columns, axis=1)


def twice_diagonal(value):
    zero = jnp.zeros_like(value)
    return jnp.concatenate(
        [jnp.concatenate([value, zero], axis=1), jnp.concatenate([zero, value], axis=1)], axis=0
    )


def stacked_diagonal(value):
    high, low = split_value(value)
    high = twice_diagonal(high.astype(F32))
    low = twice_diagonal(low.astype(F32))
    return jnp.concatenate([high, low, high], axis=0).astype(BF16)


def layer(value, weight):
    high, low = split_value(value)
    return jnp.dot(
        jnp.concatenate([high, high, low], axis=1), weight, preferred_element_type=F32
    )


def columns_of(part, half, width):
    return pl.ds(pl.multiple_of(part * width + half * (width // 2), LANES), width // 2)


def send_weight_copies(weight_ref, over_x_ref, over_y_ref, sems, first_sem):
    rows = weight_ref.shape[0] // 2
    width = weight_ref.shape[1] // FACE
    me = lax.axis_index("chan")
    half_rows = pl.ds(pl.multiple_of((lax.axis_index("seq") % 2) * rows, LANES), rows)
    copies = []
    for out_ref, half, parts in ((over_x_ref, 0, (1, 3)), (over_y_ref, 1, (2, 3))):
        for place, k in enumerate(parts):
            copies.append(
                pltpu.make_async_copy(
                    weight_ref.at[half_rows, columns_of(me ^ k, half, width)],
                    out_ref.at[:, place * (width // 2) : (place + 1) * (width // 2)],
                    sems.at[first_sem + len(copies)],
                )
            )
    return copies


def filter_kernel(blocks, block, outs, pad, *refs):
    hbm, refs = refs[:13], refs[13:]
    hre_ref, him_ref, hfirst_ref, fwd_ref, inv_ref, gate_ref, base_ref = refs[:7]
    over_x_ref, over_y_ref = refs[7:9]
    refs = refs[9:]
    w1_ref, b1_ref, w2_ref, b2_ref, w3_ref, decay_ref, feat_ref, table_ref, back_ref = refs[:9]
    skip_ref, x_ref, first_ref, sems = refs[9:]
    targets = [
        w1_ref, feat_ref, b1_ref, w2_ref, b2_ref, w3_ref, decay_ref, table_ref, back_ref,
        skip_ref, x_ref, gate_ref,
    ]
    copies = [
        pltpu.make_async_copy(hbm[i], targets[i], sems.at[i]) for i in range(len(targets))
    ]
    for copy in copies:
        copy.start()
    weight_copies = send_weight_copies(hbm[len(targets)], over_x_ref, over_y_ref, sems, len(targets))
    for copy in weight_copies:
        copy.start()
    group = lax.axis_index("seq") % outs
    length = blocks * block
    emb, order = w1_ref.shape
    first_ref[...] = jnp.zeros_like(first_ref)
    for copy in copies[:7]:
        copy.wait()

    high, low = split_value(w1_ref[...])
    high, low = high.astype(F32), low.astype(F32)
    zero = jnp.zeros_like(high)
    for i, part in enumerate((high, low, high)):
        first_ref[i * pad : i * pad + emb] = jnp.concatenate([part, zero], axis=1)
        first_ref[(3 + i) * pad : (3 + i) * pad + emb] = jnp.concatenate([zero, part], axis=1)
    b1 = jnp.concatenate([b1_ref[...]] * 2, axis=1)
    b2 = jnp.concatenate([b2_ref[...]] * 2, axis=1)
    hidden = fast_sin(
        jnp.dot(
            feat_ref[...].astype(BF16), first_ref[...].astype(BF16), preferred_element_type=F32
        )
        + b1
    )
    hidden = fast_sin(layer(hidden, stacked_diagonal(w2_ref[...])) + b2)
    lanes = pl.ds(pl.multiple_of(group * LANES, LANES), LANES)
    shaped = layer(hidden, stacked_diagonal(w3_ref[:, lanes]))

    decay = decay_ref[:, lanes]
    energy = expm1_of_negative(-2.0 * decay) / expm1_of_negative(decay * (-2.0 / length))
    times = lax.broadcasted_iota(jnp.int32, (length // 2, LANES), 0).astype(F32) * (1.0 / length)
    window = jnp.exp(-(decay * times)) * (1.0 / jnp.sqrt(energy))
    window = jnp.concatenate([window, window * jnp.exp(-0.5 * decay)], axis=1)
    taps_high, taps_low = split_value(shaped * window)

    copies[7].wait()
    high, low = split_value(table_ref[...])
    fwd_ref[:, :block] = high
    fwd_ref[:, block:] = low
    table = jnp.concatenate([high, low, high], axis=1)
    rows = lax.broadcasted_iota(jnp.int32, (2 * block, LANES), 0)
    sign = (1 - 2 * lax.rem(rows, 2)).astype(F32)
    first_row = lax.broadcasted_iota(jnp.int32, (block, LANES), 0) == 0
    spectra = [None] * blocks
    for k in range(blocks // 2):
        part = slice(k * block, (k + 1) * block)
        stacked = jnp.concatenate([taps_high[part], taps_high[part], taps_low[part]], axis=0)
        now = jnp.dot(table, stacked, preferred_element_type=F32)
        spectra[k], spectra[k + blocks // 2] = now[:, :LANES], now[:, LANES:]
    for k in range(blocks):
        spec = spectra[k] if k == 0 else spectra[k] + sign * spectra[k - 1]
        real, imag = spec[:block], spec[block:]
        hre_ref[k] = real
        him_ref[k] = jnp.where(first_row, 0.0, imag)
        hfirst_ref[k] = jnp.where(first_row, imag, real)[:8]

    for copy in copies[8:] + weight_copies:
        copy.wait()
    high, low = split_value(back_ref[...])
    inv_ref[:, : 2 * block] = high
    inv_ref[:, 2 * block : 4 * block] = low
    inv_ref[:, 4 * block :] = high
    base_ref[...] = skip_ref[...] * x_ref[...].astype(F32)


def call_filter(weights, skip, x, gate, weight, blocks, outs):
    w1, b1, w2, b2, w3, decay = weights
    block, width = x.shape
    length = blocks * block
    emb, order = w1.shape
    pad = -(-emb // 8) * 8
    forward, inverse = dft_tables(block)
    feats = filter_feature_table(length, emb, pad)
    hbm = [
        w1, feats, b1[None], w2, b2[None], w3, decay[None], forward.astype(np.float32),
        inverse.astype(np.float32), skip[None], x, gate, weight,
    ]
    shape = jax.ShapeDtypeStruct
    out_shape = [
        shape((blocks, block, LANES), F32),
        shape((blocks, block, LANES), F32),
        shape((blocks, 8, LANES), F32),
        shape((2 * block, 2 * block), BF16),
        shape((block, 6 * block), BF16),
        shape(gate.shape, BF16),
        shape(x.shape, F32),
    ]
    send_shape = [shape((weight.shape[0] // 2, weight.shape[1] // FACE), BF16)] * 2
    return pl.pallas_call(
        functools.partial(filter_kernel, blocks, block, outs, pad),
        in_specs=[pl.BlockSpec(memory_space=pltpu.HBM)] * len(hbm),
        out_specs=[pl.BlockSpec(memory_space=VMEM)] * len(out_shape)
        + [pl.BlockSpec(memory_space=pltpu.HBM)] * 2,
        out_shape=out_shape + send_shape,
        scratch_shapes=[
            VMEM(w1.shape, F32),
            VMEM((1, order), F32),
            VMEM(w2.shape, F32),
            VMEM((1, order), F32),
            VMEM(w3.shape, F32),
            VMEM((1, width), F32),
            VMEM(feats.shape, F32),
            VMEM(forward.shape, F32),
            VMEM(inverse.shape, F32),
            VMEM((1, width), F32),
            VMEM(x.shape, BF16),
            VMEM((6 * pad, 2 * order), F32),
            pltpu.SemaphoreType.DMA((len(hbm) + 3,)),
        ],
        compiler_params=pltpu.CompilerParams(vmem_limit_bytes=32 * 2**20),
        cost_estimate=pl.CostEstimate(
            flops=4 * 10**8, bytes_accessed=8 * 2**20, transcendentals=length * LANES
        ),
        name="filter_spectra",
    )(*(pltpu.with_memory_space_constraint(jnp.asarray(each), pltpu.HBM) for each in hbm))


def pack_kernel(blocks, outs, x_ref, out_ref, sems):
    copies = [
        pltpu.make_async_copy(
            x_ref.at[:, (d % outs) * LANES : (d % outs + 1) * LANES], out_ref.at[d], sems.at[d]
        )
        for d in range(blocks)
    ]
    for copy in copies:
        copy.start()
    for copy in copies:
        copy.wait()


def call_pack(x, blocks, outs):
    block, width = x.shape
    return pl.pallas_call(
        functools.partial(pack_kernel, blocks, outs),
        in_specs=[pl.BlockSpec(memory_space=pltpu.HBM)],
        out_specs=pl.BlockSpec(memory_space=VMEM),
        out_shape=jax.ShapeDtypeStruct((blocks, block, LANES), BF16),
        scratch_shapes=[pltpu.SemaphoreType.DMA((blocks,))],
        cost_estimate=pl.CostEstimate(flops=0, bytes_accessed=6 * x.size, transcendentals=0),
        name="pack_pieces",
    )(pltpu.with_memory_space_constraint(x, pltpu.HBM))


def conv_kernel(blocks, outs, block, xs_ref, hre_ref, him_ref, hfirst_ref, fwd_ref, inv_ref, *refs):
    conv_refs, (wre_ref, wim_ref, yre_ref, yim_ref) = refs[:outs], refs[outs:]
    me = lax.axis_index("seq")
    half, group = me // outs, me % outs
    earlier = blocks - outs
    for j in range(outs):
        values = jnp.concatenate([xs_ref[j], xs_ref[half * outs + j]], axis=1)
        spec = jnp.dot(
            fwd_ref[...], jnp.concatenate([values, values], axis=0), preferred_element_type=F32
        )
        before = jnp.where(half > 0, spec[:, :LANES], 0.0)
        wre_ref[j] = before[:block]
        wim_ref[j] = before[block:]
        wre_ref[earlier + j] = spec[:block, LANES:]
        wim_ref[earlier + j] = spec[block:, LANES:]

    def rows_at(start, first):
        rows = pl.ds(start, 8)
        wre = [wre_ref[j, rows, :] for j in range(blocks)]
        wim = [wim_ref[j, rows, :] for j in range(blocks)]
        for o in range(outs):
            total_re = total_im = None
            for j in range(earlier + o + 1):
                k = earlier + o - j
                hre = hre_ref[k, rows, :]
                him = him_ref[k, rows, :]
                hother = hfirst_ref[k] if first else hre
                add_re = wre[j] * hre - wim[j] * him
                add_im = wre[j] * him + wim[j] * hother
                total_re = add_re if total_re is None else total_re + add_re
                total_im = add_im if total_im is None else total_im + add_im
            yre_ref[o, rows, :] = total_re
            yim_ref[o, rows, :] = total_im

    rows_at(0, True)

    @pl.loop(1, block // 8)
    def _(tile):
        rows_at(pl.multiple_of(tile * 8, 8), False)

    def stacked(slot):
        re_high, re_low = split_value(yre_ref[slot])
        im_high, im_low = split_value(yim_ref[slot])
        return jnp.concatenate([re_high, im_high, re_high, im_high, re_low, im_low], axis=0)

    for k in range(0, outs, 2):
        pair = jnp.concatenate([stacked(group ^ k), stacked(group ^ (k + 1))], axis=1)
        conv = jnp.dot(inv_ref[...], pair, preferred_element_type=F32)
        conv_refs[k][...] = conv[:, :LANES]
        conv_refs[k + 1][...] = conv[:, LANES:]


def call_conv(xs, spectra, fwd, inv, outs):
    blocks, block, _ = xs.shape
    operands = [xs, *spectra, fwd, inv]
    return pl.pallas_call(
        functools.partial(conv_kernel, blocks, outs, block),
        in_specs=[pl.BlockSpec(memory_space=VMEM)] * len(operands),
        out_specs=[pl.BlockSpec(memory_space=VMEM)] * outs,
        out_shape=[jax.ShapeDtypeStruct((block, LANES), F32)] * outs,
        scratch_shapes=[
            VMEM((blocks, block, LANES), F32),
            VMEM((blocks, block, LANES), F32),
            VMEM((outs, block, LANES), F32),
            VMEM((outs, block, LANES), F32),
        ],
        compiler_params=pltpu.CompilerParams(vmem_limit_bytes=16 * 2**20),
        cost_estimate=pl.CostEstimate(
            flops=2 * 10**8, bytes_accessed=3 * 2**20, transcendentals=0
        ),
        name="convolve",
    )(*operands)


def gate_kernel(outs, *refs):
    conv_refs, (gate_ref, base_ref, gated_ref) = refs[:outs], refs[outs:]
    group = lax.axis_index("seq") % outs
    for k in range(outs):
        lanes = pl.ds(pl.multiple_of((group ^ k) * LANES, LANES), LANES)
        gate = gate_ref[:, lanes].astype(F32)
        gated_ref[:, lanes] = (gate * (conv_refs[k][...] + base_ref[:, lanes])).astype(BF16)


def tiles(width):
    step = min(width, 2 * LANES)
    return [slice(start, start + step) for start in range(0, width, step)]


def own_kernel(width, gated_ref, weight_ref, *refs):
    out_refs, (held_ref, sems) = refs[:4], refs[4:]
    me = lax.axis_index("chan")
    copies = [
        pltpu.make_async_copy(
            weight_ref.at[:, columns_of(me ^ k, half, width)], held_ref.at[i], sems.at[i]
        )
        for i, (k, half) in enumerate(((2, 0), (1, 1), (0, 0), (0, 1)))
    ]
    for copy in copies:
        copy.start()
    left = gated_ref[...]
    for i, copy in enumerate(copies):
        copy.wait()
        for lanes in tiles(width // 2):
            out_refs[i][:, lanes] = jnp.dot(
                left, held_ref[i, :, lanes], preferred_element_type=F32
            )


def neighbour_kernel(first, x_ref, y_ref, *refs):
    from_x, from_y, sums, outs = refs[:2], refs[2:4], refs[4:6], refs[6:]
    rows = from_x[0].shape[0]
    core = lax.axis_index("seq") % 2
    for left_ref, held, sum_ref, out_ref in (
        (x_ref, from_x, sums[0], outs[0]),
        (y_ref, from_y, sums[1], outs[1]),
    ):
        near = left_ref[:, pl.ds(pl.multiple_of(core * rows, LANES), rows)]
        far = left_ref[:, pl.ds(pl.multiple_of((1 - core) * rows, LANES), rows)]
        width = out_ref.shape[1]
        for lanes in tiles(width):
            place = slice(first * width + lanes.start, first * width + lanes.stop)
            total = jnp.dot(near, held[0][:, place], preferred_element_type=F32)
            total += jnp.dot(far, held[1][:, place], preferred_element_type=F32)
            out_ref[:, lanes] = (sum_ref[:, lanes] + total).astype(out_ref.dtype)


def last_kernel(*refs):
    sums, arrived, out_ref = refs[:2], refs[2:4], refs[4]
    width = sums[0].shape[1]
    for half in range(2):
        out_ref[:, half * width : (half + 1) * width] = (
            sums[half][...] + arrived[half][...].astype(F32)
        ).astype(BF16)


def in_vmem(kernel, operands, out_shape, name, flops, scratch=()):
    return pl.pallas_call(
        kernel,
        in_specs=[pl.BlockSpec(memory_space=VMEM)] * len(operands),
        out_specs=jax.tree.map(lambda _: pl.BlockSpec(memory_space=VMEM), out_shape),
        out_shape=out_shape,
        scratch_shapes=scratch,
        compiler_params=pltpu.CompilerParams(vmem_limit_bytes=16 * 2**20),
        cost_estimate=pl.CostEstimate(flops=flops, bytes_accessed=2**20, transcendentals=0),
        name=name,
    )(*operands)


def call_own(gated, weight):
    block, width = gated.shape
    columns = weight.shape[1] // FACE
    return pl.pallas_call(
        functools.partial(own_kernel, columns),
        in_specs=[pl.BlockSpec(memory_space=VMEM), pl.BlockSpec(memory_space=pltpu.HBM)],
        out_specs=[pl.BlockSpec(memory_space=VMEM)] * 4,
        out_shape=[jax.ShapeDtypeStruct((block, columns // 2), F32)] * 4,
        scratch_shapes=[
            VMEM((4, width, columns // 2), BF16),
            pltpu.SemaphoreType.DMA((4,)),
        ],
        compiler_params=pltpu.CompilerParams(vmem_limit_bytes=16 * 2**20),
        cost_estimate=pl.CostEstimate(
            flops=4 * block * width * columns, bytes_accessed=6 * width * columns, transcendentals=0
        ),
        name="own_channels",
    )(gated, pltpu.with_memory_space_constraint(weight, pltpu.HBM))


def split_shards(
    mixer_input,
    gate_branch,
    skip_gain,
    decay_rate,
    first_weight,
    first_bias,
    second_weight,
    second_bias,
    last_weight,
    output_weight,
):
    block, width = mixer_input.shape
    blocks = lax.axis_size("seq")
    outs = width // LANES

    pieces = call_pack(mixer_input, blocks, outs)
    xs = lax.all_to_all(pieces, "seq", 0, 0, tiled=True)
    *spectra, fwd, inv, gate, base, over_x, over_y = call_filter(
        (first_weight, first_bias, second_weight, second_bias, last_weight, decay_rate),
        skip_gain,
        mixer_input,
        gate_branch,
        output_weight,
        blocks,
        outs,
    )
    along_seq = lambda part, k: lax.ppermute(part, "seq", [(s, s ^ k) for s in range(blocks)])
    along_chan = lambda part, k: lax.ppermute(part, "chan", [(c, c ^ k) for c in range(FACE)])
    from_x, from_y = along_chan(over_x, 1), along_chan(over_y, 2)
    from_x, from_y = (from_x, along_seq(from_x, 1)), (from_y, along_seq(from_y, 1))

    conv = call_conv(xs, spectra, fwd, inv, outs)
    conv = [conv[0]] + [along_seq(conv[k], k) for k in range(1, outs)]
    shape = jax.ShapeDtypeStruct
    gated = in_vmem(
        functools.partial(gate_kernel, outs), [*conv, gate, base], shape((block, width), BF16), "gate", 10**6
    )
    x_gated, y_gated = along_chan(gated, 1), along_chan(gated, 2)
    send_a, send_b, keep_a, keep_b = call_own(gated, output_weight)
    columns = send_a.shape[1]
    flops = 4 * block * width * columns
    send_a, send_b = in_vmem(
        functools.partial(neighbour_kernel, 1),
        [x_gated, y_gated, *from_x, *from_y, send_a, send_b],
        [shape((block, columns), BF16)] * 2,
        "sums_to_send",
        flops,
    )
    got_a, got_b = along_chan(send_a, 2), along_chan(send_b, 1)
    keep_a, keep_b = in_vmem(
        functools.partial(neighbour_kernel, 0),
        [x_gated, y_gated, *from_x, *from_y, keep_a, keep_b],
        [shape((block, columns), F32)] * 2,
        "sums_to_keep",
        flops,
    )
    return in_vmem(
        last_kernel,
        [keep_a, keep_b, got_a, got_b],
        shape((block, 2 * columns), BF16),
        "last_sum",
        10**6,
    )


def contract_first(left_matrix, right_matrix):
    return lax.dot_general(
        left_matrix,
        right_matrix,
        (((0,), (0,)), ((), ())),
        precision=HIGHEST,
        preferred_element_type=F32,
    )


def filter_taps(
    first_weight, first_bias, second_weight, second_bias, last_weight, decay_rate, length
):
    features = jnp.asarray(feature_table(length, first_weight.shape[0]).T)
    hidden_one = jnp.sin(contract_first(first_weight, features) + first_bias[:, None])
    hidden_two = jnp.sin(contract_first(second_weight, hidden_one) + second_bias[:, None])
    shaped = contract_first(hidden_two, last_weight)
    positions = jnp.arange(length, dtype=jnp.int32).astype(F32)
    envelope = jnp.exp(-decay_rate[None, :] * (positions[:, None] / length))
    energy = jnp.expm1(-2.0 * decay_rate) / jnp.expm1(-2.0 * decay_rate / length)
    return shaped * envelope / jnp.sqrt(energy)[None, :]


def transform_tables(block_len):
    padded_len = 2 * block_len
    freq_index = jnp.arange(block_len + 1, dtype=jnp.int32)[:, None]
    time_index = jnp.arange(padded_len, dtype=jnp.int32)[None, :]
    angle = (freq_index * time_index % padded_len).astype(F32) * (2.0 * math.pi / padded_len)
    forward = jnp.concatenate([jnp.cos(angle), -jnp.sin(angle)], axis=0)
    later_angle = angle[:, block_len:]
    weights = jnp.where((freq_index == 0) | (freq_index == block_len), 1.0, 2.0) / padded_len
    inverse = jnp.concatenate(
        [(weights * jnp.cos(later_angle)).T, (-weights * jnp.sin(later_angle)).T], axis=1
    )
    return (forward, inverse)


def spectral_product(left_spec, right_spec, half_rows):
    left_real, left_imag = (left_spec[:half_rows], left_spec[half_rows:])
    right_real, right_imag = (right_spec[:half_rows], right_spec[half_rows:])
    return jnp.concatenate(
        [
            left_real * right_real - left_imag * right_imag,
            left_real * right_imag + left_imag * right_real,
        ],
        axis=0,
    )


def gathered_shards(
    mixer_input,
    gate_branch,
    skip_gain,
    decay_rate,
    first_weight,
    first_bias,
    second_weight,
    second_bias,
    last_weight,
    output_weight,
):
    block_len, chan_width = mixer_input.shape
    seq_count = lax.axis_size("seq")
    device = lax.axis_index("seq")
    half_rows = block_len + 1
    kernel_taps = filter_taps(
        first_weight,
        first_bias,
        second_weight,
        second_bias,
        last_weight,
        decay_rate,
        block_len * seq_count,
    )
    padded_taps = jnp.concatenate([jnp.zeros((block_len, chan_width), F32), kernel_taps], axis=0)
    forward, inverse = transform_tables(block_len)
    forward_head = forward[:, :block_len]
    gathered = lax.all_gather(mixer_input, "seq", axis=0, tiled=True)

    def one_block(block_index, total):
        rows = lax.dynamic_slice_in_dim(gathered, block_index * block_len, block_len, 0)
        source_spec = jnp.dot(
            forward_head, rows.astype(F32), precision=HIGHEST, preferred_element_type=F32
        )
        segment = lax.dynamic_slice_in_dim(
            padded_taps, (device - block_index) * block_len, 2 * block_len, 0
        )
        lag_spec = jnp.dot(forward, segment, precision=HIGHEST, preferred_element_type=F32)
        return total + spectral_product(lag_spec, source_spec, half_rows)

    total = lax.fori_loop(0, device + 1, one_block, jnp.zeros((2 * half_rows, chan_width), F32))
    convolved = jnp.dot(inverse, total, precision=HIGHEST, preferred_element_type=F32)
    values = mixer_input.astype(F32)
    gated_mix = (
        gate_branch.astype(F32) * (convolved + skip_gain[None, :] * values)
    ).astype(BF16)
    partial_out = jnp.dot(gated_mix, output_weight, preferred_element_type=F32)
    return lax.psum_scatter(partial_out, "chan", scatter_dimension=1, tiled=True).astype(BF16)


def solution(mesh):
    seq_count, chan_count = mesh.shape["seq"], mesh.shape["chan"]

    def shards(mixer_input, *rest):
        block, width = mixer_input.shape
        outs = width // LANES
        splits = (
            width % LANES == 0
            and block % LANES == 0
            and seq_count == 2 * outs
            and outs in (2, 4, 8)
            and chan_count == FACE
        )
        plan = split_shards if splits else gathered_shards
        return plan(mixer_input, *rest)

    in_specs = (
        P("seq", "chan"),
        P("seq", "chan"),
        P("chan"),
        P("chan"),
        P(),
        P(),
        P(),
        P(),
        P(None, "chan"),
        P("chan", None),
    )
    out_specs = P("seq", "chan")
    return jax.shard_map(shards, mesh=mesh, in_specs=in_specs, out_specs=out_specs, check_vma=False)
```

```python
import functools
import math

import jax
import jax.numpy as jnp
import numpy as np
from jax import lax
from jax.experimental import pallas as pl
from jax.experimental.pallas import tpu as pltpu
from jax.sharding import PartitionSpec as P

HIGHEST = lax.Precision.HIGHEST
F32 = jnp.float32
BF16 = jnp.bfloat16
LANES = 128
FACE = 4
VMEM = pltpu.VMEM


def feature_table(length, emb_width):
    band_count = (emb_width - 1) // 2
    positions = np.arange(length, dtype=np.int64)
    columns = [positions / length]
    for band in range(1, band_count + 1):
        frequency = min(
            length // 2, max(band, int((length / 2) ** ((band - 1) / (band_count - 1))))
        )
        angle = (positions * frequency % length) * (2.0 * math.pi / length)
        columns.append(np.cos(angle))
        columns.append(np.sin(angle))
    return np.stack(columns, axis=1).astype(np.float32)


def split_bf16(table):
    high = table.astype(np.float32).astype(jnp.bfloat16)
    low = (table - high.astype(np.float64)).astype(np.float32).astype(jnp.bfloat16)
    return high, low


def dft_tables(block):
    size = 2 * block
    bins = np.arange(block)[:, None]
    times = np.arange(block)[None, :]
    angle = (bins * times % size) * (2.0 * math.pi / size)
    imag = -np.sin(angle)
    imag[0] = 1.0 - 2.0 * (np.arange(block) % 2)
    forward = np.concatenate([np.cos(angle), imag], axis=0)
    weight = np.where(bins == 0, 1.0, 2.0) / size
    back_imag = -weight * np.sin(angle)
    back_imag[0] = (1.0 - 2.0 * (np.arange(block) % 2)) / size
    inverse = np.concatenate([weight * np.cos(angle), back_imag], axis=0).T
    return forward, inverse


def fast_sin(x):
    turns = jnp.floor(x * (1.0 / math.pi) + 0.5)
    rest = x - turns * 3.140625
    rest = rest - turns * 9.67502593994140625e-4
    rest = rest - turns * 1.509957990978376432e-7
    parity = turns - 2.0 * jnp.floor(turns * 0.5)
    rest = rest * (1.0 - 2.0 * parity)
    square = rest * rest
    poly = -2.5052108e-8
    for coeff in (2.7557319e-6, -1.9841270e-4, 8.3333333e-3, -1.6666667e-1):
        poly = poly * square + coeff
    return rest + rest * square * poly


def expm1_of_negative(x):
    near = jnp.maximum(x, -0.5)
    series = jnp.full_like(x, 1.0 / 3628800.0)
    for denom in (362880.0, 40320.0, 5040.0, 720.0, 120.0, 24.0, 6.0, 2.0, 1.0):
        series = series * near + 1.0 / denom
    return jnp.where(x > -0.5, near * series, jnp.exp(x) - 1.0)


def split_value(value):
    high = value.astype(BF16)
    return high, (value - high.astype(F32)).astype(BF16)


def filter_feature_table(length, emb_width, pad):
    table = feature_table(length, emb_width)
    columns = []
    for half in (table[: length // 2], table[length // 2 :]):
        high, low = (part.astype(np.float32) for part in split_bf16(half))
        for part in (high, high, low):
            columns.append(np.pad(part, ((0, 0), (0, pad - emb_width))))
    return np.concatenate(columns, axis=1)


def twice_diagonal(value):
    zero = jnp.zeros_like(value)
    return jnp.concatenate(
        [jnp.concatenate([value, zero], axis=1), jnp.concatenate([zero, value], axis=1)], axis=0
    )


def stacked_diagonal(value):
    high, low = split_value(value)
    high = twice_diagonal(high.astype(F32))
    low = twice_diagonal(low.astype(F32))
    return jnp.concatenate([high, low, high], axis=0).astype(BF16)


def layer(value, weight):
    high, low = split_value(value)
    return jnp.dot(
        jnp.concatenate([high, high, low], axis=1), weight, preferred_element_type=F32
    )


def filter_kernel(blocks, block, outs, pad, *refs):
    hbm, refs = refs[:9], refs[9:]
    hre_ref, him_ref, hfirst_ref, fwd_ref, inv_ref = refs[:5]
    refs = refs[5:]
    w1_ref, b1_ref, w2_ref, b2_ref, w3_ref, decay_ref, feat_ref, table_ref, back_ref = refs[:9]
    first_ref, sems = refs[9:]
    targets = [
        w1_ref, feat_ref, b1_ref, w2_ref, b2_ref, w3_ref, decay_ref, table_ref, back_ref
    ]
    copies = [
        pltpu.make_async_copy(hbm[i], targets[i], sems.at[i]) for i in range(len(targets))
    ]
    for copy in copies:
        copy.start()
    group = lax.axis_index("seq") % outs
    length = blocks * block
    emb, order = w1_ref.shape
    first_ref[...] = jnp.zeros_like(first_ref)
    for copy in copies[:7]:
        copy.wait()

    high, low = split_value(w1_ref[...])
    high, low = high.astype(F32), low.astype(F32)
    zero = jnp.zeros_like(high)
    for i, part in enumerate((high, low, high)):
        first_ref[i * pad : i * pad + emb] = jnp.concatenate([part, zero], axis=1)
        first_ref[(3 + i) * pad : (3 + i) * pad + emb] = jnp.concatenate([zero, part], axis=1)
    b1 = jnp.concatenate([b1_ref[...]] * 2, axis=1)
    b2 = jnp.concatenate([b2_ref[...]] * 2, axis=1)
    hidden = fast_sin(
        jnp.dot(
            feat_ref[...].astype(BF16), first_ref[...].astype(BF16), preferred_element_type=F32
        )
        + b1
    )
    hidden = fast_sin(layer(hidden, stacked_diagonal(w2_ref[...])) + b2)
    lanes = pl.ds(pl.multiple_of(group * LANES, LANES), LANES)
    shaped = layer(hidden, stacked_diagonal(w3_ref[:, lanes]))

    decay = decay_ref[:, lanes]
    energy = expm1_of_negative(-2.0 * decay) / expm1_of_negative(decay * (-2.0 / length))
    times = lax.broadcasted_iota(jnp.int32, (length // 2, LANES), 0).astype(F32) * (1.0 / length)
    window = jnp.exp(-(decay * times)) * (1.0 / jnp.sqrt(energy))
    window = jnp.concatenate([window, window * jnp.exp(-0.5 * decay)], axis=1)
    taps_high, taps_low = split_value(shaped * window)

    copies[7].wait()
    high, low = split_value(table_ref[...])
    fwd_ref[:, :block] = high
    fwd_ref[:, block:] = low
    table = jnp.concatenate([high, low, high], axis=1)
    rows = lax.broadcasted_iota(jnp.int32, (2 * block, LANES), 0)
    sign = (1 - 2 * lax.rem(rows, 2)).astype(F32)
    first_row = lax.broadcasted_iota(jnp.int32, (block, LANES), 0) == 0
    spectra = [None] * blocks
    for k in range(blocks // 2):
        part = slice(k * block, (k + 1) * block)
        stacked = jnp.concatenate([taps_high[part], taps_high[part], taps_low[part]], axis=0)
        now = jnp.dot(table, stacked, preferred_element_type=F32)
        spectra[k], spectra[k + blocks // 2] = now[:, :LANES], now[:, LANES:]
    for k in range(blocks):
        spec = spectra[k] if k == 0 else spectra[k] + sign * spectra[k - 1]
        real, imag = spec[:block], spec[block:]
        hre_ref[k] = real
        him_ref[k] = jnp.where(first_row, 0.0, imag)
        hfirst_ref[k] = jnp.where(first_row, imag, real)[:8]

    copies[8].wait()
    high, low = split_value(back_ref[...])
    inv_ref[:, : 2 * block] = high
    inv_ref[:, 2 * block : 4 * block] = low
    inv_ref[:, 4 * block :] = high


def call_filter(weights, blocks, outs, block):
    w1, b1, w2, b2, w3, decay = weights
    length = blocks * block
    emb, order = w1.shape
    pad = -(-emb // 8) * 8
    forward, inverse = dft_tables(block)
    feats = filter_feature_table(length, emb, pad)
    hbm = [
        w1, feats, b1[None], w2, b2[None], w3, decay[None], forward.astype(np.float32),
        inverse.astype(np.float32),
    ]
    out_shape = [
        VMEM((blocks, block, LANES), F32),
        VMEM((blocks, block, LANES), F32),
        VMEM((blocks, 8, LANES), F32),
        VMEM((2 * block, 2 * block), BF16),
        VMEM((block, 6 * block), BF16),
    ]
    return pl.pallas_call(
        functools.partial(filter_kernel, blocks, block, outs, pad),
        in_specs=[pl.BlockSpec(memory_space=pltpu.HBM)] * len(hbm),
        out_specs=[pl.BlockSpec(memory_space=VMEM)] * len(out_shape),
        out_shape=out_shape,
        scratch_shapes=[
            VMEM(w1.shape, F32),
            VMEM((1, order), F32),
            VMEM(w2.shape, F32),
            VMEM((1, order), F32),
            VMEM(w3.shape, F32),
            VMEM((1, w3.shape[1]), F32),
            VMEM(feats.shape, F32),
            VMEM(forward.shape, F32),
            VMEM(inverse.shape, F32),
            VMEM((6 * pad, 2 * order), F32),
            pltpu.SemaphoreType.DMA((len(hbm),)),
        ],
        compiler_params=pltpu.CompilerParams(vmem_limit_bytes=32 * 2**20),
        cost_estimate=pl.CostEstimate(
            flops=4 * 10**8, bytes_accessed=8 * 2**20, transcendentals=length * LANES
        ),
        name="filter_spectra",
    )(*(pltpu.with_memory_space_constraint(jnp.asarray(each), pltpu.HBM) for each in hbm))


def columns_of(part, half, width):
    return pl.ds(pl.multiple_of(part * width + half * (width // 2), LANES), width // 2)


def weight_copies(weight_ref, over_x_ref, over_y_ref, sems, first_sem):
    rows = weight_ref.shape[0] // 2
    width = weight_ref.shape[1] // FACE
    me = lax.axis_index("chan")
    half_rows = pl.ds(pl.multiple_of((lax.axis_index("seq") % 2) * rows, LANES), rows)
    copies = []
    for out_ref, half, parts in ((over_x_ref, 0, (1, 3)), (over_y_ref, 1, (2, 3))):
        for place, k in enumerate(parts):
            copies.append(
                pltpu.make_async_copy(
                    weight_ref.at[half_rows, columns_of(me ^ k, half, width)],
                    out_ref.at[:, place * (width // 2) : (place + 1) * (width // 2)],
                    sems.at[first_sem + len(copies)],
                )
            )
    return copies


def pack_kernel(
    x_ref, gate_ref, weight_ref, here_ref, there_ref, here_both_ref, there_both_ref, over_x_ref, over_y_ref, sems
):
    wide = 2 * LANES
    block = x_ref.shape[0]
    chip = (lax.axis_index("seq") // 2) % 2
    copies = []
    for place, alone_ref, both_ref in (
        (chip, here_ref, here_both_ref),
        (1 - chip, there_ref, there_both_ref),
    ):
        lanes = pl.ds(pl.multiple_of(place * wide, LANES), wide)
        for source, target in (
            (x_ref, alone_ref),
            (x_ref, both_ref.at[:block]),
            (gate_ref, both_ref.at[block:]),
        ):
            copies.append(
                pltpu.make_async_copy(source.at[:, lanes], target, sems.at[len(copies)])
            )
    copies += weight_copies(weight_ref, over_x_ref, over_y_ref, sems, len(copies))
    for copy in copies:
        copy.start()
    for copy in copies:
        copy.wait()


def call_pack(x, gate, weight):
    block = x.shape[0]
    shape = jax.ShapeDtypeStruct
    send = shape((weight.shape[0] // 2, weight.shape[1] // FACE), BF16)
    alone, both = (shape((rows, 2 * LANES), BF16) for rows in (block, 2 * block))
    return pl.pallas_call(
        pack_kernel,
        in_specs=[pl.BlockSpec(memory_space=pltpu.HBM)] * 3,
        out_specs=[pl.BlockSpec(memory_space=VMEM)] * 4
        + [pl.BlockSpec(memory_space=pltpu.HBM)] * 2,
        out_shape=[alone, alone, both, both, send, send],
        scratch_shapes=[pltpu.SemaphoreType.DMA((10,))],
        cost_estimate=pl.CostEstimate(flops=0, bytes_accessed=2**21, transcendentals=0),
        name="pack_pieces",
    )(*(pltpu.with_memory_space_constraint(each, pltpu.HBM) for each in (x, gate, weight)))


def conv_kernel(blocks, outs, block, *refs):
    own_refs, cross_refs, refs = refs[:outs], refs[outs : 2 * outs], refs[2 * outs :]
    skip_ref, hre_ref, him_ref, hfirst_ref, fwd_ref, inv_ref = refs[:6]
    out_refs, (wre_ref, wim_ref, yre_ref, yim_ref) = refs[6 : 6 + outs], refs[6 + outs :]
    me = lax.axis_index("seq")
    half, group = me // outs, me % outs
    earlier = blocks - outs
    mine = pl.ds(pl.multiple_of((group % 2) * LANES, LANES), LANES)
    for k in range(outs):
        values = jnp.concatenate([cross_refs[k][:, mine], own_refs[k][:block, mine]], axis=1)
        spec = jnp.dot(
            fwd_ref[...], jnp.concatenate([values, values], axis=0), preferred_element_type=F32
        )
        before = jnp.where(half > 0, spec[:, :LANES], 0.0)
        slot = group ^ k
        wre_ref[slot] = before[:block]
        wim_ref[slot] = before[block:]
        wre_ref[earlier + slot] = spec[:block, LANES:]
        wim_ref[earlier + slot] = spec[block:, LANES:]

    def rows_at(start, first):
        rows = pl.ds(start, 8)
        wre = [wre_ref[j, rows, :] for j in range(blocks)]
        wim = [wim_ref[j, rows, :] for j in range(blocks)]
        for o in range(outs):
            total_re = total_im = None
            for j in range(earlier + o + 1):
                k = earlier + o - j
                hre = hre_ref[k, rows, :]
                him = him_ref[k, rows, :]
                hother = hfirst_ref[k] if first else hre
                add_re = wre[j] * hre - wim[j] * him
                add_im = wre[j] * him + wim[j] * hother
                total_re = add_re if total_re is None else total_re + add_re
                total_im = add_im if total_im is None else total_im + add_im
            yre_ref[o, rows, :] = total_re
            yim_ref[o, rows, :] = total_im

    rows_at(0, True)

    @pl.loop(1, block // 8)
    def _(tile):
        rows_at(pl.multiple_of(tile * 8, 8), False)

    def stacked(slot):
        re_high, re_low = split_value(yre_ref[slot])
        im_high, im_low = split_value(yim_ref[slot])
        return jnp.concatenate([re_high, im_high, re_high, im_high, re_low, im_low], axis=0)

    skip = skip_ref[:, pl.ds(pl.multiple_of(group * LANES, LANES), LANES)]
    for k in range(0, outs, 2):
        pair = jnp.concatenate([stacked(group ^ k), stacked(group ^ (k + 1))], axis=1)
        conv = jnp.dot(inv_ref[...], pair, preferred_element_type=F32)
        for i in range(2):
            values = own_refs[k + i][:block, mine].astype(F32)
            gate = own_refs[k + i][block:, mine].astype(F32)
            mixed = conv[:, i * LANES : (i + 1) * LANES] + skip * values
            out_refs[k + i][...] = (gate * mixed).astype(BF16)


def call_conv(own, cross, skip, spectra, blocks):
    outs = len(own)
    block = cross[0].shape[0]
    pinned = [pltpu.with_memory_space_constraint(each, VMEM) for each in spectra]
    operands = [*own, *cross, skip[None], *pinned]
    return pl.pallas_call(
        functools.partial(conv_kernel, blocks, outs, block),
        in_specs=[pl.BlockSpec(memory_space=VMEM)] * len(operands),
        out_specs=[pl.BlockSpec(memory_space=VMEM)] * outs,
        out_shape=[jax.ShapeDtypeStruct((block, LANES), BF16)] * outs,
        scratch_shapes=[
            VMEM((blocks, block, LANES), F32),
            VMEM((blocks, block, LANES), F32),
            VMEM((outs, block, LANES), F32),
            VMEM((outs, block, LANES), F32),
        ],
        compiler_params=pltpu.CompilerParams(vmem_limit_bytes=16 * 2**20),
        cost_estimate=pl.CostEstimate(
            flops=2 * 10**8, bytes_accessed=3 * 2**20, transcendentals=0
        ),
        name="convolve",
    )(*operands)


def join_kernel(outs, *refs):
    piece_refs, joined_ref = refs[:outs], refs[outs]
    group = lax.axis_index("seq") % outs
    for k in range(outs):
        lanes = pl.ds(pl.multiple_of((group ^ k) * LANES, LANES), LANES)
        joined_ref[:, lanes] = piece_refs[k][...]


def tiles(width):
    step = min(width, 2 * LANES)
    return [slice(start, start + step) for start in range(0, width, step)]


def own_kernel(width, gated_ref, weight_ref, *refs):
    out_refs, (held_ref, sems) = refs[:4], refs[4:]
    me = lax.axis_index("chan")
    copies = [
        pltpu.make_async_copy(
            weight_ref.at[:, columns_of(me ^ k, half, width)], held_ref.at[i], sems.at[i]
        )
        for i, (k, half) in enumerate(((2, 0), (1, 1), (0, 0), (0, 1)))
    ]
    for copy in copies:
        copy.start()
    left = gated_ref[...]
    for i, copy in enumerate(copies):
        copy.wait()
        for lanes in tiles(width // 2):
            out_refs[i][:, lanes] = jnp.dot(
                left, held_ref[i, :, lanes], preferred_element_type=F32
            )


def neighbour_kernel(first, x_ref, y_ref, *refs):
    from_x, from_y, sums, outs = refs[:2], refs[2:4], refs[4:6], refs[6:]
    rows = from_x[0].shape[0]
    core = lax.axis_index("seq") % 2
    for left_ref, held, sum_ref, out_ref in (
        (x_ref, from_x, sums[0], outs[0]),
        (y_ref, from_y, sums[1], outs[1]),
    ):
        near = left_ref[:, pl.ds(pl.multiple_of(core * rows, LANES), rows)]
        far = left_ref[:, pl.ds(pl.multiple_of((1 - core) * rows, LANES), rows)]
        width = out_ref.shape[1]
        for lanes in tiles(width):
            place = slice(first * width + lanes.start, first * width + lanes.stop)
            total = jnp.dot(near, held[0][:, place], preferred_element_type=F32)
            total += jnp.dot(far, held[1][:, place], preferred_element_type=F32)
            out_ref[:, lanes] = (sum_ref[:, lanes] + total).astype(out_ref.dtype)


def last_kernel(*refs):
    sums, arrived, out_ref = refs[:2], refs[2:4], refs[4]
    width = sums[0].shape[1]
    for half in range(2):
        out_ref[:, half * width : (half + 1) * width] = (
            sums[half][...] + arrived[half][...].astype(F32)
        ).astype(BF16)


def in_vmem(kernel, operands, out_shape, name, flops, scratch=()):
    return pl.pallas_call(
        kernel,
        in_specs=[pl.BlockSpec(memory_space=VMEM)] * len(operands),
        out_specs=jax.tree.map(lambda _: pl.BlockSpec(memory_space=VMEM), out_shape),
        out_shape=out_shape,
        scratch_shapes=scratch,
        compiler_params=pltpu.CompilerParams(vmem_limit_bytes=16 * 2**20),
        cost_estimate=pl.CostEstimate(flops=flops, bytes_accessed=2**20, transcendentals=0),
        name=name,
    )(*operands)


def call_own(gated, weight):
    block, width = gated.shape
    columns = weight.shape[1] // FACE
    return pl.pallas_call(
        functools.partial(own_kernel, columns),
        in_specs=[pl.BlockSpec(memory_space=VMEM), pl.BlockSpec(memory_space=pltpu.HBM)],
        out_specs=[pl.BlockSpec(memory_space=VMEM)] * 4,
        out_shape=[jax.ShapeDtypeStruct((block, columns // 2), F32)] * 4,
        scratch_shapes=[
            VMEM((4, width, columns // 2), BF16),
            pltpu.SemaphoreType.DMA((4,)),
        ],
        compiler_params=pltpu.CompilerParams(vmem_limit_bytes=16 * 2**20),
        cost_estimate=pl.CostEstimate(
            flops=4 * block * width * columns, bytes_accessed=6 * width * columns, transcendentals=0
        ),
        name="own_channels",
    )(gated, pltpu.with_memory_space_constraint(weight, pltpu.HBM))


def split_shards(
    mixer_input,
    gate_branch,
    skip_gain,
    decay_rate,
    first_weight,
    first_bias,
    second_weight,
    second_bias,
    last_weight,
    output_weight,
):
    block, width = mixer_input.shape
    blocks = lax.axis_size("seq")
    outs = width // LANES

    def along_seq(part, k, rightwards=False):
        senders = range(outs) if rightwards else range(blocks)
        return lax.ppermute(part, "seq", [(s, s ^ k) for s in senders])

    along_chan = lambda part, k: lax.ppermute(part, "chan", [(c, c ^ k) for c in range(FACE)])
    here, there, here_both, there_both, over_x, over_y = call_pack(
        mixer_input, gate_branch, output_weight
    )
    cross = [along_seq(here, outs, True), None, along_seq(there, outs + 2, True), None]
    own = [here_both, along_seq(here_both, 1), along_seq(there_both, 2), None]
    for pieces, k in ((own, 2), (cross, 2), (cross, 0)):
        pieces[k + 1] = along_seq(pieces[k], 1)
    from_x, from_y = along_chan(over_x, 1), along_chan(over_y, 2)
    from_x, from_y = (from_x, along_seq(from_x, 1)), (from_y, along_seq(from_y, 1))

    spectra = call_filter(
        (first_weight, first_bias, second_weight, second_bias, last_weight, decay_rate),
        blocks,
        outs,
        block,
    )
    pieces = call_conv(own, cross, skip_gain, spectra, blocks)
    pieces = [pieces[0]] + [along_seq(pieces[k], k) for k in range(1, outs)]
    shape = jax.ShapeDtypeStruct
    gated = in_vmem(
        functools.partial(join_kernel, outs),
        pieces,
        shape((block, width), BF16),
        "join_pieces",
        10**6,
    )
    x_gated, y_gated = along_chan(gated, 1), along_chan(gated, 2)
    send_a, send_b, keep_a, keep_b = call_own(gated, output_weight)
    columns = send_a.shape[1]
    flops = 4 * block * width * columns
    send_a, send_b = in_vmem(
        functools.partial(neighbour_kernel, 1),
        [x_gated, y_gated, *from_x, *from_y, send_a, send_b],
        [shape((block, columns), BF16)] * 2,
        "sums_to_send",
        flops,
    )
    got_a, got_b = along_chan(send_a, 2), along_chan(send_b, 1)
    keep_a, keep_b = in_vmem(
        functools.partial(neighbour_kernel, 0),
        [x_gated, y_gated, *from_x, *from_y, keep_a, keep_b],
        [shape((block, columns), F32)] * 2,
        "sums_to_keep",
        flops,
    )
    return in_vmem(
        last_kernel,
        [keep_a, keep_b, got_a, got_b],
        shape((block, 2 * columns), BF16),
        "last_sum",
        10**6,
    )


def contract_first(left_matrix, right_matrix):
    return lax.dot_general(
        left_matrix,
        right_matrix,
        (((0,), (0,)), ((), ())),
        precision=HIGHEST,
        preferred_element_type=F32,
    )


def filter_taps(
    first_weight, first_bias, second_weight, second_bias, last_weight, decay_rate, length
):
    features = jnp.asarray(feature_table(length, first_weight.shape[0]).T)
    hidden_one = jnp.sin(contract_first(first_weight, features) + first_bias[:, None])
    hidden_two = jnp.sin(contract_first(second_weight, hidden_one) + second_bias[:, None])
    shaped = contract_first(hidden_two, last_weight)
    positions = jnp.arange(length, dtype=jnp.int32).astype(F32)
    envelope = jnp.exp(-decay_rate[None, :] * (positions[:, None] / length))
    energy = jnp.expm1(-2.0 * decay_rate) / jnp.expm1(-2.0 * decay_rate / length)
    return shaped * envelope / jnp.sqrt(energy)[None, :]


def transform_tables(block_len):
    padded_len = 2 * block_len
    freq_index = jnp.arange(block_len + 1, dtype=jnp.int32)[:, None]
    time_index = jnp.arange(padded_len, dtype=jnp.int32)[None, :]
    angle = (freq_index * time_index % padded_len).astype(F32) * (2.0 * math.pi / padded_len)
    forward = jnp.concatenate([jnp.cos(angle), -jnp.sin(angle)], axis=0)
    later_angle = angle[:, block_len:]
    weights = jnp.where((freq_index == 0) | (freq_index == block_len), 1.0, 2.0) / padded_len
    inverse = jnp.concatenate(
        [(weights * jnp.cos(later_angle)).T, (-weights * jnp.sin(later_angle)).T], axis=1
    )
    return (forward, inverse)


def spectral_product(left_spec, right_spec, half_rows):
    left_real, left_imag = (left_spec[:half_rows], left_spec[half_rows:])
    right_real, right_imag = (right_spec[:half_rows], right_spec[half_rows:])
    return jnp.concatenate(
        [
            left_real * right_real - left_imag * right_imag,
            left_real * right_imag + left_imag * right_real,
        ],
        axis=0,
    )


def gathered_shards(
    mixer_input,
    gate_branch,
    skip_gain,
    decay_rate,
    first_weight,
    first_bias,
    second_weight,
    second_bias,
    last_weight,
    output_weight,
):
    block_len, chan_width = mixer_input.shape
    seq_count = lax.axis_size("seq")
    device = lax.axis_index("seq")
    half_rows = block_len + 1
    kernel_taps = filter_taps(
        first_weight,
        first_bias,
        second_weight,
        second_bias,
        last_weight,
        decay_rate,
        block_len * seq_count,
    )
    padded_taps = jnp.concatenate([jnp.zeros((block_len, chan_width), F32), kernel_taps], axis=0)
    forward, inverse = transform_tables(block_len)
    forward_head = forward[:, :block_len]
    gathered = lax.all_gather(mixer_input, "seq", axis=0, tiled=True)

    def one_block(block_index, total):
        rows = lax.dynamic_slice_in_dim(gathered, block_index * block_len, block_len, 0)
        source_spec = jnp.dot(
            forward_head, rows.astype(F32), precision=HIGHEST, preferred_element_type=F32
        )
        segment = lax.dynamic_slice_in_dim(
            padded_taps, (device - block_index) * block_len, 2 * block_len, 0
        )
        lag_spec = jnp.dot(forward, segment, precision=HIGHEST, preferred_element_type=F32)
        return total + spectral_product(lag_spec, source_spec, half_rows)

    total = lax.fori_loop(0, device + 1, one_block, jnp.zeros((2 * half_rows, chan_width), F32))
    convolved = jnp.dot(inverse, total, precision=HIGHEST, preferred_element_type=F32)
    values = mixer_input.astype(F32)
    gated_mix = (
        gate_branch.astype(F32) * (convolved + skip_gain[None, :] * values)
    ).astype(BF16)
    partial_out = jnp.dot(gated_mix, output_weight, preferred_element_type=F32)
    return lax.psum_scatter(partial_out, "chan", scatter_dimension=1, tiled=True).astype(BF16)


def solution(mesh):
    seq_count, chan_count = mesh.shape["seq"], mesh.shape["chan"]

    def shards(mixer_input, *rest):
        block, width = mixer_input.shape
        outs = width // LANES
        splits = (
            width % LANES == 0
            and block % LANES == 0
            and seq_count == 2 * outs
            and outs == 4
            and chan_count == FACE
        )
        plan = split_shards if splits else gathered_shards
        return plan(mixer_input, *rest)

    in_specs = (
        P("seq", "chan"),
        P("seq", "chan"),
        P("chan"),
        P("chan"),
        P(),
        P(),
        P(),
        P(),
        P(None, "chan"),
        P("chan", None),
    )
    out_specs = P("seq", "chan")
    return jax.shard_map(shards, mesh=mesh, in_specs=in_specs, out_specs=out_specs, check_vma=False)
```

```python
import functools
import math

import jax
import jax.numpy as jnp
import numpy as np
from jax import lax
from jax.experimental import pallas as pl
from jax.experimental.pallas import tpu as pltpu
from jax.sharding import PartitionSpec as P

HIGHEST = lax.Precision.HIGHEST
F32 = jnp.float32
BF16 = jnp.bfloat16
LANES = 128
FACE = 4
VMEM = pltpu.VMEM


def feature_table(length, emb_width):
    band_count = (emb_width - 1) // 2
    positions = np.arange(length, dtype=np.int64)
    columns = [positions / length]
    for band in range(1, band_count + 1):
        frequency = min(
            length // 2, max(band, int((length / 2) ** ((band - 1) / (band_count - 1))))
        )
        angle = (positions * frequency % length) * (2.0 * math.pi / length)
        columns.append(np.cos(angle))
        columns.append(np.sin(angle))
    return np.stack(columns, axis=1).astype(np.float32)


def split_bf16(table):
    high = table.astype(np.float32).astype(jnp.bfloat16)
    low = (table - high.astype(np.float64)).astype(np.float32).astype(jnp.bfloat16)
    return high, low


def dft_tables(block):
    size = 2 * block
    bins = np.arange(block)[:, None]
    times = np.arange(block)[None, :]
    angle = (bins * times % size) * (2.0 * math.pi / size)
    imag = -np.sin(angle)
    imag[0] = 1.0 - 2.0 * (np.arange(block) % 2)
    forward = np.concatenate([np.cos(angle), imag], axis=0)
    weight = np.where(bins == 0, 1.0, 2.0) / size
    back_imag = -weight * np.sin(angle)
    back_imag[0] = (1.0 - 2.0 * (np.arange(block) % 2)) / size
    inverse = np.concatenate([weight * np.cos(angle), back_imag], axis=0).T
    return forward, inverse


def fast_sin(x):
    turns = jnp.floor(x * (1.0 / math.pi) + 0.5)
    rest = x - turns * 3.140625
    rest = rest - turns * 9.67502593994140625e-4
    rest = rest - turns * 1.509957990978376432e-7
    parity = turns - 2.0 * jnp.floor(turns * 0.5)
    rest = rest * (1.0 - 2.0 * parity)
    square = rest * rest
    poly = -2.5052108e-8
    for coeff in (2.7557319e-6, -1.9841270e-4, 8.3333333e-3, -1.6666667e-1):
        poly = poly * square + coeff
    return rest + rest * square * poly


def expm1_of_negative(x):
    near = jnp.maximum(x, -0.5)
    series = jnp.full_like(x, 1.0 / 3628800.0)
    for denom in (362880.0, 40320.0, 5040.0, 720.0, 120.0, 24.0, 6.0, 2.0, 1.0):
        series = series * near + 1.0 / denom
    return jnp.where(x > -0.5, near * series, jnp.exp(x) - 1.0)


def split_value(value):
    high = value.astype(BF16)
    return high, (value - high.astype(F32)).astype(BF16)


def filter_feature_table(length, emb_width, pad):
    table = feature_table(length, emb_width)
    columns = []
    for half in (table[: length // 2], table[length // 2 :]):
        high, low = (part.astype(np.float32) for part in split_bf16(half))
        for part in (high, high, low):
            columns.append(np.pad(part, ((0, 0), (0, pad - emb_width))))
    return np.concatenate(columns, axis=1)


def twice_diagonal(value):
    zero = jnp.zeros_like(value)
    return jnp.concatenate(
        [jnp.concatenate([value, zero], axis=1), jnp.concatenate([zero, value], axis=1)], axis=0
    )


def stacked_diagonal(value):
    high, low = split_value(value)
    high = twice_diagonal(high.astype(F32))
    low = twice_diagonal(low.astype(F32))
    return jnp.concatenate([high, low, high], axis=0).astype(BF16)


def layer(value, weight):
    high, low = split_value(value)
    return jnp.dot(
        jnp.concatenate([high, high, low], axis=1), weight, preferred_element_type=F32
    )


def filter_kernel(blocks, block, outs, pad, *refs):
    hbm, refs = refs[:10], refs[10:]
    hre_ref, him_ref, hfirst_ref, fwd_ref, inv_ref, skip_ref = refs[:6]
    refs = refs[6:]
    w1_ref, b1_ref, w2_ref, b2_ref, w3_ref, decay_ref, feat_ref, table_ref, back_ref = refs[:9]
    all_skip_ref, first_ref, sems = refs[9:]
    targets = [
        w1_ref, feat_ref, b1_ref, w2_ref, b2_ref, w3_ref, decay_ref, table_ref, back_ref,
        all_skip_ref,
    ]
    copies = [
        pltpu.make_async_copy(hbm[i], targets[i], sems.at[i]) for i in range(len(targets))
    ]
    for copy in copies:
        copy.start()
    group = lax.axis_index("seq") % outs
    length = blocks * block
    emb, order = w1_ref.shape
    first_ref[...] = jnp.zeros_like(first_ref)
    for copy in copies[:7]:
        copy.wait()

    high, low = split_value(w1_ref[...])
    high, low = high.astype(F32), low.astype(F32)
    zero = jnp.zeros_like(high)
    for i, part in enumerate((high, low, high)):
        first_ref[i * pad : i * pad + emb] = jnp.concatenate([part, zero], axis=1)
        first_ref[(3 + i) * pad : (3 + i) * pad + emb] = jnp.concatenate([zero, part], axis=1)
    b1 = jnp.concatenate([b1_ref[...]] * 2, axis=1)
    b2 = jnp.concatenate([b2_ref[...]] * 2, axis=1)
    hidden = fast_sin(
        jnp.dot(
            feat_ref[...].astype(BF16), first_ref[...].astype(BF16), preferred_element_type=F32
        )
        + b1
    )
    hidden = fast_sin(layer(hidden, stacked_diagonal(w2_ref[...])) + b2)
    lanes = pl.ds(pl.multiple_of(group * LANES, LANES), LANES)
    shaped = layer(hidden, stacked_diagonal(w3_ref[:, lanes]))

    decay = decay_ref[:, lanes]
    energy = expm1_of_negative(-2.0 * decay) / expm1_of_negative(decay * (-2.0 / length))
    times = lax.broadcasted_iota(jnp.int32, (length // 2, LANES), 0).astype(F32) * (1.0 / length)
    window = jnp.exp(-(decay * times)) * (1.0 / jnp.sqrt(energy))
    window = jnp.concatenate([window, window * jnp.exp(-0.5 * decay)], axis=1)
    taps_high, taps_low = split_value(shaped * window)

    copies[7].wait()
    high, low = split_value(table_ref[...])
    fwd_ref[:, :block] = high
    fwd_ref[:, block:] = low
    table = jnp.concatenate([high, low, high], axis=1)
    rows = lax.broadcasted_iota(jnp.int32, (2 * block, LANES), 0)
    sign = (1 - 2 * lax.rem(rows, 2)).astype(F32)
    first_row = lax.broadcasted_iota(jnp.int32, (block, LANES), 0) == 0
    spectra = [None] * blocks
    for k in range(blocks // 2):
        part = slice(k * block, (k + 1) * block)
        stacked = jnp.concatenate([taps_high[part], taps_high[part], taps_low[part]], axis=0)
        now = jnp.dot(table, stacked, preferred_element_type=F32)
        spectra[k], spectra[k + blocks // 2] = now[:, :LANES], now[:, LANES:]
    for k in range(blocks):
        spec = spectra[k] if k == 0 else spectra[k] + sign * spectra[k - 1]
        real, imag = spec[:block], spec[block:]
        hre_ref[k] = real
        him_ref[k] = jnp.where(first_row, 0.0, imag)
        hfirst_ref[k] = jnp.where(first_row, imag, real)[:8]

    copies[8].wait()
    copies[9].wait()
    skip_ref[...] = all_skip_ref[:, lanes]
    high, low = split_value(back_ref[...])
    inv_ref[:, : 2 * block] = high
    inv_ref[:, 2 * block : 4 * block] = low
    inv_ref[:, 4 * block :] = high


def call_filter(weights, skip, blocks, outs, block):
    w1, b1, w2, b2, w3, decay = weights
    length = blocks * block
    emb, order = w1.shape
    pad = -(-emb // 8) * 8
    forward, inverse = dft_tables(block)
    feats = filter_feature_table(length, emb, pad)
    hbm = [
        w1, feats, b1[None], w2, b2[None], w3, decay[None], forward.astype(np.float32),
        inverse.astype(np.float32), skip[None],
    ]
    out_shape = [
        VMEM((blocks, block, LANES), F32),
        VMEM((blocks, block, LANES), F32),
        VMEM((blocks, 8, LANES), F32),
        VMEM((2 * block, 2 * block), BF16),
        VMEM((block, 6 * block), BF16),
        VMEM((1, LANES), F32),
    ]
    return pl.pallas_call(
        functools.partial(filter_kernel, blocks, block, outs, pad),
        in_specs=[pl.BlockSpec(memory_space=pltpu.HBM)] * len(hbm),
        out_specs=[pl.BlockSpec(memory_space=VMEM)] * len(out_shape),
        out_shape=out_shape,
        scratch_shapes=[
            VMEM(w1.shape, F32),
            VMEM((1, order), F32),
            VMEM(w2.shape, F32),
            VMEM((1, order), F32),
            VMEM(w3.shape, F32),
            VMEM((1, w3.shape[1]), F32),
            VMEM(feats.shape, F32),
            VMEM(forward.shape, F32),
            VMEM(inverse.shape, F32),
            VMEM((1, skip.shape[0]), F32),
            VMEM((6 * pad, 2 * order), F32),
            pltpu.SemaphoreType.DMA((len(hbm),)),
        ],
        compiler_params=pltpu.CompilerParams(vmem_limit_bytes=32 * 2**20),
        cost_estimate=pl.CostEstimate(
            flops=4 * 10**8, bytes_accessed=8 * 2**20, transcendentals=length * LANES
        ),
        name="filter_spectra",
    )(*(pltpu.with_memory_space_constraint(jnp.asarray(each), pltpu.HBM) for each in hbm))


def columns_of(part, half, width):
    return pl.ds(pl.multiple_of(part * width + half * (width // 2), LANES), width // 2)


def weight_copies(weight_ref, over_x_ref, over_y_ref, sems, first_sem):
    rows = weight_ref.shape[0] // 2
    width = weight_ref.shape[1] // FACE
    me = lax.axis_index("chan")
    half_rows = pl.ds(pl.multiple_of((lax.axis_index("seq") % 2) * rows, LANES), rows)
    copies = []
    for out_ref, half, parts in ((over_x_ref, 0, (1, 3)), (over_y_ref, 1, (2, 3))):
        for place, k in enumerate(parts):
            copies.append(
                pltpu.make_async_copy(
                    weight_ref.at[half_rows, columns_of(me ^ k, half, width)],
                    out_ref.at[:, place * (width // 2) : (place + 1) * (width // 2)],
                    sems.at[first_sem + len(copies)],
                )
            )
    return copies


def pack_kernel(blocks, outs, x_ref, gate_ref, weight_ref, pieces_ref, *refs):
    gate_refs, (over_x_ref, over_y_ref, sems) = refs[:outs], refs[outs:]
    group = lax.axis_index("seq") % outs
    copies = [
        pltpu.make_async_copy(
            x_ref.at[:, (d % outs) * LANES : (d % outs + 1) * LANES], pieces_ref.at[d], sems.at[d]
        )
        for d in range(blocks)
    ]
    for k in range(outs):
        lanes = pl.ds(pl.multiple_of((group ^ k) * LANES, LANES), LANES)
        copies.append(
            pltpu.make_async_copy(gate_ref.at[:, lanes], gate_refs[k], sems.at[len(copies)])
        )
    copies += weight_copies(weight_ref, over_x_ref, over_y_ref, sems, len(copies))
    for copy in copies:
        copy.start()
    for copy in copies:
        copy.wait()


def call_pack(x, gate, weight, blocks, outs):
    block = x.shape[0]
    send = VMEM((weight.shape[0] // 2, weight.shape[1] // FACE), BF16)
    out_shape = [jax.ShapeDtypeStruct((blocks, block, LANES), BF16)]
    out_shape += [jax.ShapeDtypeStruct((block, LANES), BF16)] * outs + [send] * 2
    return pl.pallas_call(
        functools.partial(pack_kernel, blocks, outs),
        in_specs=[pl.BlockSpec(memory_space=pltpu.HBM)] * 3,
        out_specs=[pl.BlockSpec(memory_space=VMEM)] * len(out_shape),
        out_shape=out_shape,
        scratch_shapes=[pltpu.SemaphoreType.DMA((blocks + outs + 4,))],
        cost_estimate=pl.CostEstimate(flops=0, bytes_accessed=2**21, transcendentals=0),
        name="pack_pieces",
    )(*(pltpu.with_memory_space_constraint(each, pltpu.HBM) for each in (x, gate, weight)))


def conv_kernel(blocks, outs, block, xs_ref, *refs):
    gate_refs, refs = refs[:outs], refs[outs:]
    hre_ref, him_ref, hfirst_ref, fwd_ref, inv_ref, skip_ref = refs[:6]
    refs = refs[8:]
    out_refs, (wre_ref, wim_ref, yre_ref, yim_ref) = refs[:outs], refs[outs + 2 :]
    me = lax.axis_index("seq")
    half, group = me // outs, me % outs
    earlier = blocks - outs
    for j in range(outs):
        values = jnp.concatenate([xs_ref[j], xs_ref[half * outs + j]], axis=1)
        spec = jnp.dot(
            fwd_ref[...], jnp.concatenate([values, values], axis=0), preferred_element_type=F32
        )
        before = jnp.where(half > 0, spec[:, :LANES], 0.0)
        wre_ref[j] = before[:block]
        wim_ref[j] = before[block:]
        wre_ref[earlier + j] = spec[:block, LANES:]
        wim_ref[earlier + j] = spec[block:, LANES:]

    def rows_at(start, first):
        rows = pl.ds(start, 8)
        wre = [wre_ref[j, rows, :] for j in range(blocks)]
        wim = [wim_ref[j, rows, :] for j in range(blocks)]
        for o in range(outs):
            total_re = total_im = None
            for j in range(earlier + o + 1):
                k = earlier + o - j
                hre = hre_ref[k, rows, :]
                him = him_ref[k, rows, :]
                hother = hfirst_ref[k] if first else hre
                add_re = wre[j] * hre - wim[j] * him
                add_im = wre[j] * him + wim[j] * hother
                total_re = add_re if total_re is None else total_re + add_re
                total_im = add_im if total_im is None else total_im + add_im
            yre_ref[o, rows, :] = total_re
            yim_ref[o, rows, :] = total_im

    rows_at(0, True)

    @pl.loop(1, block // 8)
    def _(tile):
        rows_at(pl.multiple_of(tile * 8, 8), False)

    def stacked(slot):
        re_high, re_low = split_value(yre_ref[slot])
        im_high, im_low = split_value(yim_ref[slot])
        return jnp.concatenate([re_high, im_high, re_high, im_high, re_low, im_low], axis=0)

    skip = skip_ref[...]
    for k in range(0, outs, 2):
        pair = jnp.concatenate([stacked(group ^ k), stacked(group ^ (k + 1))], axis=1)
        conv = jnp.dot(inv_ref[...], pair, preferred_element_type=F32)
        for i in range(2):
            values = xs_ref[half * outs + (group ^ (k + i))].astype(F32)
            gate = gate_refs[k + i][...].astype(F32)
            mixed = conv[:, i * LANES : (i + 1) * LANES] + skip * values
            out_refs[k + i][...] = (gate * mixed).astype(BF16)


def call_conv(xs, gates, filters, passing):
    blocks, block, _ = xs.shape
    outs = len(gates)
    pinned = [pltpu.with_memory_space_constraint(each, VMEM) for each in filters]
    operands = [xs, *gates, *pinned]
    shape = jax.ShapeDtypeStruct
    return pl.pallas_call(
        functools.partial(conv_kernel, blocks, outs, block),
        in_specs=[pl.BlockSpec(memory_space=VMEM)] * len(operands)
        + [pl.BlockSpec(memory_space=pl.ANY)] * 2,
        out_specs=[pl.BlockSpec(memory_space=VMEM)] * outs
        + [pl.BlockSpec(memory_space=pl.ANY)] * 2,
        out_shape=[shape((block, LANES), BF16)] * outs + [shape(p.shape, p.dtype) for p in passing],
        input_output_aliases={len(operands) + i: outs + i for i in range(2)},
        scratch_shapes=[
            VMEM((blocks, block, LANES), F32),
            VMEM((blocks, block, LANES), F32),
            VMEM((outs, block, LANES), F32),
            VMEM((outs, block, LANES), F32),
        ],
        compiler_params=pltpu.CompilerParams(vmem_limit_bytes=16 * 2**20),
        cost_estimate=pl.CostEstimate(
            flops=2 * 10**8, bytes_accessed=3 * 2**20, transcendentals=0
        ),
        name="convolve",
    )(*operands, *passing)


def join_kernel(outs, *refs):
    piece_refs, joined_ref = refs[:outs], refs[outs]
    group = lax.axis_index("seq") % outs
    for k in range(outs):
        lanes = pl.ds(pl.multiple_of((group ^ k) * LANES, LANES), LANES)
        joined_ref[:, lanes] = piece_refs[k][...]


def tiles(width):
    step = min(width, 2 * LANES)
    return [slice(start, start + step) for start in range(0, width, step)]


def own_kernel(width, gated_ref, weight_ref, *refs):
    out_refs, (held_ref, sems) = refs[:4], refs[4:]
    me = lax.axis_index("chan")
    copies = [
        pltpu.make_async_copy(
            weight_ref.at[:, columns_of(me ^ k, half, width)], held_ref.at[i], sems.at[i]
        )
        for i, (k, half) in enumerate(((2, 0), (1, 1), (0, 0), (0, 1)))
    ]
    for copy in copies:
        copy.start()
    left = gated_ref[...]
    for i, copy in enumerate(copies):
        copy.wait()
        for lanes in tiles(width // 2):
            out_refs[i][:, lanes] = jnp.dot(
                left, held_ref[i, :, lanes], preferred_element_type=F32
            )


def neighbour_kernel(first, x_ref, y_ref, *refs):
    from_x, from_y, sums, outs = refs[:2], refs[2:4], refs[4:6], refs[6:]
    rows = from_x[0].shape[0]
    core = lax.axis_index("seq") % 2
    for left_ref, held, sum_ref, out_ref in (
        (x_ref, from_x, sums[0], outs[0]),
        (y_ref, from_y, sums[1], outs[1]),
    ):
        near = left_ref[:, pl.ds(pl.multiple_of(core * rows, LANES), rows)]
        far = left_ref[:, pl.ds(pl.multiple_of((1 - core) * rows, LANES), rows)]
        width = out_ref.shape[1]
        for lanes in tiles(width):
            place = slice(first * width + lanes.start, first * width + lanes.stop)
            total = jnp.dot(near, held[0][:, place], preferred_element_type=F32)
            total += jnp.dot(far, held[1][:, place], preferred_element_type=F32)
            out_ref[:, lanes] = (sum_ref[:, lanes] + total).astype(out_ref.dtype)


def last_kernel(*refs):
    sums, arrived, out_ref = refs[:2], refs[2:4], refs[4]
    width = sums[0].shape[1]
    for half in range(2):
        out_ref[:, half * width : (half + 1) * width] = (
            sums[half][...] + arrived[half][...].astype(F32)
        ).astype(BF16)


def in_vmem(kernel, operands, out_shape, name, flops, scratch=()):
    return pl.pallas_call(
        kernel,
        in_specs=[pl.BlockSpec(memory_space=VMEM)] * len(operands),
        out_specs=jax.tree.map(lambda _: pl.BlockSpec(memory_space=VMEM), out_shape),
        out_shape=out_shape,
        scratch_shapes=scratch,
        compiler_params=pltpu.CompilerParams(vmem_limit_bytes=16 * 2**20),
        cost_estimate=pl.CostEstimate(flops=flops, bytes_accessed=2**20, transcendentals=0),
        name=name,
    )(*operands)


def call_own(gated, weight):
    block, width = gated.shape
    columns = weight.shape[1] // FACE
    return pl.pallas_call(
        functools.partial(own_kernel, columns),
        in_specs=[pl.BlockSpec(memory_space=VMEM), pl.BlockSpec(memory_space=pltpu.HBM)],
        out_specs=[pl.BlockSpec(memory_space=VMEM)] * 4,
        out_shape=[jax.ShapeDtypeStruct((block, columns // 2), F32)] * 4,
        scratch_shapes=[
            VMEM((4, width, columns // 2), BF16),
            pltpu.SemaphoreType.DMA((4,)),
        ],
        compiler_params=pltpu.CompilerParams(vmem_limit_bytes=16 * 2**20),
        cost_estimate=pl.CostEstimate(
            flops=4 * block * width * columns, bytes_accessed=6 * width * columns, transcendentals=0
        ),
        name="own_channels",
    )(gated, pltpu.with_memory_space_constraint(weight, pltpu.HBM))


def split_shards(
    mixer_input,
    gate_branch,
    skip_gain,
    decay_rate,
    first_weight,
    first_bias,
    second_weight,
    second_bias,
    last_weight,
    output_weight,
):
    block, width = mixer_input.shape
    blocks = lax.axis_size("seq")
    outs = width // LANES

    along_seq = lambda part, k: lax.ppermute(part, "seq", [(s, s ^ k) for s in range(blocks)])
    along_chan = lambda part, k: lax.ppermute(part, "chan", [(c, c ^ k) for c in range(FACE)])
    to_partners = lambda parts: [parts[0]] + [along_seq(parts[k], k) for k in range(1, outs)]

    xs, *gates, over_x, over_y = call_pack(
        mixer_input, gate_branch, output_weight, blocks, outs
    )
    xs = lax.all_to_all(xs, "seq", 0, 0, tiled=True)
    from_x, from_y = along_chan(over_x, 1), along_chan(over_y, 2)
    filters = call_filter(
        (first_weight, first_bias, second_weight, second_bias, last_weight, decay_rate),
        skip_gain,
        blocks,
        outs,
        block,
    )
    *pieces, from_x, from_y = call_conv(xs, to_partners(gates), filters, (from_x, from_y))
    from_x, from_y = (from_x, along_seq(from_x, 1)), (from_y, along_seq(from_y, 1))
    pieces = to_partners(pieces)
    shape = jax.ShapeDtypeStruct
    gated = in_vmem(
        functools.partial(join_kernel, outs),
        pieces,
        shape((block, width), BF16),
        "join_pieces",
        10**6,
    )
    x_gated, y_gated = along_chan(gated, 1), along_chan(gated, 2)
    send_a, send_b, keep_a, keep_b = call_own(gated, output_weight)
    columns = send_a.shape[1]
    flops = 4 * block * width * columns
    send_a, send_b = in_vmem(
        functools.partial(neighbour_kernel, 1),
        [x_gated, y_gated, *from_x, *from_y, send_a, send_b],
        [shape((block, columns), BF16)] * 2,
        "sums_to_send",
        flops,
    )
    got_a, got_b = along_chan(send_a, 2), along_chan(send_b, 1)
    keep_a, keep_b = in_vmem(
        functools.partial(neighbour_kernel, 0),
        [x_gated, y_gated, *from_x, *from_y, keep_a, keep_b],
        [shape((block, columns), F32)] * 2,
        "sums_to_keep",
        flops,
    )
    return in_vmem(
        last_kernel,
        [keep_a, keep_b, got_a, got_b],
        shape((block, 2 * columns), BF16),
        "last_sum",
        10**6,
    )


def contract_first(left_matrix, right_matrix):
    return lax.dot_general(
        left_matrix,
        right_matrix,
        (((0,), (0,)), ((), ())),
        precision=HIGHEST,
        preferred_element_type=F32,
    )


def filter_taps(
    first_weight, first_bias, second_weight, second_bias, last_weight, decay_rate, length
):
    features = jnp.asarray(feature_table(length, first_weight.shape[0]).T)
    hidden_one = jnp.sin(contract_first(first_weight, features) + first_bias[:, None])
    hidden_two = jnp.sin(contract_first(second_weight, hidden_one) + second_bias[:, None])
    shaped = contract_first(hidden_two, last_weight)
    positions = jnp.arange(length, dtype=jnp.int32).astype(F32)
    envelope = jnp.exp(-decay_rate[None, :] * (positions[:, None] / length))
    energy = jnp.expm1(-2.0 * decay_rate) / jnp.expm1(-2.0 * decay_rate / length)
    return shaped * envelope / jnp.sqrt(energy)[None, :]


def transform_tables(block_len):
    padded_len = 2 * block_len
    freq_index = jnp.arange(block_len + 1, dtype=jnp.int32)[:, None]
    time_index = jnp.arange(padded_len, dtype=jnp.int32)[None, :]
    angle = (freq_index * time_index % padded_len).astype(F32) * (2.0 * math.pi / padded_len)
    forward = jnp.concatenate([jnp.cos(angle), -jnp.sin(angle)], axis=0)
    later_angle = angle[:, block_len:]
    weights = jnp.where((freq_index == 0) | (freq_index == block_len), 1.0, 2.0) / padded_len
    inverse = jnp.concatenate(
        [(weights * jnp.cos(later_angle)).T, (-weights * jnp.sin(later_angle)).T], axis=1
    )
    return (forward, inverse)


def spectral_product(left_spec, right_spec, half_rows):
    left_real, left_imag = (left_spec[:half_rows], left_spec[half_rows:])
    right_real, right_imag = (right_spec[:half_rows], right_spec[half_rows:])
    return jnp.concatenate(
        [
            left_real * right_real - left_imag * right_imag,
            left_real * right_imag + left_imag * right_real,
        ],
        axis=0,
    )


def gathered_shards(
    mixer_input,
    gate_branch,
    skip_gain,
    decay_rate,
    first_weight,
    first_bias,
    second_weight,
    second_bias,
    last_weight,
    output_weight,
):
    block_len, chan_width = mixer_input.shape
    seq_count = lax.axis_size("seq")
    device = lax.axis_index("seq")
    half_rows = block_len + 1
    kernel_taps = filter_taps(
        first_weight,
        first_bias,
        second_weight,
        second_bias,
        last_weight,
        decay_rate,
        block_len * seq_count,
    )
    padded_taps = jnp.concatenate([jnp.zeros((block_len, chan_width), F32), kernel_taps], axis=0)
    forward, inverse = transform_tables(block_len)
    forward_head = forward[:, :block_len]
    gathered = lax.all_gather(mixer_input, "seq", axis=0, tiled=True)

    def one_block(block_index, total):
        rows = lax.dynamic_slice_in_dim(gathered, block_index * block_len, block_len, 0)
        source_spec = jnp.dot(
            forward_head, rows.astype(F32), precision=HIGHEST, preferred_element_type=F32
        )
        segment = lax.dynamic_slice_in_dim(
            padded_taps, (device - block_index) * block_len, 2 * block_len, 0
        )
        lag_spec = jnp.dot(forward, segment, precision=HIGHEST, preferred_element_type=F32)
        return total + spectral_product(lag_spec, source_spec, half_rows)

    total = lax.fori_loop(0, device + 1, one_block, jnp.zeros((2 * half_rows, chan_width), F32))
    convolved = jnp.dot(inverse, total, precision=HIGHEST, preferred_element_type=F32)
    values = mixer_input.astype(F32)
    gated_mix = (
        gate_branch.astype(F32) * (convolved + skip_gain[None, :] * values)
    ).astype(BF16)
    partial_out = jnp.dot(gated_mix, output_weight, preferred_element_type=F32)
    return lax.psum_scatter(partial_out, "chan", scatter_dimension=1, tiled=True).astype(BF16)


def solution(mesh):
    seq_count, chan_count = mesh.shape["seq"], mesh.shape["chan"]

    def shards(mixer_input, *rest):
        block, width = mixer_input.shape
        outs = width // LANES
        splits = (
            width % LANES == 0
            and block % LANES == 0
            and seq_count == 2 * outs
            and outs == 4
            and chan_count == FACE
        )
        plan = split_shards if splits else gathered_shards
        return plan(mixer_input, *rest)

    in_specs = (
        P("seq", "chan"),
        P("seq", "chan"),
        P("chan"),
        P("chan"),
        P(),
        P(),
        P(),
        P(),
        P(None, "chan"),
        P("chan", None),
    )
    out_specs = P("seq", "chan")
    return jax.shard_map(shards, mesh=mesh, in_specs=in_specs, out_specs=out_specs, check_vma=False)
```

```python
import functools
import math

import jax
import jax.numpy as jnp
import numpy as np
from jax import lax
from jax.experimental import pallas as pl
from jax.experimental.pallas import tpu as pltpu
from jax.sharding import PartitionSpec as P

HIGHEST = lax.Precision.HIGHEST
F32 = jnp.float32
BF16 = jnp.bfloat16
LANES = 128
WIDE = 2 * LANES
CORES = 2
CHIPS = 4
FACE = 4
VMEM = pltpu.VMEM


def feature_table(length, emb_width):
    band_count = (emb_width - 1) // 2
    positions = np.arange(length, dtype=np.int64)
    columns = [positions / length]
    for band in range(1, band_count + 1):
        frequency = min(
            length // 2, max(band, int((length / 2) ** ((band - 1) / (band_count - 1))))
        )
        angle = (positions * frequency % length) * (2.0 * math.pi / length)
        columns.append(np.cos(angle))
        columns.append(np.sin(angle))
    return np.stack(columns, axis=1).astype(np.float32)


def split_bf16(table):
    high = table.astype(np.float32).astype(jnp.bfloat16)
    low = (table - high.astype(np.float64)).astype(np.float32).astype(jnp.bfloat16)
    return high, low


def dft_tables(block):
    size = 2 * block
    bins = np.arange(block)[:, None]
    times = np.arange(block)[None, :]
    angle = (bins * times % size) * (2.0 * math.pi / size)
    imag = -np.sin(angle)
    imag[0] = 1.0 - 2.0 * (np.arange(block) % 2)
    forward = np.concatenate([np.cos(angle), imag], axis=0)
    weight = np.where(bins == 0, 1.0, 2.0) / size
    back_imag = -weight * np.sin(angle)
    back_imag[0] = (1.0 - 2.0 * (np.arange(block) % 2)) / size
    inverse = np.concatenate([weight * np.cos(angle), back_imag], axis=0).T
    return forward, inverse


def fast_sin(x):
    turns = jnp.floor(x * (1.0 / math.pi) + 0.5)
    rest = x - turns * 3.140625
    rest = rest - turns * 9.67502593994140625e-4
    rest = rest - turns * 1.509957990978376432e-7
    parity = turns - 2.0 * jnp.floor(turns * 0.5)
    rest = rest * (1.0 - 2.0 * parity)
    square = rest * rest
    poly = -2.5052108e-8
    for coeff in (2.7557319e-6, -1.9841270e-4, 8.3333333e-3, -1.6666667e-1):
        poly = poly * square + coeff
    return rest + rest * square * poly


def expm1_of_negative(x):
    near = jnp.maximum(x, -0.5)
    series = jnp.full_like(x, 1.0 / 3628800.0)
    for denom in (362880.0, 40320.0, 5040.0, 720.0, 120.0, 24.0, 6.0, 2.0, 1.0):
        series = series * near + 1.0 / denom
    return jnp.where(x > -0.5, near * series, jnp.exp(x) - 1.0)


def split_value(value):
    high = value.astype(BF16)
    return high, (value - high.astype(F32)).astype(BF16)


def filter_feature_table(length, emb_width, pad):
    table = feature_table(length, emb_width)
    columns = []
    for half in (table[: length // 2], table[length // 2 :]):
        high, low = (part.astype(np.float32) for part in split_bf16(half))
        for part in (high, high, low):
            columns.append(np.pad(part, ((0, 0), (0, pad - emb_width))))
    return np.concatenate(columns, axis=1)


def twice_diagonal(value):
    zero = jnp.zeros_like(value)
    return jnp.concatenate(
        [jnp.concatenate([value, zero], axis=1), jnp.concatenate([zero, value], axis=1)], axis=0
    )


def stacked_diagonal(value):
    high, low = split_value(value)
    high = twice_diagonal(high.astype(F32))
    low = twice_diagonal(low.astype(F32))
    return jnp.concatenate([high, low, high], axis=0).astype(BF16)


def layer(value, weight):
    high, low = split_value(value)
    return jnp.dot(
        jnp.concatenate([high, high, low], axis=1), weight, preferred_element_type=F32
    )


def filter_kernel(blocks, block, pad, *refs):
    hbm, refs = refs[:10], refs[11:]
    hre_ref, him_ref, hfirst_ref, fwd_ref, inv_ref, skip_ref = refs[:6]
    refs = refs[6:]
    w1_ref, b1_ref, w2_ref, b2_ref, w3_ref, decay_ref, feat_ref, table_ref, back_ref = refs[:9]
    all_skip_ref, first_ref, sems = refs[9:]
    targets = [
        w1_ref, feat_ref, b1_ref, w2_ref, b2_ref, w3_ref, decay_ref, table_ref, back_ref,
        all_skip_ref,
    ]
    copies = [
        pltpu.make_async_copy(hbm[i], targets[i], sems.at[i]) for i in range(len(targets))
    ]
    for copy in copies:
        copy.start()
    core = lax.axis_index("seq") % CORES
    length = blocks * block
    emb, order = w1_ref.shape
    first_ref[...] = jnp.zeros_like(first_ref)
    for copy in copies[:7]:
        copy.wait()

    high, low = split_value(w1_ref[...])
    high, low = high.astype(F32), low.astype(F32)
    zero = jnp.zeros_like(high)
    for i, part in enumerate((high, low, high)):
        first_ref[i * pad : i * pad + emb] = jnp.concatenate([part, zero], axis=1)
        first_ref[(3 + i) * pad : (3 + i) * pad + emb] = jnp.concatenate([zero, part], axis=1)
    b1 = jnp.concatenate([b1_ref[...]] * 2, axis=1)
    b2 = jnp.concatenate([b2_ref[...]] * 2, axis=1)
    hidden = fast_sin(
        jnp.dot(
            feat_ref[...].astype(BF16), first_ref[...].astype(BF16), preferred_element_type=F32
        )
        + b1
    )
    hidden = fast_sin(layer(hidden, stacked_diagonal(w2_ref[...])) + b2)
    lanes = pl.ds(pl.multiple_of(core * WIDE, LANES), WIDE)
    shaped = layer(hidden, stacked_diagonal(w3_ref[:, lanes]))

    decay = decay_ref[:, lanes]
    energy = expm1_of_negative(-2.0 * decay) / expm1_of_negative(decay * (-2.0 / length))
    times = lax.broadcasted_iota(jnp.int32, (length // 2, WIDE), 0).astype(F32) * (1.0 / length)
    window = jnp.exp(-(decay * times)) * (1.0 / jnp.sqrt(energy))
    window = jnp.concatenate([window, window * jnp.exp(-0.5 * decay)], axis=1)
    taps_high, taps_low = split_value(shaped * window)

    copies[7].wait()
    high, low = split_value(table_ref[...])
    fwd_ref[:, :block] = high
    fwd_ref[:, block:] = low
    table = jnp.concatenate([high, low, high], axis=1)
    rows = lax.broadcasted_iota(jnp.int32, (2 * block, WIDE), 0)
    sign = (1 - 2 * lax.rem(rows, 2)).astype(F32)
    first_row = lax.broadcasted_iota(jnp.int32, (block, WIDE), 0) == 0
    spectra = [None] * blocks
    for k in range(blocks // 2):
        part = slice(k * block, (k + 1) * block)
        stacked = jnp.concatenate([taps_high[part], taps_high[part], taps_low[part]], axis=0)
        now = jnp.dot(table, stacked, preferred_element_type=F32)
        spectra[k], spectra[k + blocks // 2] = now[:, :WIDE], now[:, WIDE:]
    for k in range(blocks):
        spec = spectra[k] if k == 0 else spectra[k] + sign * spectra[k - 1]
        real, imag = spec[:block], spec[block:]
        hre_ref[k] = real
        him_ref[k] = jnp.where(first_row, 0.0, imag)
        hfirst_ref[k] = jnp.where(first_row, imag, real)[:8]

    copies[8].wait()
    copies[9].wait()
    skip_ref[...] = all_skip_ref[:, lanes]
    high, low = split_value(back_ref[...])
    inv_ref[:, : 2 * block] = high
    inv_ref[:, 2 * block : 4 * block] = low
    inv_ref[:, 4 * block :] = high


def call_filter(weights, skip, after, blocks, block):
    w1, b1, w2, b2, w3, decay = weights
    length = blocks * block
    emb, order = w1.shape
    pad = -(-emb // 8) * 8
    forward, inverse = dft_tables(block)
    feats = filter_feature_table(length, emb, pad)
    hbm = [
        w1, feats, b1[None], w2, b2[None], w3, decay[None], forward.astype(np.float32),
        inverse.astype(np.float32), skip[None],
    ]
    out_shape = [
        VMEM((blocks, block, WIDE), F32),
        VMEM((blocks, block, WIDE), F32),
        VMEM((blocks, 8, WIDE), F32),
        VMEM((2 * block, 2 * block), BF16),
        VMEM((block, 6 * block), BF16),
        VMEM((1, WIDE), F32),
    ]
    return pl.pallas_call(
        functools.partial(filter_kernel, blocks, block, pad),
        in_specs=[pl.BlockSpec(memory_space=pltpu.HBM)] * len(hbm)
        + [pl.BlockSpec(memory_space=pl.ANY)],
        out_specs=[pl.BlockSpec(memory_space=VMEM)] * len(out_shape),
        out_shape=out_shape,
        scratch_shapes=[
            VMEM(w1.shape, F32),
            VMEM((1, order), F32),
            VMEM(w2.shape, F32),
            VMEM((1, order), F32),
            VMEM(w3.shape, F32),
            VMEM((1, w3.shape[1]), F32),
            VMEM(feats.shape, F32),
            VMEM(forward.shape, F32),
            VMEM(inverse.shape, F32),
            VMEM((1, skip.shape[0]), F32),
            VMEM((6 * pad, 2 * order), F32),
            pltpu.SemaphoreType.DMA((len(hbm),)),
        ],
        compiler_params=pltpu.CompilerParams(vmem_limit_bytes=32 * 2**20),
        cost_estimate=pl.CostEstimate(
            flops=4 * 10**8, bytes_accessed=8 * 2**20, transcendentals=length * LANES
        ),
        name="filter_spectra",
    )(*(pltpu.with_memory_space_constraint(jnp.asarray(each), pltpu.HBM) for each in hbm), after)


def lanes_of(core):
    return pl.ds(pl.multiple_of(core * WIDE, LANES), WIDE)


def columns_of(part, half, width):
    return pl.ds(pl.multiple_of(part * width + half * (width // 2), LANES), width // 2)


def weight_copies(weight_ref, over_x_ref, over_y_ref, sems, first_sem):
    rows = weight_ref.shape[0] // 2
    width = weight_ref.shape[1] // FACE
    me = lax.axis_index("chan")
    half_rows = pl.ds(pl.multiple_of((lax.axis_index("seq") % 2) * rows, LANES), rows)
    copies = []
    for out_ref, half, parts in ((over_x_ref, 0, (1, 3)), (over_y_ref, 1, (2, 3))):
        for place, k in enumerate(parts):
            copies.append(
                pltpu.make_async_copy(
                    weight_ref.at[half_rows, columns_of(me ^ k, half, width)],
                    out_ref.at[:, place * (width // 2) : (place + 1) * (width // 2)],
                    sems.at[first_sem + len(copies)],
                )
            )
    return copies


def pack_kernel(x_ref, gate_ref, weight_ref, mine_ref, other_ref, over_x_ref, over_y_ref, sems):
    block = x_ref.shape[0]
    core = lax.axis_index("seq") % CORES
    copies = []
    for place, out_ref in ((1 - core, other_ref), (core, mine_ref)):
        for source, rows in ((x_ref, slice(0, block)), (gate_ref, slice(block, 2 * block))):
            copies.append(
                pltpu.make_async_copy(
                    source.at[:, lanes_of(place)], out_ref.at[rows], sems.at[len(copies)]
                )
            )
    copies += weight_copies(weight_ref, over_x_ref, over_y_ref, sems, len(copies))
    for copy in copies:
        copy.start()
    for copy in copies:
        copy.wait()


def call_pack(x, gate, weight):
    both = VMEM((2 * x.shape[0], WIDE), BF16)
    send = VMEM((weight.shape[0] // 2, weight.shape[1] // FACE), BF16)
    return pl.pallas_call(
        pack_kernel,
        in_specs=[pl.BlockSpec(memory_space=pltpu.HBM)] * 3,
        out_specs=[pl.BlockSpec(memory_space=VMEM)] * 4,
        out_shape=[both, both, send, send],
        scratch_shapes=[pltpu.SemaphoreType.DMA((8,))],
        cost_estimate=pl.CostEstimate(flops=0, bytes_accessed=2**21, transcendentals=0),
        name="pack_pieces",
    )(*(pltpu.with_memory_space_constraint(each, pltpu.HBM) for each in (x, gate, weight)))


def order_kernel(mine_ref, theirs_ref, x_ref, gate_ref):
    block = mine_ref.shape[0] // 2
    core = lax.axis_index("seq") % CORES
    for place, source in ((core, mine_ref), (1 - core, theirs_ref)):
        rows = pl.ds(pl.multiple_of(place * block, LANES), block)
        x_ref[rows] = source[:block]
        gate_ref[rows] = source[block:]


def conv_kernel(blocks, block, *refs):
    source_refs, gate_ref, refs = refs[:CHIPS], refs[CHIPS], refs[CHIPS + 1 :]
    hre_ref, him_ref, hfirst_ref, fwd_ref, inv_ref, skip_ref = refs[:6]
    keep_ref, send_ref = refs[8:10]
    wre_ref, wim_ref, yre_ref, yim_ref = refs[12:]
    me = lax.axis_index("seq")
    core, chip = me % CORES, me // CORES
    behind = [jnp.zeros((), jnp.int32)]
    for k in range(CHIPS):
        distance = chip - (chip ^ k)
        if k:
            behind.append(jnp.maximum(distance, 1) * CORES)
        for b in range(CORES):
            values = source_refs[k][b * block : (b + 1) * block]
            spec = jnp.dot(
                fwd_ref[...], jnp.concatenate([values, values], axis=0), preferred_element_type=F32
            )
            if k:
                spec = jnp.where(distance > 0, spec, 0.0)
            wre_ref[k * CORES + b] = spec[:block]
            wim_ref[k * CORES + b] = spec[block:]

    def rows_at(start, first):
        rows = pl.ds(start, 8)
        for lanes in (slice(0, LANES), slice(LANES, WIDE)):
            totals = [None] * (2 * CORES)
            for k in range(CHIPS):
                for b in range(CORES):
                    wre = wre_ref[k * CORES + b, rows, lanes]
                    wim = wim_ref[k * CORES + b, rows, lanes]
                    for o in range(CORES):
                        if k == 0 and o < b:
                            continue
                        lag = behind[k] + (o - b)
                        hre = hre_ref[lag, rows, lanes]
                        him = him_ref[lag, rows, lanes]
                        hother = hfirst_ref[lag, :, lanes] if first else hre
                        adds = (wre * hre - wim * him, wre * him + wim * hother)
                        for i, add in enumerate(adds):
                            old = totals[2 * o + i]
                            totals[2 * o + i] = add if old is None else old + add
            for o in range(CORES):
                yre_ref[o, rows, lanes] = totals[2 * o]
                yim_ref[o, rows, lanes] = totals[2 * o + 1]

    rows_at(0, True)

    @pl.loop(1, block // 8)
    def _(tile):
        rows_at(pl.multiple_of(tile * 8, 8), False)

    for place, out_ref in ((1 - core, send_ref), (core, keep_ref)):
        re_high, re_low = split_value(yre_ref[place])
        im_high, im_low = split_value(yim_ref[place])
        stacked = jnp.concatenate([re_high, im_high, re_high, im_high, re_low, im_low], axis=0)
        conv = jnp.dot(inv_ref[...], stacked, preferred_element_type=F32)
        rows = pl.ds(pl.multiple_of(place * block, LANES), block)
        values = source_refs[0][rows].astype(F32)
        gate = gate_ref[rows].astype(F32)
        out_ref[...] = (gate * (conv + skip_ref[...] * values)).astype(BF16)


def call_conv(sources, gate, filters, passing, blocks, block):
    pinned = [pltpu.with_memory_space_constraint(each, VMEM) for each in filters]
    operands = [*sources, gate, *pinned]
    shape = jax.ShapeDtypeStruct
    return pl.pallas_call(
        functools.partial(conv_kernel, blocks, block),
        in_specs=[pl.BlockSpec(memory_space=VMEM)] * len(operands)
        + [pl.BlockSpec(memory_space=pl.ANY)] * 2,
        out_specs=[pl.BlockSpec(memory_space=VMEM)] * 2
        + [pl.BlockSpec(memory_space=pl.ANY)] * 2,
        out_shape=[shape((block, WIDE), BF16)] * 2 + [shape(p.shape, p.dtype) for p in passing],
        input_output_aliases={len(operands) + i: 2 + i for i in range(2)},
        scratch_shapes=[
            VMEM((blocks, block, WIDE), F32),
            VMEM((blocks, block, WIDE), F32),
            VMEM((CORES, block, WIDE), F32),
            VMEM((CORES, block, WIDE), F32),
        ],
        compiler_params=pltpu.CompilerParams(vmem_limit_bytes=16 * 2**20),
        cost_estimate=pl.CostEstimate(
            flops=3 * 10**8, bytes_accessed=3 * 2**20, transcendentals=0
        ),
        name="convolve",
    )(*operands, *passing)


def join_kernel(mine_ref, theirs_ref, joined_ref):
    core = lax.axis_index("seq") % CORES
    joined_ref[:, lanes_of(core)] = mine_ref[...]
    joined_ref[:, lanes_of(1 - core)] = theirs_ref[...]


def tiles(width):
    step = min(width, 2 * LANES)
    return [slice(start, start + step) for start in range(0, width, step)]


def own_kernel(width, gated_ref, weight_ref, *refs):
    out_refs, (held_ref, sems) = refs[:4], refs[4:]
    me = lax.axis_index("chan")
    copies = [
        pltpu.make_async_copy(
            weight_ref.at[:, columns_of(me ^ k, half, width)], held_ref.at[i], sems.at[i]
        )
        for i, (k, half) in enumerate(((2, 0), (1, 1), (0, 0), (0, 1)))
    ]
    for copy in copies:
        copy.start()
    left = gated_ref[...]
    for i, copy in enumerate(copies):
        copy.wait()
        for lanes in tiles(width // 2):
            out_refs[i][:, lanes] = jnp.dot(
                left, held_ref[i, :, lanes], preferred_element_type=F32
            )


def neighbour_kernel(first, x_ref, y_ref, *refs):
    from_x, from_y, sums, outs = refs[:2], refs[2:4], refs[4:6], refs[6:]
    rows = from_x[0].shape[0]
    core = lax.axis_index("seq") % 2
    for left_ref, held, sum_ref, out_ref in (
        (x_ref, from_x, sums[0], outs[0]),
        (y_ref, from_y, sums[1], outs[1]),
    ):
        near = left_ref[:, pl.ds(pl.multiple_of(core * rows, LANES), rows)]
        far = left_ref[:, pl.ds(pl.multiple_of((1 - core) * rows, LANES), rows)]
        width = out_ref.shape[1]
        for lanes in tiles(width):
            place = slice(first * width + lanes.start, first * width + lanes.stop)
            total = jnp.dot(near, held[0][:, place], preferred_element_type=F32)
            total += jnp.dot(far, held[1][:, place], preferred_element_type=F32)
            out_ref[:, lanes] = (sum_ref[:, lanes] + total).astype(out_ref.dtype)


def last_kernel(*refs):
    sums, arrived, out_ref = refs[:2], refs[2:4], refs[4]
    width = sums[0].shape[1]
    for half in range(2):
        out_ref[:, half * width : (half + 1) * width] = (
            sums[half][...] + arrived[half][...].astype(F32)
        ).astype(BF16)


def in_vmem(kernel, operands, out_shape, name, flops, scratch=()):
    return pl.pallas_call(
        kernel,
        in_specs=[pl.BlockSpec(memory_space=VMEM)] * len(operands),
        out_specs=jax.tree.map(lambda _: pl.BlockSpec(memory_space=VMEM), out_shape),
        out_shape=out_shape,
        scratch_shapes=scratch,
        compiler_params=pltpu.CompilerParams(vmem_limit_bytes=16 * 2**20),
        cost_estimate=pl.CostEstimate(flops=flops, bytes_accessed=2**20, transcendentals=0),
        name=name,
    )(*operands)


def call_own(gated, weight):
    block, width = gated.shape
    columns = weight.shape[1] // FACE
    return pl.pallas_call(
        functools.partial(own_kernel, columns),
        in_specs=[pl.BlockSpec(memory_space=VMEM), pl.BlockSpec(memory_space=pltpu.HBM)],
        out_specs=[pl.BlockSpec(memory_space=VMEM)] * 4,
        out_shape=[jax.ShapeDtypeStruct((block, columns // 2), F32)] * 4,
        scratch_shapes=[
            VMEM((4, width, columns // 2), BF16),
            pltpu.SemaphoreType.DMA((4,)),
        ],
        compiler_params=pltpu.CompilerParams(vmem_limit_bytes=16 * 2**20),
        cost_estimate=pl.CostEstimate(
            flops=4 * block * width * columns, bytes_accessed=6 * width * columns, transcendentals=0
        ),
        name="own_channels",
    )(gated, pltpu.with_memory_space_constraint(weight, pltpu.HBM))


def split_shards(
    mixer_input,
    gate_branch,
    skip_gain,
    decay_rate,
    first_weight,
    first_bias,
    second_weight,
    second_bias,
    last_weight,
    output_weight,
):
    block, width = mixer_input.shape
    blocks = lax.axis_size("seq")
    shape = jax.ShapeDtypeStruct
    along_chan = lambda part, k: lax.ppermute(part, "chan", [(c, c ^ k) for c in range(FACE)])

    def along_seq(part, k, senders=range(blocks)):
        return lax.ppermute(part, "seq", [(s, s ^ k) for s in senders])

    mine, other, over_x, over_y = call_pack(mixer_input, gate_branch, output_weight)
    from_x, from_y = along_chan(over_x, 1), along_chan(over_y, 2)
    x, gate = in_vmem(
        order_kernel,
        [mine, along_seq(other, 1)],
        [shape((2 * block, WIDE), BF16)] * 2,
        "order_tokens",
        10**6,
    )
    far = along_seq(x, 4, [s for s in range(blocks) if s // 4 == 0])
    near = along_seq(x, 2, [s for s in range(blocks) if s // 2 % 2 == 0])
    passed = along_seq(far, 2, [s for s in range(blocks) if s // 4 == 1])
    filters = call_filter(
        (first_weight, first_bias, second_weight, second_bias, last_weight, decay_rate),
        skip_gain,
        x,
        blocks,
        block,
    )
    keep, send, from_x, from_y = call_conv(
        [x, near, far, passed], gate, filters, (from_x, from_y), blocks, block
    )
    from_x, from_y = (from_x, along_seq(from_x, 1)), (from_y, along_seq(from_y, 1))
    gated = in_vmem(
        join_kernel, [keep, along_seq(send, 1)], shape((block, width), BF16), "join_channels", 10**6
    )
    x_gated, y_gated = along_chan(gated, 1), along_chan(gated, 2)
    send_a, send_b, keep_a, keep_b = call_own(gated, output_weight)
    columns = send_a.shape[1]
    flops = 4 * block * width * columns
    send_a, send_b = in_vmem(
        functools.partial(neighbour_kernel, 1),
        [x_gated, y_gated, *from_x, *from_y, send_a, send_b],
        [shape((block, columns), BF16)] * 2,
        "sums_to_send",
        flops,
    )
    got_a, got_b = along_chan(send_a, 2), along_chan(send_b, 1)
    keep_a, keep_b = in_vmem(
        functools.partial(neighbour_kernel, 0),
        [x_gated, y_gated, *from_x, *from_y, keep_a, keep_b],
        [shape((block, columns), F32)] * 2,
        "sums_to_keep",
        flops,
    )
    return in_vmem(
        last_kernel,
        [keep_a, keep_b, got_a, got_b],
        shape((block, 2 * columns), BF16),
        "last_sum",
        10**6,
    )


def contract_first(left_matrix, right_matrix):
    return lax.dot_general(
        left_matrix,
        right_matrix,
        (((0,), (0,)), ((), ())),
        precision=HIGHEST,
        preferred_element_type=F32,
    )


def filter_taps(
    first_weight, first_bias, second_weight, second_bias, last_weight, decay_rate, length
):
    features = jnp.asarray(feature_table(length, first_weight.shape[0]).T)
    hidden_one = jnp.sin(contract_first(first_weight, features) + first_bias[:, None])
    hidden_two = jnp.sin(contract_first(second_weight, hidden_one) + second_bias[:, None])
    shaped = contract_first(hidden_two, last_weight)
    positions = jnp.arange(length, dtype=jnp.int32).astype(F32)
    envelope = jnp.exp(-decay_rate[None, :] * (positions[:, None] / length))
    energy = jnp.expm1(-2.0 * decay_rate) / jnp.expm1(-2.0 * decay_rate / length)
    return shaped * envelope / jnp.sqrt(energy)[None, :]


def transform_tables(block_len):
    padded_len = 2 * block_len
    freq_index = jnp.arange(block_len + 1, dtype=jnp.int32)[:, None]
    time_index = jnp.arange(padded_len, dtype=jnp.int32)[None, :]
    angle = (freq_index * time_index % padded_len).astype(F32) * (2.0 * math.pi / padded_len)
    forward = jnp.concatenate([jnp.cos(angle), -jnp.sin(angle)], axis=0)
    later_angle = angle[:, block_len:]
    weights = jnp.where((freq_index == 0) | (freq_index == block_len), 1.0, 2.0) / padded_len
    inverse = jnp.concatenate(
        [(weights * jnp.cos(later_angle)).T, (-weights * jnp.sin(later_angle)).T], axis=1
    )
    return (forward, inverse)


def spectral_product(left_spec, right_spec, half_rows):
    left_real, left_imag = (left_spec[:half_rows], left_spec[half_rows:])
    right_real, right_imag = (right_spec[:half_rows], right_spec[half_rows:])
    return jnp.concatenate(
        [
            left_real * right_real - left_imag * right_imag,
            left_real * right_imag + left_imag * right_real,
        ],
        axis=0,
    )


def gathered_shards(
    mixer_input,
    gate_branch,
    skip_gain,
    decay_rate,
    first_weight,
    first_bias,
    second_weight,
    second_bias,
    last_weight,
    output_weight,
):
    block_len, chan_width = mixer_input.shape
    seq_count = lax.axis_size("seq")
    device = lax.axis_index("seq")
    half_rows = block_len + 1
    kernel_taps = filter_taps(
        first_weight,
        first_bias,
        second_weight,
        second_bias,
        last_weight,
        decay_rate,
        block_len * seq_count,
    )
    padded_taps = jnp.concatenate([jnp.zeros((block_len, chan_width), F32), kernel_taps], axis=0)
    forward, inverse = transform_tables(block_len)
    forward_head = forward[:, :block_len]
    gathered = lax.all_gather(mixer_input, "seq", axis=0, tiled=True)

    def one_block(block_index, total):
        rows = lax.dynamic_slice_in_dim(gathered, block_index * block_len, block_len, 0)
        source_spec = jnp.dot(
            forward_head, rows.astype(F32), precision=HIGHEST, preferred_element_type=F32
        )
        segment = lax.dynamic_slice_in_dim(
            padded_taps, (device - block_index) * block_len, 2 * block_len, 0
        )
        lag_spec = jnp.dot(forward, segment, precision=HIGHEST, preferred_element_type=F32)
        return total + spectral_product(lag_spec, source_spec, half_rows)

    total = lax.fori_loop(0, device + 1, one_block, jnp.zeros((2 * half_rows, chan_width), F32))
    convolved = jnp.dot(inverse, total, precision=HIGHEST, preferred_element_type=F32)
    values = mixer_input.astype(F32)
    gated_mix = (
        gate_branch.astype(F32) * (convolved + skip_gain[None, :] * values)
    ).astype(BF16)
    partial_out = jnp.dot(gated_mix, output_weight, preferred_element_type=F32)
    return lax.psum_scatter(partial_out, "chan", scatter_dimension=1, tiled=True).astype(BF16)


def solution(mesh):
    seq_count, chan_count = mesh.shape["seq"], mesh.shape["chan"]

    def shards(mixer_input, *rest):
        block, width = mixer_input.shape
        splits = (
            width == CORES * WIDE
            and block % LANES == 0
            and seq_count == CORES * CHIPS
            and chan_count == FACE
        )
        plan = split_shards if splits else gathered_shards
        return plan(mixer_input, *rest)

    in_specs = (
        P("seq", "chan"),
        P("seq", "chan"),
        P("chan"),
        P("chan"),
        P(),
        P(),
        P(),
        P(),
        P(None, "chan"),
        P("chan", None),
    )
    out_specs = P("seq", "chan")
    return jax.shard_map(shards, mesh=mesh, in_specs=in_specs, out_specs=out_specs, check_vma=False)
```

```python
import functools
import math

import jax
import jax.numpy as jnp
import numpy as np
from jax import lax
from jax.experimental import pallas as pl
from jax.experimental.pallas import tpu as pltpu
from jax.sharding import PartitionSpec as P

HIGHEST = lax.Precision.HIGHEST
F32 = jnp.float32
BF16 = jnp.bfloat16
LANES = 128
WIDE = 2 * LANES
CORES = 2
CHIPS = 4
FACE = 4
VMEM = pltpu.VMEM


def feature_table(length, emb_width):
    band_count = (emb_width - 1) // 2
    positions = np.arange(length, dtype=np.int64)
    columns = [positions / length]
    for band in range(1, band_count + 1):
        frequency = min(
            length // 2, max(band, int((length / 2) ** ((band - 1) / (band_count - 1))))
        )
        angle = (positions * frequency % length) * (2.0 * math.pi / length)
        columns.append(np.cos(angle))
        columns.append(np.sin(angle))
    return np.stack(columns, axis=1).astype(np.float32)


def split_bf16(table):
    high = table.astype(np.float32).astype(jnp.bfloat16)
    low = (table - high.astype(np.float64)).astype(np.float32).astype(jnp.bfloat16)
    return high, low


def dft_tables(block):
    size = 2 * block
    bins = np.arange(block)[:, None]
    times = np.arange(block)[None, :]
    angle = (bins * times % size) * (2.0 * math.pi / size)
    imag = -np.sin(angle)
    imag[0] = 1.0 - 2.0 * (np.arange(block) % 2)
    forward = np.concatenate([np.cos(angle), imag], axis=0)
    weight = np.where(bins == 0, 1.0, 2.0) / size
    back_imag = -weight * np.sin(angle)
    back_imag[0] = (1.0 - 2.0 * (np.arange(block) % 2)) / size
    inverse = np.concatenate([weight * np.cos(angle), back_imag], axis=0).T
    return forward, inverse


def fast_sin(x):
    turns = jnp.floor(x * (1.0 / math.pi) + 0.5)
    rest = x - turns * 3.140625
    rest = rest - turns * 9.67502593994140625e-4
    rest = rest - turns * 1.509957990978376432e-7
    parity = turns - 2.0 * jnp.floor(turns * 0.5)
    rest = rest * (1.0 - 2.0 * parity)
    square = rest * rest
    poly = -2.5052108e-8
    for coeff in (2.7557319e-6, -1.9841270e-4, 8.3333333e-3, -1.6666667e-1):
        poly = poly * square + coeff
    return rest + rest * square * poly


def expm1_of_negative(x):
    near = jnp.maximum(x, -0.5)
    series = jnp.full_like(x, 1.0 / 3628800.0)
    for denom in (362880.0, 40320.0, 5040.0, 720.0, 120.0, 24.0, 6.0, 2.0, 1.0):
        series = series * near + 1.0 / denom
    return jnp.where(x > -0.5, near * series, jnp.exp(x) - 1.0)


def split_value(value):
    high = value.astype(BF16)
    return high, (value - high.astype(F32)).astype(BF16)


def filter_feature_table(length, emb_width, pad):
    table = feature_table(length, emb_width)
    columns = []
    for half in (table[: length // 2], table[length // 2 :]):
        high, low = (part.astype(np.float32) for part in split_bf16(half))
        for part in (high, high, low):
            columns.append(np.pad(part, ((0, 0), (0, pad - emb_width))))
    return np.concatenate(columns, axis=1)


def twice_diagonal(value):
    zero = jnp.zeros_like(value)
    return jnp.concatenate(
        [jnp.concatenate([value, zero], axis=1), jnp.concatenate([zero, value], axis=1)], axis=0
    )


def stacked_diagonal(value):
    high, low = split_value(value)
    high = twice_diagonal(high.astype(F32))
    low = twice_diagonal(low.astype(F32))
    return jnp.concatenate([high, low, high], axis=0).astype(BF16)


def layer(value, weight):
    high, low = split_value(value)
    return jnp.dot(
        jnp.concatenate([high, high, low], axis=1), weight, preferred_element_type=F32
    )


def filter_kernel(blocks, block, pad, *refs):
    hbm, refs = refs[:10], refs[11:]
    hre_ref, him_ref, hfirst_ref, fwd_ref, inv_ref, skip_ref = refs[:6]
    refs = refs[6:]
    w1_ref, b1_ref, w2_ref, b2_ref, w3_ref, decay_ref, feat_ref, table_ref, back_ref = refs[:9]
    all_skip_ref, first_ref, sems = refs[9:]
    targets = [
        w1_ref, feat_ref, b1_ref, w2_ref, b2_ref, w3_ref, decay_ref, table_ref, back_ref,
        all_skip_ref,
    ]
    copies = [
        pltpu.make_async_copy(hbm[i], targets[i], sems.at[i]) for i in range(len(targets))
    ]
    for copy in copies:
        copy.start()
    core = lax.axis_index("seq") % CORES
    length = blocks * block
    emb, order = w1_ref.shape
    first_ref[...] = jnp.zeros_like(first_ref)
    for copy in copies[:7]:
        copy.wait()

    high, low = split_value(w1_ref[...])
    high, low = high.astype(F32), low.astype(F32)
    zero = jnp.zeros_like(high)
    for i, part in enumerate((high, low, high)):
        first_ref[i * pad : i * pad + emb] = jnp.concatenate([part, zero], axis=1)
        first_ref[(3 + i) * pad : (3 + i) * pad + emb] = jnp.concatenate([zero, part], axis=1)
    b1 = jnp.concatenate([b1_ref[...]] * 2, axis=1)
    b2 = jnp.concatenate([b2_ref[...]] * 2, axis=1)
    hidden = fast_sin(
        jnp.dot(
            feat_ref[...].astype(BF16), first_ref[...].astype(BF16), preferred_element_type=F32
        )
        + b1
    )
    hidden = fast_sin(layer(hidden, stacked_diagonal(w2_ref[...])) + b2)
    lanes = pl.ds(pl.multiple_of(core * WIDE, LANES), WIDE)
    shaped = layer(hidden, stacked_diagonal(w3_ref[:, lanes]))

    decay = decay_ref[:, lanes]
    energy = expm1_of_negative(-2.0 * decay) / expm1_of_negative(decay * (-2.0 / length))
    times = lax.broadcasted_iota(jnp.int32, (length // 2, WIDE), 0).astype(F32) * (1.0 / length)
    window = jnp.exp(-(decay * times)) * (1.0 / jnp.sqrt(energy))
    window = jnp.concatenate([window, window * jnp.exp(-0.5 * decay)], axis=1)
    taps_high, taps_low = split_value(shaped * window)

    copies[7].wait()
    high, low = split_value(table_ref[...])
    fwd_ref[:, :block] = high
    fwd_ref[:, block:] = low
    table = jnp.concatenate([high, low, high], axis=1)
    rows = lax.broadcasted_iota(jnp.int32, (2 * block, WIDE), 0)
    sign = (1 - 2 * lax.rem(rows, 2)).astype(F32)
    first_row = lax.broadcasted_iota(jnp.int32, (block, WIDE), 0) == 0
    spectra = [None] * blocks
    for k in range(blocks // 2):
        part = slice(k * block, (k + 1) * block)
        stacked = jnp.concatenate([taps_high[part], taps_high[part], taps_low[part]], axis=0)
        now = jnp.dot(table, stacked, preferred_element_type=F32)
        spectra[k], spectra[k + blocks // 2] = now[:, :WIDE], now[:, WIDE:]
    for k in range(blocks):
        spec = spectra[k] if k == 0 else spectra[k] + sign * spectra[k - 1]
        real, imag = spec[:block], spec[block:]
        hre_ref[k] = real
        him_ref[k] = jnp.where(first_row, 0.0, imag)
        hfirst_ref[k] = jnp.where(first_row, imag, real)[:8]

    copies[8].wait()
    copies[9].wait()
    skip_ref[...] = all_skip_ref[:, lanes]
    high, low = split_value(back_ref[...])
    inv_ref[:, : 2 * block] = high
    inv_ref[:, 2 * block : 4 * block] = low
    inv_ref[:, 4 * block :] = high


def call_filter(weights, skip, after, blocks, block):
    w1, b1, w2, b2, w3, decay = weights
    length = blocks * block
    emb, order = w1.shape
    pad = -(-emb // 8) * 8
    forward, inverse = dft_tables(block)
    feats = filter_feature_table(length, emb, pad)
    hbm = [
        w1, feats, b1[None], w2, b2[None], w3, decay[None], forward.astype(np.float32),
        inverse.astype(np.float32), skip[None],
    ]
    out_shape = [
        VMEM((blocks, block, WIDE), F32),
        VMEM((blocks, block, WIDE), F32),
        VMEM((blocks, 8, WIDE), F32),
        VMEM((2 * block, 2 * block), BF16),
        VMEM((block, 6 * block), BF16),
        VMEM((1, WIDE), F32),
    ]
    return pl.pallas_call(
        functools.partial(filter_kernel, blocks, block, pad),
        in_specs=[pl.BlockSpec(memory_space=pltpu.HBM)] * len(hbm)
        + [pl.BlockSpec(memory_space=pl.ANY)],
        out_specs=[pl.BlockSpec(memory_space=VMEM)] * len(out_shape),
        out_shape=out_shape,
        scratch_shapes=[
            VMEM(w1.shape, F32),
            VMEM((1, order), F32),
            VMEM(w2.shape, F32),
            VMEM((1, order), F32),
            VMEM(w3.shape, F32),
            VMEM((1, w3.shape[1]), F32),
            VMEM(feats.shape, F32),
            VMEM(forward.shape, F32),
            VMEM(inverse.shape, F32),
            VMEM((1, skip.shape[0]), F32),
            VMEM((6 * pad, 2 * order), F32),
            pltpu.SemaphoreType.DMA((len(hbm),)),
        ],
        compiler_params=pltpu.CompilerParams(vmem_limit_bytes=32 * 2**20),
        cost_estimate=pl.CostEstimate(
            flops=4 * 10**8, bytes_accessed=8 * 2**20, transcendentals=length * LANES
        ),
        name="filter_spectra",
    )(*(pltpu.with_memory_space_constraint(jnp.asarray(each), pltpu.HBM) for each in hbm), after)


def lanes_of(core):
    return pl.ds(pl.multiple_of(core * WIDE, LANES), WIDE)


def columns_of(part, half, width):
    return pl.ds(pl.multiple_of(part * width + half * (width // 2), LANES), width // 2)


def weight_copies(weight_ref, over_x_ref, over_y_ref, sems, first_sem):
    rows = weight_ref.shape[0] // 2
    width = weight_ref.shape[1] // FACE
    me = lax.axis_index("chan")
    half_rows = pl.ds(pl.multiple_of((lax.axis_index("seq") % 2) * rows, LANES), rows)
    copies = []
    for out_ref, half, parts in ((over_x_ref, 0, (1, 3)), (over_y_ref, 1, (2, 3))):
        for place, k in enumerate(parts):
            copies.append(
                pltpu.make_async_copy(
                    weight_ref.at[half_rows, columns_of(me ^ k, half, width)],
                    out_ref.at[:, place * (width // 2) : (place + 1) * (width // 2)],
                    sems.at[first_sem + len(copies)],
                )
            )
    return copies


def pack_kernel(x_ref, gate_ref, weight_ref, mine_ref, other_ref, over_x_ref, over_y_ref, sems):
    block = x_ref.shape[0]
    core = lax.axis_index("seq") % CORES
    copies = []
    for place, out_ref in ((1 - core, other_ref), (core, mine_ref)):
        for source, rows in ((x_ref, slice(0, block)), (gate_ref, slice(block, 2 * block))):
            copies.append(
                pltpu.make_async_copy(
                    source.at[:, lanes_of(place)], out_ref.at[rows], sems.at[len(copies)]
                )
            )
    copies += weight_copies(weight_ref, over_x_ref, over_y_ref, sems, len(copies))
    for copy in copies:
        copy.start()
    for copy in copies:
        copy.wait()


def call_pack(x, gate, weight):
    both = VMEM((2 * x.shape[0], WIDE), BF16)
    send = VMEM((weight.shape[0] // 2, weight.shape[1] // FACE), BF16)
    return pl.pallas_call(
        pack_kernel,
        in_specs=[pl.BlockSpec(memory_space=pltpu.HBM)] * 3,
        out_specs=[pl.BlockSpec(memory_space=VMEM)] * 4,
        out_shape=[both, both, send, send],
        scratch_shapes=[pltpu.SemaphoreType.DMA((8,))],
        cost_estimate=pl.CostEstimate(flops=0, bytes_accessed=2**21, transcendentals=0),
        name="pack_pieces",
    )(*(pltpu.with_memory_space_constraint(each, pltpu.HBM) for each in (x, gate, weight)))


def nothing_kernel(*refs):
    del refs


def once_there(value, other):
    return pl.pallas_call(
        nothing_kernel,
        in_specs=[pl.BlockSpec(memory_space=pl.ANY)] * 2,
        out_specs=pl.BlockSpec(memory_space=pl.ANY),
        out_shape=jax.ShapeDtypeStruct(value.shape, value.dtype),
        input_output_aliases={0: 0},
        name="once_there",
    )(value, other)


def conv_kernel(blocks, block, *refs):
    own_refs, refs = refs[:CORES], refs[CORES:]
    far_refs, refs = refs[: blocks - CORES], refs[blocks - CORES :]
    hre_ref, him_ref, hfirst_ref, fwd_ref, inv_ref, skip_ref = refs[:6]
    keep_ref, send_ref = refs[8:10]
    wre_ref, wim_ref, yre_ref, yim_ref = refs[12:]
    me = lax.axis_index("seq")
    core, chip = me % CORES, me // CORES
    behind = [jnp.zeros((), jnp.int32)]
    for k in range(CHIPS):
        distance = chip - (chip ^ k)
        if k:
            behind.append(jnp.maximum(distance, 1) * CORES)
        for i, b in enumerate((core, 1 - core)):
            if k:
                values = far_refs[(k - 1) * CORES + i][:, lanes_of(core)]
            else:
                values = own_refs[i][:block]
            spec = jnp.dot(
                fwd_ref[...], jnp.concatenate([values, values], axis=0), preferred_element_type=F32
            )
            if k:
                spec = jnp.where(distance > 0, spec, 0.0)
            wre_ref[k * CORES + b] = spec[:block]
            wim_ref[k * CORES + b] = spec[block:]

    def rows_at(start, first):
        rows = pl.ds(start, 8)
        for lanes in (slice(0, LANES), slice(LANES, WIDE)):
            totals = [None] * (2 * CORES)
            for k in range(CHIPS):
                for b in range(CORES):
                    wre = wre_ref[k * CORES + b, rows, lanes]
                    wim = wim_ref[k * CORES + b, rows, lanes]
                    for o in range(CORES):
                        if k == 0 and o < b:
                            continue
                        lag = behind[k] + (o - b)
                        hre = hre_ref[lag, rows, lanes]
                        him = him_ref[lag, rows, lanes]
                        hother = hfirst_ref[lag, :, lanes] if first else hre
                        adds = (wre * hre - wim * him, wre * him + wim * hother)
                        for i, add in enumerate(adds):
                            old = totals[2 * o + i]
                            totals[2 * o + i] = add if old is None else old + add
            for o in range(CORES):
                yre_ref[o, rows, lanes] = totals[2 * o]
                yim_ref[o, rows, lanes] = totals[2 * o + 1]

    rows_at(0, True)

    @pl.loop(1, block // 8)
    def _(tile):
        rows_at(pl.multiple_of(tile * 8, 8), False)

    for place, own_ref, out_ref in (
        (1 - core, own_refs[1], send_ref),
        (core, own_refs[0], keep_ref),
    ):
        re_high, re_low = split_value(yre_ref[place])
        im_high, im_low = split_value(yim_ref[place])
        stacked = jnp.concatenate([re_high, im_high, re_high, im_high, re_low, im_low], axis=0)
        conv = jnp.dot(inv_ref[...], stacked, preferred_element_type=F32)
        values = own_ref[:block].astype(F32)
        gate = own_ref[block:].astype(F32)
        out_ref[...] = (gate * (conv + skip_ref[...] * values)).astype(BF16)


def call_conv(own, earlier, filters, passing, blocks, block):
    pinned = [pltpu.with_memory_space_constraint(each, VMEM) for each in filters]
    operands = [*own, *earlier, *pinned]
    shape = jax.ShapeDtypeStruct
    return pl.pallas_call(
        functools.partial(conv_kernel, blocks, block),
        in_specs=[pl.BlockSpec(memory_space=VMEM)] * len(operands)
        + [pl.BlockSpec(memory_space=pl.ANY)] * 2,
        out_specs=[pl.BlockSpec(memory_space=VMEM)] * 2
        + [pl.BlockSpec(memory_space=pl.ANY)] * 2,
        out_shape=[shape((block, WIDE), BF16)] * 2 + [shape(p.shape, p.dtype) for p in passing],
        input_output_aliases={len(operands) + i: 2 + i for i in range(2)},
        scratch_shapes=[
            VMEM((blocks, block, WIDE), F32),
            VMEM((blocks, block, WIDE), F32),
            VMEM((CORES, block, WIDE), F32),
            VMEM((CORES, block, WIDE), F32),
        ],
        compiler_params=pltpu.CompilerParams(vmem_limit_bytes=16 * 2**20),
        cost_estimate=pl.CostEstimate(
            flops=3 * 10**8, bytes_accessed=3 * 2**20, transcendentals=0
        ),
        name="convolve",
    )(*operands, *passing)


def join_kernel(mine_ref, theirs_ref, joined_ref):
    core = lax.axis_index("seq") % CORES
    joined_ref[:, lanes_of(core)] = mine_ref[...]
    joined_ref[:, lanes_of(1 - core)] = theirs_ref[...]


def tiles(width):
    step = min(width, 2 * LANES)
    return [slice(start, start + step) for start in range(0, width, step)]


def own_kernel(width, gated_ref, weight_ref, *refs):
    out_refs, (held_ref, sems) = refs[:4], refs[4:]
    me = lax.axis_index("chan")
    copies = [
        pltpu.make_async_copy(
            weight_ref.at[:, columns_of(me ^ k, half, width)], held_ref.at[i], sems.at[i]
        )
        for i, (k, half) in enumerate(((2, 0), (1, 1), (0, 0), (0, 1)))
    ]
    for copy in copies:
        copy.start()
    left = gated_ref[...]
    for i, copy in enumerate(copies):
        copy.wait()
        for lanes in tiles(width // 2):
            out_refs[i][:, lanes] = jnp.dot(
                left, held_ref[i, :, lanes], preferred_element_type=F32
            )


def neighbour_kernel(first, x_ref, y_ref, *refs):
    from_x, from_y, sums, outs = refs[:2], refs[2:4], refs[4:6], refs[6:]
    rows = from_x[0].shape[0]
    core = lax.axis_index("seq") % 2
    for left_ref, held, sum_ref, out_ref in (
        (x_ref, from_x, sums[0], outs[0]),
        (y_ref, from_y, sums[1], outs[1]),
    ):
        near = left_ref[:, pl.ds(pl.multiple_of(core * rows, LANES), rows)]
        far = left_ref[:, pl.ds(pl.multiple_of((1 - core) * rows, LANES), rows)]
        width = out_ref.shape[1]
        for lanes in tiles(width):
            place = slice(first * width + lanes.start, first * width + lanes.stop)
            total = jnp.dot(near, held[0][:, place], preferred_element_type=F32)
            total += jnp.dot(far, held[1][:, place], preferred_element_type=F32)
            out_ref[:, lanes] = (sum_ref[:, lanes] + total).astype(out_ref.dtype)


def last_kernel(*refs):
    sums, arrived, out_ref = refs[:2], refs[2:4], refs[4]
    width = sums[0].shape[1]
    for half in range(2):
        out_ref[:, half * width : (half + 1) * width] = (
            sums[half][...] + arrived[half][...].astype(F32)
        ).astype(BF16)


def in_vmem(kernel, operands, out_shape, name, flops, scratch=()):
    return pl.pallas_call(
        kernel,
        in_specs=[pl.BlockSpec(memory_space=VMEM)] * len(operands),
        out_specs=jax.tree.map(lambda _: pl.BlockSpec(memory_space=VMEM), out_shape),
        out_shape=out_shape,
        scratch_shapes=scratch,
        compiler_params=pltpu.CompilerParams(vmem_limit_bytes=16 * 2**20),
        cost_estimate=pl.CostEstimate(flops=flops, bytes_accessed=2**20, transcendentals=0),
        name=name,
    )(*operands)


def call_own(gated, weight):
    block, width = gated.shape
    columns = weight.shape[1] // FACE
    return pl.pallas_call(
        functools.partial(own_kernel, columns),
        in_specs=[pl.BlockSpec(memory_space=VMEM), pl.BlockSpec(memory_space=pltpu.HBM)],
        out_specs=[pl.BlockSpec(memory_space=VMEM)] * 4,
        out_shape=[jax.ShapeDtypeStruct((block, columns // 2), F32)] * 4,
        scratch_shapes=[
            VMEM((4, width, columns // 2), BF16),
            pltpu.SemaphoreType.DMA((4,)),
        ],
        compiler_params=pltpu.CompilerParams(vmem_limit_bytes=16 * 2**20),
        cost_estimate=pl.CostEstimate(
            flops=4 * block * width * columns, bytes_accessed=6 * width * columns, transcendentals=0
        ),
        name="own_channels",
    )(gated, pltpu.with_memory_space_constraint(weight, pltpu.HBM))


def split_shards(
    mixer_input,
    gate_branch,
    skip_gain,
    decay_rate,
    first_weight,
    first_bias,
    second_weight,
    second_bias,
    last_weight,
    output_weight,
):
    block, width = mixer_input.shape
    blocks = lax.axis_size("seq")
    shape = jax.ShapeDtypeStruct
    along_chan = lambda part, k: lax.ppermute(part, "chan", [(c, c ^ k) for c in range(FACE)])

    def along_seq(part, k, senders=range(blocks)):
        return lax.ppermute(part, "seq", [(s, s ^ k) for s in senders])

    far = along_seq(mixer_input, 4, [s for s in range(blocks) if s // 4 == 0])
    near = along_seq(mixer_input, 2, [s for s in range(blocks) if s // 2 % 2 == 0])
    mine, other, over_x, over_y = call_pack(mixer_input, gate_branch, output_weight)
    from_x, from_y = along_chan(over_x, 1), along_chan(over_y, 2)
    filters = call_filter(
        (first_weight, first_bias, second_weight, second_bias, last_weight, decay_rate),
        skip_gain,
        mine,
        blocks,
        block,
    )
    far = once_there(far, filters[-1])
    passed = along_seq(far, 2, [s for s in range(blocks) if s // 4 == 1])
    earlier = []
    for part in (near, far, passed):
        earlier += [part, along_seq(part, 1)]
    keep, send, from_x, from_y = call_conv(
        (mine, along_seq(other, 1)), earlier, filters, (from_x, from_y), blocks, block
    )
    from_x, from_y = (from_x, along_seq(from_x, 1)), (from_y, along_seq(from_y, 1))
    gated = in_vmem(
        join_kernel, [keep, along_seq(send, 1)], shape((block, width), BF16), "join_channels", 10**6
    )
    x_gated, y_gated = along_chan(gated, 1), along_chan(gated, 2)
    send_a, send_b, keep_a, keep_b = call_own(gated, output_weight)
    columns = send_a.shape[1]
    flops = 4 * block * width * columns
    send_a, send_b = in_vmem(
        functools.partial(neighbour_kernel, 1),
        [x_gated, y_gated, *from_x, *from_y, send_a, send_b],
        [shape((block, columns), BF16)] * 2,
        "sums_to_send",
        flops,
    )
    got_a, got_b = along_chan(send_a, 2), along_chan(send_b, 1)
    keep_a, keep_b = in_vmem(
        functools.partial(neighbour_kernel, 0),
        [x_gated, y_gated, *from_x, *from_y, keep_a, keep_b],
        [shape((block, columns), F32)] * 2,
        "sums_to_keep",
        flops,
    )
    return in_vmem(
        last_kernel,
        [keep_a, keep_b, got_a, got_b],
        shape((block, 2 * columns), BF16),
        "last_sum",
        10**6,
    )


def contract_first(left_matrix, right_matrix):
    return lax.dot_general(
        left_matrix,
        right_matrix,
        (((0,), (0,)), ((), ())),
        precision=HIGHEST,
        preferred_element_type=F32,
    )


def filter_taps(
    first_weight, first_bias, second_weight, second_bias, last_weight, decay_rate, length
):
    features = jnp.asarray(feature_table(length, first_weight.shape[0]).T)
    hidden_one = jnp.sin(contract_first(first_weight, features) + first_bias[:, None])
    hidden_two = jnp.sin(contract_first(second_weight, hidden_one) + second_bias[:, None])
    shaped = contract_first(hidden_two, last_weight)
    positions = jnp.arange(length, dtype=jnp.int32).astype(F32)
    envelope = jnp.exp(-decay_rate[None, :] * (positions[:, None] / length))
    energy = jnp.expm1(-2.0 * decay_rate) / jnp.expm1(-2.0 * decay_rate / length)
    return shaped * envelope / jnp.sqrt(energy)[None, :]


def transform_tables(block_len):
    padded_len = 2 * block_len
    freq_index = jnp.arange(block_len + 1, dtype=jnp.int32)[:, None]
    time_index = jnp.arange(padded_len, dtype=jnp.int32)[None, :]
    angle = (freq_index * time_index % padded_len).astype(F32) * (2.0 * math.pi / padded_len)
    forward = jnp.concatenate([jnp.cos(angle), -jnp.sin(angle)], axis=0)
    later_angle = angle[:, block_len:]
    weights = jnp.where((freq_index == 0) | (freq_index == block_len), 1.0, 2.0) / padded_len
    inverse = jnp.concatenate(
        [(weights * jnp.cos(later_angle)).T, (-weights * jnp.sin(later_angle)).T], axis=1
    )
    return (forward, inverse)


def spectral_product(left_spec, right_spec, half_rows):
    left_real, left_imag = (left_spec[:half_rows], left_spec[half_rows:])
    right_real, right_imag = (right_spec[:half_rows], right_spec[half_rows:])
    return jnp.concatenate(
        [
            left_real * right_real - left_imag * right_imag,
            left_real * right_imag + left_imag * right_real,
        ],
        axis=0,
    )


def gathered_shards(
    mixer_input,
    gate_branch,
    skip_gain,
    decay_rate,
    first_weight,
    first_bias,
    second_weight,
    second_bias,
    last_weight,
    output_weight,
):
    block_len, chan_width = mixer_input.shape
    seq_count = lax.axis_size("seq")
    device = lax.axis_index("seq")
    half_rows = block_len + 1
    kernel_taps = filter_taps(
        first_weight,
        first_bias,
        second_weight,
        second_bias,
        last_weight,
        decay_rate,
        block_len * seq_count,
    )
    padded_taps = jnp.concatenate([jnp.zeros((block_len, chan_width), F32), kernel_taps], axis=0)
    forward, inverse = transform_tables(block_len)
    forward_head = forward[:, :block_len]
    gathered = lax.all_gather(mixer_input, "seq", axis=0, tiled=True)

    def one_block(block_index, total):
        rows = lax.dynamic_slice_in_dim(gathered, block_index * block_len, block_len, 0)
        source_spec = jnp.dot(
            forward_head, rows.astype(F32), precision=HIGHEST, preferred_element_type=F32
        )
        segment = lax.dynamic_slice_in_dim(
            padded_taps, (device - block_index) * block_len, 2 * block_len, 0
        )
        lag_spec = jnp.dot(forward, segment, precision=HIGHEST, preferred_element_type=F32)
        return total + spectral_product(lag_spec, source_spec, half_rows)

    total = lax.fori_loop(0, device + 1, one_block, jnp.zeros((2 * half_rows, chan_width), F32))
    convolved = jnp.dot(inverse, total, precision=HIGHEST, preferred_element_type=F32)
    values = mixer_input.astype(F32)
    gated_mix = (
        gate_branch.astype(F32) * (convolved + skip_gain[None, :] * values)
    ).astype(BF16)
    partial_out = jnp.dot(gated_mix, output_weight, preferred_element_type=F32)
    return lax.psum_scatter(partial_out, "chan", scatter_dimension=1, tiled=True).astype(BF16)


def solution(mesh):
    seq_count, chan_count = mesh.shape["seq"], mesh.shape["chan"]

    def shards(mixer_input, *rest):
        block, width = mixer_input.shape
        splits = (
            width == CORES * WIDE
            and block % LANES == 0
            and seq_count == CORES * CHIPS
            and chan_count == FACE
        )
        plan = split_shards if splits else gathered_shards
        return plan(mixer_input, *rest)

    in_specs = (
        P("seq", "chan"),
        P("seq", "chan"),
        P("chan"),
        P("chan"),
        P(),
        P(),
        P(),
        P(),
        P(None, "chan"),
        P("chan", None),
    )
    out_specs = P("seq", "chan")
    return jax.shard_map(shards, mesh=mesh, in_specs=in_specs, out_specs=out_specs, check_vma=False)
```

```python
import functools
import math

import jax
import jax.numpy as jnp
import numpy as np
from jax import lax
from jax.experimental import pallas as pl
from jax.experimental.pallas import tpu as pltpu
from jax.sharding import PartitionSpec as P

HIGHEST = lax.Precision.HIGHEST
F32 = jnp.float32
BF16 = jnp.bfloat16
LANES = 128
FACE = 4
VMEM = pltpu.VMEM


def feature_table(length, emb_width):
    band_count = (emb_width - 1) // 2
    positions = np.arange(length, dtype=np.int64)
    columns = [positions / length]
    for band in range(1, band_count + 1):
        frequency = min(
            length // 2, max(band, int((length / 2) ** ((band - 1) / (band_count - 1))))
        )
        angle = (positions * frequency % length) * (2.0 * math.pi / length)
        columns.append(np.cos(angle))
        columns.append(np.sin(angle))
    return np.stack(columns, axis=1).astype(np.float32)


def split_bf16(table):
    high = table.astype(np.float32).astype(jnp.bfloat16)
    low = (table - high.astype(np.float64)).astype(np.float32).astype(jnp.bfloat16)
    return high, low


def dft_tables(block):
    size = 2 * block
    bins = np.arange(block)[:, None]
    times = np.arange(block)[None, :]
    angle = (bins * times % size) * (2.0 * math.pi / size)
    imag = -np.sin(angle)
    imag[0] = 1.0 - 2.0 * (np.arange(block) % 2)
    forward = np.concatenate([np.cos(angle), imag], axis=0)
    weight = np.where(bins == 0, 1.0, 2.0) / size
    back_imag = -weight * np.sin(angle)
    back_imag[0] = (1.0 - 2.0 * (np.arange(block) % 2)) / size
    inverse = np.concatenate([weight * np.cos(angle), back_imag], axis=0).T
    return forward, inverse


def fast_sin(x):
    turns = jnp.floor(x * (1.0 / math.pi) + 0.5)
    rest = x - turns * 3.140625
    rest = rest - turns * 9.67502593994140625e-4
    rest = rest - turns * 1.509957990978376432e-7
    parity = turns - 2.0 * jnp.floor(turns * 0.5)
    rest = rest * (1.0 - 2.0 * parity)
    square = rest * rest
    poly = -2.5052108e-8
    for coeff in (2.7557319e-6, -1.9841270e-4, 8.3333333e-3, -1.6666667e-1):
        poly = poly * square + coeff
    return rest + rest * square * poly


def expm1_of_negative(x):
    near = jnp.maximum(x, -0.5)
    series = jnp.full_like(x, 1.0 / 3628800.0)
    for denom in (362880.0, 40320.0, 5040.0, 720.0, 120.0, 24.0, 6.0, 2.0, 1.0):
        series = series * near + 1.0 / denom
    return jnp.where(x > -0.5, near * series, jnp.exp(x) - 1.0)


def split_value(value):
    high = value.astype(BF16)
    return high, (value - high.astype(F32)).astype(BF16)


def filter_feature_table(length, emb_width, pad):
    table = feature_table(length, emb_width)
    columns = []
    for half in (table[: length // 2], table[length // 2 :]):
        high, low = (part.astype(np.float32) for part in split_bf16(half))
        for part in (high, high, low):
            columns.append(np.pad(part, ((0, 0), (0, pad - emb_width))))
    return np.concatenate(columns, axis=1)


def twice_diagonal(value):
    zero = jnp.zeros_like(value)
    return jnp.concatenate(
        [jnp.concatenate([value, zero], axis=1), jnp.concatenate([zero, value], axis=1)], axis=0
    )


def stacked_diagonal(value):
    high, low = split_value(value)
    high = twice_diagonal(high.astype(F32))
    low = twice_diagonal(low.astype(F32))
    return jnp.concatenate([high, low, high], axis=0).astype(BF16)


def layer(value, weight):
    high, low = split_value(value)
    return jnp.dot(
        jnp.concatenate([high, high, low], axis=1), weight, preferred_element_type=F32
    )


def filter_kernel(blocks, block, outs, pad, *refs):
    hbm, refs = refs[:10], refs[10:]
    hre_ref, him_ref, hfirst_ref, fwd_ref, inv_ref, skip_ref = refs[:6]
    refs = refs[6:]
    w1_ref, b1_ref, w2_ref, b2_ref, w3_ref, decay_ref, feat_ref, table_ref, back_ref = refs[:9]
    all_skip_ref, first_ref, sems = refs[9:]
    targets = [
        w1_ref, feat_ref, b1_ref, w2_ref, b2_ref, w3_ref, decay_ref, table_ref, back_ref,
        all_skip_ref,
    ]
    copies = [
        pltpu.make_async_copy(hbm[i], targets[i], sems.at[i]) for i in range(len(targets))
    ]
    for copy in copies:
        copy.start()
    group = lax.axis_index("seq") % outs
    length = blocks * block
    emb, order = w1_ref.shape
    first_ref[...] = jnp.zeros_like(first_ref)
    for copy in copies[:7]:
        copy.wait()

    high, low = split_value(w1_ref[...])
    high, low = high.astype(F32), low.astype(F32)
    zero = jnp.zeros_like(high)
    for i, part in enumerate((high, low, high)):
        first_ref[i * pad : i * pad + emb] = jnp.concatenate([part, zero], axis=1)
        first_ref[(3 + i) * pad : (3 + i) * pad + emb] = jnp.concatenate([zero, part], axis=1)
    b1 = jnp.concatenate([b1_ref[...]] * 2, axis=1)
    b2 = jnp.concatenate([b2_ref[...]] * 2, axis=1)
    hidden = fast_sin(
        jnp.dot(
            feat_ref[...].astype(BF16), first_ref[...].astype(BF16), preferred_element_type=F32
        )
        + b1
    )
    hidden = fast_sin(layer(hidden, stacked_diagonal(w2_ref[...])) + b2)
    lanes = pl.ds(pl.multiple_of(group * LANES, LANES), LANES)
    shaped = layer(hidden, stacked_diagonal(w3_ref[:, lanes]))

    decay = decay_ref[:, lanes]
    energy = expm1_of_negative(-2.0 * decay) / expm1_of_negative(decay * (-2.0 / length))
    times = lax.broadcasted_iota(jnp.int32, (length // 2, LANES), 0).astype(F32) * (1.0 / length)
    window = jnp.exp(-(decay * times)) * (1.0 / jnp.sqrt(energy))
    window = jnp.concatenate([window, window * jnp.exp(-0.5 * decay)], axis=1)
    taps_high, taps_low = split_value(shaped * window)

    copies[7].wait()
    high, low = split_value(table_ref[...])
    fwd_ref[:, :block] = high
    fwd_ref[:, block:] = low
    table = jnp.concatenate([high, low, high], axis=1)
    rows = lax.broadcasted_iota(jnp.int32, (2 * block, LANES), 0)
    sign = (1 - 2 * lax.rem(rows, 2)).astype(F32)
    first_row = lax.broadcasted_iota(jnp.int32, (block, LANES), 0) == 0
    spectra = [None] * blocks
    for k in range(blocks // 2):
        part = slice(k * block, (k + 1) * block)
        stacked = jnp.concatenate([taps_high[part], taps_high[part], taps_low[part]], axis=0)
        now = jnp.dot(table, stacked, preferred_element_type=F32)
        spectra[k], spectra[k + blocks // 2] = now[:, :LANES], now[:, LANES:]
    for k in range(blocks):
        spec = spectra[k] if k == 0 else spectra[k] + sign * spectra[k - 1]
        real, imag = spec[:block], spec[block:]
        hre_ref[k] = real
        him_ref[k] = jnp.where(first_row, 0.0, imag)
        hfirst_ref[k] = jnp.where(first_row, imag, real)[:8]

    copies[8].wait()
    copies[9].wait()
    skip_ref[...] = all_skip_ref[:, lanes]
    high, low = split_value(back_ref[...])
    inv_ref[:, : 2 * block] = high
    inv_ref[:, 2 * block : 4 * block] = low
    inv_ref[:, 4 * block :] = high


def call_filter(weights, skip, blocks, outs, block):
    w1, b1, w2, b2, w3, decay = weights
    length = blocks * block
    emb, order = w1.shape
    pad = -(-emb // 8) * 8
    forward, inverse = dft_tables(block)
    feats = filter_feature_table(length, emb, pad)
    hbm = [
        w1, feats, b1[None], w2, b2[None], w3, decay[None], forward.astype(np.float32),
        inverse.astype(np.float32), skip[None],
    ]
    out_shape = [
        VMEM((blocks, block, LANES), F32),
        VMEM((blocks, block, LANES), F32),
        VMEM((blocks, 8, LANES), F32),
        VMEM((2 * block, 2 * block), BF16),
        VMEM((block, 6 * block), BF16),
        VMEM((1, LANES), F32),
    ]
    return pl.pallas_call(
        functools.partial(filter_kernel, blocks, block, outs, pad),
        in_specs=[pl.BlockSpec(memory_space=pltpu.HBM)] * len(hbm),
        out_specs=[pl.BlockSpec(memory_space=VMEM)] * len(out_shape),
        out_shape=out_shape,
        scratch_shapes=[
            VMEM(w1.shape, F32),
            VMEM((1, order), F32),
            VMEM(w2.shape, F32),
            VMEM((1, order), F32),
            VMEM(w3.shape, F32),
            VMEM((1, w3.shape[1]), F32),
            VMEM(feats.shape, F32),
            VMEM(forward.shape, F32),
            VMEM(inverse.shape, F32),
            VMEM((1, skip.shape[0]), F32),
            VMEM((6 * pad, 2 * order), F32),
            pltpu.SemaphoreType.DMA((len(hbm),)),
        ],
        compiler_params=pltpu.CompilerParams(vmem_limit_bytes=32 * 2**20),
        cost_estimate=pl.CostEstimate(
            flops=4 * 10**8, bytes_accessed=8 * 2**20, transcendentals=length * LANES
        ),
        name="filter_spectra",
    )(*(pltpu.with_memory_space_constraint(jnp.asarray(each), pltpu.HBM) for each in hbm))


def rounds(core):
    return 1 + core, 2 - core


def block_of(part, width):
    return pl.ds(pl.multiple_of(part * width, LANES), width)


def pack_kernel(blocks, outs, x_ref, gate_ref, weight_ref, pieces_ref, *refs):
    gate_refs, (over_ref, sems) = refs[:outs], refs[outs:]
    me = lax.axis_index("seq")
    group = me % outs
    width = weight_ref.shape[1] // FACE
    gathered, summed = rounds(me % 2)
    partner = lax.axis_index("chan") ^ gathered
    pairs = [
        (x_ref.at[:, (d % outs) * LANES : (d % outs + 1) * LANES], pieces_ref.at[d])
        for d in range(blocks)
    ]
    for k in range(outs):
        lanes = pl.ds(pl.multiple_of((group ^ k) * LANES, LANES), LANES)
        pairs.append((gate_ref.at[:, lanes], gate_refs[k]))
    for place, part in enumerate((partner, partner ^ summed)):
        pairs.append(
            (
                weight_ref.at[:, block_of(part, width)],
                over_ref.at[:, place * width : (place + 1) * width],
            )
        )
    copies = [pltpu.make_async_copy(*pair, sems.at[i]) for i, pair in enumerate(pairs)]
    for copy in copies:
        copy.start()
    for copy in copies:
        copy.wait()


def call_pack(x, gate, weight, blocks, outs):
    block = x.shape[0]
    out_shape = [VMEM((blocks, block, LANES), BF16)]
    out_shape += [VMEM((block, LANES), BF16)] * outs
    out_shape += [VMEM((weight.shape[0], weight.shape[1] // 2), BF16)]
    return pl.pallas_call(
        functools.partial(pack_kernel, blocks, outs),
        in_specs=[pl.BlockSpec(memory_space=pltpu.HBM)] * 3,
        out_specs=[pl.BlockSpec(memory_space=VMEM)] * len(out_shape),
        out_shape=out_shape,
        scratch_shapes=[pltpu.SemaphoreType.DMA((blocks + outs + 2,))],
        compiler_params=pltpu.CompilerParams(vmem_limit_bytes=16 * 2**20),
        cost_estimate=pl.CostEstimate(flops=0, bytes_accessed=2**21, transcendentals=0),
        name="pack_pieces",
    )(*(pltpu.with_memory_space_constraint(each, pltpu.HBM) for each in (x, gate, weight)))


def conv_kernel(blocks, outs, block, xs_ref, *refs):
    gate_refs, refs = refs[:outs], refs[outs:]
    hre_ref, him_ref, hfirst_ref, fwd_ref, inv_ref, skip_ref = refs[:6]
    refs = refs[6:]
    out_refs, (wre_ref, wim_ref, yre_ref, yim_ref) = refs[:outs], refs[outs:]
    me = lax.axis_index("seq")
    half, group = me // outs, me % outs
    earlier = blocks - outs
    for j in range(outs):
        values = jnp.concatenate([xs_ref[j], xs_ref[half * outs + j]], axis=1)
        spec = jnp.dot(
            fwd_ref[...], jnp.concatenate([values, values], axis=0), preferred_element_type=F32
        )
        before = jnp.where(half > 0, spec[:, :LANES], 0.0)
        wre_ref[j] = before[:block]
        wim_ref[j] = before[block:]
        wre_ref[earlier + j] = spec[:block, LANES:]
        wim_ref[earlier + j] = spec[block:, LANES:]

    def rows_at(start, first):
        rows = pl.ds(start, 8)
        wre = [wre_ref[j, rows, :] for j in range(blocks)]
        wim = [wim_ref[j, rows, :] for j in range(blocks)]
        for o in range(outs):
            total_re = total_im = None
            for j in range(earlier + o + 1):
                k = earlier + o - j
                hre = hre_ref[k, rows, :]
                him = him_ref[k, rows, :]
                hother = hfirst_ref[k] if first else hre
                add_re = wre[j] * hre - wim[j] * him
                add_im = wre[j] * him + wim[j] * hother
                total_re = add_re if total_re is None else total_re + add_re
                total_im = add_im if total_im is None else total_im + add_im
            yre_ref[o, rows, :] = total_re
            yim_ref[o, rows, :] = total_im

    rows_at(0, True)

    @pl.loop(1, block // 8)
    def _(tile):
        rows_at(pl.multiple_of(tile * 8, 8), False)

    def stacked(slot):
        re_high, re_low = split_value(yre_ref[slot])
        im_high, im_low = split_value(yim_ref[slot])
        return jnp.concatenate([re_high, im_high, re_high, im_high, re_low, im_low], axis=0)

    skip = skip_ref[...]
    for k in range(0, outs, 2):
        pair = jnp.concatenate([stacked(group ^ k), stacked(group ^ (k + 1))], axis=1)
        conv = jnp.dot(inv_ref[...], pair, preferred_element_type=F32)
        for i in range(2):
            values = xs_ref[half * outs + (group ^ (k + i))].astype(F32)
            gate = gate_refs[k + i][...].astype(F32)
            mixed = conv[:, i * LANES : (i + 1) * LANES] + skip * values
            out_refs[k + i][...] = (gate * mixed).astype(BF16)


def call_conv(xs, gates, filters):
    blocks, block, _ = xs.shape
    outs = len(gates)
    scratch = [VMEM((blocks, block, LANES), F32)] * 2 + [VMEM((outs, block, LANES), F32)] * 2
    return in_vmem(
        functools.partial(conv_kernel, blocks, outs, block),
        [xs, *gates, *filters],
        [jax.ShapeDtypeStruct((block, LANES), BF16)] * outs,
        "convolve",
        2 * 10**8,
        scratch,
    )


def join_kernel(outs, *refs):
    piece_refs, joined_ref = refs[:outs], refs[outs]
    group = lax.axis_index("seq") % outs
    for k in range(outs):
        lanes = pl.ds(pl.multiple_of((group ^ k) * LANES, LANES), LANES)
        joined_ref[:, lanes] = piece_refs[k][...]


def tiles(width):
    step = min(width, 2 * LANES)
    return [slice(start, start + step) for start in range(0, width, step)]


def own_kernel(width, gated_ref, weight_ref, send_ref, keep_ref, held_ref, sems):
    me = lax.axis_index("chan")
    _, summed = rounds(lax.axis_index("seq") % 2)
    half = width // 2
    copies = []
    for i in range(4):
        part = me ^ summed if i < 2 else me
        lanes = pl.ds(pl.multiple_of(part * width + (i % 2) * half, LANES), half)
        copies.append(
            pltpu.make_async_copy(weight_ref.at[:, lanes], held_ref.at[i], sems.at[i])
        )
    for copy in copies:
        copy.start()
    left = gated_ref[...]
    for i, copy in enumerate(copies):
        copy.wait()
        out_ref = send_ref if i < 2 else keep_ref
        for lanes in tiles(half):
            place = slice((i % 2) * half + lanes.start, (i % 2) * half + lanes.stop)
            out_ref[:, place] = jnp.dot(left, held_ref[i, :, lanes], preferred_element_type=F32)


def neighbour_kernel(first, theirs_ref, held_ref, sum_ref, out_ref):
    left = theirs_ref[...]
    for lanes in tiles(out_ref.shape[1]):
        place = slice(first + lanes.start, first + lanes.stop)
        total = jnp.dot(left, held_ref[:, place], preferred_element_type=F32)
        out_ref[:, lanes] = (sum_ref[:, lanes] + total).astype(out_ref.dtype)


def last_kernel(sum_ref, arrived_ref, out_ref):
    out_ref[...] = (sum_ref[...] + arrived_ref[...].astype(F32)).astype(BF16)


def in_vmem(kernel, operands, out_shape, name, flops, scratch=(), last=False):
    pin = lambda each: each if last else VMEM(each.shape, each.dtype)
    return pl.pallas_call(
        kernel,
        in_specs=[pl.BlockSpec(memory_space=VMEM)] * len(operands),
        out_specs=jax.tree.map(lambda _: pl.BlockSpec(memory_space=VMEM), out_shape),
        out_shape=jax.tree.map(pin, out_shape),
        scratch_shapes=scratch,
        compiler_params=pltpu.CompilerParams(vmem_limit_bytes=16 * 2**20),
        cost_estimate=pl.CostEstimate(flops=flops, bytes_accessed=2**20, transcendentals=0),
        name=name,
    )(*(pltpu.with_memory_space_constraint(each, VMEM) for each in operands))


def call_own(gated, weight):
    block, width = gated.shape
    columns = weight.shape[1] // FACE
    return pl.pallas_call(
        functools.partial(own_kernel, columns),
        in_specs=[pl.BlockSpec(memory_space=VMEM), pl.BlockSpec(memory_space=pltpu.HBM)],
        out_specs=[pl.BlockSpec(memory_space=VMEM)] * 2,
        out_shape=[VMEM((block, columns), F32)] * 2,
        scratch_shapes=[
            VMEM((4, width, columns // 2), BF16),
            pltpu.SemaphoreType.DMA((4,)),
        ],
        compiler_params=pltpu.CompilerParams(vmem_limit_bytes=16 * 2**20),
        cost_estimate=pl.CostEstimate(
            flops=4 * block * width * columns, bytes_accessed=6 * width * columns, transcendentals=0
        ),
        name="own_channels",
    )(
        pltpu.with_memory_space_constraint(gated, VMEM),
        pltpu.with_memory_space_constraint(weight, pltpu.HBM),
    )


def split_shards(
    mixer_input,
    gate_branch,
    skip_gain,
    decay_rate,
    first_weight,
    first_bias,
    second_weight,
    second_bias,
    last_weight,
    output_weight,
):
    block, width = mixer_input.shape
    blocks = lax.axis_size("seq")
    outs = width // LANES

    along_seq = lambda part, k: lax.ppermute(part, "seq", [(s, s ^ k) for s in range(blocks)])
    to_partners = lambda parts: [parts[0]] + [along_seq(parts[k], k) for k in range(1, outs)]

    def along_chan(part, turn):
        pairs = [
            (s * FACE + c, s * FACE + (c ^ rounds(s % 2)[turn]))
            for s in range(blocks)
            for c in range(FACE)
        ]
        return lax.ppermute(part, ("seq", "chan"), pairs)

    xs, *gates, over = call_pack(mixer_input, gate_branch, output_weight, blocks, outs)
    xs = lax.all_to_all(xs, "seq", 0, 0, tiled=True)
    held = along_chan(over, 0)
    filters = call_filter(
        (first_weight, first_bias, second_weight, second_bias, last_weight, decay_rate),
        skip_gain,
        blocks,
        outs,
        block,
    )
    pieces = to_partners(call_conv(xs, to_partners(gates), filters))
    shape = jax.ShapeDtypeStruct
    gated = in_vmem(
        functools.partial(join_kernel, outs), pieces, shape((block, width), BF16), "join_pieces", 10**6
    )
    theirs = along_chan(gated, 0)
    send, keep = call_own(gated, output_weight)
    columns = send.shape[1]
    flops = 2 * block * width * columns
    send = in_vmem(
        functools.partial(neighbour_kernel, columns),
        [theirs, held, send],
        shape((block, columns), BF16),
        "sums_to_send",
        flops,
    )
    arrived = along_chan(send, 1)
    keep = in_vmem(
        functools.partial(neighbour_kernel, 0),
        [theirs, held, keep],
        shape((block, columns), F32),
        "sums_to_keep",
        flops,
    )
    return in_vmem(
        last_kernel, [keep, arrived], shape((block, columns), BF16), "last_sum", 10**6, last=True
    )


def contract_first(left_matrix, right_matrix):
    return lax.dot_general(
        left_matrix,
        right_matrix,
        (((0,), (0,)), ((), ())),
        precision=HIGHEST,
        preferred_element_type=F32,
    )


def filter_taps(
    first_weight, first_bias, second_weight, second_bias, last_weight, decay_rate, length
):
    features = jnp.asarray(feature_table(length, first_weight.shape[0]).T)
    hidden_one = jnp.sin(contract_first(first_weight, features) + first_bias[:, None])
    hidden_two = jnp.sin(contract_first(second_weight, hidden_one) + second_bias[:, None])
    shaped = contract_first(hidden_two, last_weight)
    positions = jnp.arange(length, dtype=jnp.int32).astype(F32)
    envelope = jnp.exp(-decay_rate[None, :] * (positions[:, None] / length))
    energy = jnp.expm1(-2.0 * decay_rate) / jnp.expm1(-2.0 * decay_rate / length)
    return shaped * envelope / jnp.sqrt(energy)[None, :]


def transform_tables(block_len):
    padded_len = 2 * block_len
    freq_index = jnp.arange(block_len + 1, dtype=jnp.int32)[:, None]
    time_index = jnp.arange(padded_len, dtype=jnp.int32)[None, :]
    angle = (freq_index * time_index % padded_len).astype(F32) * (2.0 * math.pi / padded_len)
    forward = jnp.concatenate([jnp.cos(angle), -jnp.sin(angle)], axis=0)
    later_angle = angle[:, block_len:]
    weights = jnp.where((freq_index == 0) | (freq_index == block_len), 1.0, 2.0) / padded_len
    inverse = jnp.concatenate(
        [(weights * jnp.cos(later_angle)).T, (-weights * jnp.sin(later_angle)).T], axis=1
    )
    return (forward, inverse)


def spectral_product(left_spec, right_spec, half_rows):
    left_real, left_imag = (left_spec[:half_rows], left_spec[half_rows:])
    right_real, right_imag = (right_spec[:half_rows], right_spec[half_rows:])
    return jnp.concatenate(
        [
            left_real * right_real - left_imag * right_imag,
            left_real * right_imag + left_imag * right_real,
        ],
        axis=0,
    )


def gathered_shards(
    mixer_input,
    gate_branch,
    skip_gain,
    decay_rate,
    first_weight,
    first_bias,
    second_weight,
    second_bias,
    last_weight,
    output_weight,
):
    block_len, chan_width = mixer_input.shape
    seq_count = lax.axis_size("seq")
    device = lax.axis_index("seq")
    half_rows = block_len + 1
    kernel_taps = filter_taps(
        first_weight,
        first_bias,
        second_weight,
        second_bias,
        last_weight,
        decay_rate,
        block_len * seq_count,
    )
    padded_taps = jnp.concatenate([jnp.zeros((block_len, chan_width), F32), kernel_taps], axis=0)
    forward, inverse = transform_tables(block_len)
    forward_head = forward[:, :block_len]
    gathered = lax.all_gather(mixer_input, "seq", axis=0, tiled=True)

    def one_block(block_index, total):
        rows = lax.dynamic_slice_in_dim(gathered, block_index * block_len, block_len, 0)
        source_spec = jnp.dot(
            forward_head, rows.astype(F32), precision=HIGHEST, preferred_element_type=F32
        )
        segment = lax.dynamic_slice_in_dim(
            padded_taps, (device - block_index) * block_len, 2 * block_len, 0
        )
        lag_spec = jnp.dot(forward, segment, precision=HIGHEST, preferred_element_type=F32)
        return total + spectral_product(lag_spec, source_spec, half_rows)

    total = lax.fori_loop(0, device + 1, one_block, jnp.zeros((2 * half_rows, chan_width), F32))
    convolved = jnp.dot(inverse, total, precision=HIGHEST, preferred_element_type=F32)
    values = mixer_input.astype(F32)
    gated_mix = (
        gate_branch.astype(F32) * (convolved + skip_gain[None, :] * values)
    ).astype(BF16)
    partial_out = jnp.dot(gated_mix, output_weight, preferred_element_type=F32)
    return lax.psum_scatter(partial_out, "chan", scatter_dimension=1, tiled=True).astype(BF16)


def solution(mesh):
    seq_count, chan_count = mesh.shape["seq"], mesh.shape["chan"]

    def shards(mixer_input, *rest):
        block, width = mixer_input.shape
        outs = width // LANES
        splits = (
            width % LANES == 0
            and block % LANES == 0
            and seq_count == 2 * outs
            and outs == 4
            and chan_count == FACE
        )
        plan = split_shards if splits else gathered_shards
        return plan(mixer_input, *rest)

    in_specs = (
        P("seq", "chan"),
        P("seq", "chan"),
        P("chan"),
        P("chan"),
        P(),
        P(),
        P(),
        P(),
        P(None, "chan"),
        P("chan", None),
    )
    out_specs = P("seq", "chan")
    return jax.shard_map(shards, mesh=mesh, in_specs=in_specs, out_specs=out_specs, check_vma=False)
```

```python
import functools
import math

import jax
import jax.numpy as jnp
import numpy as np
from jax import lax
from jax.experimental import pallas as pl
from jax.experimental.pallas import tpu as pltpu
from jax.sharding import PartitionSpec as P

HIGHEST = lax.Precision.HIGHEST
F32 = jnp.float32
BF16 = jnp.bfloat16
LANES = 128
WIDE = 2 * LANES
CORES = 2
CHIPS = 4
FACE = 4
VMEM = pltpu.VMEM


def feature_table(length, emb_width):
    band_count = (emb_width - 1) // 2
    positions = np.arange(length, dtype=np.int64)
    columns = [positions / length]
    for band in range(1, band_count + 1):
        frequency = min(
            length // 2, max(band, int((length / 2) ** ((band - 1) / (band_count - 1))))
        )
        angle = (positions * frequency % length) * (2.0 * math.pi / length)
        columns.append(np.cos(angle))
        columns.append(np.sin(angle))
    return np.stack(columns, axis=1).astype(np.float32)


def split_bf16(table):
    high = table.astype(np.float32).astype(jnp.bfloat16)
    low = (table - high.astype(np.float64)).astype(np.float32).astype(jnp.bfloat16)
    return high, low


def dft_tables(block):
    size = 2 * block
    bins = np.arange(block)[:, None]
    times = np.arange(block)[None, :]
    angle = (bins * times % size) * (2.0 * math.pi / size)
    imag = -np.sin(angle)
    imag[0] = 1.0 - 2.0 * (np.arange(block) % 2)
    forward = np.concatenate([np.cos(angle), imag], axis=0)
    weight = np.where(bins == 0, 1.0, 2.0) / size
    back_imag = -weight * np.sin(angle)
    back_imag[0] = (1.0 - 2.0 * (np.arange(block) % 2)) / size
    inverse = np.concatenate([weight * np.cos(angle), back_imag], axis=0).T
    return forward, inverse


def fast_sin(x):
    turns = jnp.floor(x * (1.0 / math.pi) + 0.5)
    rest = x - turns * 3.140625
    rest = rest - turns * 9.67502593994140625e-4
    rest = rest - turns * 1.509957990978376432e-7
    parity = turns - 2.0 * jnp.floor(turns * 0.5)
    rest = rest * (1.0 - 2.0 * parity)
    square = rest * rest
    poly = -2.5052108e-8
    for coeff in (2.7557319e-6, -1.9841270e-4, 8.3333333e-3, -1.6666667e-1):
        poly = poly * square + coeff
    return rest + rest * square * poly


def expm1_of_negative(x):
    near = jnp.maximum(x, -0.5)
    series = jnp.full_like(x, 1.0 / 3628800.0)
    for denom in (362880.0, 40320.0, 5040.0, 720.0, 120.0, 24.0, 6.0, 2.0, 1.0):
        series = series * near + 1.0 / denom
    return jnp.where(x > -0.5, near * series, jnp.exp(x) - 1.0)


def split_value(value):
    high = value.astype(BF16)
    return high, (value - high.astype(F32)).astype(BF16)


def filter_feature_table(length, emb_width, pad):
    table = feature_table(length, emb_width)
    columns = []
    for half in (table[: length // 2], table[length // 2 :]):
        high, low = (part.astype(np.float32) for part in split_bf16(half))
        for part in (high, high, low):
            columns.append(np.pad(part, ((0, 0), (0, pad - emb_width))))
    return np.concatenate(columns, axis=1)


def twice_diagonal(value):
    zero = jnp.zeros_like(value)
    return jnp.concatenate(
        [jnp.concatenate([value, zero], axis=1), jnp.concatenate([zero, value], axis=1)], axis=0
    )


def stacked_diagonal(value):
    high, low = split_value(value)
    high = twice_diagonal(high.astype(F32))
    low = twice_diagonal(low.astype(F32))
    return jnp.concatenate([high, low, high], axis=0).astype(BF16)


def layer(value, weight):
    high, low = split_value(value)
    return jnp.dot(
        jnp.concatenate([high, high, low], axis=1), weight, preferred_element_type=F32
    )


def filter_kernel(blocks, block, pad, *refs):
    hbm, refs = refs[:10], refs[11:]
    hre_ref, him_ref, hfirst_ref, fwd_ref, inv_ref, skip_ref = refs[:6]
    refs = refs[6:]
    w1_ref, b1_ref, w2_ref, b2_ref, w3_ref, decay_ref, feat_ref, table_ref, back_ref = refs[:9]
    all_skip_ref, first_ref, sems = refs[9:]
    targets = [
        w1_ref, feat_ref, b1_ref, w2_ref, b2_ref, w3_ref, decay_ref, table_ref, back_ref,
        all_skip_ref,
    ]
    copies = [
        pltpu.make_async_copy(hbm[i], targets[i], sems.at[i]) for i in range(len(targets))
    ]
    for copy in copies:
        copy.start()
    core = lax.axis_index("seq") % CORES
    length = blocks * block
    emb, order = w1_ref.shape
    first_ref[...] = jnp.zeros_like(first_ref)
    for copy in copies[:7]:
        copy.wait()

    high, low = split_value(w1_ref[...])
    high, low = high.astype(F32), low.astype(F32)
    zero = jnp.zeros_like(high)
    for i, part in enumerate((high, low, high)):
        first_ref[i * pad : i * pad + emb] = jnp.concatenate([part, zero], axis=1)
        first_ref[(3 + i) * pad : (3 + i) * pad + emb] = jnp.concatenate([zero, part], axis=1)
    b1 = jnp.concatenate([b1_ref[...]] * 2, axis=1)
    b2 = jnp.concatenate([b2_ref[...]] * 2, axis=1)
    hidden = fast_sin(
        jnp.dot(
            feat_ref[...].astype(BF16), first_ref[...].astype(BF16), preferred_element_type=F32
        )
        + b1
    )
    hidden = fast_sin(layer(hidden, stacked_diagonal(w2_ref[...])) + b2)
    lanes = pl.ds(pl.multiple_of(core * WIDE, LANES), WIDE)
    shaped = layer(hidden, stacked_diagonal(w3_ref[:, lanes]))

    decay = decay_ref[:, lanes]
    energy = expm1_of_negative(-2.0 * decay) / expm1_of_negative(decay * (-2.0 / length))
    times = lax.broadcasted_iota(jnp.int32, (length // 2, WIDE), 0).astype(F32) * (1.0 / length)
    window = jnp.exp(-(decay * times)) * (1.0 / jnp.sqrt(energy))
    window = jnp.concatenate([window, window * jnp.exp(-0.5 * decay)], axis=1)
    taps_high, taps_low = split_value(shaped * window)

    copies[7].wait()
    high, low = split_value(table_ref[...])
    fwd_ref[:, :block] = high
    fwd_ref[:, block:] = low
    table = jnp.concatenate([high, low, high], axis=1)
    rows = lax.broadcasted_iota(jnp.int32, (2 * block, WIDE), 0)
    sign = (1 - 2 * lax.rem(rows, 2)).astype(F32)
    first_row = lax.broadcasted_iota(jnp.int32, (block, WIDE), 0) == 0
    spectra = [None] * blocks
    for k in range(blocks // 2):
        part = slice(k * block, (k + 1) * block)
        stacked = jnp.concatenate([taps_high[part], taps_high[part], taps_low[part]], axis=0)
        now = jnp.dot(table, stacked, preferred_element_type=F32)
        spectra[k], spectra[k + blocks // 2] = now[:, :WIDE], now[:, WIDE:]
    for k in range(blocks):
        spec = spectra[k] if k == 0 else spectra[k] + sign * spectra[k - 1]
        real, imag = spec[:block], spec[block:]
        hre_ref[k] = real
        him_ref[k] = jnp.where(first_row, 0.0, imag)
        hfirst_ref[k] = jnp.where(first_row, imag, real)[:8]

    copies[8].wait()
    copies[9].wait()
    skip_ref[...] = all_skip_ref[:, lanes]
    high, low = split_value(back_ref[...])
    inv_ref[:, : 2 * block] = high
    inv_ref[:, 2 * block : 4 * block] = low
    inv_ref[:, 4 * block :] = high


def call_filter(weights, skip, after, blocks, block):
    w1, b1, w2, b2, w3, decay = weights
    length = blocks * block
    emb, order = w1.shape
    pad = -(-emb // 8) * 8
    forward, inverse = dft_tables(block)
    feats = filter_feature_table(length, emb, pad)
    hbm = [
        w1, feats, b1[None], w2, b2[None], w3, decay[None], forward.astype(np.float32),
        inverse.astype(np.float32), skip[None],
    ]
    out_shape = [
        VMEM((blocks, block, WIDE), F32),
        VMEM((blocks, block, WIDE), F32),
        VMEM((blocks, 8, WIDE), F32),
        VMEM((2 * block, 2 * block), BF16),
        VMEM((block, 6 * block), BF16),
        VMEM((1, WIDE), F32),
    ]
    return pl.pallas_call(
        functools.partial(filter_kernel, blocks, block, pad),
        in_specs=[pl.BlockSpec(memory_space=pltpu.HBM)] * len(hbm)
        + [pl.BlockSpec(memory_space=pl.ANY)],
        out_specs=[pl.BlockSpec(memory_space=VMEM)] * len(out_shape),
        out_shape=out_shape,
        scratch_shapes=[
            VMEM(w1.shape, F32),
            VMEM((1, order), F32),
            VMEM(w2.shape, F32),
            VMEM((1, order), F32),
            VMEM(w3.shape, F32),
            VMEM((1, w3.shape[1]), F32),
            VMEM(feats.shape, F32),
            VMEM(forward.shape, F32),
            VMEM(inverse.shape, F32),
            VMEM((1, skip.shape[0]), F32),
            VMEM((6 * pad, 2 * order), F32),
            pltpu.SemaphoreType.DMA((len(hbm),)),
        ],
        compiler_params=pltpu.CompilerParams(vmem_limit_bytes=32 * 2**20),
        cost_estimate=pl.CostEstimate(
            flops=4 * 10**8, bytes_accessed=8 * 2**20, transcendentals=length * LANES
        ),
        name="filter_spectra",
    )(*(pltpu.with_memory_space_constraint(jnp.asarray(each), pltpu.HBM) for each in hbm), after)


def lanes_of(core):
    return pl.ds(pl.multiple_of(core * WIDE, LANES), WIDE)


def columns_of(part, half, width):
    return pl.ds(pl.multiple_of(part * width + half * (width // 2), LANES), width // 2)


def weight_copies(weight_ref, over_x_ref, over_y_ref, sems, first_sem):
    rows = weight_ref.shape[0] // 2
    width = weight_ref.shape[1] // FACE
    me = lax.axis_index("chan")
    half_rows = pl.ds(pl.multiple_of((lax.axis_index("seq") % 2) * rows, LANES), rows)
    copies = []
    for out_ref, half, parts in ((over_x_ref, 0, (1, 3)), (over_y_ref, 1, (2, 3))):
        for place, k in enumerate(parts):
            copies.append(
                pltpu.make_async_copy(
                    weight_ref.at[half_rows, columns_of(me ^ k, half, width)],
                    out_ref.at[:, place * (width // 2) : (place + 1) * (width // 2)],
                    sems.at[first_sem + len(copies)],
                )
            )
    return copies


def pack_kernel(x_ref, gate_ref, weight_ref, mine_ref, other_ref, over_x_ref, over_y_ref, sems):
    block = x_ref.shape[0]
    core = lax.axis_index("seq") % CORES
    copies = []
    for place, out_ref in ((1 - core, other_ref), (core, mine_ref)):
        for source, rows in ((x_ref, slice(0, block)), (gate_ref, slice(block, 2 * block))):
            copies.append(
                pltpu.make_async_copy(
                    source.at[:, lanes_of(place)], out_ref.at[rows], sems.at[len(copies)]
                )
            )
    copies += weight_copies(weight_ref, over_x_ref, over_y_ref, sems, len(copies))
    for copy in copies:
        copy.start()
    for copy in copies:
        copy.wait()


def call_pack(x, gate, weight):
    both = VMEM((2 * x.shape[0], WIDE), BF16)
    send = VMEM((weight.shape[0] // 2, weight.shape[1] // FACE), BF16)
    return pl.pallas_call(
        pack_kernel,
        in_specs=[pl.BlockSpec(memory_space=pltpu.HBM)] * 3,
        out_specs=[pl.BlockSpec(memory_space=VMEM)] * 4,
        out_shape=[both, both, send, send],
        scratch_shapes=[pltpu.SemaphoreType.DMA((8,))],
        cost_estimate=pl.CostEstimate(flops=0, bytes_accessed=2**21, transcendentals=0),
        name="pack_pieces",
    )(*(pltpu.with_memory_space_constraint(each, pltpu.HBM) for each in (x, gate, weight)))


def order_kernel(mine_ref, theirs_ref, x_ref, gate_ref):
    block = mine_ref.shape[0] // 2
    core = lax.axis_index("seq") % CORES
    for place, source in ((core, mine_ref), (1 - core, theirs_ref)):
        rows = pl.ds(pl.multiple_of(place * block, LANES), block)
        x_ref[rows] = source[:block]
        gate_ref[rows] = source[block:]


def conv_kernel(blocks, block, *refs):
    x_ref, tokens_ref, gate_ref, refs = refs[0], refs[1], refs[2], refs[3:]
    hre_ref, him_ref, hfirst_ref, fwd_ref, inv_ref, skip_ref = refs[:6]
    keep_ref, send_ref = refs[8:10]
    wre_ref, wim_ref, yre_ref, yim_ref = refs[12:]
    me = lax.axis_index("seq")
    core, chip = me % CORES, me // CORES
    behind = [jnp.zeros((), jnp.int32)]
    for k in range(CHIPS):
        distance = chip - (chip ^ k)
        if k:
            behind.append(jnp.maximum(distance, 1) * CORES)
        for b in range(CORES):
            rows = slice(b * block, (b + 1) * block)
            values = tokens_ref[chip ^ k, rows] if k else x_ref[rows]
            spec = jnp.dot(
                fwd_ref[...], jnp.concatenate([values, values], axis=0), preferred_element_type=F32
            )
            if k:
                spec = jnp.where(distance > 0, spec, 0.0)
            wre_ref[k * CORES + b] = spec[:block]
            wim_ref[k * CORES + b] = spec[block:]

    def rows_at(start, first):
        rows = pl.ds(start, 8)
        for lanes in (slice(0, LANES), slice(LANES, WIDE)):
            totals = [None] * (2 * CORES)
            for k in range(CHIPS):
                for b in range(CORES):
                    wre = wre_ref[k * CORES + b, rows, lanes]
                    wim = wim_ref[k * CORES + b, rows, lanes]
                    for o in range(CORES):
                        if k == 0 and o < b:
                            continue
                        lag = behind[k] + (o - b)
                        hre = hre_ref[lag, rows, lanes]
                        him = him_ref[lag, rows, lanes]
                        hother = hfirst_ref[lag, :, lanes] if first else hre
                        adds = (wre * hre - wim * him, wre * him + wim * hother)
                        for i, add in enumerate(adds):
                            old = totals[2 * o + i]
                            totals[2 * o + i] = add if old is None else old + add
            for o in range(CORES):
                yre_ref[o, rows, lanes] = totals[2 * o]
                yim_ref[o, rows, lanes] = totals[2 * o + 1]

    rows_at(0, True)

    @pl.loop(1, block // 8)
    def _(tile):
        rows_at(pl.multiple_of(tile * 8, 8), False)

    for place, out_ref in ((1 - core, send_ref), (core, keep_ref)):
        re_high, re_low = split_value(yre_ref[place])
        im_high, im_low = split_value(yim_ref[place])
        stacked = jnp.concatenate([re_high, im_high, re_high, im_high, re_low, im_low], axis=0)
        conv = jnp.dot(inv_ref[...], stacked, preferred_element_type=F32)
        rows = pl.ds(pl.multiple_of(place * block, LANES), block)
        values = x_ref[rows].astype(F32)
        gate = gate_ref[rows].astype(F32)
        out_ref[...] = (gate * (conv + skip_ref[...] * values)).astype(BF16)


def call_conv(x, tokens, gate, filters, passing, blocks, block):
    pinned = [pltpu.with_memory_space_constraint(each, VMEM) for each in filters]
    operands = [x, tokens, gate, *pinned]
    shape = jax.ShapeDtypeStruct
    return pl.pallas_call(
        functools.partial(conv_kernel, blocks, block),
        in_specs=[pl.BlockSpec(memory_space=VMEM)] * len(operands)
        + [pl.BlockSpec(memory_space=pl.ANY)] * 2,
        out_specs=[pl.BlockSpec(memory_space=VMEM)] * 2
        + [pl.BlockSpec(memory_space=pl.ANY)] * 2,
        out_shape=[shape((block, WIDE), BF16)] * 2 + [shape(p.shape, p.dtype) for p in passing],
        input_output_aliases={len(operands) + i: 2 + i for i in range(2)},
        scratch_shapes=[
            VMEM((blocks, block, WIDE), F32),
            VMEM((blocks, block, WIDE), F32),
            VMEM((CORES, block, WIDE), F32),
            VMEM((CORES, block, WIDE), F32),
        ],
        compiler_params=pltpu.CompilerParams(vmem_limit_bytes=16 * 2**20),
        cost_estimate=pl.CostEstimate(
            flops=3 * 10**8, bytes_accessed=3 * 2**20, transcendentals=0
        ),
        name="convolve",
    )(*operands, *passing)


def join_kernel(mine_ref, theirs_ref, joined_ref):
    core = lax.axis_index("seq") % CORES
    joined_ref[:, lanes_of(core)] = mine_ref[...]
    joined_ref[:, lanes_of(1 - core)] = theirs_ref[...]


def tiles(width):
    step = min(width, 2 * LANES)
    return [slice(start, start + step) for start in range(0, width, step)]


def own_kernel(width, gated_ref, weight_ref, *refs):
    out_refs, (held_ref, sems) = refs[:4], refs[4:]
    me = lax.axis_index("chan")
    copies = [
        pltpu.make_async_copy(
            weight_ref.at[:, columns_of(me ^ k, half, width)], held_ref.at[i], sems.at[i]
        )
        for i, (k, half) in enumerate(((2, 0), (1, 1), (0, 0), (0, 1)))
    ]
    for copy in copies:
        copy.start()
    left = gated_ref[...]
    for i, copy in enumerate(copies):
        copy.wait()
        for lanes in tiles(width // 2):
            out_refs[i][:, lanes] = jnp.dot(
                left, held_ref[i, :, lanes], preferred_element_type=F32
            )


def neighbour_kernel(first, x_ref, y_ref, *refs):
    from_x, from_y, sums, outs = refs[:2], refs[2:4], refs[4:6], refs[6:]
    rows = from_x[0].shape[0]
    core = lax.axis_index("seq") % 2
    for left_ref, held, sum_ref, out_ref in (
        (x_ref, from_x, sums[0], outs[0]),
        (y_ref, from_y, sums[1], outs[1]),
    ):
        near = left_ref[:, pl.ds(pl.multiple_of(core * rows, LANES), rows)]
        far = left_ref[:, pl.ds(pl.multiple_of((1 - core) * rows, LANES), rows)]
        width = out_ref.shape[1]
        for lanes in tiles(width):
            place = slice(first * width + lanes.start, first * width + lanes.stop)
            total = jnp.dot(near, held[0][:, place], preferred_element_type=F32)
            total += jnp.dot(far, held[1][:, place], preferred_element_type=F32)
            out_ref[:, lanes] = (sum_ref[:, lanes] + total).astype(out_ref.dtype)


def last_kernel(*refs):
    sums, arrived, out_ref = refs[:2], refs[2:4], refs[4]
    width = sums[0].shape[1]
    for half in range(2):
        out_ref[:, half * width : (half + 1) * width] = (
            sums[half][...] + arrived[half][...].astype(F32)
        ).astype(BF16)


def in_vmem(kernel, operands, out_shape, name, flops, scratch=()):
    return pl.pallas_call(
        kernel,
        in_specs=[pl.BlockSpec(memory_space=VMEM)] * len(operands),
        out_specs=jax.tree.map(lambda _: pl.BlockSpec(memory_space=VMEM), out_shape),
        out_shape=out_shape,
        scratch_shapes=scratch,
        compiler_params=pltpu.CompilerParams(vmem_limit_bytes=16 * 2**20),
        cost_estimate=pl.CostEstimate(flops=flops, bytes_accessed=2**20, transcendentals=0),
        name=name,
    )(*operands)


def call_own(gated, weight):
    block, width = gated.shape
    columns = weight.shape[1] // FACE
    return pl.pallas_call(
        functools.partial(own_kernel, columns),
        in_specs=[pl.BlockSpec(memory_space=VMEM), pl.BlockSpec(memory_space=pltpu.HBM)],
        out_specs=[pl.BlockSpec(memory_space=VMEM)] * 4,
        out_shape=[jax.ShapeDtypeStruct((block, columns // 2), F32)] * 4,
        scratch_shapes=[
            VMEM((4, width, columns // 2), BF16),
            pltpu.SemaphoreType.DMA((4,)),
        ],
        compiler_params=pltpu.CompilerParams(vmem_limit_bytes=16 * 2**20),
        cost_estimate=pl.CostEstimate(
            flops=4 * block * width * columns, bytes_accessed=6 * width * columns, transcendentals=0
        ),
        name="own_channels",
    )(gated, pltpu.with_memory_space_constraint(weight, pltpu.HBM))


def split_shards(
    mixer_input,
    gate_branch,
    skip_gain,
    decay_rate,
    first_weight,
    first_bias,
    second_weight,
    second_bias,
    last_weight,
    output_weight,
):
    block, width = mixer_input.shape
    blocks = lax.axis_size("seq")
    shape = jax.ShapeDtypeStruct
    along_chan = lambda part, k: lax.ppermute(part, "chan", [(c, c ^ k) for c in range(FACE)])

    def along_seq(part, k, senders=range(blocks)):
        return lax.ppermute(part, "seq", [(s, s ^ k) for s in senders])

    mine, other, over_x, over_y = call_pack(mixer_input, gate_branch, output_weight)
    from_x, from_y = along_chan(over_x, 1), along_chan(over_y, 2)
    x, gate = in_vmem(
        order_kernel,
        [mine, along_seq(other, 1)],
        [shape((2 * block, WIDE), BF16)] * 2,
        "order_tokens",
        10**6,
    )
    same_core = [list(range(core, blocks, CORES)) for core in range(CORES)]
    tokens = lax.all_gather(x, "seq", axis_index_groups=same_core)
    filters = call_filter(
        (first_weight, first_bias, second_weight, second_bias, last_weight, decay_rate),
        skip_gain,
        x,
        blocks,
        block,
    )
    keep, send, from_x, from_y = call_conv(
        x, tokens, gate, filters, (from_x, from_y), blocks, block
    )
    from_x, from_y = (from_x, along_seq(from_x, 1)), (from_y, along_seq(from_y, 1))
    gated = in_vmem(
        join_kernel, [keep, along_seq(send, 1)], shape((block, width), BF16), "join_channels", 10**6
    )
    x_gated, y_gated = along_chan(gated, 1), along_chan(gated, 2)
    send_a, send_b, keep_a, keep_b = call_own(gated, output_weight)
    columns = send_a.shape[1]
    flops = 4 * block * width * columns
    send_a, send_b = in_vmem(
        functools.partial(neighbour_kernel, 1),
        [x_gated, y_gated, *from_x, *from_y, send_a, send_b],
        [shape((block, columns), BF16)] * 2,
        "sums_to_send",
        flops,
    )
    got_a, got_b = along_chan(send_a, 2), along_chan(send_b, 1)
    keep_a, keep_b = in_vmem(
        functools.partial(neighbour_kernel, 0),
        [x_gated, y_gated, *from_x, *from_y, keep_a, keep_b],
        [shape((block, columns), F32)] * 2,
        "sums_to_keep",
        flops,
    )
    return in_vmem(
        last_kernel,
        [keep_a, keep_b, got_a, got_b],
        shape((block, 2 * columns), BF16),
        "last_sum",
        10**6,
    )


def contract_first(left_matrix, right_matrix):
    return lax.dot_general(
        left_matrix,
        right_matrix,
        (((0,), (0,)), ((), ())),
        precision=HIGHEST,
        preferred_element_type=F32,
    )


def filter_taps(
    first_weight, first_bias, second_weight, second_bias, last_weight, decay_rate, length
):
    features = jnp.asarray(feature_table(length, first_weight.shape[0]).T)
    hidden_one = jnp.sin(contract_first(first_weight, features) + first_bias[:, None])
    hidden_two = jnp.sin(contract_first(second_weight, hidden_one) + second_bias[:, None])
    shaped = contract_first(hidden_two, last_weight)
    positions = jnp.arange(length, dtype=jnp.int32).astype(F32)
    envelope = jnp.exp(-decay_rate[None, :] * (positions[:, None] / length))
    energy = jnp.expm1(-2.0 * decay_rate) / jnp.expm1(-2.0 * decay_rate / length)
    return shaped * envelope / jnp.sqrt(energy)[None, :]


def transform_tables(block_len):
    padded_len = 2 * block_len
    freq_index = jnp.arange(block_len + 1, dtype=jnp.int32)[:, None]
    time_index = jnp.arange(padded_len, dtype=jnp.int32)[None, :]
    angle = (freq_index * time_index % padded_len).astype(F32) * (2.0 * math.pi / padded_len)
    forward = jnp.concatenate([jnp.cos(angle), -jnp.sin(angle)], axis=0)
    later_angle = angle[:, block_len:]
    weights = jnp.where((freq_index == 0) | (freq_index == block_len), 1.0, 2.0) / padded_len
    inverse = jnp.concatenate(
        [(weights * jnp.cos(later_angle)).T, (-weights * jnp.sin(later_angle)).T], axis=1
    )
    return (forward, inverse)


def spectral_product(left_spec, right_spec, half_rows):
    left_real, left_imag = (left_spec[:half_rows], left_spec[half_rows:])
    right_real, right_imag = (right_spec[:half_rows], right_spec[half_rows:])
    return jnp.concatenate(
        [
            left_real * right_real - left_imag * right_imag,
            left_real * right_imag + left_imag * right_real,
        ],
        axis=0,
    )


def gathered_shards(
    mixer_input,
    gate_branch,
    skip_gain,
    decay_rate,
    first_weight,
    first_bias,
    second_weight,
    second_bias,
    last_weight,
    output_weight,
):
    block_len, chan_width = mixer_input.shape
    seq_count = lax.axis_size("seq")
    device = lax.axis_index("seq")
    half_rows = block_len + 1
    kernel_taps = filter_taps(
        first_weight,
        first_bias,
        second_weight,
        second_bias,
        last_weight,
        decay_rate,
        block_len * seq_count,
    )
    padded_taps = jnp.concatenate([jnp.zeros((block_len, chan_width), F32), kernel_taps], axis=0)
    forward, inverse = transform_tables(block_len)
    forward_head = forward[:, :block_len]
    gathered = lax.all_gather(mixer_input, "seq", axis=0, tiled=True)

    def one_block(block_index, total):
        rows = lax.dynamic_slice_in_dim(gathered, block_index * block_len, block_len, 0)
        source_spec = jnp.dot(
            forward_head, rows.astype(F32), precision=HIGHEST, preferred_element_type=F32
        )
        segment = lax.dynamic_slice_in_dim(
            padded_taps, (device - block_index) * block_len, 2 * block_len, 0
        )
        lag_spec = jnp.dot(forward, segment, precision=HIGHEST, preferred_element_type=F32)
        return total + spectral_product(lag_spec, source_spec, half_rows)

    total = lax.fori_loop(0, device + 1, one_block, jnp.zeros((2 * half_rows, chan_width), F32))
    convolved = jnp.dot(inverse, total, precision=HIGHEST, preferred_element_type=F32)
    values = mixer_input.astype(F32)
    gated_mix = (
        gate_branch.astype(F32) * (convolved + skip_gain[None, :] * values)
    ).astype(BF16)
    partial_out = jnp.dot(gated_mix, output_weight, preferred_element_type=F32)
    return lax.psum_scatter(partial_out, "chan", scatter_dimension=1, tiled=True).astype(BF16)


def solution(mesh):
    seq_count, chan_count = mesh.shape["seq"], mesh.shape["chan"]

    def shards(mixer_input, *rest):
        block, width = mixer_input.shape
        splits = (
            width == CORES * WIDE
            and block % LANES == 0
            and seq_count == CORES * CHIPS
            and chan_count == FACE
        )
        plan = split_shards if splits else gathered_shards
        return plan(mixer_input, *rest)

    in_specs = (
        P("seq", "chan"),
        P("seq", "chan"),
        P("chan"),
        P("chan"),
        P(),
        P(),
        P(),
        P(),
        P(None, "chan"),
        P("chan", None),
    )
    out_specs = P("seq", "chan")
    return jax.shard_map(shards, mesh=mesh, in_specs=in_specs, out_specs=out_specs, check_vma=False)
```

```python
import functools
import math

import jax
import jax.numpy as jnp
import numpy as np
from jax import lax
from jax.experimental import pallas as pl
from jax.experimental.pallas import tpu as pltpu
from jax.sharding import PartitionSpec as P

HIGHEST = lax.Precision.HIGHEST
F32 = jnp.float32
BF16 = jnp.bfloat16
LANES = 128
FACE = 4
VMEM = pltpu.VMEM


def feature_table(length, emb_width):
    band_count = (emb_width - 1) // 2
    positions = np.arange(length, dtype=np.int64)
    columns = [positions / length]
    for band in range(1, band_count + 1):
        frequency = min(
            length // 2, max(band, int((length / 2) ** ((band - 1) / (band_count - 1))))
        )
        angle = (positions * frequency % length) * (2.0 * math.pi / length)
        columns.append(np.cos(angle))
        columns.append(np.sin(angle))
    return np.stack(columns, axis=1).astype(np.float32)


def split_bf16(table):
    high = table.astype(np.float32).astype(jnp.bfloat16)
    low = (table - high.astype(np.float64)).astype(np.float32).astype(jnp.bfloat16)
    return high, low


def dft_tables(block):
    size = 2 * block
    bins = np.arange(block)[:, None]
    times = np.arange(block)[None, :]
    angle = (bins * times % size) * (2.0 * math.pi / size)
    imag = -np.sin(angle)
    imag[0] = 1.0 - 2.0 * (np.arange(block) % 2)
    forward = np.concatenate([np.cos(angle), imag], axis=0)
    weight = np.where(bins == 0, 1.0, 2.0) / size
    back_imag = -weight * np.sin(angle)
    back_imag[0] = (1.0 - 2.0 * (np.arange(block) % 2)) / size
    inverse = np.concatenate([weight * np.cos(angle), back_imag], axis=0).T
    return forward, inverse


def fast_sin(x):
    turns = jnp.floor(x * (1.0 / math.pi) + 0.5)
    rest = x - turns * 3.140625
    rest = rest - turns * 9.67502593994140625e-4
    rest = rest - turns * 1.509957990978376432e-7
    parity = turns - 2.0 * jnp.floor(turns * 0.5)
    rest = rest * (1.0 - 2.0 * parity)
    square = rest * rest
    poly = -2.5052108e-8
    for coeff in (2.7557319e-6, -1.9841270e-4, 8.3333333e-3, -1.6666667e-1):
        poly = poly * square + coeff
    return rest + rest * square * poly


def expm1_of_negative(x):
    near = jnp.maximum(x, -0.5)
    series = jnp.full_like(x, 1.0 / 3628800.0)
    for denom in (362880.0, 40320.0, 5040.0, 720.0, 120.0, 24.0, 6.0, 2.0, 1.0):
        series = series * near + 1.0 / denom
    return jnp.where(x > -0.5, near * series, jnp.exp(x) - 1.0)


def split_value(value):
    high = value.astype(BF16)
    return high, (value - high.astype(F32)).astype(BF16)


def filter_feature_table(length, emb_width, pad):
    table = feature_table(length, emb_width)
    columns = []
    for half in (table[: length // 2], table[length // 2 :]):
        high, low = (part.astype(np.float32) for part in split_bf16(half))
        for part in (high, high, low):
            columns.append(np.pad(part, ((0, 0), (0, pad - emb_width))))
    return np.concatenate(columns, axis=1)


def twice_diagonal(value):
    zero = jnp.zeros_like(value)
    return jnp.concatenate(
        [jnp.concatenate([value, zero], axis=1), jnp.concatenate([zero, value], axis=1)], axis=0
    )


def stacked_diagonal(value):
    high, low = split_value(value)
    high = twice_diagonal(high.astype(F32))
    low = twice_diagonal(low.astype(F32))
    return jnp.concatenate([high, low, high], axis=0).astype(BF16)


def layer(value, weight):
    high, low = split_value(value)
    return jnp.dot(
        jnp.concatenate([high, high, low], axis=1), weight, preferred_element_type=F32
    )


def filter_kernel(blocks, block, outs, pad, *refs):
    hbm, refs = refs[:11], refs[11:]
    hre_ref, him_ref, hfirst_ref, fwd_ref, inv_ref, skip_ref, gate_ref = refs[:7]
    refs = refs[7:]
    w1_ref, b1_ref, w2_ref, b2_ref, w3_ref, decay_ref, feat_ref, table_ref, back_ref = refs[:9]
    all_skip_ref, first_ref, sems = refs[9:]
    targets = [
        w1_ref, feat_ref, b1_ref, w2_ref, b2_ref, w3_ref, decay_ref, table_ref, back_ref,
        all_skip_ref,
    ]
    copies = [
        pltpu.make_async_copy(hbm[i], targets[i], sems.at[i]) for i in range(len(targets))
    ]
    group = lax.axis_index("seq") % outs
    lanes = pl.ds(pl.multiple_of(group * LANES, LANES), LANES)
    copies.append(pltpu.make_async_copy(hbm[10].at[:, lanes], gate_ref, sems.at[10]))
    for copy in copies:
        copy.start()
    length = blocks * block
    emb, order = w1_ref.shape
    first_ref[...] = jnp.zeros_like(first_ref)
    for copy in copies[:7]:
        copy.wait()

    high, low = split_value(w1_ref[...])
    high, low = high.astype(F32), low.astype(F32)
    zero = jnp.zeros_like(high)
    for i, part in enumerate((high, low, high)):
        first_ref[i * pad : i * pad + emb] = jnp.concatenate([part, zero], axis=1)
        first_ref[(3 + i) * pad : (3 + i) * pad + emb] = jnp.concatenate([zero, part], axis=1)
    b1 = jnp.concatenate([b1_ref[...]] * 2, axis=1)
    b2 = jnp.concatenate([b2_ref[...]] * 2, axis=1)
    hidden = fast_sin(
        jnp.dot(
            feat_ref[...].astype(BF16), first_ref[...].astype(BF16), preferred_element_type=F32
        )
        + b1
    )
    hidden = fast_sin(layer(hidden, stacked_diagonal(w2_ref[...])) + b2)
    shaped = layer(hidden, stacked_diagonal(w3_ref[:, lanes]))

    decay = decay_ref[:, lanes]
    energy = expm1_of_negative(-2.0 * decay) / expm1_of_negative(decay * (-2.0 / length))
    times = lax.broadcasted_iota(jnp.int32, (length // 2, LANES), 0).astype(F32) * (1.0 / length)
    window = jnp.exp(-(decay * times)) * (1.0 / jnp.sqrt(energy))
    window = jnp.concatenate([window, window * jnp.exp(-0.5 * decay)], axis=1)
    taps_high, taps_low = split_value(shaped * window)

    copies[7].wait()
    high, low = split_value(table_ref[...])
    fwd_ref[:, :block] = high
    fwd_ref[:, block:] = low
    table = jnp.concatenate([high, low, high], axis=1)
    rows = lax.broadcasted_iota(jnp.int32, (2 * block, LANES), 0)
    sign = (1 - 2 * lax.rem(rows, 2)).astype(F32)
    first_row = lax.broadcasted_iota(jnp.int32, (block, LANES), 0) == 0
    spectra = [None] * blocks
    for k in range(blocks // 2):
        part = slice(k * block, (k + 1) * block)
        stacked = jnp.concatenate([taps_high[part], taps_high[part], taps_low[part]], axis=0)
        now = jnp.dot(table, stacked, preferred_element_type=F32)
        spectra[k], spectra[k + blocks // 2] = now[:, :LANES], now[:, LANES:]
    for k in range(blocks):
        spec = spectra[k] if k == 0 else spectra[k] + sign * spectra[k - 1]
        real, imag = spec[:block], spec[block:]
        hre_ref[k] = real
        him_ref[k] = jnp.where(first_row, 0.0, imag)
        hfirst_ref[k] = jnp.where(first_row, imag, real)[:8]

    for copy in copies[8:]:
        copy.wait()
    skip_ref[...] = all_skip_ref[:, lanes]
    high, low = split_value(back_ref[...])
    inv_ref[:, : 2 * block] = high
    inv_ref[:, 2 * block : 4 * block] = low
    inv_ref[:, 4 * block :] = high


def call_filter(weights, skip, gate, blocks, outs, block):
    w1, b1, w2, b2, w3, decay = weights
    length = blocks * block
    emb, order = w1.shape
    pad = -(-emb // 8) * 8
    forward, inverse = dft_tables(block)
    feats = filter_feature_table(length, emb, pad)
    hbm = [
        w1, feats, b1[None], w2, b2[None], w3, decay[None], forward.astype(np.float32),
        inverse.astype(np.float32), skip[None], gate,
    ]
    out_shape = [
        VMEM((blocks, block, LANES), F32),
        VMEM((blocks, block, LANES), F32),
        VMEM((blocks, 8, LANES), F32),
        VMEM((2 * block, 2 * block), BF16),
        VMEM((block, 6 * block), BF16),
        VMEM((1, LANES), F32),
        VMEM((block, LANES), BF16),
    ]
    return pl.pallas_call(
        functools.partial(filter_kernel, blocks, block, outs, pad),
        in_specs=[pl.BlockSpec(memory_space=pltpu.HBM)] * len(hbm),
        out_specs=[pl.BlockSpec(memory_space=VMEM)] * len(out_shape),
        out_shape=out_shape,
        scratch_shapes=[
            VMEM(w1.shape, F32),
            VMEM((1, order), F32),
            VMEM(w2.shape, F32),
            VMEM((1, order), F32),
            VMEM(w3.shape, F32),
            VMEM((1, w3.shape[1]), F32),
            VMEM(feats.shape, F32),
            VMEM(forward.shape, F32),
            VMEM(inverse.shape, F32),
            VMEM((1, skip.shape[0]), F32),
            VMEM((6 * pad, 2 * order), F32),
            pltpu.SemaphoreType.DMA((len(hbm),)),
        ],
        compiler_params=pltpu.CompilerParams(vmem_limit_bytes=32 * 2**20),
        cost_estimate=pl.CostEstimate(
            flops=4 * 10**8, bytes_accessed=8 * 2**20, transcendentals=length * LANES
        ),
        name="filter_spectra",
    )(*(pltpu.with_memory_space_constraint(jnp.asarray(each), pltpu.HBM) for each in hbm))


def columns_of(part, half, width):
    return pl.ds(pl.multiple_of(part * width + half * (width // 2), LANES), width // 2)


def weight_copies(weight_ref, over_x_ref, over_y_ref, sems, first_sem):
    rows = weight_ref.shape[0] // 2
    width = weight_ref.shape[1] // FACE
    me = lax.axis_index("chan")
    half_rows = pl.ds(pl.multiple_of((lax.axis_index("seq") % 2) * rows, LANES), rows)
    copies = []
    for out_ref, half, parts in ((over_x_ref, 0, (1, 3)), (over_y_ref, 1, (2, 3))):
        for place, k in enumerate(parts):
            copies.append(
                pltpu.make_async_copy(
                    weight_ref.at[half_rows, columns_of(me ^ k, half, width)],
                    out_ref.at[:, place * (width // 2) : (place + 1) * (width // 2)],
                    sems.at[first_sem + len(copies)],
                )
            )
    return copies


def pack_kernel(blocks, outs, x_ref, gate_ref, weight_ref, pieces_ref, *refs):
    gate_refs, (over_x_ref, over_y_ref, sems) = refs[: outs - 1], refs[outs - 1 :]
    group = lax.axis_index("seq") % outs
    copies = [
        pltpu.make_async_copy(
            x_ref.at[:, (d % outs) * LANES : (d % outs + 1) * LANES], pieces_ref.at[d], sems.at[d]
        )
        for d in range(blocks)
    ]
    for k in range(1, outs):
        lanes = pl.ds(pl.multiple_of((group ^ k) * LANES, LANES), LANES)
        copies.append(
            pltpu.make_async_copy(gate_ref.at[:, lanes], gate_refs[k - 1], sems.at[len(copies)])
        )
    copies += weight_copies(weight_ref, over_x_ref, over_y_ref, sems, len(copies))
    for copy in copies:
        copy.start()
    for copy in copies:
        copy.wait()


def call_pack(x, gate, weight, blocks, outs):
    block = x.shape[0]
    send = VMEM((weight.shape[0] // 2, weight.shape[1] // FACE), BF16)
    out_shape = [jax.ShapeDtypeStruct((blocks, block, LANES), BF16)]
    out_shape += [jax.ShapeDtypeStruct((block, LANES), BF16)] * (outs - 1) + [send] * 2
    return pl.pallas_call(
        functools.partial(pack_kernel, blocks, outs),
        in_specs=[pl.BlockSpec(memory_space=pltpu.HBM)] * 3,
        out_specs=[pl.BlockSpec(memory_space=VMEM)] * len(out_shape),
        out_shape=out_shape,
        scratch_shapes=[pltpu.SemaphoreType.DMA((blocks + outs + 3,))],
        cost_estimate=pl.CostEstimate(flops=0, bytes_accessed=2**21, transcendentals=0),
        name="pack_pieces",
    )(*(pltpu.with_memory_space_constraint(each, pltpu.HBM) for each in (x, gate, weight)))


def conv_kernel(blocks, outs, block, xs_ref, *refs):
    hre_ref, him_ref, hfirst_ref, fwd_ref, inv_ref, skip_ref, gate_ref = refs[:7]
    refs = refs[9:]
    out_refs, (wre_ref, wim_ref, yre_ref, yim_ref) = refs[:outs], refs[outs + 2 :]
    me = lax.axis_index("seq")
    half, group = me // outs, me % outs
    earlier = blocks - outs
    for j in range(outs):
        values = jnp.concatenate([xs_ref[j], xs_ref[half * outs + j]], axis=1)
        spec = jnp.dot(
            fwd_ref[...], jnp.concatenate([values, values], axis=0), preferred_element_type=F32
        )
        before = jnp.where(half > 0, spec[:, :LANES], 0.0)
        wre_ref[j] = before[:block]
        wim_ref[j] = before[block:]
        wre_ref[earlier + j] = spec[:block, LANES:]
        wim_ref[earlier + j] = spec[block:, LANES:]

    def rows_at(start, first):
        rows = pl.ds(start, 8)
        wre = [wre_ref[j, rows, :] for j in range(blocks)]
        wim = [wim_ref[j, rows, :] for j in range(blocks)]
        for o in range(outs):
            total_re = total_im = None
            for j in range(earlier + o + 1):
                k = earlier + o - j
                hre = hre_ref[k, rows, :]
                him = him_ref[k, rows, :]
                hother = hfirst_ref[k] if first else hre
                add_re = wre[j] * hre - wim[j] * him
                add_im = wre[j] * him + wim[j] * hother
                total_re = add_re if total_re is None else total_re + add_re
                total_im = add_im if total_im is None else total_im + add_im
            yre_ref[o, rows, :] = total_re
            yim_ref[o, rows, :] = total_im

    rows_at(0, True)

    @pl.loop(1, block // 8)
    def _(tile):
        rows_at(pl.multiple_of(tile * 8, 8), False)

    def stacked(slot):
        re_high, re_low = split_value(yre_ref[slot])
        im_high, im_low = split_value(yim_ref[slot])
        return jnp.concatenate([re_high, im_high, re_high, im_high, re_low, im_low], axis=0)

    skip = skip_ref[...]
    for k in range(0, outs, 2):
        pair = jnp.concatenate([stacked(group ^ k), stacked(group ^ (k + 1))], axis=1)
        conv = jnp.dot(inv_ref[...], pair, preferred_element_type=F32)
        for i in range(2):
            values = xs_ref[half * outs + (group ^ (k + i))].astype(F32)
            mixed = conv[:, i * LANES : (i + 1) * LANES] + skip * values
            if k + i == 0:
                mixed = (gate_ref[...].astype(F32) * mixed).astype(BF16)
            out_refs[k + i][...] = mixed


def gate_kernel(count, *refs):
    for k in range(count):
        gate = refs[count + k][...].astype(F32)
        refs[2 * count + k][...] = (gate * refs[k][...]).astype(BF16)


def call_conv(xs, filters, passing, outs):
    blocks, block, _ = xs.shape
    pinned = [pltpu.with_memory_space_constraint(each, VMEM) for each in filters]
    operands = [xs, *pinned]
    shape = jax.ShapeDtypeStruct
    return pl.pallas_call(
        functools.partial(conv_kernel, blocks, outs, block),
        in_specs=[pl.BlockSpec(memory_space=VMEM)] * len(operands)
        + [pl.BlockSpec(memory_space=pl.ANY)] * 2,
        out_specs=[pl.BlockSpec(memory_space=VMEM)] * outs
        + [pl.BlockSpec(memory_space=pl.ANY)] * 2,
        out_shape=[shape((block, LANES), F32 if k else BF16) for k in range(outs)]
        + [shape(p.shape, p.dtype) for p in passing],
        input_output_aliases={len(operands) + i: outs + i for i in range(2)},
        scratch_shapes=[
            VMEM((blocks, block, LANES), F32),
            VMEM((blocks, block, LANES), F32),
            VMEM((outs, block, LANES), F32),
            VMEM((outs, block, LANES), F32),
        ],
        compiler_params=pltpu.CompilerParams(vmem_limit_bytes=16 * 2**20),
        cost_estimate=pl.CostEstimate(
            flops=2 * 10**8, bytes_accessed=3 * 2**20, transcendentals=0
        ),
        name="convolve",
    )(*operands, *passing)


def join_kernel(outs, *refs):
    piece_refs, joined_ref = refs[:outs], refs[outs]
    group = lax.axis_index("seq") % outs
    for k in range(outs):
        lanes = pl.ds(pl.multiple_of((group ^ k) * LANES, LANES), LANES)
        joined_ref[:, lanes] = piece_refs[k][...]


def tiles(width):
    step = min(width, 2 * LANES)
    return [slice(start, start + step) for start in range(0, width, step)]


def own_kernel(width, gated_ref, weight_ref, *refs):
    out_refs, (held_ref, sems) = refs[:4], refs[4:]
    me = lax.axis_index("chan")
    copies = [
        pltpu.make_async_copy(
            weight_ref.at[:, columns_of(me ^ k, half, width)], held_ref.at[i], sems.at[i]
        )
        for i, (k, half) in enumerate(((2, 0), (1, 1), (0, 0), (0, 1)))
    ]
    for copy in copies:
        copy.start()
    left = gated_ref[...]
    for i, copy in enumerate(copies):
        copy.wait()
        for lanes in tiles(width // 2):
            out_refs[i][:, lanes] = jnp.dot(
                left, held_ref[i, :, lanes], preferred_element_type=F32
            )


def neighbour_kernel(first, x_ref, y_ref, *refs):
    from_x, from_y, sums, outs = refs[:2], refs[2:4], refs[4:6], refs[6:]
    rows = from_x[0].shape[0]
    core = lax.axis_index("seq") % 2
    for left_ref, held, sum_ref, out_ref in (
        (x_ref, from_x, sums[0], outs[0]),
        (y_ref, from_y, sums[1], outs[1]),
    ):
        near = left_ref[:, pl.ds(pl.multiple_of(core * rows, LANES), rows)]
        far = left_ref[:, pl.ds(pl.multiple_of((1 - core) * rows, LANES), rows)]
        width = out_ref.shape[1]
        for lanes in tiles(width):
            place = slice(first * width + lanes.start, first * width + lanes.stop)
            total = jnp.dot(near, held[0][:, place], preferred_element_type=F32)
            total += jnp.dot(far, held[1][:, place], preferred_element_type=F32)
            out_ref[:, lanes] = (sum_ref[:, lanes] + total).astype(out_ref.dtype)


def last_kernel(*refs):
    sums, arrived, out_ref = refs[:2], refs[2:4], refs[4]
    width = sums[0].shape[1]
    for half in range(2):
        out_ref[:, half * width : (half + 1) * width] = (
            sums[half][...] + arrived[half][...].astype(F32)
        ).astype(BF16)


def in_vmem(kernel, operands, out_shape, name, flops, scratch=()):
    return pl.pallas_call(
        kernel,
        in_specs=[pl.BlockSpec(memory_space=VMEM)] * len(operands),
        out_specs=jax.tree.map(lambda _: pl.BlockSpec(memory_space=VMEM), out_shape),
        out_shape=out_shape,
        scratch_shapes=scratch,
        compiler_params=pltpu.CompilerParams(vmem_limit_bytes=16 * 2**20),
        cost_estimate=pl.CostEstimate(flops=flops, bytes_accessed=2**20, transcendentals=0),
        name=name,
    )(*operands)


def call_own(gated, weight):
    block, width = gated.shape
    columns = weight.shape[1] // FACE
    return pl.pallas_call(
        functools.partial(own_kernel, columns),
        in_specs=[pl.BlockSpec(memory_space=VMEM), pl.BlockSpec(memory_space=pltpu.HBM)],
        out_specs=[pl.BlockSpec(memory_space=VMEM)] * 4,
        out_shape=[jax.ShapeDtypeStruct((block, columns // 2), F32)] * 4,
        scratch_shapes=[
            VMEM((4, width, columns // 2), BF16),
            pltpu.SemaphoreType.DMA((4,)),
        ],
        compiler_params=pltpu.CompilerParams(vmem_limit_bytes=16 * 2**20),
        cost_estimate=pl.CostEstimate(
            flops=4 * block * width * columns, bytes_accessed=6 * width * columns, transcendentals=0
        ),
        name="own_channels",
    )(gated, pltpu.with_memory_space_constraint(weight, pltpu.HBM))


def split_shards(
    mixer_input,
    gate_branch,
    skip_gain,
    decay_rate,
    first_weight,
    first_bias,
    second_weight,
    second_bias,
    last_weight,
    output_weight,
):
    block, width = mixer_input.shape
    blocks = lax.axis_size("seq")
    outs = width // LANES

    along_seq = lambda part, k: lax.ppermute(part, "seq", [(s, s ^ k) for s in range(blocks)])
    along_chan = lambda part, k: lax.ppermute(part, "chan", [(c, c ^ k) for c in range(FACE)])
    shape = jax.ShapeDtypeStruct

    xs, *gates, over_x, over_y = call_pack(
        mixer_input, gate_branch, output_weight, blocks, outs
    )
    xs = lax.all_to_all(xs, "seq", 0, 0, tiled=True)
    from_x, from_y = along_chan(over_x, 1), along_chan(over_y, 2)
    filters = call_filter(
        (first_weight, first_bias, second_weight, second_bias, last_weight, decay_rate),
        skip_gain,
        gate_branch,
        blocks,
        outs,
        block,
    )
    gates = [along_seq(gates[k - 1], k) for k in range(1, outs)]
    first, *mixed, from_x, from_y = call_conv(xs, filters, (from_x, from_y), outs)
    from_x, from_y = (from_x, along_seq(from_x, 1)), (from_y, along_seq(from_y, 1))
    pieces = in_vmem(
        functools.partial(gate_kernel, outs - 1),
        [*mixed, *gates],
        [shape((block, LANES), BF16)] * (outs - 1),
        "apply_gates",
        10**6,
    )
    pieces = [first] + [along_seq(pieces[k - 1], k) for k in range(1, outs)]
    gated = in_vmem(
        functools.partial(join_kernel, outs),
        pieces,
        shape((block, width), BF16),
        "join_pieces",
        10**6,
    )
    x_gated, y_gated = along_chan(gated, 1), along_chan(gated, 2)
    send_a, send_b, keep_a, keep_b = call_own(gated, output_weight)
    columns = send_a.shape[1]
    flops = 4 * block * width * columns
    send_a, send_b = in_vmem(
        functools.partial(neighbour_kernel, 1),
        [x_gated, y_gated, *from_x, *from_y, send_a, send_b],
        [shape((block, columns), BF16)] * 2,
        "sums_to_send",
        flops,
    )
    got_a, got_b = along_chan(send_a, 2), along_chan(send_b, 1)
    keep_a, keep_b = in_vmem(
        functools.partial(neighbour_kernel, 0),
        [x_gated, y_gated, *from_x, *from_y, keep_a, keep_b],
        [shape((block, columns), F32)] * 2,
        "sums_to_keep",
        flops,
    )
    return in_vmem(
        last_kernel,
        [keep_a, keep_b, got_a, got_b],
        shape((block, 2 * columns), BF16),
        "last_sum",
        10**6,
    )


def contract_first(left_matrix, right_matrix):
    return lax.dot_general(
        left_matrix,
        right_matrix,
        (((0,), (0,)), ((), ())),
        precision=HIGHEST,
        preferred_element_type=F32,
    )


def filter_taps(
    first_weight, first_bias, second_weight, second_bias, last_weight, decay_rate, length
):
    features = jnp.asarray(feature_table(length, first_weight.shape[0]).T)
    hidden_one = jnp.sin(contract_first(first_weight, features) + first_bias[:, None])
    hidden_two = jnp.sin(contract_first(second_weight, hidden_one) + second_bias[:, None])
    shaped = contract_first(hidden_two, last_weight)
    positions = jnp.arange(length, dtype=jnp.int32).astype(F32)
    envelope = jnp.exp(-decay_rate[None, :] * (positions[:, None] / length))
    energy = jnp.expm1(-2.0 * decay_rate) / jnp.expm1(-2.0 * decay_rate / length)
    return shaped * envelope / jnp.sqrt(energy)[None, :]


def transform_tables(block_len):
    padded_len = 2 * block_len
    freq_index = jnp.arange(block_len + 1, dtype=jnp.int32)[:, None]
    time_index = jnp.arange(padded_len, dtype=jnp.int32)[None, :]
    angle = (freq_index * time_index % padded_len).astype(F32) * (2.0 * math.pi / padded_len)
    forward = jnp.concatenate([jnp.cos(angle), -jnp.sin(angle)], axis=0)
    later_angle = angle[:, block_len:]
    weights = jnp.where((freq_index == 0) | (freq_index == block_len), 1.0, 2.0) / padded_len
    inverse = jnp.concatenate(
        [(weights * jnp.cos(later_angle)).T, (-weights * jnp.sin(later_angle)).T], axis=1
    )
    return (forward, inverse)


def spectral_product(left_spec, right_spec, half_rows):
    left_real, left_imag = (left_spec[:half_rows], left_spec[half_rows:])
    right_real, right_imag = (right_spec[:half_rows], right_spec[half_rows:])
    return jnp.concatenate(
        [
            left_real * right_real - left_imag * right_imag,
            left_real * right_imag + left_imag * right_real,
        ],
        axis=0,
    )


def gathered_shards(
    mixer_input,
    gate_branch,
    skip_gain,
    decay_rate,
    first_weight,
    first_bias,
    second_weight,
    second_bias,
    last_weight,
    output_weight,
):
    block_len, chan_width = mixer_input.shape
    seq_count = lax.axis_size("seq")
    device = lax.axis_index("seq")
    half_rows = block_len + 1
    kernel_taps = filter_taps(
        first_weight,
        first_bias,
        second_weight,
        second_bias,
        last_weight,
        decay_rate,
        block_len * seq_count,
    )
    padded_taps = jnp.concatenate([jnp.zeros((block_len, chan_width), F32), kernel_taps], axis=0)
    forward, inverse = transform_tables(block_len)
    forward_head = forward[:, :block_len]
    gathered = lax.all_gather(mixer_input, "seq", axis=0, tiled=True)

    def one_block(block_index, total):
        rows = lax.dynamic_slice_in_dim(gathered, block_index * block_len, block_len, 0)
        source_spec = jnp.dot(
            forward_head, rows.astype(F32), precision=HIGHEST, preferred_element_type=F32
        )
        segment = lax.dynamic_slice_in_dim(
            padded_taps, (device - block_index) * block_len, 2 * block_len, 0
        )
        lag_spec = jnp.dot(forward, segment, precision=HIGHEST, preferred_element_type=F32)
        return total + spectral_product(lag_spec, source_spec, half_rows)

    total = lax.fori_loop(0, device + 1, one_block, jnp.zeros((2 * half_rows, chan_width), F32))
    convolved = jnp.dot(inverse, total, precision=HIGHEST, preferred_element_type=F32)
    values = mixer_input.astype(F32)
    gated_mix = (
        gate_branch.astype(F32) * (convolved + skip_gain[None, :] * values)
    ).astype(BF16)
    partial_out = jnp.dot(gated_mix, output_weight, preferred_element_type=F32)
    return lax.psum_scatter(partial_out, "chan", scatter_dimension=1, tiled=True).astype(BF16)


def solution(mesh):
    seq_count, chan_count = mesh.shape["seq"], mesh.shape["chan"]

    def shards(mixer_input, *rest):
        block, width = mixer_input.shape
        outs = width // LANES
        splits = (
            width % LANES == 0
            and block % LANES == 0
            and seq_count == 2 * outs
            and outs == 4
            and chan_count == FACE
        )
        plan = split_shards if splits else gathered_shards
        return plan(mixer_input, *rest)

    in_specs = (
        P("seq", "chan"),
        P("seq", "chan"),
        P("chan"),
        P("chan"),
        P(),
        P(),
        P(),
        P(),
        P(None, "chan"),
        P("chan", None),
    )
    out_specs = P("seq", "chan")
    return jax.shard_map(shards, mesh=mesh, in_specs=in_specs, out_specs=out_specs, check_vma=False)
```

```python
import functools
import math

import jax
import jax.numpy as jnp
import numpy as np
from jax import lax
from jax.experimental import pallas as pl
from jax.experimental.pallas import tpu as pltpu
from jax.sharding import PartitionSpec as P

HIGHEST = lax.Precision.HIGHEST
F32 = jnp.float32
BF16 = jnp.bfloat16
LANES = 128
FACE = 4
VMEM = pltpu.VMEM


def feature_table(length, emb_width):
    band_count = (emb_width - 1) // 2
    positions = np.arange(length, dtype=np.int64)
    columns = [positions / length]
    for band in range(1, band_count + 1):
        frequency = min(
            length // 2, max(band, int((length / 2) ** ((band - 1) / (band_count - 1))))
        )
        angle = (positions * frequency % length) * (2.0 * math.pi / length)
        columns.append(np.cos(angle))
        columns.append(np.sin(angle))
    return np.stack(columns, axis=1).astype(np.float32)


def split_bf16(table):
    high = table.astype(np.float32).astype(jnp.bfloat16)
    low = (table - high.astype(np.float64)).astype(np.float32).astype(jnp.bfloat16)
    return high, low


def dft_tables(block):
    size = 2 * block
    bins = np.arange(block)[:, None]
    times = np.arange(block)[None, :]
    angle = (bins * times % size) * (2.0 * math.pi / size)
    imag = -np.sin(angle)
    imag[0] = 1.0 - 2.0 * (np.arange(block) % 2)
    forward = np.concatenate([np.cos(angle), imag], axis=0)
    weight = np.where(bins == 0, 1.0, 2.0) / size
    back_imag = -weight * np.sin(angle)
    back_imag[0] = (1.0 - 2.0 * (np.arange(block) % 2)) / size
    inverse = np.concatenate([weight * np.cos(angle), back_imag], axis=0).T
    return forward, inverse


def fast_sin(x):
    turns = jnp.floor(x * (1.0 / math.pi) + 0.5)
    rest = x - turns * 3.140625
    rest = rest - turns * 9.67502593994140625e-4
    rest = rest - turns * 1.509957990978376432e-7
    parity = turns - 2.0 * jnp.floor(turns * 0.5)
    rest = rest * (1.0 - 2.0 * parity)
    square = rest * rest
    poly = -2.5052108e-8
    for coeff in (2.7557319e-6, -1.9841270e-4, 8.3333333e-3, -1.6666667e-1):
        poly = poly * square + coeff
    return rest + rest * square * poly


def expm1_of_negative(x):
    near = jnp.maximum(x, -0.5)
    series = jnp.full_like(x, 1.0 / 3628800.0)
    for denom in (362880.0, 40320.0, 5040.0, 720.0, 120.0, 24.0, 6.0, 2.0, 1.0):
        series = series * near + 1.0 / denom
    return jnp.where(x > -0.5, near * series, jnp.exp(x) - 1.0)


def split_value(value):
    high = value.astype(BF16)
    return high, (value - high.astype(F32)).astype(BF16)


def filter_feature_table(length, emb_width, pad):
    table = feature_table(length, emb_width)
    columns = []
    for half in (table[: length // 2], table[length // 2 :]):
        high, low = (part.astype(np.float32) for part in split_bf16(half))
        for part in (high, high, low):
            columns.append(np.pad(part, ((0, 0), (0, pad - emb_width))))
    return np.concatenate(columns, axis=1)


def twice_diagonal(value):
    zero = jnp.zeros_like(value)
    return jnp.concatenate(
        [jnp.concatenate([value, zero], axis=1), jnp.concatenate([zero, value], axis=1)], axis=0
    )


def stacked_diagonal(value):
    high, low = split_value(value)
    high = twice_diagonal(high.astype(F32))
    low = twice_diagonal(low.astype(F32))
    return jnp.concatenate([high, low, high], axis=0).astype(BF16)


def layer(value, weight):
    high, low = split_value(value)
    return jnp.dot(
        jnp.concatenate([high, high, low], axis=1), weight, preferred_element_type=F32
    )


def filter_kernel(blocks, block, outs, pad, *refs):
    hbm, refs = refs[:11], refs[11:]
    hre_ref, him_ref, hfirst_ref, fwd_ref, inv_ref, skip_ref, gate_ref = refs[:7]
    refs = refs[7:]
    w1_ref, b1_ref, w2_ref, b2_ref, w3_ref, decay_ref, feat_ref, table_ref, back_ref = refs[:9]
    all_skip_ref, first_ref, sems = refs[9:]
    targets = [
        w1_ref, feat_ref, b1_ref, w2_ref, b2_ref, w3_ref, decay_ref, table_ref, back_ref,
        all_skip_ref,
    ]
    copies = [
        pltpu.make_async_copy(hbm[i], targets[i], sems.at[i]) for i in range(len(targets))
    ]
    group = lax.axis_index("seq") % outs
    lanes = pl.ds(pl.multiple_of(group * LANES, LANES), LANES)
    copies.append(pltpu.make_async_copy(hbm[10].at[:, lanes], gate_ref, sems.at[10]))
    for copy in copies:
        copy.start()
    length = blocks * block
    emb, order = w1_ref.shape
    first_ref[...] = jnp.zeros_like(first_ref)
    for copy in copies[:7]:
        copy.wait()

    high, low = split_value(w1_ref[...])
    high, low = high.astype(F32), low.astype(F32)
    zero = jnp.zeros_like(high)
    for i, part in enumerate((high, low, high)):
        first_ref[i * pad : i * pad + emb] = jnp.concatenate([part, zero], axis=1)
        first_ref[(3 + i) * pad : (3 + i) * pad + emb] = jnp.concatenate([zero, part], axis=1)
    b1 = jnp.concatenate([b1_ref[...]] * 2, axis=1)
    b2 = jnp.concatenate([b2_ref[...]] * 2, axis=1)
    hidden = fast_sin(
        jnp.dot(
            feat_ref[...].astype(BF16), first_ref[...].astype(BF16), preferred_element_type=F32
        )
        + b1
    )
    hidden = fast_sin(layer(hidden, stacked_diagonal(w2_ref[...])) + b2)
    shaped = layer(hidden, stacked_diagonal(w3_ref[:, lanes]))

    decay = decay_ref[:, lanes]
    energy = expm1_of_negative(-2.0 * decay) / expm1_of_negative(decay * (-2.0 / length))
    times = lax.broadcasted_iota(jnp.int32, (length // 2, LANES), 0).astype(F32) * (1.0 / length)
    window = jnp.exp(-(decay * times)) * (1.0 / jnp.sqrt(energy))
    window = jnp.concatenate([window, window * jnp.exp(-0.5 * decay)], axis=1)
    taps_high, taps_low = split_value(shaped * window)

    copies[7].wait()
    high, low = split_value(table_ref[...])
    fwd_ref[:, :block] = high
    fwd_ref[:, block:] = low
    table = jnp.concatenate([high, low, high], axis=1)
    rows = lax.broadcasted_iota(jnp.int32, (2 * block, LANES), 0)
    sign = (1 - 2 * lax.rem(rows, 2)).astype(F32)
    first_row = lax.broadcasted_iota(jnp.int32, (block, LANES), 0) == 0
    spectra = [None] * blocks
    for k in range(blocks // 2):
        part = slice(k * block, (k + 1) * block)
        stacked = jnp.concatenate([taps_high[part], taps_high[part], taps_low[part]], axis=0)
        now = jnp.dot(table, stacked, preferred_element_type=F32)
        spectra[k], spectra[k + blocks // 2] = now[:, :LANES], now[:, LANES:]
    for k in range(blocks):
        spec = spectra[k] if k == 0 else spectra[k] + sign * spectra[k - 1]
        real, imag = spec[:block], spec[block:]
        hre_ref[k] = real
        him_ref[k] = jnp.where(first_row, 0.0, imag)
        hfirst_ref[k] = jnp.where(first_row, imag, real)[:8]

    for copy in copies[8:]:
        copy.wait()
    skip_ref[...] = all_skip_ref[:, lanes]
    high, low = split_value(back_ref[...])
    inv_ref[:, : 2 * block] = high
    inv_ref[:, 2 * block : 4 * block] = low
    inv_ref[:, 4 * block :] = high


def call_filter(weights, skip, gate, blocks, outs, block):
    w1, b1, w2, b2, w3, decay = weights
    length = blocks * block
    emb, order = w1.shape
    pad = -(-emb // 8) * 8
    forward, inverse = dft_tables(block)
    feats = filter_feature_table(length, emb, pad)
    hbm = [
        w1, feats, b1[None], w2, b2[None], w3, decay[None], forward.astype(np.float32),
        inverse.astype(np.float32), skip[None], gate,
    ]
    out_shape = [
        VMEM((blocks, block, LANES), F32),
        VMEM((blocks, block, LANES), F32),
        VMEM((blocks, 8, LANES), F32),
        VMEM((2 * block, 2 * block), BF16),
        VMEM((block, 6 * block), BF16),
        VMEM((1, LANES), F32),
        VMEM((block, LANES), BF16),
    ]
    return pl.pallas_call(
        functools.partial(filter_kernel, blocks, block, outs, pad),
        in_specs=[pl.BlockSpec(memory_space=pltpu.HBM)] * len(hbm),
        out_specs=[pl.BlockSpec(memory_space=VMEM)] * len(out_shape),
        out_shape=out_shape,
        scratch_shapes=[
            VMEM(w1.shape, F32),
            VMEM((1, order), F32),
            VMEM(w2.shape, F32),
            VMEM((1, order), F32),
            VMEM(w3.shape, F32),
            VMEM((1, w3.shape[1]), F32),
            VMEM(feats.shape, F32),
            VMEM(forward.shape, F32),
            VMEM(inverse.shape, F32),
            VMEM((1, skip.shape[0]), F32),
            VMEM((6 * pad, 2 * order), F32),
            pltpu.SemaphoreType.DMA((len(hbm),)),
        ],
        compiler_params=pltpu.CompilerParams(vmem_limit_bytes=32 * 2**20),
        cost_estimate=pl.CostEstimate(
            flops=4 * 10**8, bytes_accessed=8 * 2**20, transcendentals=length * LANES
        ),
        name="filter_spectra",
    )(*(pltpu.with_memory_space_constraint(jnp.asarray(each), pltpu.HBM) for each in hbm))


def columns_of(part, half, width):
    return pl.ds(pl.multiple_of(part * width + half * (width // 2), LANES), width // 2)


def weight_copies(weight_ref, over_x_ref, over_y_ref, sems, first_sem):
    rows = weight_ref.shape[0] // 2
    width = weight_ref.shape[1] // FACE
    me = lax.axis_index("chan")
    half_rows = pl.ds(pl.multiple_of((lax.axis_index("seq") % 2) * rows, LANES), rows)
    copies = []
    for out_ref, half, parts in ((over_x_ref, 0, (1, 3)), (over_y_ref, 1, (2, 3))):
        for place, k in enumerate(parts):
            copies.append(
                pltpu.make_async_copy(
                    weight_ref.at[half_rows, columns_of(me ^ k, half, width)],
                    out_ref.at[:, place * (width // 2) : (place + 1) * (width // 2)],
                    sems.at[first_sem + len(copies)],
                )
            )
    return copies


def pack_kernel(blocks, outs, x_ref, gate_ref, weight_ref, pieces_ref, *refs):
    gate_refs, refs = refs[: outs - 1], refs[outs - 1 :]
    over_x_ref, over_y_ref, x_held_ref, gate_held_ref, sems = refs
    group = lax.axis_index("seq") % outs
    arrive = [
        pltpu.make_async_copy(x_ref, x_held_ref, sems.at[0]),
        pltpu.make_async_copy(gate_ref, gate_held_ref, sems.at[1]),
    ]
    others = weight_copies(weight_ref, over_x_ref, over_y_ref, sems, 2)
    for copy in arrive + others:
        copy.start()
    first = 2 + len(others)
    leave = [
        pltpu.make_async_copy(
            x_held_ref.at[:, (d % outs) * LANES : (d % outs + 1) * LANES],
            pieces_ref.at[d],
            sems.at[first + d],
        )
        for d in range(blocks)
    ]
    first += blocks
    for k in range(1, outs):
        lanes = pl.ds(pl.multiple_of((group ^ k) * LANES, LANES), LANES)
        leave.append(
            pltpu.make_async_copy(
                gate_held_ref.at[:, lanes], gate_refs[k - 1], sems.at[first + k - 1]
            )
        )
    arrive[0].wait()
    for copy in leave[:blocks]:
        copy.start()
    arrive[1].wait()
    for copy in leave[blocks:]:
        copy.start()
    for copy in others + leave:
        copy.wait()


def call_pack(x, gate, weight, blocks, outs):
    block = x.shape[0]
    send = VMEM((weight.shape[0] // 2, weight.shape[1] // FACE), BF16)
    out_shape = [pltpu.HBM((blocks, block, LANES), BF16)]
    out_shape += [pltpu.HBM((block, LANES), BF16)] * (outs - 1) + [send] * 2
    return pl.pallas_call(
        functools.partial(pack_kernel, blocks, outs),
        in_specs=[pl.BlockSpec(memory_space=pltpu.HBM)] * 3,
        out_specs=[pl.BlockSpec(memory_space=pltpu.HBM)] * outs
        + [pl.BlockSpec(memory_space=VMEM)] * 2,
        out_shape=out_shape,
        scratch_shapes=[
            VMEM(x.shape, BF16),
            VMEM(gate.shape, BF16),
            pltpu.SemaphoreType.DMA((blocks + outs + 5,)),
        ],
        cost_estimate=pl.CostEstimate(flops=0, bytes_accessed=2**21, transcendentals=0),
        name="pack_pieces",
    )(*(pltpu.with_memory_space_constraint(each, pltpu.HBM) for each in (x, gate, weight)))


def conv_kernel(blocks, outs, block, xs_ref, *refs):
    hre_ref, him_ref, hfirst_ref, fwd_ref, inv_ref, skip_ref = refs[:6]
    gate_refs, refs = refs[6 : 6 + outs], refs[8 + outs :]
    out_refs, (wre_ref, wim_ref, yre_ref, yim_ref) = refs[:outs], refs[outs + 2 :]
    me = lax.axis_index("seq")
    half, group = me // outs, me % outs
    earlier = blocks - outs
    for j in range(outs):
        values = jnp.concatenate([xs_ref[j], xs_ref[half * outs + j]], axis=1)
        spec = jnp.dot(
            fwd_ref[...], jnp.concatenate([values, values], axis=0), preferred_element_type=F32
        )
        before = jnp.where(half > 0, spec[:, :LANES], 0.0)
        wre_ref[j] = before[:block]
        wim_ref[j] = before[block:]
        wre_ref[earlier + j] = spec[:block, LANES:]
        wim_ref[earlier + j] = spec[block:, LANES:]

    def rows_at(start, first):
        rows = pl.ds(start, 8)
        wre = [wre_ref[j, rows, :] for j in range(blocks)]
        wim = [wim_ref[j, rows, :] for j in range(blocks)]
        for o in range(outs):
            total_re = total_im = None
            for j in range(earlier + o + 1):
                k = earlier + o - j
                hre = hre_ref[k, rows, :]
                him = him_ref[k, rows, :]
                hother = hfirst_ref[k] if first else hre
                add_re = wre[j] * hre - wim[j] * him
                add_im = wre[j] * him + wim[j] * hother
                total_re = add_re if total_re is None else total_re + add_re
                total_im = add_im if total_im is None else total_im + add_im
            yre_ref[o, rows, :] = total_re
            yim_ref[o, rows, :] = total_im

    rows_at(0, True)

    @pl.loop(1, block // 8)
    def _(tile):
        rows_at(pl.multiple_of(tile * 8, 8), False)

    def stacked(slot):
        re_high, re_low = split_value(yre_ref[slot])
        im_high, im_low = split_value(yim_ref[slot])
        return jnp.concatenate([re_high, im_high, re_high, im_high, re_low, im_low], axis=0)

    skip = skip_ref[...]
    for k in range(0, outs, 2):
        pair = jnp.concatenate([stacked(group ^ k), stacked(group ^ (k + 1))], axis=1)
        conv = jnp.dot(inv_ref[...], pair, preferred_element_type=F32)
        for i in range(2):
            values = xs_ref[half * outs + (group ^ (k + i))].astype(F32)
            gate = gate_refs[k + i][...].astype(F32)
            mixed = conv[:, i * LANES : (i + 1) * LANES] + skip * values
            out_refs[k + i][...] = (gate * mixed).astype(BF16)


def call_conv(xs, filters, gates, passing, outs):
    blocks, block, _ = xs.shape
    pinned = [pltpu.with_memory_space_constraint(each, VMEM) for each in filters]
    operands = [xs, *pinned, *gates]
    shape = jax.ShapeDtypeStruct
    return pl.pallas_call(
        functools.partial(conv_kernel, blocks, outs, block),
        in_specs=[pl.BlockSpec(memory_space=VMEM)] * len(operands)
        + [pl.BlockSpec(memory_space=pl.ANY)] * 2,
        out_specs=[pl.BlockSpec(memory_space=VMEM)] * outs
        + [pl.BlockSpec(memory_space=pl.ANY)] * 2,
        out_shape=[shape((block, LANES), BF16)] * outs + [shape(p.shape, p.dtype) for p in passing],
        input_output_aliases={len(operands) + i: outs + i for i in range(2)},
        scratch_shapes=[
            VMEM((blocks, block, LANES), F32),
            VMEM((blocks, block, LANES), F32),
            VMEM((outs, block, LANES), F32),
            VMEM((outs, block, LANES), F32),
        ],
        compiler_params=pltpu.CompilerParams(vmem_limit_bytes=16 * 2**20),
        cost_estimate=pl.CostEstimate(
            flops=2 * 10**8, bytes_accessed=3 * 2**20, transcendentals=0
        ),
        name="convolve",
    )(*operands, *passing)


def join_kernel(outs, *refs):
    piece_refs, joined_ref = refs[:outs], refs[outs]
    group = lax.axis_index("seq") % outs
    for k in range(outs):
        lanes = pl.ds(pl.multiple_of((group ^ k) * LANES, LANES), LANES)
        joined_ref[:, lanes] = piece_refs[k][...]


def tiles(width):
    step = min(width, 2 * LANES)
    return [slice(start, start + step) for start in range(0, width, step)]


def own_kernel(width, gated_ref, weight_ref, *refs):
    out_refs, (held_ref, sems) = refs[:4], refs[4:]
    me = lax.axis_index("chan")
    copies = [
        pltpu.make_async_copy(
            weight_ref.at[:, columns_of(me ^ k, half, width)], held_ref.at[i], sems.at[i]
        )
        for i, (k, half) in enumerate(((2, 0), (1, 1), (0, 0), (0, 1)))
    ]
    for copy in copies:
        copy.start()
    left = gated_ref[...]
    for i, copy in enumerate(copies):
        copy.wait()
        for lanes in tiles(width // 2):
            out_refs[i][:, lanes] = jnp.dot(
                left, held_ref[i, :, lanes], preferred_element_type=F32
            )


def neighbour_kernel(first, x_ref, y_ref, *refs):
    from_x, from_y, sums, outs = refs[:2], refs[2:4], refs[4:6], refs[6:]
    rows = from_x[0].shape[0]
    core = lax.axis_index("seq") % 2
    for left_ref, held, sum_ref, out_ref in (
        (x_ref, from_x, sums[0], outs[0]),
        (y_ref, from_y, sums[1], outs[1]),
    ):
        near = left_ref[:, pl.ds(pl.multiple_of(core * rows, LANES), rows)]
        far = left_ref[:, pl.ds(pl.multiple_of((1 - core) * rows, LANES), rows)]
        width = out_ref.shape[1]
        for lanes in tiles(width):
            place = slice(first * width + lanes.start, first * width + lanes.stop)
            total = jnp.dot(near, held[0][:, place], preferred_element_type=F32)
            total += jnp.dot(far, held[1][:, place], preferred_element_type=F32)
            out_ref[:, lanes] = (sum_ref[:, lanes] + total).astype(out_ref.dtype)


def last_kernel(*refs):
    sums, arrived, out_ref = refs[:2], refs[2:4], refs[4]
    width = sums[0].shape[1]
    for half in range(2):
        out_ref[:, half * width : (half + 1) * width] = (
            sums[half][...] + arrived[half][...].astype(F32)
        ).astype(BF16)


def in_vmem(kernel, operands, out_shape, name, flops, scratch=()):
    return pl.pallas_call(
        kernel,
        in_specs=[pl.BlockSpec(memory_space=VMEM)] * len(operands),
        out_specs=jax.tree.map(lambda _: pl.BlockSpec(memory_space=VMEM), out_shape),
        out_shape=out_shape,
        scratch_shapes=scratch,
        compiler_params=pltpu.CompilerParams(vmem_limit_bytes=16 * 2**20),
        cost_estimate=pl.CostEstimate(flops=flops, bytes_accessed=2**20, transcendentals=0),
        name=name,
    )(*operands)


def call_own(gated, weight):
    block, width = gated.shape
    columns = weight.shape[1] // FACE
    return pl.pallas_call(
        functools.partial(own_kernel, columns),
        in_specs=[pl.BlockSpec(memory_space=VMEM), pl.BlockSpec(memory_space=pltpu.HBM)],
        out_specs=[pl.BlockSpec(memory_space=VMEM)] * 4,
        out_shape=[jax.ShapeDtypeStruct((block, columns // 2), F32)] * 4,
        scratch_shapes=[
            VMEM((4, width, columns // 2), BF16),
            pltpu.SemaphoreType.DMA((4,)),
        ],
        compiler_params=pltpu.CompilerParams(vmem_limit_bytes=16 * 2**20),
        cost_estimate=pl.CostEstimate(
            flops=4 * block * width * columns, bytes_accessed=6 * width * columns, transcendentals=0
        ),
        name="own_channels",
    )(gated, pltpu.with_memory_space_constraint(weight, pltpu.HBM))


def split_shards(
    mixer_input,
    gate_branch,
    skip_gain,
    decay_rate,
    first_weight,
    first_bias,
    second_weight,
    second_bias,
    last_weight,
    output_weight,
):
    block, width = mixer_input.shape
    blocks = lax.axis_size("seq")
    outs = width // LANES

    along_seq = lambda part, k: lax.ppermute(part, "seq", [(s, s ^ k) for s in range(blocks)])
    along_chan = lambda part, k: lax.ppermute(part, "chan", [(c, c ^ k) for c in range(FACE)])
    shape = jax.ShapeDtypeStruct

    xs, *gates, over_x, over_y = call_pack(
        mixer_input, gate_branch, output_weight, blocks, outs
    )
    xs = lax.all_to_all(xs, "seq", 0, 0, tiled=True)
    from_x, from_y = along_chan(over_x, 1), along_chan(over_y, 2)
    filters = call_filter(
        (first_weight, first_bias, second_weight, second_bias, last_weight, decay_rate),
        skip_gain,
        gate_branch,
        blocks,
        outs,
        block,
    )
    gates = [along_seq(gates[k - 1], k) for k in range(1, outs)]
    *pieces, from_x, from_y = call_conv(xs, filters, gates, (from_x, from_y), outs)
    from_x, from_y = (from_x, along_seq(from_x, 1)), (from_y, along_seq(from_y, 1))
    pieces = [pieces[0]] + [along_seq(pieces[k], k) for k in range(1, outs)]
    gated = in_vmem(
        functools.partial(join_kernel, outs),
        pieces,
        shape((block, width), BF16),
        "join_pieces",
        10**6,
    )
    x_gated, y_gated = along_chan(gated, 1), along_chan(gated, 2)
    send_a, send_b, keep_a, keep_b = call_own(gated, output_weight)
    columns = send_a.shape[1]
    flops = 4 * block * width * columns
    send_a, send_b = in_vmem(
        functools.partial(neighbour_kernel, 1),
        [x_gated, y_gated, *from_x, *from_y, send_a, send_b],
        [shape((block, columns), BF16)] * 2,
        "sums_to_send",
        flops,
    )
    got_a, got_b = along_chan(send_a, 2), along_chan(send_b, 1)
    keep_a, keep_b = in_vmem(
        functools.partial(neighbour_kernel, 0),
        [x_gated, y_gated, *from_x, *from_y, keep_a, keep_b],
        [shape((block, columns), F32)] * 2,
        "sums_to_keep",
        flops,
    )
    return in_vmem(
        last_kernel,
        [keep_a, keep_b, got_a, got_b],
        shape((block, 2 * columns), BF16),
        "last_sum",
        10**6,
    )


def contract_first(left_matrix, right_matrix):
    return lax.dot_general(
        left_matrix,
        right_matrix,
        (((0,), (0,)), ((), ())),
        precision=HIGHEST,
        preferred_element_type=F32,
    )


def filter_taps(
    first_weight, first_bias, second_weight, second_bias, last_weight, decay_rate, length
):
    features = jnp.asarray(feature_table(length, first_weight.shape[0]).T)
    hidden_one = jnp.sin(contract_first(first_weight, features) + first_bias[:, None])
    hidden_two = jnp.sin(contract_first(second_weight, hidden_one) + second_bias[:, None])
    shaped = contract_first(hidden_two, last_weight)
    positions = jnp.arange(length, dtype=jnp.int32).astype(F32)
    envelope = jnp.exp(-decay_rate[None, :] * (positions[:, None] / length))
    energy = jnp.expm1(-2.0 * decay_rate) / jnp.expm1(-2.0 * decay_rate / length)
    return shaped * envelope / jnp.sqrt(energy)[None, :]


def transform_tables(block_len):
    padded_len = 2 * block_len
    freq_index = jnp.arange(block_len + 1, dtype=jnp.int32)[:, None]
    time_index = jnp.arange(padded_len, dtype=jnp.int32)[None, :]
    angle = (freq_index * time_index % padded_len).astype(F32) * (2.0 * math.pi / padded_len)
    forward = jnp.concatenate([jnp.cos(angle), -jnp.sin(angle)], axis=0)
    later_angle = angle[:, block_len:]
    weights = jnp.where((freq_index == 0) | (freq_index == block_len), 1.0, 2.0) / padded_len
    inverse = jnp.concatenate(
        [(weights * jnp.cos(later_angle)).T, (-weights * jnp.sin(later_angle)).T], axis=1
    )
    return (forward, inverse)


def spectral_product(left_spec, right_spec, half_rows):
    left_real, left_imag = (left_spec[:half_rows], left_spec[half_rows:])
    right_real, right_imag = (right_spec[:half_rows], right_spec[half_rows:])
    return jnp.concatenate(
        [
            left_real * right_real - left_imag * right_imag,
            left_real * right_imag + left_imag * right_real,
        ],
        axis=0,
    )


def gathered_shards(
    mixer_input,
    gate_branch,
    skip_gain,
    decay_rate,
    first_weight,
    first_bias,
    second_weight,
    second_bias,
    last_weight,
    output_weight,
):
    block_len, chan_width = mixer_input.shape
    seq_count = lax.axis_size("seq")
    device = lax.axis_index("seq")
    half_rows = block_len + 1
    kernel_taps = filter_taps(
        first_weight,
        first_bias,
        second_weight,
        second_bias,
        last_weight,
        decay_rate,
        block_len * seq_count,
    )
    padded_taps = jnp.concatenate([jnp.zeros((block_len, chan_width), F32), kernel_taps], axis=0)
    forward, inverse = transform_tables(block_len)
    forward_head = forward[:, :block_len]
    gathered = lax.all_gather(mixer_input, "seq", axis=0, tiled=True)

    def one_block(block_index, total):
        rows = lax.dynamic_slice_in_dim(gathered, block_index * block_len, block_len, 0)
        source_spec = jnp.dot(
            forward_head, rows.astype(F32), precision=HIGHEST, preferred_element_type=F32
        )
        segment = lax.dynamic_slice_in_dim(
            padded_taps, (device - block_index) * block_len, 2 * block_len, 0
        )
        lag_spec = jnp.dot(forward, segment, precision=HIGHEST, preferred_element_type=F32)
        return total + spectral_product(lag_spec, source_spec, half_rows)

    total = lax.fori_loop(0, device + 1, one_block, jnp.zeros((2 * half_rows, chan_width), F32))
    convolved = jnp.dot(inverse, total, precision=HIGHEST, preferred_element_type=F32)
    values = mixer_input.astype(F32)
    gated_mix = (
        gate_branch.astype(F32) * (convolved + skip_gain[None, :] * values)
    ).astype(BF16)
    partial_out = jnp.dot(gated_mix, output_weight, preferred_element_type=F32)
    return lax.psum_scatter(partial_out, "chan", scatter_dimension=1, tiled=True).astype(BF16)


def solution(mesh):
    seq_count, chan_count = mesh.shape["seq"], mesh.shape["chan"]

    def shards(mixer_input, *rest):
        block, width = mixer_input.shape
        outs = width // LANES
        splits = (
            width % LANES == 0
            and block % LANES == 0
            and seq_count == 2 * outs
            and outs == 4
            and chan_count == FACE
        )
        plan = split_shards if splits else gathered_shards
        return plan(mixer_input, *rest)

    in_specs = (
        P("seq", "chan"),
        P("seq", "chan"),
        P("chan"),
        P("chan"),
        P(),
        P(),
        P(),
        P(),
        P(None, "chan"),
        P("chan", None),
    )
    out_specs = P("seq", "chan")
    return jax.shard_map(shards, mesh=mesh, in_specs=in_specs, out_specs=out_specs, check_vma=False)
```

```python
import functools
import math

import jax
import jax.numpy as jnp
import numpy as np
from jax import lax
from jax.experimental import pallas as pl
from jax.experimental.pallas import tpu as pltpu
from jax.sharding import PartitionSpec as P

HIGHEST = lax.Precision.HIGHEST
F32 = jnp.float32
BF16 = jnp.bfloat16
LANES = 128
FACE = 4
VMEM = pltpu.VMEM


def feature_table(length, emb_width):
    band_count = (emb_width - 1) // 2
    positions = np.arange(length, dtype=np.int64)
    columns = [positions / length]
    for band in range(1, band_count + 1):
        frequency = min(
            length // 2, max(band, int((length / 2) ** ((band - 1) / (band_count - 1))))
        )
        angle = (positions * frequency % length) * (2.0 * math.pi / length)
        columns.append(np.cos(angle))
        columns.append(np.sin(angle))
    return np.stack(columns, axis=1).astype(np.float32)


def split_bf16(table):
    high = table.astype(np.float32).astype(jnp.bfloat16)
    low = (table - high.astype(np.float64)).astype(np.float32).astype(jnp.bfloat16)
    return high, low


def dft_tables(block):
    size = 2 * block
    bins = np.arange(block)[:, None]
    times = np.arange(block)[None, :]
    angle = (bins * times % size) * (2.0 * math.pi / size)
    imag = -np.sin(angle)
    imag[0] = 1.0 - 2.0 * (np.arange(block) % 2)
    forward = np.concatenate([np.cos(angle), imag], axis=0)
    weight = np.where(bins == 0, 1.0, 2.0) / size
    back_imag = -weight * np.sin(angle)
    back_imag[0] = (1.0 - 2.0 * (np.arange(block) % 2)) / size
    inverse = np.concatenate([weight * np.cos(angle), back_imag], axis=0).T
    return forward, inverse


def fast_sin(x):
    turns = jnp.floor(x * (1.0 / math.pi) + 0.5)
    rest = x - turns * 3.140625
    rest = rest - turns * 9.67502593994140625e-4
    rest = rest - turns * 1.509957990978376432e-7
    parity = turns - 2.0 * jnp.floor(turns * 0.5)
    rest = rest * (1.0 - 2.0 * parity)
    square = rest * rest
    poly = -2.5052108e-8
    for coeff in (2.7557319e-6, -1.9841270e-4, 8.3333333e-3, -1.6666667e-1):
        poly = poly * square + coeff
    return rest + rest * square * poly


def expm1_of_negative(x):
    near = jnp.maximum(x, -0.5)
    series = jnp.full_like(x, 1.0 / 3628800.0)
    for denom in (362880.0, 40320.0, 5040.0, 720.0, 120.0, 24.0, 6.0, 2.0, 1.0):
        series = series * near + 1.0 / denom
    return jnp.where(x > -0.5, near * series, jnp.exp(x) - 1.0)


def split_value(value):
    high = value.astype(BF16)
    return high, (value - high.astype(F32)).astype(BF16)


def filter_feature_table(length, emb_width, pad):
    table = feature_table(length, emb_width)
    columns = []
    for half in (table[: length // 2], table[length // 2 :]):
        high, low = (part.astype(np.float32) for part in split_bf16(half))
        for part in (high, high, low):
            columns.append(np.pad(part, ((0, 0), (0, pad - emb_width))))
    return np.concatenate(columns, axis=1)


def twice_diagonal(value):
    zero = jnp.zeros_like(value)
    return jnp.concatenate(
        [jnp.concatenate([value, zero], axis=1), jnp.concatenate([zero, value], axis=1)], axis=0
    )


def stacked_diagonal(value):
    high, low = split_value(value)
    high = twice_diagonal(high.astype(F32))
    low = twice_diagonal(low.astype(F32))
    return jnp.concatenate([high, low, high], axis=0).astype(BF16)


def layer(value, weight):
    high, low = split_value(value)
    return jnp.dot(
        jnp.concatenate([high, high, low], axis=1), weight, preferred_element_type=F32
    )


def filter_kernel(blocks, block, outs, pad, *refs):
    hbm, refs = refs[:11], refs[11:]
    hre_ref, him_ref, hfirst_ref, fwd_ref, inv_ref, skip_ref, gate_ref = refs[:7]
    refs = refs[7:]
    w1_ref, b1_ref, w2_ref, b2_ref, w3_ref, decay_ref, feat_ref, table_ref, back_ref = refs[:9]
    all_skip_ref, first_ref, sems = refs[9:]
    targets = [
        w1_ref, feat_ref, b1_ref, w2_ref, b2_ref, w3_ref, decay_ref, table_ref, back_ref,
        all_skip_ref,
    ]
    copies = [
        pltpu.make_async_copy(hbm[i], targets[i], sems.at[i]) for i in range(len(targets))
    ]
    group = lax.axis_index("seq") % outs
    lanes = pl.ds(pl.multiple_of(group * LANES, LANES), LANES)
    copies.append(pltpu.make_async_copy(hbm[10].at[:, lanes], gate_ref, sems.at[10]))
    for copy in copies:
        copy.start()
    length = blocks * block
    emb, order = w1_ref.shape
    first_ref[...] = jnp.zeros_like(first_ref)
    for copy in copies[:7]:
        copy.wait()

    high, low = split_value(w1_ref[...])
    high, low = high.astype(F32), low.astype(F32)
    zero = jnp.zeros_like(high)
    for i, part in enumerate((high, low, high)):
        first_ref[i * pad : i * pad + emb] = jnp.concatenate([part, zero], axis=1)
        first_ref[(3 + i) * pad : (3 + i) * pad + emb] = jnp.concatenate([zero, part], axis=1)
    b1 = jnp.concatenate([b1_ref[...]] * 2, axis=1)
    b2 = jnp.concatenate([b2_ref[...]] * 2, axis=1)
    hidden = fast_sin(
        jnp.dot(
            feat_ref[...].astype(BF16), first_ref[...].astype(BF16), preferred_element_type=F32
        )
        + b1
    )
    hidden = fast_sin(layer(hidden, stacked_diagonal(w2_ref[...])) + b2)
    shaped = layer(hidden, stacked_diagonal(w3_ref[:, lanes]))

    decay = decay_ref[:, lanes]
    energy = expm1_of_negative(-2.0 * decay) / expm1_of_negative(decay * (-2.0 / length))
    times = lax.broadcasted_iota(jnp.int32, (length // 2, LANES), 0).astype(F32) * (1.0 / length)
    window = jnp.exp(-(decay * times)) * (1.0 / jnp.sqrt(energy))
    window = jnp.concatenate([window, window * jnp.exp(-0.5 * decay)], axis=1)
    taps_high, taps_low = split_value(shaped * window)

    copies[7].wait()
    high, low = split_value(table_ref[...])
    fwd_ref[:, :block] = high
    fwd_ref[:, block:] = low
    table = jnp.concatenate([high, low, high], axis=1)
    rows = lax.broadcasted_iota(jnp.int32, (2 * block, LANES), 0)
    sign = (1 - 2 * lax.rem(rows, 2)).astype(F32)
    first_row = lax.broadcasted_iota(jnp.int32, (block, LANES), 0) == 0
    spectra = [None] * blocks
    for k in range(blocks // 2):
        part = slice(k * block, (k + 1) * block)
        stacked = jnp.concatenate([taps_high[part], taps_high[part], taps_low[part]], axis=0)
        now = jnp.dot(table, stacked, preferred_element_type=F32)
        spectra[k], spectra[k + blocks // 2] = now[:, :LANES], now[:, LANES:]
    for k in range(blocks):
        spec = spectra[k] if k == 0 else spectra[k] + sign * spectra[k - 1]
        real, imag = spec[:block], spec[block:]
        hre_ref[k] = real
        him_ref[k] = jnp.where(first_row, 0.0, imag)
        hfirst_ref[k] = jnp.where(first_row, imag, real)[:8]

    for copy in copies[8:]:
        copy.wait()
    skip_ref[...] = all_skip_ref[:, lanes]
    high, low = split_value(back_ref[...])
    inv_ref[:, : 2 * block] = high
    inv_ref[:, 2 * block : 4 * block] = low
    inv_ref[:, 4 * block :] = high


def call_filter(weights, skip, gate, blocks, outs, block):
    w1, b1, w2, b2, w3, decay = weights
    length = blocks * block
    emb, order = w1.shape
    pad = -(-emb // 8) * 8
    forward, inverse = dft_tables(block)
    feats = filter_feature_table(length, emb, pad)
    hbm = [
        w1, feats, b1[None], w2, b2[None], w3, decay[None], forward.astype(np.float32),
        inverse.astype(np.float32), skip[None], gate,
    ]
    out_shape = [
        VMEM((blocks, block, LANES), F32),
        VMEM((blocks, block, LANES), F32),
        VMEM((blocks, 8, LANES), F32),
        VMEM((2 * block, 2 * block), BF16),
        VMEM((block, 6 * block), BF16),
        VMEM((1, LANES), F32),
        VMEM((block, LANES), BF16),
    ]
    return pl.pallas_call(
        functools.partial(filter_kernel, blocks, block, outs, pad),
        in_specs=[pl.BlockSpec(memory_space=pltpu.HBM)] * len(hbm),
        out_specs=[pl.BlockSpec(memory_space=VMEM)] * len(out_shape),
        out_shape=out_shape,
        scratch_shapes=[
            VMEM(w1.shape, F32),
            VMEM((1, order), F32),
            VMEM(w2.shape, F32),
            VMEM((1, order), F32),
            VMEM(w3.shape, F32),
            VMEM((1, w3.shape[1]), F32),
            VMEM(feats.shape, F32),
            VMEM(forward.shape, F32),
            VMEM(inverse.shape, F32),
            VMEM((1, skip.shape[0]), F32),
            VMEM((6 * pad, 2 * order), F32),
            pltpu.SemaphoreType.DMA((len(hbm),)),
        ],
        compiler_params=pltpu.CompilerParams(vmem_limit_bytes=32 * 2**20),
        cost_estimate=pl.CostEstimate(
            flops=4 * 10**8, bytes_accessed=8 * 2**20, transcendentals=length * LANES
        ),
        name="filter_spectra",
    )(*(pltpu.with_memory_space_constraint(jnp.asarray(each), pltpu.HBM) for each in hbm))


def columns_of(part, half, width):
    return pl.ds(pl.multiple_of(part * width + half * (width // 2), LANES), width // 2)


def weight_copies(weight_ref, over_x_ref, over_y_ref, sems, first_sem):
    rows = weight_ref.shape[0] // 2
    width = weight_ref.shape[1] // FACE
    me = lax.axis_index("chan")
    half_rows = pl.ds(pl.multiple_of((lax.axis_index("seq") % 2) * rows, LANES), rows)
    copies = []
    for out_ref, half, parts in ((over_x_ref, 0, (1, 3)), (over_y_ref, 1, (2, 3))):
        for place, k in enumerate(parts):
            copies.append(
                pltpu.make_async_copy(
                    weight_ref.at[half_rows, columns_of(me ^ k, half, width)],
                    out_ref.at[:, place * (width // 2) : (place + 1) * (width // 2)],
                    sems.at[first_sem + len(copies)],
                )
            )
    return copies


def pack_kernel(blocks, outs, x_ref, gate_ref, weight_ref, pieces_ref, *refs):
    gate_refs, refs = refs[: outs - 1], refs[outs - 1 :]
    over_x_ref, over_y_ref, x_held_ref, gate_held_ref, sems = refs
    group = lax.axis_index("seq") % outs
    arrive = [
        pltpu.make_async_copy(x_ref, x_held_ref, sems.at[0]),
        pltpu.make_async_copy(gate_ref, gate_held_ref, sems.at[1]),
    ]
    others = weight_copies(weight_ref, over_x_ref, over_y_ref, sems, 2)
    for copy in arrive + others:
        copy.start()
    first = 2 + len(others)
    leave = [
        pltpu.make_async_copy(
            x_held_ref.at[:, (d % outs) * LANES : (d % outs + 1) * LANES],
            pieces_ref.at[d],
            sems.at[first + d],
        )
        for d in range(blocks)
    ]
    first += blocks
    for k in range(1, outs):
        lanes = pl.ds(pl.multiple_of((group ^ k) * LANES, LANES), LANES)
        leave.append(
            pltpu.make_async_copy(
                gate_held_ref.at[:, lanes], gate_refs[k - 1], sems.at[first + k - 1]
            )
        )
    arrive[0].wait()
    for copy in leave[:blocks]:
        copy.start()
    arrive[1].wait()
    for copy in leave[blocks:]:
        copy.start()
    for copy in others + leave:
        copy.wait()


def call_pack(x, gate, weight, blocks, outs):
    block = x.shape[0]
    send = VMEM((weight.shape[0] // 2, weight.shape[1] // FACE), BF16)
    out_shape = [pltpu.HBM((blocks, block, LANES), BF16)]
    out_shape += [pltpu.HBM((block, LANES), BF16)] * (outs - 1) + [send] * 2
    return pl.pallas_call(
        functools.partial(pack_kernel, blocks, outs),
        in_specs=[pl.BlockSpec(memory_space=pltpu.HBM)] * 3,
        out_specs=[pl.BlockSpec(memory_space=pltpu.HBM)] * outs
        + [pl.BlockSpec(memory_space=VMEM)] * 2,
        out_shape=out_shape,
        scratch_shapes=[
            VMEM(x.shape, BF16),
            VMEM(gate.shape, BF16),
            pltpu.SemaphoreType.DMA((blocks + outs + 5,)),
        ],
        cost_estimate=pl.CostEstimate(flops=0, bytes_accessed=2**21, transcendentals=0),
        name="pack_pieces",
    )(*(pltpu.with_memory_space_constraint(each, pltpu.HBM) for each in (x, gate, weight)))


def conv_kernel(blocks, outs, block, xs_ref, *refs):
    hre_ref, him_ref, hfirst_ref, fwd_ref, inv_ref, skip_ref = refs[:6]
    gate_refs, refs = refs[6 : 6 + outs], refs[8 + outs :]
    out_refs, (wre_ref, wim_ref, yre_ref, yim_ref) = refs[:outs], refs[outs + 2 :]
    me = lax.axis_index("seq")
    half, group = me // outs, me % outs
    earlier = blocks - outs
    for j in range(outs):
        values = jnp.concatenate([xs_ref[j], xs_ref[half * outs + j]], axis=1)
        spec = jnp.dot(
            fwd_ref[...], jnp.concatenate([values, values], axis=0), preferred_element_type=F32
        )
        before = jnp.where(half > 0, spec[:, :LANES], 0.0)
        wre_ref[j] = before[:block]
        wim_ref[j] = before[block:]
        wre_ref[earlier + j] = spec[:block, LANES:]
        wim_ref[earlier + j] = spec[block:, LANES:]

    def rows_at(start, first):
        rows = pl.ds(start, 8)
        wre = [wre_ref[j, rows, :] for j in range(blocks)]
        wim = [wim_ref[j, rows, :] for j in range(blocks)]
        for o in range(outs):
            total_re = total_im = None
            for j in range(earlier + o + 1):
                k = earlier + o - j
                hre = hre_ref[k, rows, :]
                him = him_ref[k, rows, :]
                hother = hfirst_ref[k] if first else hre
                add_re = wre[j] * hre - wim[j] * him
                add_im = wre[j] * him + wim[j] * hother
                total_re = add_re if total_re is None else total_re + add_re
                total_im = add_im if total_im is None else total_im + add_im
            yre_ref[o, rows, :] = total_re
            yim_ref[o, rows, :] = total_im

    rows_at(0, True)

    @pl.loop(1, block // 8)
    def _(tile):
        rows_at(pl.multiple_of(tile * 8, 8), False)

    def stacked(slot):
        re_high, re_low = split_value(yre_ref[slot])
        im_high, im_low = split_value(yim_ref[slot])
        return jnp.concatenate([re_high, im_high, re_high, im_high, re_low, im_low], axis=0)

    skip = skip_ref[...]
    for k in range(0, outs, 2):
        pair = jnp.concatenate([stacked(group ^ k), stacked(group ^ (k + 1))], axis=1)
        conv = jnp.dot(inv_ref[...], pair, preferred_element_type=F32)
        for i in range(2):
            values = xs_ref[half * outs + (group ^ (k + i))].astype(F32)
            gate = gate_refs[k + i][...].astype(F32)
            mixed = conv[:, i * LANES : (i + 1) * LANES] + skip * values
            out_refs[k + i][...] = (gate * mixed).astype(BF16)


def call_conv(xs, filters, gates, passing, outs):
    blocks, block, _ = xs.shape
    pinned = [pltpu.with_memory_space_constraint(each, VMEM) for each in filters]
    operands = [xs, *pinned, *gates]
    shape = jax.ShapeDtypeStruct
    return pl.pallas_call(
        functools.partial(conv_kernel, blocks, outs, block),
        in_specs=[pl.BlockSpec(memory_space=VMEM)] * len(operands)
        + [pl.BlockSpec(memory_space=pl.ANY)] * 2,
        out_specs=[pl.BlockSpec(memory_space=VMEM)] * outs
        + [pl.BlockSpec(memory_space=pl.ANY)] * 2,
        out_shape=[shape((block, LANES), BF16)] * outs + [shape(p.shape, p.dtype) for p in passing],
        input_output_aliases={len(operands) + i: outs + i for i in range(2)},
        scratch_shapes=[
            VMEM((blocks, block, LANES), F32),
            VMEM((blocks, block, LANES), F32),
            VMEM((outs, block, LANES), F32),
            VMEM((outs, block, LANES), F32),
        ],
        compiler_params=pltpu.CompilerParams(vmem_limit_bytes=16 * 2**20),
        cost_estimate=pl.CostEstimate(
            flops=2 * 10**8, bytes_accessed=3 * 2**20, transcendentals=0
        ),
        name="convolve",
    )(*operands, *passing)


def join_kernel(outs, *refs):
    piece_refs, joined_ref = refs[:outs], refs[outs]
    group = lax.axis_index("seq") % outs
    for k in range(outs):
        lanes = pl.ds(pl.multiple_of((group ^ k) * LANES, LANES), LANES)
        joined_ref[:, lanes] = piece_refs[k][...]


def tiles(width):
    step = min(width, 2 * LANES)
    return [slice(start, start + step) for start in range(0, width, step)]


def own_kernel(width, gated_ref, weight_ref, *refs):
    out_refs, (held_ref, sems) = refs[:4], refs[4:]
    me = lax.axis_index("chan")
    copies = [
        pltpu.make_async_copy(
            weight_ref.at[:, columns_of(me ^ k, half, width)], held_ref.at[i], sems.at[i]
        )
        for i, (k, half) in enumerate(((2, 0), (1, 1), (0, 0), (0, 1)))
    ]
    for copy in copies:
        copy.start()
    left = gated_ref[...]
    for i, copy in enumerate(copies):
        copy.wait()
        for lanes in tiles(width // 2):
            out_refs[i][:, lanes] = jnp.dot(
                left, held_ref[i, :, lanes], preferred_element_type=F32
            )


def neighbour_kernel(first, x_ref, y_ref, *refs):
    from_x, from_y, sums, outs = refs[:2], refs[2:4], refs[4:6], refs[6:]
    rows = from_x[0].shape[0]
    core = lax.axis_index("seq") % 2
    for left_ref, held, sum_ref, out_ref in (
        (x_ref, from_x, sums[0], outs[0]),
        (y_ref, from_y, sums[1], outs[1]),
    ):
        near = left_ref[:, pl.ds(pl.multiple_of(core * rows, LANES), rows)]
        far = left_ref[:, pl.ds(pl.multiple_of((1 - core) * rows, LANES), rows)]
        width = out_ref.shape[1]
        for lanes in tiles(width):
            place = slice(first * width + lanes.start, first * width + lanes.stop)
            total = jnp.dot(near, held[0][:, place], preferred_element_type=F32)
            total += jnp.dot(far, held[1][:, place], preferred_element_type=F32)
            out_ref[:, lanes] = (sum_ref[:, lanes] + total).astype(out_ref.dtype)


def last_kernel(*refs):
    sums, arrived, out_ref = refs[:2], refs[2:4], refs[4]
    width = sums[0].shape[1]
    for half in range(2):
        out_ref[:, half * width : (half + 1) * width] = (
            sums[half][...] + arrived[half][...].astype(F32)
        ).astype(BF16)


def in_vmem(kernel, operands, out_shape, name, flops, scratch=()):
    return pl.pallas_call(
        kernel,
        in_specs=[pl.BlockSpec(memory_space=VMEM)] * len(operands),
        out_specs=jax.tree.map(lambda _: pl.BlockSpec(memory_space=VMEM), out_shape),
        out_shape=out_shape,
        scratch_shapes=scratch,
        compiler_params=pltpu.CompilerParams(vmem_limit_bytes=16 * 2**20),
        cost_estimate=pl.CostEstimate(flops=flops, bytes_accessed=2**20, transcendentals=0),
        name=name,
    )(*operands)


def call_own(gated, weight):
    block, width = gated.shape
    columns = weight.shape[1] // FACE
    return pl.pallas_call(
        functools.partial(own_kernel, columns),
        in_specs=[pl.BlockSpec(memory_space=VMEM), pl.BlockSpec(memory_space=pltpu.HBM)],
        out_specs=[pl.BlockSpec(memory_space=VMEM)] * 4,
        out_shape=[jax.ShapeDtypeStruct((block, columns // 2), F32)] * 4,
        scratch_shapes=[
            VMEM((4, width, columns // 2), BF16),
            pltpu.SemaphoreType.DMA((4,)),
        ],
        compiler_params=pltpu.CompilerParams(vmem_limit_bytes=16 * 2**20),
        cost_estimate=pl.CostEstimate(
            flops=4 * block * width * columns, bytes_accessed=6 * width * columns, transcendentals=0
        ),
        name="own_channels",
    )(gated, pltpu.with_memory_space_constraint(weight, pltpu.HBM))


def split_shards(
    mixer_input,
    gate_branch,
    skip_gain,
    decay_rate,
    first_weight,
    first_bias,
    second_weight,
    second_bias,
    last_weight,
    output_weight,
):
    block, width = mixer_input.shape
    blocks = lax.axis_size("seq")
    outs = width // LANES

    along_seq = lambda part, k: lax.ppermute(part, "seq", [(s, s ^ k) for s in range(blocks)])

    def to_partners(parts):
        return [along_seq(parts[k - 1], k) for k in reversed(range(1, outs))][::-1]

    along_chan = lambda part, k: lax.ppermute(part, "chan", [(c, c ^ k) for c in range(FACE)])
    shape = jax.ShapeDtypeStruct

    xs, *gates, over_x, over_y = call_pack(
        mixer_input, gate_branch, output_weight, blocks, outs
    )
    xs = lax.all_to_all(xs, "seq", 0, 0, tiled=True)
    from_x, from_y = along_chan(over_x, 1), along_chan(over_y, 2)
    filters = call_filter(
        (first_weight, first_bias, second_weight, second_bias, last_weight, decay_rate),
        skip_gain,
        gate_branch,
        blocks,
        outs,
        block,
    )
    gates = to_partners(gates)
    *pieces, from_x, from_y = call_conv(xs, filters, gates, (from_x, from_y), outs)
    pieces = [pieces[0]] + to_partners(pieces[1:])
    from_x, from_y = (from_x, along_seq(from_x, 1)), (from_y, along_seq(from_y, 1))
    gated = in_vmem(
        functools.partial(join_kernel, outs),
        pieces,
        shape((block, width), BF16),
        "join_pieces",
        10**6,
    )
    x_gated, y_gated = along_chan(gated, 1), along_chan(gated, 2)
    send_a, send_b, keep_a, keep_b = call_own(gated, output_weight)
    columns = send_a.shape[1]
    flops = 4 * block * width * columns
    send_a, send_b = in_vmem(
        functools.partial(neighbour_kernel, 1),
        [x_gated, y_gated, *from_x, *from_y, send_a, send_b],
        [shape((block, columns), BF16)] * 2,
        "sums_to_send",
        flops,
    )
    got_a, got_b = along_chan(send_a, 2), along_chan(send_b, 1)
    keep_a, keep_b = in_vmem(
        functools.partial(neighbour_kernel, 0),
        [x_gated, y_gated, *from_x, *from_y, keep_a, keep_b],
        [shape((block, columns), F32)] * 2,
        "sums_to_keep",
        flops,
    )
    return in_vmem(
        last_kernel,
        [keep_a, keep_b, got_a, got_b],
        shape((block, 2 * columns), BF16),
        "last_sum",
        10**6,
    )


def contract_first(left_matrix, right_matrix):
    return lax.dot_general(
        left_matrix,
        right_matrix,
        (((0,), (0,)), ((), ())),
        precision=HIGHEST,
        preferred_element_type=F32,
    )


def filter_taps(
    first_weight, first_bias, second_weight, second_bias, last_weight, decay_rate, length
):
    features = jnp.asarray(feature_table(length, first_weight.shape[0]).T)
    hidden_one = jnp.sin(contract_first(first_weight, features) + first_bias[:, None])
    hidden_two = jnp.sin(contract_first(second_weight, hidden_one) + second_bias[:, None])
    shaped = contract_first(hidden_two, last_weight)
    positions = jnp.arange(length, dtype=jnp.int32).astype(F32)
    envelope = jnp.exp(-decay_rate[None, :] * (positions[:, None] / length))
    energy = jnp.expm1(-2.0 * decay_rate) / jnp.expm1(-2.0 * decay_rate / length)
    return shaped * envelope / jnp.sqrt(energy)[None, :]


def transform_tables(block_len):
    padded_len = 2 * block_len
    freq_index = jnp.arange(block_len + 1, dtype=jnp.int32)[:, None]
    time_index = jnp.arange(padded_len, dtype=jnp.int32)[None, :]
    angle = (freq_index * time_index % padded_len).astype(F32) * (2.0 * math.pi / padded_len)
    forward = jnp.concatenate([jnp.cos(angle), -jnp.sin(angle)], axis=0)
    later_angle = angle[:, block_len:]
    weights = jnp.where((freq_index == 0) | (freq_index == block_len), 1.0, 2.0) / padded_len
    inverse = jnp.concatenate(
        [(weights * jnp.cos(later_angle)).T, (-weights * jnp.sin(later_angle)).T], axis=1
    )
    return (forward, inverse)


def spectral_product(left_spec, right_spec, half_rows):
    left_real, left_imag = (left_spec[:half_rows], left_spec[half_rows:])
    right_real, right_imag = (right_spec[:half_rows], right_spec[half_rows:])
    return jnp.concatenate(
        [
            left_real * right_real - left_imag * right_imag,
            left_real * right_imag + left_imag * right_real,
        ],
        axis=0,
    )


def gathered_shards(
    mixer_input,
    gate_branch,
    skip_gain,
    decay_rate,
    first_weight,
    first_bias,
    second_weight,
    second_bias,
    last_weight,
    output_weight,
):
    block_len, chan_width = mixer_input.shape
    seq_count = lax.axis_size("seq")
    device = lax.axis_index("seq")
    half_rows = block_len + 1
    kernel_taps = filter_taps(
        first_weight,
        first_bias,
        second_weight,
        second_bias,
        last_weight,
        decay_rate,
        block_len * seq_count,
    )
    padded_taps = jnp.concatenate([jnp.zeros((block_len, chan_width), F32), kernel_taps], axis=0)
    forward, inverse = transform_tables(block_len)
    forward_head = forward[:, :block_len]
    gathered = lax.all_gather(mixer_input, "seq", axis=0, tiled=True)

    def one_block(block_index, total):
        rows = lax.dynamic_slice_in_dim(gathered, block_index * block_len, block_len, 0)
        source_spec = jnp.dot(
            forward_head, rows.astype(F32), precision=HIGHEST, preferred_element_type=F32
        )
        segment = lax.dynamic_slice_in_dim(
            padded_taps, (device - block_index) * block_len, 2 * block_len, 0
        )
        lag_spec = jnp.dot(forward, segment, precision=HIGHEST, preferred_element_type=F32)
        return total + spectral_product(lag_spec, source_spec, half_rows)

    total = lax.fori_loop(0, device + 1, one_block, jnp.zeros((2 * half_rows, chan_width), F32))
    convolved = jnp.dot(inverse, total, precision=HIGHEST, preferred_element_type=F32)
    values = mixer_input.astype(F32)
    gated_mix = (
        gate_branch.astype(F32) * (convolved + skip_gain[None, :] * values)
    ).astype(BF16)
    partial_out = jnp.dot(gated_mix, output_weight, preferred_element_type=F32)
    return lax.psum_scatter(partial_out, "chan", scatter_dimension=1, tiled=True).astype(BF16)


def solution(mesh):
    seq_count, chan_count = mesh.shape["seq"], mesh.shape["chan"]

    def shards(mixer_input, *rest):
        block, width = mixer_input.shape
        outs = width // LANES
        splits = (
            width % LANES == 0
            and block % LANES == 0
            and seq_count == 2 * outs
            and outs == 4
            and chan_count == FACE
        )
        plan = split_shards if splits else gathered_shards
        return plan(mixer_input, *rest)

    in_specs = (
        P("seq", "chan"),
        P("seq", "chan"),
        P("chan"),
        P("chan"),
        P(),
        P(),
        P(),
        P(),
        P(None, "chan"),
        P("chan", None),
    )
    out_specs = P("seq", "chan")
    return jax.shard_map(shards, mesh=mesh, in_specs=in_specs, out_specs=out_specs, check_vma=False)
```

```python
import functools
import math

import jax
import jax.numpy as jnp
import numpy as np
from jax import lax
from jax.experimental import pallas as pl
from jax.experimental.pallas import tpu as pltpu
from jax.sharding import PartitionSpec as P

HIGHEST = lax.Precision.HIGHEST
F32 = jnp.float32
BF16 = jnp.bfloat16
LANES = 128
FACE = 4
VMEM = pltpu.VMEM


def feature_table(length, emb_width):
    band_count = (emb_width - 1) // 2
    positions = np.arange(length, dtype=np.int64)
    columns = [positions / length]
    for band in range(1, band_count + 1):
        frequency = min(
            length // 2, max(band, int((length / 2) ** ((band - 1) / (band_count - 1))))
        )
        angle = (positions * frequency % length) * (2.0 * math.pi / length)
        columns.append(np.cos(angle))
        columns.append(np.sin(angle))
    return np.stack(columns, axis=1).astype(np.float32)


def split_bf16(table):
    high = table.astype(np.float32).astype(jnp.bfloat16)
    low = (table - high.astype(np.float64)).astype(np.float32).astype(jnp.bfloat16)
    return high, low


def dft_tables(block):
    size = 2 * block
    bins = np.arange(block)[:, None]
    times = np.arange(block)[None, :]
    angle = (bins * times % size) * (2.0 * math.pi / size)
    imag = -np.sin(angle)
    imag[0] = 1.0 - 2.0 * (np.arange(block) % 2)
    forward = np.concatenate([np.cos(angle), imag], axis=0)
    weight = np.where(bins == 0, 1.0, 2.0) / size
    back_imag = -weight * np.sin(angle)
    back_imag[0] = (1.0 - 2.0 * (np.arange(block) % 2)) / size
    inverse = np.concatenate([weight * np.cos(angle), back_imag], axis=0).T
    return forward, inverse


def fast_sin(x):
    turns = jnp.floor(x * (1.0 / math.pi) + 0.5)
    rest = x - turns * 3.140625
    rest = rest - turns * 9.67502593994140625e-4
    rest = rest - turns * 1.509957990978376432e-7
    parity = turns - 2.0 * jnp.floor(turns * 0.5)
    rest = rest * (1.0 - 2.0 * parity)
    square = rest * rest
    poly = -2.5052108e-8
    for coeff in (2.7557319e-6, -1.9841270e-4, 8.3333333e-3, -1.6666667e-1):
        poly = poly * square + coeff
    return rest + rest * square * poly


def expm1_of_negative(x):
    near = jnp.maximum(x, -0.5)
    series = jnp.full_like(x, 1.0 / 3628800.0)
    for denom in (362880.0, 40320.0, 5040.0, 720.0, 120.0, 24.0, 6.0, 2.0, 1.0):
        series = series * near + 1.0 / denom
    return jnp.where(x > -0.5, near * series, jnp.exp(x) - 1.0)


def split_value(value):
    high = value.astype(BF16)
    return high, (value - high.astype(F32)).astype(BF16)


def filter_feature_table(length, emb_width, pad):
    table = feature_table(length, emb_width)
    columns = []
    for half in (table[: length // 2], table[length // 2 :]):
        high, low = (part.astype(np.float32) for part in split_bf16(half))
        for part in (high, high, low):
            columns.append(np.pad(part, ((0, 0), (0, pad - emb_width))))
    return np.concatenate(columns, axis=1)


def twice_diagonal(value):
    zero = jnp.zeros_like(value)
    return jnp.concatenate(
        [jnp.concatenate([value, zero], axis=1), jnp.concatenate([zero, value], axis=1)], axis=0
    )


def stacked_diagonal(value):
    high, low = split_value(value)
    high = twice_diagonal(high.astype(F32))
    low = twice_diagonal(low.astype(F32))
    return jnp.concatenate([high, low, high], axis=0).astype(BF16)


def layer(value, weight):
    high, low = split_value(value)
    return jnp.dot(
        jnp.concatenate([high, high, low], axis=1), weight, preferred_element_type=F32
    )


def filter_kernel(blocks, block, outs, pad, *refs):
    hbm, refs = refs[:11], refs[11:]
    hre_ref, him_ref, hfirst_ref, fwd_ref, inv_ref, skip_ref, gate_ref = refs[:7]
    refs = refs[7:]
    w1_ref, b1_ref, w2_ref, b2_ref, w3_ref, decay_ref, feat_ref, table_ref, back_ref = refs[:9]
    all_skip_ref, first_ref, sems = refs[9:]
    targets = [
        w1_ref, feat_ref, b1_ref, w2_ref, b2_ref, w3_ref, decay_ref, table_ref, back_ref,
        all_skip_ref,
    ]
    copies = [
        pltpu.make_async_copy(hbm[i], targets[i], sems.at[i]) for i in range(len(targets))
    ]
    group = lax.axis_index("seq") % outs
    lanes = pl.ds(pl.multiple_of(group * LANES, LANES), LANES)
    copies.append(pltpu.make_async_copy(hbm[10].at[:, lanes], gate_ref, sems.at[10]))
    for copy in copies:
        copy.start()
    length = blocks * block
    emb, order = w1_ref.shape
    first_ref[...] = jnp.zeros_like(first_ref)
    for copy in copies[:7]:
        copy.wait()

    high, low = split_value(w1_ref[...])
    high, low = high.astype(F32), low.astype(F32)
    zero = jnp.zeros_like(high)
    for i, part in enumerate((high, low, high)):
        first_ref[i * pad : i * pad + emb] = jnp.concatenate([part, zero], axis=1)
        first_ref[(3 + i) * pad : (3 + i) * pad + emb] = jnp.concatenate([zero, part], axis=1)
    b1 = jnp.concatenate([b1_ref[...]] * 2, axis=1)
    b2 = jnp.concatenate([b2_ref[...]] * 2, axis=1)
    hidden = fast_sin(
        jnp.dot(
            feat_ref[...].astype(BF16), first_ref[...].astype(BF16), preferred_element_type=F32
        )
        + b1
    )
    hidden = fast_sin(layer(hidden, stacked_diagonal(w2_ref[...])) + b2)
    shaped = layer(hidden, stacked_diagonal(w3_ref[:, lanes]))

    decay = decay_ref[:, lanes]
    energy = expm1_of_negative(-2.0 * decay) / expm1_of_negative(decay * (-2.0 / length))
    times = lax.broadcasted_iota(jnp.int32, (length // 2, LANES), 0).astype(F32) * (1.0 / length)
    window = jnp.exp(-(decay * times)) * (1.0 / jnp.sqrt(energy))
    window = jnp.concatenate([window, window * jnp.exp(-0.5 * decay)], axis=1)
    taps_high, taps_low = split_value(shaped * window)

    copies[7].wait()
    high, low = split_value(table_ref[...])
    fwd_ref[:, :block] = high
    fwd_ref[:, block:] = low
    table = jnp.concatenate([high, low, high], axis=1)
    rows = lax.broadcasted_iota(jnp.int32, (2 * block, LANES), 0)
    sign = (1 - 2 * lax.rem(rows, 2)).astype(F32)
    first_row = lax.broadcasted_iota(jnp.int32, (block, LANES), 0) == 0
    spectra = [None] * blocks
    for k in range(blocks // 2):
        part = slice(k * block, (k + 1) * block)
        stacked = jnp.concatenate([taps_high[part], taps_high[part], taps_low[part]], axis=0)
        now = jnp.dot(table, stacked, preferred_element_type=F32)
        spectra[k], spectra[k + blocks // 2] = now[:, :LANES], now[:, LANES:]
    for k in range(blocks):
        spec = spectra[k] if k == 0 else spectra[k] + sign * spectra[k - 1]
        real, imag = spec[:block], spec[block:]
        hre_ref[k] = real
        him_ref[k] = jnp.where(first_row, 0.0, imag)
        hfirst_ref[k] = jnp.where(first_row, imag, real)[:8]

    for copy in copies[8:]:
        copy.wait()
    skip_ref[...] = all_skip_ref[:, lanes]
    high, low = split_value(back_ref[...])
    inv_ref[:, : 2 * block] = high
    inv_ref[:, 2 * block : 4 * block] = low
    inv_ref[:, 4 * block :] = high


def call_filter(weights, skip, gate, blocks, outs, block):
    w1, b1, w2, b2, w3, decay = weights
    length = blocks * block
    emb, order = w1.shape
    pad = -(-emb // 8) * 8
    forward, inverse = dft_tables(block)
    feats = filter_feature_table(length, emb, pad)
    hbm = [
        w1, feats, b1[None], w2, b2[None], w3, decay[None], forward.astype(np.float32),
        inverse.astype(np.float32), skip[None], gate,
    ]
    out_shape = [
        VMEM((blocks, block, LANES), F32),
        VMEM((blocks, block, LANES), F32),
        VMEM((blocks, 8, LANES), F32),
        VMEM((2 * block, 2 * block), BF16),
        VMEM((block, 6 * block), BF16),
        VMEM((1, LANES), F32),
        VMEM((block, LANES), BF16),
    ]
    return pl.pallas_call(
        functools.partial(filter_kernel, blocks, block, outs, pad),
        in_specs=[pl.BlockSpec(memory_space=pltpu.HBM)] * len(hbm),
        out_specs=[pl.BlockSpec(memory_space=VMEM)] * len(out_shape),
        out_shape=out_shape,
        scratch_shapes=[
            VMEM(w1.shape, F32),
            VMEM((1, order), F32),
            VMEM(w2.shape, F32),
            VMEM((1, order), F32),
            VMEM(w3.shape, F32),
            VMEM((1, w3.shape[1]), F32),
            VMEM(feats.shape, F32),
            VMEM(forward.shape, F32),
            VMEM(inverse.shape, F32),
            VMEM((1, skip.shape[0]), F32),
            VMEM((6 * pad, 2 * order), F32),
            pltpu.SemaphoreType.DMA((len(hbm),)),
        ],
        compiler_params=pltpu.CompilerParams(vmem_limit_bytes=32 * 2**20),
        cost_estimate=pl.CostEstimate(
            flops=4 * 10**8, bytes_accessed=8 * 2**20, transcendentals=length * LANES
        ),
        name="filter_spectra",
    )(*(pltpu.with_memory_space_constraint(jnp.asarray(each), pltpu.HBM) for each in hbm))


def rounds(core):
    return 1 + core, 2 - core


def block_of(part, width):
    return pl.ds(pl.multiple_of(part * width, LANES), width)


def pack_kernel(blocks, outs, x_ref, gate_ref, weight_ref, pieces_ref, *refs):
    gate_refs, refs = refs[: outs - 1], refs[outs - 1 :]
    over_ref, x_held_ref, gate_held_ref, sems = refs
    group = lax.axis_index("seq") % outs
    width = weight_ref.shape[1] // FACE
    gathered, summed = rounds(lax.axis_index("seq") % 2)
    partner = lax.axis_index("chan") ^ gathered
    arrive = [
        pltpu.make_async_copy(x_ref, x_held_ref, sems.at[0]),
        pltpu.make_async_copy(gate_ref, gate_held_ref, sems.at[1]),
    ]
    others = [
        pltpu.make_async_copy(
            weight_ref.at[:, block_of(part, width)],
            over_ref.at[:, place * width : (place + 1) * width],
            sems.at[2 + place],
        )
        for place, part in enumerate((partner, partner ^ summed))
    ]
    for copy in arrive + others:
        copy.start()
    first = 2 + len(others)
    leave = [
        pltpu.make_async_copy(
            x_held_ref.at[:, (d % outs) * LANES : (d % outs + 1) * LANES],
            pieces_ref.at[d],
            sems.at[first + d],
        )
        for d in range(blocks)
    ]
    first += blocks
    for k in range(1, outs):
        lanes = pl.ds(pl.multiple_of((group ^ k) * LANES, LANES), LANES)
        leave.append(
            pltpu.make_async_copy(
                gate_held_ref.at[:, lanes], gate_refs[k - 1], sems.at[first + k - 1]
            )
        )
    arrive[0].wait()
    for copy in leave[:blocks]:
        copy.start()
    arrive[1].wait()
    for copy in leave[blocks:]:
        copy.start()
    for copy in others + leave:
        copy.wait()


def call_pack(x, gate, weight, blocks, outs):
    block = x.shape[0]
    send = VMEM((weight.shape[0], weight.shape[1] // 2), BF16)
    out_shape = [pltpu.HBM((blocks, block, LANES), BF16)]
    out_shape += [pltpu.HBM((block, LANES), BF16)] * (outs - 1) + [send]
    return pl.pallas_call(
        functools.partial(pack_kernel, blocks, outs),
        in_specs=[pl.BlockSpec(memory_space=pltpu.HBM)] * 3,
        out_specs=[pl.BlockSpec(memory_space=pltpu.HBM)] * outs
        + [pl.BlockSpec(memory_space=VMEM)],
        out_shape=out_shape,
        scratch_shapes=[
            VMEM(x.shape, BF16),
            VMEM(gate.shape, BF16),
            pltpu.SemaphoreType.DMA((blocks + outs + 3,)),
        ],
        compiler_params=pltpu.CompilerParams(vmem_limit_bytes=16 * 2**20),
        cost_estimate=pl.CostEstimate(flops=0, bytes_accessed=2**21, transcendentals=0),
        name="pack_pieces",
    )(*(pltpu.with_memory_space_constraint(each, pltpu.HBM) for each in (x, gate, weight)))


def conv_kernel(blocks, outs, block, xs_ref, *refs):
    hre_ref, him_ref, hfirst_ref, fwd_ref, inv_ref, skip_ref = refs[:6]
    gate_refs, refs = refs[6 : 6 + outs], refs[6 + outs :]
    out_refs, (wre_ref, wim_ref, yre_ref, yim_ref) = refs[:outs], refs[outs:]
    me = lax.axis_index("seq")
    half, group = me // outs, me % outs
    earlier = blocks - outs
    for j in range(outs):
        values = jnp.concatenate([xs_ref[j], xs_ref[half * outs + j]], axis=1)
        spec = jnp.dot(
            fwd_ref[...], jnp.concatenate([values, values], axis=0), preferred_element_type=F32
        )
        before = jnp.where(half > 0, spec[:, :LANES], 0.0)
        wre_ref[j] = before[:block]
        wim_ref[j] = before[block:]
        wre_ref[earlier + j] = spec[:block, LANES:]
        wim_ref[earlier + j] = spec[block:, LANES:]

    def rows_at(start, first):
        rows = pl.ds(start, 8)
        wre = [wre_ref[j, rows, :] for j in range(blocks)]
        wim = [wim_ref[j, rows, :] for j in range(blocks)]
        for o in range(outs):
            total_re = total_im = None
            for j in range(earlier + o + 1):
                k = earlier + o - j
                hre = hre_ref[k, rows, :]
                him = him_ref[k, rows, :]
                hother = hfirst_ref[k] if first else hre
                add_re = wre[j] * hre - wim[j] * him
                add_im = wre[j] * him + wim[j] * hother
                total_re = add_re if total_re is None else total_re + add_re
                total_im = add_im if total_im is None else total_im + add_im
            yre_ref[o, rows, :] = total_re
            yim_ref[o, rows, :] = total_im

    rows_at(0, True)

    @pl.loop(1, block // 8)
    def _(tile):
        rows_at(pl.multiple_of(tile * 8, 8), False)

    def stacked(slot):
        re_high, re_low = split_value(yre_ref[slot])
        im_high, im_low = split_value(yim_ref[slot])
        return jnp.concatenate([re_high, im_high, re_high, im_high, re_low, im_low], axis=0)

    skip = skip_ref[...]
    for k in range(0, outs, 2):
        pair = jnp.concatenate([stacked(group ^ k), stacked(group ^ (k + 1))], axis=1)
        conv = jnp.dot(inv_ref[...], pair, preferred_element_type=F32)
        for i in range(2):
            values = xs_ref[half * outs + (group ^ (k + i))].astype(F32)
            gate = gate_refs[k + i][...].astype(F32)
            mixed = conv[:, i * LANES : (i + 1) * LANES] + skip * values
            out_refs[k + i][...] = (gate * mixed).astype(BF16)


def call_conv(xs, filters, gates, outs):
    blocks, block, _ = xs.shape
    pinned = [pltpu.with_memory_space_constraint(each, VMEM) for each in filters]
    operands = [xs, *pinned, *gates]
    shape = jax.ShapeDtypeStruct
    return pl.pallas_call(
        functools.partial(conv_kernel, blocks, outs, block),
        in_specs=[pl.BlockSpec(memory_space=VMEM)] * len(operands),
        out_specs=[pl.BlockSpec(memory_space=VMEM)] * outs,
        out_shape=[shape((block, LANES), BF16)] * outs,
        scratch_shapes=[
            VMEM((blocks, block, LANES), F32),
            VMEM((blocks, block, LANES), F32),
            VMEM((outs, block, LANES), F32),
            VMEM((outs, block, LANES), F32),
        ],
        compiler_params=pltpu.CompilerParams(vmem_limit_bytes=16 * 2**20),
        cost_estimate=pl.CostEstimate(
            flops=2 * 10**8, bytes_accessed=3 * 2**20, transcendentals=0
        ),
        name="convolve",
    )(*operands)


def join_kernel(outs, *refs):
    piece_refs, joined_ref = refs[:outs], refs[outs]
    group = lax.axis_index("seq") % outs
    for k in range(outs):
        lanes = pl.ds(pl.multiple_of((group ^ k) * LANES, LANES), LANES)
        joined_ref[:, lanes] = piece_refs[k][...]


def tiles(width):
    step = min(width, 2 * LANES)
    return [slice(start, start + step) for start in range(0, width, step)]


def own_kernel(width, gated_ref, weight_ref, send_ref, keep_ref, held_ref, sems):
    me = lax.axis_index("chan")
    _, summed = rounds(lax.axis_index("seq") % 2)
    half = width // 2
    copies = []
    for i in range(4):
        part = me ^ summed if i < 2 else me
        lanes = pl.ds(pl.multiple_of(part * width + (i % 2) * half, LANES), half)
        copies.append(
            pltpu.make_async_copy(weight_ref.at[:, lanes], held_ref.at[i], sems.at[i])
        )
    for copy in copies:
        copy.start()
    left = gated_ref[...]
    for i, copy in enumerate(copies):
        copy.wait()
        out_ref = send_ref if i < 2 else keep_ref
        for lanes in tiles(half):
            place = slice((i % 2) * half + lanes.start, (i % 2) * half + lanes.stop)
            out_ref[:, place] = jnp.dot(left, held_ref[i, :, lanes], preferred_element_type=F32)


def neighbour_kernel(first, theirs_ref, held_ref, sum_ref, out_ref):
    left = theirs_ref[...]
    for lanes in tiles(out_ref.shape[1]):
        place = slice(first + lanes.start, first + lanes.stop)
        total = jnp.dot(left, held_ref[:, place], preferred_element_type=F32)
        out_ref[:, lanes] = (sum_ref[:, lanes] + total).astype(out_ref.dtype)


def last_kernel(sum_ref, arrived_ref, out_ref):
    out_ref[...] = (sum_ref[...] + arrived_ref[...].astype(F32)).astype(BF16)


def in_vmem(kernel, operands, out_shape, name, flops, scratch=()):
    return pl.pallas_call(
        kernel,
        in_specs=[pl.BlockSpec(memory_space=VMEM)] * len(operands),
        out_specs=jax.tree.map(lambda _: pl.BlockSpec(memory_space=VMEM), out_shape),
        out_shape=out_shape,
        scratch_shapes=scratch,
        compiler_params=pltpu.CompilerParams(vmem_limit_bytes=16 * 2**20),
        cost_estimate=pl.CostEstimate(flops=flops, bytes_accessed=2**20, transcendentals=0),
        name=name,
    )(*operands)


def call_own(gated, weight):
    block, width = gated.shape
    columns = weight.shape[1] // FACE
    return pl.pallas_call(
        functools.partial(own_kernel, columns),
        in_specs=[pl.BlockSpec(memory_space=VMEM), pl.BlockSpec(memory_space=pltpu.HBM)],
        out_specs=[pl.BlockSpec(memory_space=VMEM)] * 2,
        out_shape=[jax.ShapeDtypeStruct((block, columns), F32)] * 2,
        scratch_shapes=[
            VMEM((4, width, columns // 2), BF16),
            pltpu.SemaphoreType.DMA((4,)),
        ],
        compiler_params=pltpu.CompilerParams(vmem_limit_bytes=16 * 2**20),
        cost_estimate=pl.CostEstimate(
            flops=4 * block * width * columns, bytes_accessed=6 * width * columns, transcendentals=0
        ),
        name="own_channels",
    )(gated, pltpu.with_memory_space_constraint(weight, pltpu.HBM))


def split_shards(
    mixer_input,
    gate_branch,
    skip_gain,
    decay_rate,
    first_weight,
    first_bias,
    second_weight,
    second_bias,
    last_weight,
    output_weight,
):
    block, width = mixer_input.shape
    blocks = lax.axis_size("seq")
    outs = width // LANES

    along_seq = lambda part, k: lax.ppermute(part, "seq", [(s, s ^ k) for s in range(blocks)])
    def along_chan(part, turn):
        pairs = [
            (s * FACE + c, s * FACE + (c ^ rounds(s % 2)[turn]))
            for s in range(blocks)
            for c in range(FACE)
        ]
        return lax.ppermute(part, ("seq", "chan"), pairs)

    shape = jax.ShapeDtypeStruct

    xs, *gates, over = call_pack(mixer_input, gate_branch, output_weight, blocks, outs)
    xs = lax.all_to_all(xs, "seq", 0, 0, tiled=True)
    held = along_chan(over, 0)
    filters = call_filter(
        (first_weight, first_bias, second_weight, second_bias, last_weight, decay_rate),
        skip_gain,
        gate_branch,
        blocks,
        outs,
        block,
    )
    gates = [along_seq(gates[k - 1], k) for k in range(1, outs)]
    pieces = call_conv(xs, filters, gates, outs)
    pieces = [pieces[0]] + [along_seq(pieces[k], k) for k in range(1, outs)]
    gated = in_vmem(
        functools.partial(join_kernel, outs),
        pieces,
        shape((block, width), BF16),
        "join_pieces",
        10**6,
    )
    theirs = along_chan(gated, 0)
    send, keep = call_own(gated, output_weight)
    columns = send.shape[1]
    flops = 2 * block * width * columns
    send = in_vmem(
        functools.partial(neighbour_kernel, columns),
        [theirs, held, send],
        shape((block, columns), BF16),
        "sums_to_send",
        flops,
    )
    arrived = along_chan(send, 1)
    keep = in_vmem(
        functools.partial(neighbour_kernel, 0),
        [theirs, held, keep],
        shape((block, columns), F32),
        "sums_to_keep",
        flops,
    )
    return in_vmem(
        last_kernel, [keep, arrived], shape((block, columns), BF16), "last_sum", 10**6
    )


def contract_first(left_matrix, right_matrix):
    return lax.dot_general(
        left_matrix,
        right_matrix,
        (((0,), (0,)), ((), ())),
        precision=HIGHEST,
        preferred_element_type=F32,
    )


def filter_taps(
    first_weight, first_bias, second_weight, second_bias, last_weight, decay_rate, length
):
    features = jnp.asarray(feature_table(length, first_weight.shape[0]).T)
    hidden_one = jnp.sin(contract_first(first_weight, features) + first_bias[:, None])
    hidden_two = jnp.sin(contract_first(second_weight, hidden_one) + second_bias[:, None])
    shaped = contract_first(hidden_two, last_weight)
    positions = jnp.arange(length, dtype=jnp.int32).astype(F32)
    envelope = jnp.exp(-decay_rate[None, :] * (positions[:, None] / length))
    energy = jnp.expm1(-2.0 * decay_rate) / jnp.expm1(-2.0 * decay_rate / length)
    return shaped * envelope / jnp.sqrt(energy)[None, :]


def transform_tables(block_len):
    padded_len = 2 * block_len
    freq_index = jnp.arange(block_len + 1, dtype=jnp.int32)[:, None]
    time_index = jnp.arange(padded_len, dtype=jnp.int32)[None, :]
    angle = (freq_index * time_index % padded_len).astype(F32) * (2.0 * math.pi / padded_len)
    forward = jnp.concatenate([jnp.cos(angle), -jnp.sin(angle)], axis=0)
    later_angle = angle[:, block_len:]
    weights = jnp.where((freq_index == 0) | (freq_index == block_len), 1.0, 2.0) / padded_len
    inverse = jnp.concatenate(
        [(weights * jnp.cos(later_angle)).T, (-weights * jnp.sin(later_angle)).T], axis=1
    )
    return (forward, inverse)


def spectral_product(left_spec, right_spec, half_rows):
    left_real, left_imag = (left_spec[:half_rows], left_spec[half_rows:])
    right_real, right_imag = (right_spec[:half_rows], right_spec[half_rows:])
    return jnp.concatenate(
        [
            left_real * right_real - left_imag * right_imag,
            left_real * right_imag + left_imag * right_real,
        ],
        axis=0,
    )


def gathered_shards(
    mixer_input,
    gate_branch,
    skip_gain,
    decay_rate,
    first_weight,
    first_bias,
    second_weight,
    second_bias,
    last_weight,
    output_weight,
):
    block_len, chan_width = mixer_input.shape
    seq_count = lax.axis_size("seq")
    device = lax.axis_index("seq")
    half_rows = block_len + 1
    kernel_taps = filter_taps(
        first_weight,
        first_bias,
        second_weight,
        second_bias,
        last_weight,
        decay_rate,
        block_len * seq_count,
    )
    padded_taps = jnp.concatenate([jnp.zeros((block_len, chan_width), F32), kernel_taps], axis=0)
    forward, inverse = transform_tables(block_len)
    forward_head = forward[:, :block_len]
    gathered = lax.all_gather(mixer_input, "seq", axis=0, tiled=True)

    def one_block(block_index, total):
        rows = lax.dynamic_slice_in_dim(gathered, block_index * block_len, block_len, 0)
        source_spec = jnp.dot(
            forward_head, rows.astype(F32), precision=HIGHEST, preferred_element_type=F32
        )
        segment = lax.dynamic_slice_in_dim(
            padded_taps, (device - block_index) * block_len, 2 * block_len, 0
        )
        lag_spec = jnp.dot(forward, segment, precision=HIGHEST, preferred_element_type=F32)
        return total + spectral_product(lag_spec, source_spec, half_rows)

    total = lax.fori_loop(0, device + 1, one_block, jnp.zeros((2 * half_rows, chan_width), F32))
    convolved = jnp.dot(inverse, total, precision=HIGHEST, preferred_element_type=F32)
    values = mixer_input.astype(F32)
    gated_mix = (
        gate_branch.astype(F32) * (convolved + skip_gain[None, :] * values)
    ).astype(BF16)
    partial_out = jnp.dot(gated_mix, output_weight, preferred_element_type=F32)
    return lax.psum_scatter(partial_out, "chan", scatter_dimension=1, tiled=True).astype(BF16)


def solution(mesh):
    seq_count, chan_count = mesh.shape["seq"], mesh.shape["chan"]

    def shards(mixer_input, *rest):
        block, width = mixer_input.shape
        outs = width // LANES
        splits = (
            width % LANES == 0
            and block % LANES == 0
            and seq_count == 2 * outs
            and outs == 4
            and chan_count == FACE
        )
        plan = split_shards if splits else gathered_shards
        return plan(mixer_input, *rest)

    in_specs = (
        P("seq", "chan"),
        P("seq", "chan"),
        P("chan"),
        P("chan"),
        P(),
        P(),
        P(),
        P(),
        P(None, "chan"),
        P("chan", None),
    )
    out_specs = P("seq", "chan")
    return jax.shard_map(shards, mesh=mesh, in_specs=in_specs, out_specs=out_specs, check_vma=False)
```

```python
import functools
import math

import jax
import jax.numpy as jnp
import numpy as np
from jax import lax
from jax.experimental import pallas as pl
from jax.experimental.pallas import tpu as pltpu
from jax.sharding import PartitionSpec as P

HIGHEST = lax.Precision.HIGHEST
F32 = jnp.float32
BF16 = jnp.bfloat16
LANES = 128
FACE = 4
VMEM = pltpu.VMEM


def feature_table(length, emb_width):
    band_count = (emb_width - 1) // 2
    positions = np.arange(length, dtype=np.int64)
    columns = [positions / length]
    for band in range(1, band_count + 1):
        frequency = min(
            length // 2, max(band, int((length / 2) ** ((band - 1) / (band_count - 1))))
        )
        angle = (positions * frequency % length) * (2.0 * math.pi / length)
        columns.append(np.cos(angle))
        columns.append(np.sin(angle))
    return np.stack(columns, axis=1).astype(np.float32)


def split_bf16(table):
    high = table.astype(np.float32).astype(jnp.bfloat16)
    low = (table - high.astype(np.float64)).astype(np.float32).astype(jnp.bfloat16)
    return high, low


def dft_tables(block):
    size = 2 * block
    bins = np.arange(block)[:, None]
    times = np.arange(block)[None, :]
    angle = (bins * times % size) * (2.0 * math.pi / size)
    imag = -np.sin(angle)
    imag[0] = 1.0 - 2.0 * (np.arange(block) % 2)
    forward = np.concatenate([np.cos(angle), imag], axis=0)
    weight = np.where(bins == 0, 1.0, 2.0) / size
    back_imag = -weight * np.sin(angle)
    back_imag[0] = (1.0 - 2.0 * (np.arange(block) % 2)) / size
    inverse = np.concatenate([weight * np.cos(angle), back_imag], axis=0).T
    return forward, inverse


def fast_sin(x):
    turns = jnp.floor(x * (1.0 / math.pi) + 0.5)
    rest = x - turns * 3.140625
    rest = rest - turns * 9.67502593994140625e-4
    rest = rest - turns * 1.509957990978376432e-7
    parity = turns - 2.0 * jnp.floor(turns * 0.5)
    rest = rest * (1.0 - 2.0 * parity)
    square = rest * rest
    poly = -2.5052108e-8
    for coeff in (2.7557319e-6, -1.9841270e-4, 8.3333333e-3, -1.6666667e-1):
        poly = poly * square + coeff
    return rest + rest * square * poly


def expm1_of_negative(x):
    near = jnp.maximum(x, -0.5)
    series = jnp.full_like(x, 1.0 / 3628800.0)
    for denom in (362880.0, 40320.0, 5040.0, 720.0, 120.0, 24.0, 6.0, 2.0, 1.0):
        series = series * near + 1.0 / denom
    return jnp.where(x > -0.5, near * series, jnp.exp(x) - 1.0)


def split_value(value):
    high = value.astype(BF16)
    return high, (value - high.astype(F32)).astype(BF16)


def filter_feature_table(length, emb_width, pad):
    table = feature_table(length, emb_width)
    columns = []
    for half in (table[: length // 2], table[length // 2 :]):
        high, low = (part.astype(np.float32) for part in split_bf16(half))
        for part in (high, high, low):
            columns.append(np.pad(part, ((0, 0), (0, pad - emb_width))))
    return np.concatenate(columns, axis=1)


def twice_diagonal(value):
    zero = jnp.zeros_like(value)
    return jnp.concatenate(
        [jnp.concatenate([value, zero], axis=1), jnp.concatenate([zero, value], axis=1)], axis=0
    )


def stacked_diagonal(value):
    high, low = split_value(value)
    high = twice_diagonal(high.astype(F32))
    low = twice_diagonal(low.astype(F32))
    return jnp.concatenate([high, low, high], axis=0).astype(BF16)


def layer(value, weight):
    high, low = split_value(value)
    return jnp.dot(
        jnp.concatenate([high, high, low], axis=1), weight, preferred_element_type=F32
    )


def filter_kernel(blocks, block, outs, pad, *refs):
    hbm, refs = refs[:11], refs[11:]
    hre_ref, him_ref, hfirst_ref, fwd_ref, inv_ref, skip_ref, gate_ref = refs[:7]
    refs = refs[7:]
    w1_ref, b1_ref, w2_ref, b2_ref, w3_ref, decay_ref, feat_ref, table_ref, back_ref = refs[:9]
    all_skip_ref, first_ref, sems = refs[9:]
    targets = [
        w1_ref, feat_ref, b1_ref, w2_ref, b2_ref, w3_ref, decay_ref, table_ref, back_ref,
        all_skip_ref,
    ]
    copies = [
        pltpu.make_async_copy(hbm[i], targets[i], sems.at[i]) for i in range(len(targets))
    ]
    group = lax.axis_index("seq") % outs
    lanes = pl.ds(pl.multiple_of(group * LANES, LANES), LANES)
    copies.append(pltpu.make_async_copy(hbm[10].at[:, lanes], gate_ref, sems.at[10]))
    for copy in copies:
        copy.start()
    length = blocks * block
    emb, order = w1_ref.shape
    first_ref[...] = jnp.zeros_like(first_ref)
    for copy in copies[:7]:
        copy.wait()

    high, low = split_value(w1_ref[...])
    high, low = high.astype(F32), low.astype(F32)
    zero = jnp.zeros_like(high)
    for i, part in enumerate((high, low, high)):
        first_ref[i * pad : i * pad + emb] = jnp.concatenate([part, zero], axis=1)
        first_ref[(3 + i) * pad : (3 + i) * pad + emb] = jnp.concatenate([zero, part], axis=1)
    b1 = jnp.concatenate([b1_ref[...]] * 2, axis=1)
    b2 = jnp.concatenate([b2_ref[...]] * 2, axis=1)
    hidden = fast_sin(
        jnp.dot(
            feat_ref[...].astype(BF16), first_ref[...].astype(BF16), preferred_element_type=F32
        )
        + b1
    )
    hidden = fast_sin(layer(hidden, stacked_diagonal(w2_ref[...])) + b2)
    shaped = layer(hidden, stacked_diagonal(w3_ref[:, lanes]))

    decay = decay_ref[:, lanes]
    energy = expm1_of_negative(-2.0 * decay) / expm1_of_negative(decay * (-2.0 / length))
    times = lax.broadcasted_iota(jnp.int32, (length // 2, LANES), 0).astype(F32) * (1.0 / length)
    window = jnp.exp(-(decay * times)) * (1.0 / jnp.sqrt(energy))
    window = jnp.concatenate([window, window * jnp.exp(-0.5 * decay)], axis=1)
    taps_high, taps_low = split_value(shaped * window)

    copies[7].wait()
    high, low = split_value(table_ref[...])
    fwd_ref[:, :block] = high
    fwd_ref[:, block:] = low
    table = jnp.concatenate([high, low, high], axis=1)
    rows = lax.broadcasted_iota(jnp.int32, (2 * block, LANES), 0)
    sign = (1 - 2 * lax.rem(rows, 2)).astype(F32)
    first_row = lax.broadcasted_iota(jnp.int32, (block, LANES), 0) == 0
    spectra = [None] * blocks
    for k in range(blocks // 2):
        part = slice(k * block, (k + 1) * block)
        stacked = jnp.concatenate([taps_high[part], taps_high[part], taps_low[part]], axis=0)
        now = jnp.dot(table, stacked, preferred_element_type=F32)
        spectra[k], spectra[k + blocks // 2] = now[:, :LANES], now[:, LANES:]
    for k in range(blocks):
        spec = spectra[k] if k == 0 else spectra[k] + sign * spectra[k - 1]
        real, imag = spec[:block], spec[block:]
        hre_ref[k] = real
        him_ref[k] = jnp.where(first_row, 0.0, imag)
        hfirst_ref[k] = jnp.where(first_row, imag, real)[:8]

    for copy in copies[8:]:
        copy.wait()
    skip_ref[...] = all_skip_ref[:, lanes]
    high, low = split_value(back_ref[...])
    inv_ref[:, : 2 * block] = high
    inv_ref[:, 2 * block : 4 * block] = low
    inv_ref[:, 4 * block :] = high


def call_filter(weights, skip, gate, blocks, outs, block):
    w1, b1, w2, b2, w3, decay = weights
    length = blocks * block
    emb, order = w1.shape
    pad = -(-emb // 8) * 8
    forward, inverse = dft_tables(block)
    feats = filter_feature_table(length, emb, pad)
    hbm = [
        w1, feats, b1[None], w2, b2[None], w3, decay[None], forward.astype(np.float32),
        inverse.astype(np.float32), skip[None], gate,
    ]
    out_shape = [
        VMEM((blocks, block, LANES), F32),
        VMEM((blocks, block, LANES), F32),
        VMEM((blocks, 8, LANES), F32),
        VMEM((2 * block, 2 * block), BF16),
        VMEM((block, 6 * block), BF16),
        VMEM((1, LANES), F32),
        VMEM((block, LANES), BF16),
    ]
    return pl.pallas_call(
        functools.partial(filter_kernel, blocks, block, outs, pad),
        in_specs=[pl.BlockSpec(memory_space=pltpu.HBM)] * len(hbm),
        out_specs=[pl.BlockSpec(memory_space=VMEM)] * len(out_shape),
        out_shape=out_shape,
        scratch_shapes=[
            VMEM(w1.shape, F32),
            VMEM((1, order), F32),
            VMEM(w2.shape, F32),
            VMEM((1, order), F32),
            VMEM(w3.shape, F32),
            VMEM((1, w3.shape[1]), F32),
            VMEM(feats.shape, F32),
            VMEM(forward.shape, F32),
            VMEM(inverse.shape, F32),
            VMEM((1, skip.shape[0]), F32),
            VMEM((6 * pad, 2 * order), F32),
            pltpu.SemaphoreType.DMA((len(hbm),)),
        ],
        compiler_params=pltpu.CompilerParams(vmem_limit_bytes=8 * 2**20),
        cost_estimate=pl.CostEstimate(
            flops=4 * 10**8, bytes_accessed=8 * 2**20, transcendentals=length * LANES
        ),
        name="filter_spectra",
    )(*(pltpu.with_memory_space_constraint(jnp.asarray(each), pltpu.HBM) for each in hbm))


def rounds(core):
    return 1 + core, 2 - core


def block_of(part, width):
    return pl.ds(pl.multiple_of(part * width, LANES), width)


def pack_kernel(blocks, outs, x_ref, gate_ref, weight_ref, pieces_ref, *refs):
    gate_refs, refs = refs[: outs - 1], refs[outs - 1 :]
    over_ref, x_held_ref, gate_held_ref, sems = refs
    group = lax.axis_index("seq") % outs
    width = weight_ref.shape[1] // FACE
    gathered, summed = rounds(lax.axis_index("seq") % 2)
    partner = lax.axis_index("chan") ^ gathered
    arrive = [
        pltpu.make_async_copy(x_ref, x_held_ref, sems.at[0]),
        pltpu.make_async_copy(gate_ref, gate_held_ref, sems.at[1]),
    ]
    others = [
        pltpu.make_async_copy(
            weight_ref.at[:, block_of(part, width)],
            over_ref.at[:, place * width : (place + 1) * width],
            sems.at[2 + place],
        )
        for place, part in enumerate((partner, partner ^ summed))
    ]
    for copy in arrive + others:
        copy.start()
    first = 2 + len(others)
    leave = [
        pltpu.make_async_copy(
            x_held_ref.at[:, (d % outs) * LANES : (d % outs + 1) * LANES],
            pieces_ref.at[d],
            sems.at[first + d],
        )
        for d in range(blocks)
    ]
    first += blocks
    for k in range(1, outs):
        lanes = pl.ds(pl.multiple_of((group ^ k) * LANES, LANES), LANES)
        leave.append(
            pltpu.make_async_copy(
                gate_held_ref.at[:, lanes], gate_refs[k - 1], sems.at[first + k - 1]
            )
        )
    arrive[0].wait()
    for copy in leave[:blocks]:
        copy.start()
    arrive[1].wait()
    for copy in leave[blocks:]:
        copy.start()
    for copy in others + leave:
        copy.wait()


def call_pack(x, gate, weight, blocks, outs):
    block = x.shape[0]
    send = VMEM((weight.shape[0], weight.shape[1] // 2), BF16)
    out_shape = [pltpu.HBM((blocks, block, LANES), BF16)]
    out_shape += [pltpu.HBM((block, LANES), BF16)] * (outs - 1) + [send]
    return pl.pallas_call(
        functools.partial(pack_kernel, blocks, outs),
        in_specs=[pl.BlockSpec(memory_space=pltpu.HBM)] * 3,
        out_specs=[pl.BlockSpec(memory_space=pltpu.HBM)] * outs
        + [pl.BlockSpec(memory_space=VMEM)],
        out_shape=out_shape,
        scratch_shapes=[
            VMEM(x.shape, BF16),
            VMEM(gate.shape, BF16),
            pltpu.SemaphoreType.DMA((blocks + outs + 3,)),
        ],
        compiler_params=pltpu.CompilerParams(vmem_limit_bytes=8 * 2**20),
        cost_estimate=pl.CostEstimate(flops=0, bytes_accessed=2**21, transcendentals=0),
        name="pack_pieces",
    )(*(pltpu.with_memory_space_constraint(each, pltpu.HBM) for each in (x, gate, weight)))


def conv_kernel(blocks, outs, block, xs_ref, *refs):
    hre_ref, him_ref, hfirst_ref, fwd_ref, inv_ref, skip_ref = refs[:6]
    gate_refs, refs = refs[6 : 6 + outs], refs[6 + outs :]
    out_refs, (wre_ref, wim_ref, yre_ref, yim_ref) = refs[:outs], refs[outs:]
    me = lax.axis_index("seq")
    half, group = me // outs, me % outs
    earlier = blocks - outs
    for j in range(outs):
        values = jnp.concatenate([xs_ref[j], xs_ref[half * outs + j]], axis=1)
        spec = jnp.dot(
            fwd_ref[...], jnp.concatenate([values, values], axis=0), preferred_element_type=F32
        )
        before = jnp.where(half > 0, spec[:, :LANES], 0.0)
        wre_ref[j] = before[:block]
        wim_ref[j] = before[block:]
        wre_ref[earlier + j] = spec[:block, LANES:]
        wim_ref[earlier + j] = spec[block:, LANES:]

    def rows_at(start, first):
        rows = pl.ds(start, 8)
        wre = [wre_ref[j, rows, :] for j in range(blocks)]
        wim = [wim_ref[j, rows, :] for j in range(blocks)]
        for o in range(outs):
            total_re = total_im = None
            for j in range(earlier + o + 1):
                k = earlier + o - j
                hre = hre_ref[k, rows, :]
                him = him_ref[k, rows, :]
                hother = hfirst_ref[k] if first else hre
                add_re = wre[j] * hre - wim[j] * him
                add_im = wre[j] * him + wim[j] * hother
                total_re = add_re if total_re is None else total_re + add_re
                total_im = add_im if total_im is None else total_im + add_im
            yre_ref[o, rows, :] = total_re
            yim_ref[o, rows, :] = total_im

    rows_at(0, True)

    @pl.loop(1, block // 8)
    def _(tile):
        rows_at(pl.multiple_of(tile * 8, 8), False)

    def stacked(slot):
        re_high, re_low = split_value(yre_ref[slot])
        im_high, im_low = split_value(yim_ref[slot])
        return jnp.concatenate([re_high, im_high, re_high, im_high, re_low, im_low], axis=0)

    skip = skip_ref[...]
    for k in range(0, outs, 2):
        pair = jnp.concatenate([stacked(group ^ k), stacked(group ^ (k + 1))], axis=1)
        conv = jnp.dot(inv_ref[...], pair, preferred_element_type=F32)
        for i in range(2):
            values = xs_ref[half * outs + (group ^ (k + i))].astype(F32)
            gate = gate_refs[k + i][...].astype(F32)
            mixed = conv[:, i * LANES : (i + 1) * LANES] + skip * values
            out_refs[k + i][...] = (gate * mixed).astype(BF16)


def call_conv(xs, filters, gates, outs):
    blocks, block, _ = xs.shape
    pinned = [pltpu.with_memory_space_constraint(each, VMEM) for each in filters]
    operands = [xs, *pinned, *gates]
    shape = jax.ShapeDtypeStruct
    return pl.pallas_call(
        functools.partial(conv_kernel, blocks, outs, block),
        in_specs=[pl.BlockSpec(memory_space=VMEM)] * len(operands),
        out_specs=[pl.BlockSpec(memory_space=VMEM)] * outs,
        out_shape=[shape((block, LANES), BF16)] * outs,
        scratch_shapes=[
            VMEM((blocks, block, LANES), F32),
            VMEM((blocks, block, LANES), F32),
            VMEM((outs, block, LANES), F32),
            VMEM((outs, block, LANES), F32),
        ],
        compiler_params=pltpu.CompilerParams(vmem_limit_bytes=8 * 2**20),
        cost_estimate=pl.CostEstimate(
            flops=2 * 10**8, bytes_accessed=3 * 2**20, transcendentals=0
        ),
        name="convolve",
    )(*operands)


def join_kernel(outs, *refs):
    piece_refs, joined_ref = refs[:outs], refs[outs]
    group = lax.axis_index("seq") % outs
    for k in range(outs):
        lanes = pl.ds(pl.multiple_of((group ^ k) * LANES, LANES), LANES)
        joined_ref[:, lanes] = piece_refs[k][...]


def tiles(width):
    step = min(width, 2 * LANES)
    return [slice(start, start + step) for start in range(0, width, step)]


def own_kernel(width, gated_ref, weight_ref, send_ref, keep_ref, held_ref, sems):
    me = lax.axis_index("chan")
    _, summed = rounds(lax.axis_index("seq") % 2)
    half = width // 2
    copies = []
    for i in range(4):
        part = me ^ summed if i < 2 else me
        lanes = pl.ds(pl.multiple_of(part * width + (i % 2) * half, LANES), half)
        copies.append(
            pltpu.make_async_copy(weight_ref.at[:, lanes], held_ref.at[i], sems.at[i])
        )
    for copy in copies:
        copy.start()
    left = gated_ref[...]
    for i, copy in enumerate(copies):
        copy.wait()
        out_ref = send_ref if i < 2 else keep_ref
        for lanes in tiles(half):
            place = slice((i % 2) * half + lanes.start, (i % 2) * half + lanes.stop)
            out_ref[:, place] = jnp.dot(left, held_ref[i, :, lanes], preferred_element_type=F32)


def neighbour_kernel(first, theirs_ref, held_ref, sum_ref, out_ref):
    left = theirs_ref[...]
    for lanes in tiles(out_ref.shape[1]):
        place = slice(first + lanes.start, first + lanes.stop)
        total = jnp.dot(left, held_ref[:, place], preferred_element_type=F32)
        out_ref[:, lanes] = (sum_ref[:, lanes] + total).astype(out_ref.dtype)


def last_kernel(sum_ref, arrived_ref, out_ref):
    out_ref[...] = (sum_ref[...] + arrived_ref[...].astype(F32)).astype(BF16)


def in_vmem(kernel, operands, out_shape, name, flops, scratch=()):
    return pl.pallas_call(
        kernel,
        in_specs=[pl.BlockSpec(memory_space=VMEM)] * len(operands),
        out_specs=jax.tree.map(lambda _: pl.BlockSpec(memory_space=VMEM), out_shape),
        out_shape=out_shape,
        scratch_shapes=scratch,
        compiler_params=pltpu.CompilerParams(vmem_limit_bytes=8 * 2**20),
        cost_estimate=pl.CostEstimate(flops=flops, bytes_accessed=2**20, transcendentals=0),
        name=name,
    )(*operands)


def call_own(gated, weight):
    block, width = gated.shape
    columns = weight.shape[1] // FACE
    return pl.pallas_call(
        functools.partial(own_kernel, columns),
        in_specs=[pl.BlockSpec(memory_space=VMEM), pl.BlockSpec(memory_space=pltpu.HBM)],
        out_specs=[pl.BlockSpec(memory_space=VMEM)] * 2,
        out_shape=[jax.ShapeDtypeStruct((block, columns), F32)] * 2,
        scratch_shapes=[
            VMEM((4, width, columns // 2), BF16),
            pltpu.SemaphoreType.DMA((4,)),
        ],
        compiler_params=pltpu.CompilerParams(vmem_limit_bytes=8 * 2**20),
        cost_estimate=pl.CostEstimate(
            flops=4 * block * width * columns, bytes_accessed=6 * width * columns, transcendentals=0
        ),
        name="own_channels",
    )(gated, pltpu.with_memory_space_constraint(weight, pltpu.HBM))


def split_shards(
    mixer_input,
    gate_branch,
    skip_gain,
    decay_rate,
    first_weight,
    first_bias,
    second_weight,
    second_bias,
    last_weight,
    output_weight,
):
    block, width = mixer_input.shape
    blocks = lax.axis_size("seq")
    outs = width // LANES

    along_seq = lambda part, k: lax.ppermute(part, "seq", [(s, s ^ k) for s in range(blocks)])
    def along_chan(part, turn):
        pairs = [
            (s * FACE + c, s * FACE + (c ^ rounds(s % 2)[turn]))
            for s in range(blocks)
            for c in range(FACE)
        ]
        return lax.ppermute(part, ("seq", "chan"), pairs)

    shape = jax.ShapeDtypeStruct

    xs, *gates, over = call_pack(mixer_input, gate_branch, output_weight, blocks, outs)
    xs = lax.all_to_all(xs, "seq", 0, 0, tiled=True)
    held = along_chan(over, 0)
    filters = call_filter(
        (first_weight, first_bias, second_weight, second_bias, last_weight, decay_rate),
        skip_gain,
        gate_branch,
        blocks,
        outs,
        block,
    )
    gates = [along_seq(gates[k - 1], k) for k in range(1, outs)]
    pieces = call_conv(xs, filters, gates, outs)
    pieces = [pieces[0]] + [along_seq(pieces[k], k) for k in range(1, outs)]
    gated = in_vmem(
        functools.partial(join_kernel, outs),
        pieces,
        shape((block, width), BF16),
        "join_pieces",
        10**6,
    )
    theirs = along_chan(gated, 0)
    send, keep = call_own(gated, output_weight)
    columns = send.shape[1]
    flops = 2 * block * width * columns
    send = in_vmem(
        functools.partial(neighbour_kernel, columns),
        [theirs, held, send],
        shape((block, columns), BF16),
        "sums_to_send",
        flops,
    )
    arrived = along_chan(send, 1)
    keep = in_vmem(
        functools.partial(neighbour_kernel, 0),
        [theirs, held, keep],
        shape((block, columns), F32),
        "sums_to_keep",
        flops,
    )
    return in_vmem(
        last_kernel, [keep, arrived], shape((block, columns), BF16), "last_sum", 10**6
    )


def contract_first(left_matrix, right_matrix):
    return lax.dot_general(
        left_matrix,
        right_matrix,
        (((0,), (0,)), ((), ())),
        precision=HIGHEST,
        preferred_element_type=F32,
    )


def filter_taps(
    first_weight, first_bias, second_weight, second_bias, last_weight, decay_rate, length
):
    features = jnp.asarray(feature_table(length, first_weight.shape[0]).T)
    hidden_one = jnp.sin(contract_first(first_weight, features) + first_bias[:, None])
    hidden_two = jnp.sin(contract_first(second_weight, hidden_one) + second_bias[:, None])
    shaped = contract_first(hidden_two, last_weight)
    positions = jnp.arange(length, dtype=jnp.int32).astype(F32)
    envelope = jnp.exp(-decay_rate[None, :] * (positions[:, None] / length))
    energy = jnp.expm1(-2.0 * decay_rate) / jnp.expm1(-2.0 * decay_rate / length)
    return shaped * envelope / jnp.sqrt(energy)[None, :]


def transform_tables(block_len):
    padded_len = 2 * block_len
    freq_index = jnp.arange(block_len + 1, dtype=jnp.int32)[:, None]
    time_index = jnp.arange(padded_len, dtype=jnp.int32)[None, :]
    angle = (freq_index * time_index % padded_len).astype(F32) * (2.0 * math.pi / padded_len)
    forward = jnp.concatenate([jnp.cos(angle), -jnp.sin(angle)], axis=0)
    later_angle = angle[:, block_len:]
    weights = jnp.where((freq_index == 0) | (freq_index == block_len), 1.0, 2.0) / padded_len
    inverse = jnp.concatenate(
        [(weights * jnp.cos(later_angle)).T, (-weights * jnp.sin(later_angle)).T], axis=1
    )
    return (forward, inverse)


def spectral_product(left_spec, right_spec, half_rows):
    left_real, left_imag = (left_spec[:half_rows], left_spec[half_rows:])
    right_real, right_imag = (right_spec[:half_rows], right_spec[half_rows:])
    return jnp.concatenate(
        [
            left_real * right_real - left_imag * right_imag,
            left_real * right_imag + left_imag * right_real,
        ],
        axis=0,
    )


def gathered_shards(
    mixer_input,
    gate_branch,
    skip_gain,
    decay_rate,
    first_weight,
    first_bias,
    second_weight,
    second_bias,
    last_weight,
    output_weight,
):
    block_len, chan_width = mixer_input.shape
    seq_count = lax.axis_size("seq")
    device = lax.axis_index("seq")
    half_rows = block_len + 1
    kernel_taps = filter_taps(
        first_weight,
        first_bias,
        second_weight,
        second_bias,
        last_weight,
        decay_rate,
        block_len * seq_count,
    )
    padded_taps = jnp.concatenate([jnp.zeros((block_len, chan_width), F32), kernel_taps], axis=0)
    forward, inverse = transform_tables(block_len)
    forward_head = forward[:, :block_len]
    gathered = lax.all_gather(mixer_input, "seq", axis=0, tiled=True)

    def one_block(block_index, total):
        rows = lax.dynamic_slice_in_dim(gathered, block_index * block_len, block_len, 0)
        source_spec = jnp.dot(
            forward_head, rows.astype(F32), precision=HIGHEST, preferred_element_type=F32
        )
        segment = lax.dynamic_slice_in_dim(
            padded_taps, (device - block_index) * block_len, 2 * block_len, 0
        )
        lag_spec = jnp.dot(forward, segment, precision=HIGHEST, preferred_element_type=F32)
        return total + spectral_product(lag_spec, source_spec, half_rows)

    total = lax.fori_loop(0, device + 1, one_block, jnp.zeros((2 * half_rows, chan_width), F32))
    convolved = jnp.dot(inverse, total, precision=HIGHEST, preferred_element_type=F32)
    values = mixer_input.astype(F32)
    gated_mix = (
        gate_branch.astype(F32) * (convolved + skip_gain[None, :] * values)
    ).astype(BF16)
    partial_out = jnp.dot(gated_mix, output_weight, preferred_element_type=F32)
    return lax.psum_scatter(partial_out, "chan", scatter_dimension=1, tiled=True).astype(BF16)


def solution(mesh):
    seq_count, chan_count = mesh.shape["seq"], mesh.shape["chan"]

    def shards(mixer_input, *rest):
        block, width = mixer_input.shape
        outs = width // LANES
        splits = (
            width % LANES == 0
            and block % LANES == 0
            and seq_count == 2 * outs
            and outs == 4
            and chan_count == FACE
        )
        plan = split_shards if splits else gathered_shards
        return plan(mixer_input, *rest)

    in_specs = (
        P("seq", "chan"),
        P("seq", "chan"),
        P("chan"),
        P("chan"),
        P(),
        P(),
        P(),
        P(),
        P(None, "chan"),
        P("chan", None),
    )
    out_specs = P("seq", "chan")
    return jax.shard_map(shards, mesh=mesh, in_specs=in_specs, out_specs=out_specs, check_vma=False)
```
